32 devices in a mesh: fsdp: 4 (over y, x), ctx: 8 (over z, core).
Axes of the slice: x: 2, y: 2, z: 4, core: 2. Of those that a mesh axis runs over, the one named last changes fastest.
Arguments:
- hidden_in: bfloat16 [4096, 2048], P(('fsdp', 'ctx')), may hold values from -6 to 6
- layer_vec: bfloat16 [4096, 256], P(('fsdp', 'ctx')), may hold values from -6 to 6
- positions: int32 [4096], P(('fsdp', 'ctx')), may hold values from 0 to 1023, as said below
- w_attn: bfloat16 [2048, 5248], P(('fsdp', 'ctx')), may hold values from -0.125 to 0.125
- w_mlp: bfloat16 [2048, 24576], P(('fsdp', 'ctx')), may hold values from -0.125 to 0.125
- pl_gate: bfloat16 [2048, 256], replicated, may hold values from -0.125 to 0.125
- pl_proj: bfloat16 [256, 2048], replicated, may hold values from -0.375 to 0.375
- gains: float32 [6, 2048], replicated, may hold values from 0.5 to 1.5
- head_gains: float32 [2, 256], replicated, may hold values from 0.25 to 0.5
- out_grad: bfloat16 [4096, 2048], P(('fsdp', 'ctx')), may hold values from -6 to 6
Outputs:
- hidden_out: bfloat16 [4096, 2048], P(('fsdp', 'ctx'))
- hidden_in_grad: float32 [4096, 2048], P(('fsdp', 'ctx'))
- layer_vec_grad: float32 [4096, 256], P(('fsdp', 'ctx'))
- w_attn_grad: float32 [2048, 5248], P(('fsdp', 'ctx'))
- w_mlp_grad: float32 [2048, 24576], P(('fsdp', 'ctx'))
- pl_gate_grad: float32 [2048, 256], replicated
- pl_proj_grad: float32 [256, 2048], replicated
- gains_grad: float32 [6, 2048], replicated
- head_gains_grad: float32 [2, 256], replicated
The draws below stay inside these ranges and needn't reach their ends.
Inputs may be any that keep to these rules, and one draw needn't show every extreme that they name: `positions`: each of the 4 packed rows of 1024 tokens holds whole documents; a position is 0 at a row's first token and at each document's first token and rises by one along a document. In every row one document starts within the row's first 128 tokens and ends at the row's last token; in one row it starts at the row's first token.
All inputs are finite; a program needn't handle non-finite values.
Results may differ from the reference program's by a relative error of at most 0.02.
Values may be sent and summed in bfloat16 or wider, within the bound.
A program may use at most 384 MiB of HBM per device.

```python
import math
import jax
import jax.numpy as jnp
from jax import lax

D = 2048
FF = 8192
QH = 8
KVH = 2
HEAD = 256
RANK = 64
PL = 256
WINDOW = 512
TOK_DEV = 128
TOKENS = 4096
ATTN_COLS = 5248
MLP_COLS = 24576
N_FSDP = 4
N_CTX = 8


def draw_positions(key, part):
    key = jax.random.fold_in(key, 11)
    row_total = TOK_DEV * N_CTX
    random_ints = jax.random.randint(jax.random.fold_in(key, 1), (N_FSDP, row_total), 0, 2 * WINDOW)
    long_starts = jax.random.randint(jax.random.fold_in(key, 2), (N_FSDP, 1), 1, max(2, TOK_DEV // 2))
    chosen_row = jax.random.randint(jax.random.fold_in(key, 3), (), 0, N_FSDP)
    row_ids = jnp.arange(N_FSDP, dtype=jnp.int32)[:, None]
    long_starts = jnp.where(row_ids == chosen_row, 0, long_starts).astype(jnp.int32)
    index_row = jnp.arange(row_total, dtype=jnp.int32)[None, :]
    begins = (random_ints == 0) & (index_row < long_starts) | (index_row == 0) | (index_row == long_starts)
    latest = lax.cummax(jnp.where(begins, index_row, 0), axis=1)
    return (index_row - latest).reshape(N_FSDP * row_total).astype(jnp.int32)


def levels(rng, dims, cuts, low, high):
    gain = 1.0
    for position, blocks in cuts:
        heights = jax.random.uniform(jax.random.fold_in(jax.random.fold_in(rng, 6), position), (blocks,), jnp.float32, low / len(cuts), high / len(cuts))
        gain = gain * jnp.repeat(jnp.exp(heights), dims[position] // blocks).reshape((-1,) + (1,) * (len(dims) - 1 - position))
    return gain


def normal_values(key, dims, deviation, bound, split=(), kind=jnp.bfloat16):
    array = deviation * jax.random.normal(key, dims, jnp.float32)
    if split:
        array = array * levels(key, dims, split, -0.22, 0.18)
    return jnp.clip(array, -bound, bound).astype(kind)


def setup_inputs(seed: int = 0) -> dict:
    key_list = jax.random.split(jax.random.key(seed), 11)
    return {
        "hidden_in": normal_values(key_list[0], (TOKENS, D), 1.0, 6.0, ((0, 32),)),
        "layer_vec": normal_values(key_list[1], (TOKENS, PL), 1.0, 6.0, ((0, 32),)),
        "positions": draw_positions(jax.random.fold_in(key_list[10], 71), 0),
        "w_attn": normal_values(key_list[3], (D, ATTN_COLS), D ** -0.5, 0.125, ((0, 32),)),
        "w_mlp": normal_values(key_list[4], (D, MLP_COLS), D ** -0.5, 0.125, ((0, 32),)),
        "pl_gate": normal_values(key_list[5], (D, PL), D ** -0.5, 0.125),
        "pl_proj": normal_values(key_list[6], (PL, D), PL ** -0.5, 0.375),
        "gains": jnp.clip(1.0 + 0.1 * jax.random.normal(key_list[7], (6, D), jnp.float32), 0.5, 1.5),
        "head_gains": jnp.clip(jnp.exp(jax.random.uniform(key_list[8], (2, HEAD), jnp.float32, math.log(0.25), math.log(0.5))), 0.25, 0.5),
        "out_grad": normal_values(key_list[9], (TOKENS, D), 1.0, 6.0, ((0, 32),)),
    }


EPSILON = 1e-06
THETA = 10000.0
NEG_LARGE = -1e+30
HIGHEST = lax.Precision.HIGHEST

@jax.custom_vjp
def low(v):
    return lax.optimization_barrier(v.astype(jnp.bfloat16)).astype(jnp.float32)

@jax.custom_vjp
def low_back(v):
    return v

def low_keep(v):
    return (low(v), None)

def low_pass(kept, grad):
    return (grad,)

def back_keep(v):
    return (v, None)

def back_low(kept, grad):
    return (low(grad),)
low.defvjp(low_keep, low_pass)
low_back.defvjp(back_keep, back_low)

def rms_norm(values, scale_vec):
    return values * lax.rsqrt(lax.optimization_barrier(jnp.mean(values * values, axis=-1, keepdims=True)) + EPSILON) * scale_vec

def rotary(values, positions):
    half_size = values.shape[-1] // 2
    frequency = jnp.exp(jnp.arange(half_size, dtype=jnp.float32) * (-2.0 * math.log(THETA) / values.shape[-1]))
    angles = positions.astype(jnp.float32)[:, None] * frequency[None, :]
    cosine = jnp.cos(angles)[:, None, :]
    sine_part = jnp.sin(angles)[:, None, :]
    first_half = values[..., :half_size]
    second_half = values[..., half_size:]
    return jnp.concatenate([first_half * cosine - second_half * sine_part, second_half * cosine + first_half * sine_part], axis=-1)

def attend_block(queries, keys_pad, values_pad, block_pos):
    block_rows = queries.shape[0]
    span_rows = keys_pad.shape[0]
    scores = jnp.einsum('qgrd,kgd->grqk', queries, keys_pad, precision=HIGHEST)
    scores = low_back(scores)
    distance = jnp.arange(block_rows, dtype=jnp.int32)[:, None] + WINDOW - jnp.arange(span_rows, dtype=jnp.int32)[None, :]
    reach = jnp.minimum(block_pos, WINDOW - 1)[:, None]
    allowed = (distance >= 0) & (distance <= reach)
    scores = jnp.where(allowed[None, None], scores, NEG_LARGE)
    weights_soft = low(jax.nn.softmax(scores, axis=-1))
    return jnp.einsum('grqk,kgd->qgrd', weights_soft, values_pad, precision=HIGHEST)

def attention(queries, keys, values, positions):
    row_total = queries.shape[0]
    block_rows = min(512, row_total)
    block_count = row_total // block_rows
    keys_padded = jnp.pad(keys, ((WINDOW, 0), (0, 0), (0, 0)))
    values_padded = jnp.pad(values, ((WINDOW, 0), (0, 0), (0, 0)))
    checked = jax.checkpoint(attend_block)

    def one_block(block_index):
        offset = (block_index * block_rows).astype(jnp.int32)
        q_block = lax.dynamic_slice_in_dim(queries, offset, block_rows, 0)
        k_block = lax.dynamic_slice_in_dim(keys_padded, offset, block_rows + WINDOW, 0)
        v_block = lax.dynamic_slice_in_dim(values_padded, offset, block_rows + WINDOW, 0)
        p_block = lax.dynamic_slice_in_dim(positions, offset, block_rows, 0)
        return checked(q_block, k_block, v_block, p_block)
    blocks_out = lax.map(one_block, jnp.arange(block_count, dtype=jnp.int32))
    return blocks_out.reshape(row_total, QH * HEAD)

def layer_forward(hidden, vector_in, w_attn, w_mlp, pl_gate, pl_proj, gains, head_gains, seq_positions):
    row_total = hidden.shape[0]
    q_width = QH * HEAD
    kv_width = KVH * HEAD
    in_cols = q_width + 2 * kv_width + RANK
    normed_in = rms_norm(hidden, gains[0])
    projected = low_back(jnp.dot(low(normed_in), w_attn[:, :in_cols], precision=HIGHEST))
    q_raw = projected[:, :q_width].reshape(row_total, QH, HEAD)
    k_raw = projected[:, q_width:q_width + kv_width].reshape(row_total, KVH, HEAD)
    v_raw = projected[:, q_width + kv_width:q_width + 2 * kv_width].reshape(row_total, KVH, HEAD)
    latent = low(projected[:, q_width + 2 * kv_width:])
    queries = low(rotary(rms_norm(q_raw, head_gains[0]), seq_positions))
    keys = low(rotary(rms_norm(k_raw, head_gains[1]), seq_positions))
    values = low(rms_norm(v_raw, 1.0))
    grouped = queries.reshape(row_total, KVH, QH // KVH, HEAD)
    mixed = low(low_back(attention(grouped, keys, values, seq_positions)))
    laurel_up = low_back(jnp.dot(latent, w_attn[:, in_cols:in_cols + RANK].T, precision=HIGHEST))
    attn_out = low_back(jnp.dot(mixed, w_attn[:, in_cols + RANK:].T, precision=HIGHEST))
    laurel_res = normed_in + rms_norm(laurel_up, gains[1])
    after_attn = hidden + rms_norm(attn_out, gains[2])
    joined = (after_attn + laurel_res) / math.sqrt(2.0)
    ffn_in = low(rms_norm(joined, gains[3]))
    gate_up = low_back(jnp.dot(ffn_in, w_mlp[:, :2 * FF], precision=HIGHEST))
    activated = low(jax.nn.gelu(gate_up[:, :FF], approximate=True) * gate_up[:, FF:])
    ffn_out = low_back(jnp.dot(activated, w_mlp[:, 2 * FF:].T, precision=HIGHEST))
    after_ffn = joined + rms_norm(ffn_out, gains[4])
    vec_gate = low_back(jnp.dot(low(after_ffn), pl_gate, precision=HIGHEST))
    vec_mixed = low(jax.nn.gelu(vec_gate, approximate=True) * vector_in)
    vec_out = low_back(jnp.dot(vec_mixed, pl_proj, precision=HIGHEST))
    return after_ffn + rms_norm(vec_out, gains[5])

def reference(hidden_in, layer_vec, positions, w_attn, w_mlp, pl_gate, pl_proj, gains, head_gains, out_grad):
    row_total = TOK_DEV * N_CTX
    weight_list = (w_attn.astype(jnp.float32), w_mlp.astype(jnp.float32), pl_gate.astype(jnp.float32), pl_proj.astype(jnp.float32), gains.astype(jnp.float32), head_gains.astype(jnp.float32))

    def one_sequence(grad_sums, seq_index):
        offset = (seq_index * row_total).astype(jnp.int32)
        hidden = lax.dynamic_slice_in_dim(hidden_in, offset, row_total, 0).astype(jnp.float32)
        vector_in = lax.dynamic_slice_in_dim(layer_vec, offset, row_total, 0).astype(jnp.float32)
        seq_positions = lax.dynamic_slice_in_dim(positions, offset, row_total, 0)
        cotangent = lax.dynamic_slice_in_dim(out_grad, offset, row_total, 0).astype(jnp.float32)

        def forward(hidden_val, vector_val, attn_val, mlp_val, gate_val, proj_val, gain_val, head_val):
            return layer_forward(hidden_val, vector_val, attn_val, mlp_val, gate_val, proj_val, gain_val, head_val, seq_positions)
        output, pullback = jax.vjp(forward, hidden, vector_in, weight_list[0], weight_list[1], weight_list[2], weight_list[3], weight_list[4], weight_list[5])
        grads = pullback(cotangent)
        new_sums = tuple((total + part for total, part in zip(grad_sums, grads[2:])))
        return (new_sums, (output.astype(jnp.bfloat16), grads[0], grads[1]))
    zero_sums = tuple((jnp.zeros(weight.shape, jnp.float32) for weight in weight_list))
    grad_sums, stacked = lax.scan(one_sequence, zero_sums, jnp.arange(N_FSDP, dtype=jnp.int32))
    return (stacked[0].reshape(TOKENS, D), stacked[1].reshape(TOKENS, D), stacked[2].reshape(TOKENS, PL), grad_sums[0], grad_sums[1], grad_sums[2], grad_sums[3], grad_sums[4], grad_sums[5])
```

```python
import math

import jax
import jax.numpy as jnp
from jax import lax
from jax.experimental import pallas as pl
from jax.experimental.pallas import tpu as pltpu
from jax.sharding import PartitionSpec as P

QH = 8
KVH = 2
HEAD = 256
RANK = 64
WINDOW = 512


EPSILON = 1e-06
THETA = 10000.0
NEG_LARGE = -1e30


def passed_along(block, axis, distance):
    devices = range(lax.axis_size(axis))
    route = [(i - distance, i) for i in devices if i - distance in devices]
    return lax.ppermute(block, axis, route)


def rms_norm(values, scale_vec):
    return (
        values * lax.rsqrt(jnp.mean(values * values, axis=-1, keepdims=True) + EPSILON) * scale_vec
    )


def value_norm(values):
    return rms_norm(values, 1.0)


def rotary(values, positions):
    half_size = values.shape[-1] // 2
    frequency = jnp.exp(
        jnp.arange(half_size, dtype=jnp.float32) * (-2.0 * math.log(THETA) / values.shape[-1])
    )
    angles = positions.astype(jnp.float32)[:, None] * frequency[None, :]
    cosine = jnp.cos(angles)[:, None, :]
    sine_part = jnp.sin(angles)[:, None, :]
    first_half = values[..., :half_size]
    second_half = values[..., half_size:]
    return jnp.concatenate(
        [
            first_half * cosine - second_half * sine_part,
            second_half * cosine + first_half * sine_part,
        ],
        axis=-1,
    )


def plain_dot(left_side, right_side):
    return jnp.dot(left_side, right_side, preferred_element_type=jnp.float32)


def times_transposed(left_side, right_side):
    return lax.dot_general(
        left_side, right_side, (((1,), (1,)), ((), ())), preferred_element_type=jnp.float32
    )


def contract_rows(left_side, right_side):
    return lax.dot_general(
        left_side, right_side, (((0,), (0,)), ((), ())), preferred_element_type=jnp.float32
    )


def activate(gate_up_val):
    half_cols = gate_up_val.shape[1] // 2
    return jax.nn.gelu(gate_up_val[:, :half_cols], approximate=True) * gate_up_val[:, half_cols:]


def vec_mix(gate_val, vector_val):
    return jax.nn.gelu(gate_val, approximate=True) * vector_val


def per_device(
    hidden_in, layer_vec, positions, w_attn, w_mlp, pl_gate, pl_proj, gains, head_gains, out_grad
):
    row_count = hidden_in.shape[0]
    model_width = hidden_in.shape[1]
    q_width = QH * HEAD
    kv_width = KVH * HEAD
    in_cols = q_width + 2 * kv_width + RANK
    group_size = QH // KVH
    ff_width = w_mlp.shape[1] // 3
    shard_height = w_mlp.shape[0]
    fsdp_count = lax.axis_size("fsdp")
    ctx_count = lax.axis_size("ctx")
    quarter = ff_width // fsdp_count

    def permute_cols(matrix):
        return (
            matrix.reshape(-1, fsdp_count, ctx_count, shard_height)
            .transpose(0, 2, 1, 3)
            .reshape(-1, model_width)
        )

    def restore_cols(matrix):
        return (
            matrix.reshape(-1, ctx_count, fsdp_count, shard_height)
            .transpose(0, 2, 1, 3)
            .reshape(-1, model_width)
        )

    def qk_prep(raw_heads, scale_vec):
        return rotary(rms_norm(raw_heads, scale_vec), positions)

    hidden = hidden_in.astype(jnp.float32)
    normed_in = rms_norm(hidden, gains[0])
    normed_low = normed_in.astype(jnp.bfloat16)
    projected = plain_dot(
        normed_low, lax.all_gather(w_attn[:, :in_cols], ("fsdp", "ctx"), axis=0, tiled=True)
    )
    q_raw = projected[:, :q_width].reshape(row_count, QH, HEAD)
    k_raw = projected[:, q_width : q_width + kv_width].reshape(row_count, KVH, HEAD)
    v_raw = projected[:, q_width + kv_width : q_width + 2 * kv_width].reshape(row_count, KVH, HEAD)
    latent = projected[:, q_width + 2 * kv_width :].astype(jnp.bfloat16)
    queries = qk_prep(q_raw, head_gains[0]).astype(jnp.bfloat16)
    keys_own = qk_prep(k_raw, head_gains[1]).astype(jnp.bfloat16)
    values_own = value_norm(v_raw).astype(jnp.bfloat16)
    kv_own = jnp.concatenate(
        [keys_own.reshape(row_count, kv_width), values_own.reshape(row_count, kv_width)], axis=1
    )
    hop_count = (WINDOW - 1) // row_count + 1
    earlier = []
    moving = kv_own
    for step_back in range(hop_count):
        moving = passed_along(moving, "ctx", 1)
        earlier.append(moving)
    kv_all = jnp.concatenate(earlier[::-1] + [kv_own], axis=0)
    span_rows = kv_all.shape[0]
    keys_all = kv_all[:, :kv_width].reshape(span_rows, KVH, HEAD)
    values_all = kv_all[:, kv_width:].reshape(span_rows, KVH, HEAD)
    grouped = queries.reshape(row_count, KVH, group_size, HEAD)
    distance = (
        jnp.arange(row_count, dtype=jnp.int32)[:, None]
        + hop_count * row_count
        - jnp.arange(span_rows, dtype=jnp.int32)[None, :]
    )
    allowed = (distance >= 0) & (distance <= jnp.minimum(positions, WINDOW - 1)[:, None])
    scores = jnp.einsum("qgrd,kgd->grqk", grouped, keys_all, preferred_element_type=jnp.float32)
    scores = jnp.where(allowed[None, None], scores, NEG_LARGE)
    row_max = jnp.max(scores, axis=-1, keepdims=True)
    exp_scores = jnp.exp(scores - row_max)
    row_sum = jnp.sum(exp_scores, axis=-1, keepdims=True)
    log_total = row_max + jnp.log(row_sum)
    probs_low = (exp_scores / row_sum).astype(jnp.bfloat16)
    mixed = jnp.einsum("grqk,kgd->qgrd", probs_low, values_all, preferred_element_type=jnp.float32)
    mixed = mixed.reshape(row_count, q_width).astype(jnp.bfloat16)
    shard_rows = lax.all_gather(w_attn[:, in_cols:], ("fsdp", "ctx"), axis=0, tiled=True)
    laurel_part = times_transposed(latent, shard_rows[:, :RANK])
    attn_part = times_transposed(mixed, shard_rows[:, RANK:])
    out_pair = jnp.stack([laurel_part, attn_part], axis=1)
    laurel_up = out_pair[:, 0]
    attn_out = out_pair[:, 1]
    laurel_res = normed_in + rms_norm(laurel_up, gains[1])
    after_attn = hidden + rms_norm(attn_out, gains[2])
    joined = (after_attn + laurel_res) / math.sqrt(2.0)
    ffn_low = rms_norm(joined, gains[3]).astype(jnp.bfloat16)
    sent_rows = w_mlp.reshape(shard_height, 3, fsdp_count, quarter)
    sent_tokens = jnp.broadcast_to(
        ffn_low[:, None, None, :], (row_count, 1, fsdp_count, model_width)
    )
    got_rows, got_tokens = (
        lax.all_to_all(sent_rows, "fsdp", split_axis=2, concat_axis=0, tiled=True),
        lax.all_to_all(sent_tokens, "fsdp", split_axis=2, concat_axis=0, tiled=True),
    )
    quarter_rows = lax.all_gather(got_rows, "ctx", axis=0, tiled=True).reshape(
        model_width, 3, quarter
    )
    w_gate_up = quarter_rows[:, :2].reshape(model_width, 2 * quarter)
    w_down = quarter_rows[:, 2]
    ffn_perm = permute_cols(got_tokens.reshape(fsdp_count * row_count, model_width))
    gate_up = plain_dot(ffn_perm, w_gate_up)
    activated = activate(gate_up).astype(jnp.bfloat16)
    ffn_out = lax.psum_scatter(
        restore_cols(times_transposed(activated, w_down)), "fsdp", scatter_dimension=0, tiled=True
    )
    after_ffn = joined + rms_norm(ffn_out, gains[4])
    after_low = after_ffn.astype(jnp.bfloat16)
    vec_gate = plain_dot(after_low, pl_gate)
    vector_in = layer_vec.astype(jnp.float32)
    vec_mixed = vec_mix(vec_gate, vector_in).astype(jnp.bfloat16)
    vec_out = plain_dot(vec_mixed, pl_proj)
    result_out = after_ffn + rms_norm(vec_out, gains[5])
    upstream = out_grad.astype(jnp.float32)
    unused_out, vec_norm_back = jax.vjp(rms_norm, vec_out, gains[5])
    d_vec_out, d_gain_vec = vec_norm_back(upstream)
    d_vec_out_low = d_vec_out.astype(jnp.bfloat16)
    d_vec_mixed = times_transposed(d_vec_out_low, pl_proj)
    grad_pl_proj = contract_rows(vec_mixed, d_vec_out_low)
    unused_out, mix_back = jax.vjp(vec_mix, vec_gate, vector_in)
    d_vec_gate, d_vector_in = mix_back(d_vec_mixed)
    d_vec_gate_low = d_vec_gate.astype(jnp.bfloat16)
    grad_after = upstream + times_transposed(d_vec_gate_low, pl_gate)
    grad_pl_gate = contract_rows(after_low, d_vec_gate_low)
    unused_out, ffn_norm_back = jax.vjp(rms_norm, ffn_out, gains[4])
    d_ffn_out, d_gain_ffn = ffn_norm_back(grad_after)
    d_ffn_low = d_ffn_out.astype(jnp.bfloat16)
    unused_out, act_back = jax.vjp(activate, gate_up)
    d_ffn_all = lax.all_gather(d_ffn_low, "fsdp", axis=0, tiled=True)
    d_ffn_perm = permute_cols(d_ffn_all)
    d_activated = plain_dot(d_ffn_perm, w_down)
    d_gate_up = act_back(d_activated)[0].astype(jnp.bfloat16)
    d_ffn_in = lax.psum_scatter(
        restore_cols(times_transposed(d_gate_up, w_gate_up)).astype(jnp.bfloat16),
        "fsdp",
        scatter_dimension=0,
        tiled=True,
    ).astype(jnp.float32)
    summed = lax.psum_scatter(
        jnp.concatenate(
            [contract_rows(ffn_perm, d_gate_up), contract_rows(d_ffn_perm, activated)], axis=1
        ).astype(jnp.bfloat16),
        "ctx",
        scatter_dimension=0,
        tiled=True,
    ).astype(jnp.float32)
    grad_w_mlp = (
        lax.all_to_all(
            summed.reshape(fsdp_count * shard_height, 3, 1, quarter).astype(jnp.bfloat16),
            "fsdp",
            split_axis=0,
            concat_axis=2,
            tiled=True,
        )
        .astype(jnp.float32)
        .reshape(shard_height, 3 * ff_width)
    )
    unused_out, pre_norm_back = jax.vjp(rms_norm, joined, gains[3])
    d_joined_part, d_gain_pre = pre_norm_back(d_ffn_in)
    d_joined = grad_after + d_joined_part
    d_half = d_joined / math.sqrt(2.0)
    unused_out, laurel_norm_back = jax.vjp(rms_norm, laurel_up, gains[1])
    d_laurel_up, d_gain_laurel = laurel_norm_back(d_half)
    unused_out, attn_norm_back = jax.vjp(rms_norm, attn_out, gains[2])
    d_attn_out, d_gain_attn = attn_norm_back(d_half)
    d_laurel_low = d_laurel_up.astype(jnp.bfloat16)
    d_attn_low = d_attn_out.astype(jnp.bfloat16)
    shard_rows = lax.all_gather(w_attn[:, in_cols:], ("fsdp", "ctx"), axis=0, tiled=True)
    d_latent = plain_dot(d_laurel_low, shard_rows[:, :RANK])
    d_mixed = plain_dot(d_attn_low, shard_rows[:, RANK:])
    d_grouped = d_mixed.astype(jnp.bfloat16).reshape(row_count, KVH, group_size, HEAD)
    again = jnp.einsum("qgrd,kgd->grqk", grouped, keys_all, preferred_element_type=jnp.float32)
    again = jnp.where(allowed[None, None], again, NEG_LARGE)
    probs = jnp.exp(again - log_total)
    d_probs = jnp.einsum(
        "qgrd,kgd->grqk", d_grouped, values_all, preferred_element_type=jnp.float32
    )
    inner_sum = jnp.sum(probs * d_probs, axis=-1, keepdims=True)
    d_scores = (probs * (d_probs - inner_sum)).astype(jnp.bfloat16)
    d_queries = jnp.einsum(
        "grqk,kgd->qgrd", d_scores, keys_all, preferred_element_type=jnp.float32
    ).reshape(row_count, QH, HEAD)
    d_keys_all = jnp.einsum("grqk,qgrd->kgd", d_scores, grouped, preferred_element_type=jnp.float32)
    d_values_all = jnp.einsum(
        "grqk,qgrd->kgd", probs.astype(jnp.bfloat16), d_grouped, preferred_element_type=jnp.float32
    )
    d_kv_all = jnp.concatenate(
        [d_keys_all.reshape(span_rows, kv_width), d_values_all.reshape(span_rows, kv_width)], axis=1
    )
    returned = d_kv_all[:row_count]
    for step_back in range(1, hop_count + 1):
        returned = (
            passed_along(returned.astype(jnp.bfloat16), "ctx", -1).astype(returned.dtype)
            + d_kv_all[step_back * row_count : (step_back + 1) * row_count]
        )
    d_keys_own = returned[:, :kv_width].reshape(row_count, KVH, HEAD)
    d_values_own = returned[:, kv_width:].reshape(row_count, KVH, HEAD)
    unused_out, query_back = jax.vjp(qk_prep, q_raw, head_gains[0])
    d_q_raw, d_head_query = query_back(d_queries)
    unused_out, key_back = jax.vjp(qk_prep, k_raw, head_gains[1])
    d_k_raw, d_head_key = key_back(d_keys_own)
    unused_out, value_back = jax.vjp(value_norm, v_raw)
    d_v_raw = value_back(d_values_own)[0]
    d_projected = jnp.concatenate(
        [
            d_q_raw.reshape(row_count, q_width),
            d_k_raw.reshape(row_count, kv_width),
            d_v_raw.reshape(row_count, kv_width),
            d_latent,
        ],
        axis=1,
    ).astype(jnp.bfloat16)
    d_normed_part = times_transposed(
        d_projected, lax.all_gather(w_attn[:, :in_cols], ("fsdp", "ctx"), axis=0, tiled=True)
    )
    unused_out, input_norm_back = jax.vjp(rms_norm, hidden, gains[0])
    d_hidden_part, d_gain_input = input_norm_back(d_half + d_normed_part)
    grad_hidden = d_half + d_hidden_part
    grad_w_attn = lax.psum_scatter(
        jnp.concatenate(
            [
                contract_rows(normed_low, d_projected),
                contract_rows(d_laurel_low, latent),
                contract_rows(d_attn_low, mixed),
            ],
            axis=1,
        ),
        ("fsdp", "ctx"),
        scatter_dimension=0,
        tiled=True,
    )
    gain_rows = jnp.stack(
        [d_gain_input, d_gain_laurel, d_gain_attn, d_gain_pre, d_gain_ffn, d_gain_vec]
    )
    head_rows = jnp.stack([d_head_query, d_head_key])
    grad_gains, grad_heads, grad_gate_all, grad_proj_all = lax.psum(
        (gain_rows, head_rows, grad_pl_gate, grad_pl_proj), ("fsdp", "ctx")
    )
    return (
        result_out.astype(jnp.bfloat16),
        grad_hidden,
        d_vector_in,
        grad_w_attn,
        grad_w_mlp,
        grad_gate_all,
        grad_proj_all,
        grad_gains,
        grad_heads,
    )

MESH = pl.DeviceIdType.MESH
VMEM_LIMIT = 60 * 1024 * 1024
ORDER = ((0, 0), (0, 1), (1, 0), (1, 1), (3, 0), (3, 1), (2, 0), (2, 1))


class Place:
    def __init__(self):
        self.f = lax.axis_index("fsdp")
        self.c = lax.axis_index("ctx")
        self.z = self.c // 2
        self.k = self.c % 2
        self.x_side = self.f + 1 - 2 * (self.f % 2)
        self.y_side = (self.f + 2) % 4
        self.diag = 3 - self.f
        self.sibling = (self.f, self.c + 1 - 2 * self.k)
        self.up = (self.f, self.c + 2)
        self.down = (self.f, self.c - 2)
        self.has_up = self.z < 3
        self.has_down = self.z > 0

    def peer(self, i):
        dz, dk = ORDER[i]
        return ((self.z + dz) % 4) * 2 + (self.k + dk) % 2

    def origin(self, i):
        dz, dk = ORDER[i]
        return ((self.z + 4 - dz) % 4) * 2 + (self.k + 2 - dk) % 2


def rows_at(start, count):
    return pl.ds(pl.multiple_of(start, 16), count)


def cols_at(start, count):
    return pl.ds(pl.multiple_of(start, 128), count)


def remote(src, dst, send_sem, recv_sem, target):
    return pltpu.make_async_remote_copy(
        src_ref=src,
        dst_ref=dst,
        send_sem=send_sem,
        recv_sem=recv_sem,
        device_id=target,
        device_id_type=MESH,
    )


def greet(place, line, plane):
    barrier = pltpu.get_barrier_semaphore()
    count = 0

    def tell(target):
        pl.semaphore_signal(barrier, inc=1, device_id=target, device_id_type=MESH)

    if line == "all":
        for i in range(1, 8):
            tell((place.f, place.peer(i)))
        count += 7
    elif line == "chain":
        for i in (1, 2, 4):
            tell((place.f, place.peer(i)))
        count += 3
    if plane:
        tell((place.x_side, place.c))
        tell((place.y_side, place.c))
        count += 2
    pl.semaphore_wait(barrier, count)


class ChainGather:
    SEMS = [pltpu.SemaphoreType.DMA((2, 10)), pltpu.SemaphoreType.DMA((1,))]

    def __init__(self, place, own, out, sems):
        self.place, self.own, self.out = place, own, out
        self.sems, self.local_sem = sems
        self.rows = own.shape[0]

    def block(self, origin_z, core=None):
        core = self.place.k if core is None else core
        return self.out.at[rows_at((origin_z * 2 + core) * self.rows, self.rows)]

    def copy(self, src, dst, index, target):
        return remote(src, dst, self.sems.at[0, index], self.sems.at[1, index], target)

    def local(self):
        return pltpu.make_async_copy(self.own, self.block(self.place.z), self.local_sem.at[0])

    def upward(self, step):
        src = self.own if step == 0 else self.block(self.place.z - step)
        return self.copy(src, self.block(self.place.z - step), step, self.place.up)

    def downward(self, step):
        src = self.own if step == 0 else self.block(self.place.z + step)
        return self.copy(src, self.block(self.place.z + step), 3 + step, self.place.down)

    def across(self, origin_z, own=False):
        src = self.own if own else self.block(origin_z)
        return self.copy(src, self.block(origin_z), 6 + origin_z, self.place.sibling)

    def start(self):
        place = self.place

        @pl.when(place.has_up)
        def _():
            self.upward(0).start()

        @pl.when(place.has_down)
        def _():
            self.downward(0).start()

        self.across(place.z, True).start()
        self.local().start()

    def step(self, step):
        place = self.place

        @pl.when(place.z - step >= 0)
        def _():
            self.copy(self.own, self.block(place.z - step), step - 1, place.up).wait_recv()
            if step < 3:

                @pl.when(place.has_up)
                def _():
                    self.upward(step).start()

            self.across(place.z - step).start()

        @pl.when(place.z + step <= 3)
        def _():
            self.copy(self.own, self.block(place.z + step), 3 + step - 1, place.down).wait_recv()
            if step < 3:

                @pl.when(place.has_down)
                def _():
                    self.downward(step).start()

            self.across(place.z + step).start()

    def finish(self):
        place = self.place
        for origin in range(4):
            copy = self.copy(
                self.own, self.block(origin, 1 - place.k), 6 + origin, place.sibling
            )
            copy.wait_recv()
            copy.wait_send()
        for step in range(3):

            @pl.when((place.z - step >= 0) & place.has_up)
            def _(step=step):
                self.upward(step).wait_send()

            @pl.when((place.z + step <= 3) & place.has_down)
            def _(step=step):
                self.downward(step).wait_send()

        self.local().wait()


class ChainScatter:
    @staticmethod
    def scratch(rows, cols):
        return [
            pltpu.VMEM((4, rows, cols), jnp.bfloat16),
            pltpu.VMEM((6, rows, cols), jnp.bfloat16),
            pltpu.VMEM((6, rows, cols), jnp.bfloat16),
            pltpu.SemaphoreType.DMA((2, 10)),
        ]

    def __init__(self, place, partial, scratch):
        self.place, self.partial = place, partial
        self.from_sibling, self.arrived, self.going, self.sems = scratch
        self.rows = partial.shape[0] // 8

    def block(self, origin_z, core):
        return self.partial.at[rows_at((origin_z * 2 + core) * self.rows, self.rows)]

    def across(self, dest):
        return remote(
            self.block(dest, 1 - self.place.k),
            self.from_sibling.at[dest],
            self.sems.at[0, 6 + dest],
            self.sems.at[1, 6 + dest],
            self.place.sibling,
        )

    def moved(self, slot, target):
        return remote(
            self.going.at[slot],
            self.arrived.at[slot],
            self.sems.at[0, slot],
            self.sems.at[1, slot],
            target,
        )

    def start(self):
        for dest in (3, 0, 2, 1):
            self.across(dest).start()

    def pair_sum(self, dest):
        return self.block(dest, self.place.k)[...].astype(jnp.float32) + self.from_sibling[
            dest
        ].astype(jnp.float32)

    def step(self, i):
        place = self.place
        top, bottom = 3 - i, i

        @pl.when(place.z < top)
        def _():
            slot = top - 1
            self.across(top).wait_recv()
            total = self.pair_sum(top)

            @pl.when(place.z == 0)
            def _():
                self.going[slot] = total.astype(jnp.bfloat16)

            @pl.when(place.z > 0)
            def _():
                self.moved(slot, place.up).wait_recv()
                self.going[slot] = (total + self.arrived[slot].astype(jnp.float32)).astype(
                    jnp.bfloat16
                )

            self.moved(slot, place.up).start()

        @pl.when(place.z > bottom)
        def _():
            slot = 3 + bottom
            self.across(bottom).wait_recv()
            total = self.pair_sum(bottom)

            @pl.when(place.z == 3)
            def _():
                self.going[slot] = total.astype(jnp.bfloat16)

            @pl.when(place.z < 3)
            def _():
                self.moved(slot, place.down).wait_recv()
                self.going[slot] = (total + self.arrived[slot].astype(jnp.float32)).astype(
                    jnp.bfloat16
                )

            self.moved(slot, place.down).start()

    def finish(self, out):
        place = self.place
        for dest in range(4):

            @pl.when(place.z == dest)
            def _(dest=dest):
                self.across(dest).wait_recv()
                total = self.pair_sum(dest)
                if dest > 0:
                    self.moved(dest - 1, place.up).wait_recv()
                    total = total + self.arrived[dest - 1].astype(jnp.float32)
                if dest < 3:
                    self.moved(3 + dest, place.down).wait_recv()
                    total = total + self.arrived[3 + dest].astype(jnp.float32)
                out[...] = total

        for dest in range(4):
            self.across(dest).wait_send()
        for i in range(3):
            top, bottom = 3 - i, i

            @pl.when(place.z < top)
            def _(top=top):
                self.moved(top - 1, place.up).wait_send()

            @pl.when(place.z > bottom)
            def _(bottom=bottom):
                self.moved(3 + bottom, place.down).wait_send()


class Spread:
    @staticmethod
    def sems(pieces, outs):
        return [
            pltpu.SemaphoreType.DMA((2, 8, pieces)),
            pltpu.SemaphoreType.DMA((2, 4, 8, outs)),
        ]

    def __init__(self, place, weight, outs, pieces, sems):
        self.place, self.weight, self.outs, self.pieces = place, weight, outs, pieces
        self.swap_sems, self.plane_sems = sems
        self.rows = weight.shape[0]

    def spot(self, f, c):
        return (f * 8 + c) * self.rows

    def swap(self, i, p, origin):
        column, width, out, out_column = self.pieces[p]
        peer = self.place.peer(i)
        src = self.weight.at[:, cols_at(column(peer), width)]
        dst = self.outs[out].at[
            rows_at(self.spot(self.place.f, origin), self.rows), pl.ds(out_column, width)
        ]
        if i == 0:
            return pltpu.make_async_copy(src, dst, self.swap_sems.at[0, 0, p])
        return remote(
            src,
            dst,
            self.swap_sems.at[0, i, p],
            self.swap_sems.at[1, i, p],
            (self.place.f, peer),
        )

    def whole(self, f, c, out):
        return self.outs[out].at[rows_at(self.spot(f, c), self.rows)]

    def part(self, f, c, out, half):
        count = self.rows // 2
        return self.outs[out].at[rows_at(self.spot(f, c) + half * count, count)]

    def plane(self, kind, i, out, ref, target):
        return remote(
            ref,
            ref,
            self.plane_sems.at[0, kind, i, out],
            self.plane_sems.at[1, kind, i, out],
            (target, self.place.c),
        )

    def start(self, first=0, last=8):
        for i in range(first, last):
            for p in range(len(self.pieces)):
                self.swap(i, p, self.place.c).start()

    def forward(self, i):
        place = self.place
        origin = place.origin(i)
        for p in range(len(self.pieces)):
            copy = self.swap(i, p, origin)
            if i == 0:
                copy.wait()
            else:
                copy.wait_recv()
        for out in range(len(self.outs)):
            ref = self.whole(place.f, origin, out)
            self.plane(0, i, out, ref, place.x_side).start()
            self.plane(1, i, out, ref, place.y_side).start()

    def relay(self, i):
        place = self.place
        origin = place.origin(i)
        for out in range(len(self.outs)):
            self.plane(0, i, out, self.whole(place.x_side, origin, out), place.x_side).wait_recv()
            self.plane(2, i, out, self.part(place.x_side, origin, out, 0), place.y_side).start()
            self.plane(1, i, out, self.whole(place.y_side, origin, out), place.y_side).wait_recv()
            self.plane(3, i, out, self.part(place.y_side, origin, out, 1), place.x_side).start()

    def finish(self):
        place = self.place
        for i in range(8):
            origin = place.origin(i)
            for out in range(len(self.outs)):
                self.plane(
                    2, i, out, self.part(place.diag, origin, out, 0), place.y_side
                ).wait_recv()
                self.plane(
                    3, i, out, self.part(place.diag, origin, out, 1), place.x_side
                ).wait_recv()
        for i in range(8):
            origin = place.origin(i)
            if i:
                for p in range(len(self.pieces)):
                    self.swap(i, p, place.c).wait_send()
            for out in range(len(self.outs)):
                own = self.whole(place.f, origin, out)
                self.plane(0, i, out, own, place.x_side).wait_send()
                self.plane(1, i, out, own, place.y_side).wait_send()
                half = self.part(place.f, origin, out, 0)
                self.plane(2, i, out, half, place.y_side).wait_send()
                self.plane(3, i, out, half, place.x_side).wait_send()


class Drain:
    @staticmethod
    def scratch(rows, widths):
        half = rows // 2
        lists = []
        for width in widths:
            lists += [
                pltpu.VMEM((2, 8, 2, half, width), jnp.bfloat16),
                pltpu.VMEM((2, 8, half, width), jnp.bfloat16),
                pltpu.VMEM((2, 8, half, width), jnp.bfloat16),
                pltpu.VMEM((8, rows, width), jnp.bfloat16),
            ]
        return lists

    @staticmethod
    def sems(pieces, outs):
        return [
            pltpu.SemaphoreType.DMA((2, 2, 8, 2, outs)),
            pltpu.SemaphoreType.DMA((2, 2, 8, outs)),
            pltpu.SemaphoreType.DMA((2, 8, pieces)),
        ]

    def __init__(self, place, grads, land, pieces, scratch, sems):
        self.place, self.grads, self.land, self.pieces = place, grads, land, pieces
        self.first = scratch[0::4]
        self.second = scratch[1::4]
        self.going = scratch[2::4]
        self.done = scratch[3::4]
        self.first_sems, self.second_sems, self.swap_sems = sems
        self.rows = land.shape[0]
        self.half = self.rows // 2

    def part(self, g, f, c, half):
        return self.grads[g].at[rows_at((f * 8 + c) * self.rows + half * self.half, self.half)]

    def sides(self, axis):
        place = self.place
        return (place.x_side, place.y_side) if axis == 0 else (place.y_side, place.x_side)

    def first_copy(self, axis, i, which, g):
        near, _ = self.sides(axis)
        f = near if which == 0 else self.place.diag
        return remote(
            self.part(g, f, self.place.peer(i), axis),
            self.first[g].at[axis, i, which],
            self.first_sems.at[0, axis, i, which, g],
            self.first_sems.at[1, axis, i, which, g],
            (near, self.place.c),
        )

    def second_copy(self, axis, i, g):
        _, far = self.sides(axis)
        return remote(
            self.going[g].at[axis, i],
            self.second[g].at[axis, i],
            self.second_sems.at[0, axis, i, g],
            self.second_sems.at[1, axis, i, g],
            (far, self.place.c),
        )

    def swap(self, i, p, origin):
        column, width, g, g_column = self.pieces[p]
        src = self.done[g].at[i, :, pl.ds(g_column, width)]
        dst = self.land.at[:, cols_at(column(origin), width)]
        if i == 0:
            return pltpu.make_async_copy(src, dst, self.swap_sems.at[0, 0, p])
        return remote(
            src,
            dst,
            self.swap_sems.at[0, i, p],
            self.swap_sems.at[1, i, p],
            (self.place.f, self.place.peer(i)),
        )

    def start(self, i):
        for g in range(len(self.grads)):
            for which in (1, 0):
                for axis in range(2):
                    self.first_copy(axis, i, which, g).start()

    def middle(self, i):
        place = self.place
        for g in range(len(self.grads)):
            for axis in range(2):
                _, far = self.sides(axis)
                self.first_copy(axis, i, 1, g).wait_recv()
                mine = self.part(g, far, place.peer(i), axis)
                self.going[g][axis, i] = (
                    mine[...].astype(jnp.float32) + self.first[g][axis, i, 1].astype(jnp.float32)
                ).astype(jnp.bfloat16)
                self.second_copy(axis, i, g).start()

    def last(self, i):
        place = self.place
        for g in range(len(self.grads)):
            for axis in range(2):
                self.first_copy(axis, i, 0, g).wait_recv()
                self.second_copy(axis, i, g).wait_recv()
                mine = self.part(g, place.f, place.peer(i), axis)
                self.done[g][i, pl.ds(axis * self.half, self.half)] = (
                    mine[...].astype(jnp.float32)
                    + self.first[g][axis, i, 0].astype(jnp.float32)
                    + self.second[g][axis, i].astype(jnp.float32)
                ).astype(jnp.bfloat16)
        for p in range(len(self.pieces)):
            self.swap(i, p, place.c).start()

    def finish(self):
        place = self.place
        for i in range(8):
            for p in range(len(self.pieces)):
                copy = self.swap(i, p, place.origin(i))
                if i == 0:
                    copy.wait()
                else:
                    copy.wait_recv()
                    copy.wait_send()
            for g in range(len(self.grads)):
                for axis in range(2):
                    for which in range(2):
                        self.first_copy(axis, i, which, g).wait_send()
                    self.second_copy(axis, i, g).wait_send()


ANY = pl.BlockSpec(memory_space=pl.ANY)
VMEM = pl.BlockSpec(memory_space=pltpu.VMEM)


def comm_call(kernel, ident, out_shape, in_specs, out_specs, scratch):
    return pl.pallas_call(
        kernel,
        out_shape=out_shape,
        in_specs=in_specs,
        out_specs=out_specs,
        scratch_shapes=scratch,
        compiler_params=pltpu.CompilerParams(
            collective_id=ident, has_side_effects=True, vmem_limit_bytes=VMEM_LIMIT
        ),
    )


def bf16(*shape):
    return jax.ShapeDtypeStruct(shape, jnp.bfloat16)


def gather_tokens(own, ident):
    def kernel(own_ref, out_ref, *sems):
        place = Place()
        greet(place, "chain", False)
        gather = ChainGather(place, own_ref, out_ref, sems)
        gather.start()
        for step in (1, 2, 3):
            gather.step(step)
        gather.finish()

    rows, cols = own.shape
    return comm_call(kernel, ident, bf16(8 * rows, cols), [ANY], ANY, ChainGather.SEMS)(own)


def scatter_tokens(partial, ident):
    rows, cols = partial.shape[0] // 8, partial.shape[1]

    def kernel(partial_ref, out_ref, *scratch):
        place = Place()
        greet(place, "chain", False)
        scatter = ChainScatter(place, partial_ref, scratch)
        scatter.start()
        for i in range(3):
            scatter.step(i)
        scatter.finish(out_ref)

    return comm_call(
        kernel,
        ident,
        jax.ShapeDtypeStruct((rows, cols), jnp.float32),
        [VMEM],
        VMEM,
        ChainScatter.scratch(rows, cols),
    )(partial)


def spread_weights(weight, widths, pieces, ident, own=None):
    rows = weight.shape[0]
    outs = [bf16(32 * rows, width) for width in widths]
    count = len(widths)

    def kernel(*refs):
        refs = list(refs)
        weight_ref = refs.pop(0)
        own_ref = refs.pop(0) if own is not None else None
        out_refs = [refs.pop(0) for _ in widths]
        all_ref = refs.pop(0) if own is not None else None
        sems = [refs.pop(0) for _ in range(2)]
        place = Place()
        greet(place, "all", True)
        spread = Spread(place, weight_ref, out_refs, pieces, sems)
        if own is not None:
            gather = ChainGather(place, own_ref, all_ref, refs)
            gather.start()
        spread.start()
        for i in range(8):
            spread.forward(i)
            if i:
                spread.relay(i - 1)
            if own is not None and i in (3, 5, 7):
                gather.step((3, 5, 7).index(i) + 1)
        spread.relay(7)
        spread.finish()
        if own is not None:
            gather.finish()

    scratch = Spread.sems(len(pieces), count)
    args = [weight]
    if own is not None:
        outs.append(bf16(8 * own.shape[0], own.shape[1]))
        scratch = scratch + ChainGather.SEMS
        args.append(own)
    return comm_call(kernel, ident, outs, [ANY] * len(args), [ANY] * len(outs), scratch)(*args)


def drain_gradients(grads, rows, land_cols, pieces, ident):
    widths = [g.shape[1] for g in grads]
    count = len(grads)

    def kernel(*refs):
        refs = list(refs)
        grad_refs = [refs.pop(0) for _ in grads]
        land = refs.pop(0)
        scratch = [refs.pop(0) for _ in range(4 * count)]
        place = Place()
        greet(place, "all", True)
        drain = Drain(place, grad_refs, land, pieces, scratch, refs)
        for i in range(8):
            drain.start(i)
        for i in range(8):
            drain.middle(i)
            if i:
                drain.last(i - 1)
        drain.last(7)
        drain.finish()

    return comm_call(
        kernel,
        ident,
        bf16(rows, land_cols),
        [VMEM] * count,
        ANY,
        Drain.scratch(rows, widths) + Drain.sems(len(pieces), count),
    )(*grads)


ATTN_PIECES = (
    (lambda c: 256 * c, 256, 0, 0),
    (lambda c: 2048 + 256 * (c // 4), 256, 0, 256),
    (lambda c: 2560 + 256 * (c // 4), 256, 0, 512),
    (lambda c: 3200 + 256 * c, 256, 1, 0),
)
ATTN_LAND = (
    (lambda c: 1024 * c, 768, 0, 0),
    (lambda c: 1024 * c + 768, 256, 1, 0),
)
MLP_PIECES = (
    (lambda c: 1024 * c, 1024, 0, 0),
    (lambda c: 8192 + 1024 * c, 1024, 0, 1024),
    (lambda c: 16384 + 1024 * c, 1024, 1, 0),
)


def per_device_split(
    hidden_in, layer_vec, positions, w_attn, w_mlp, pl_gate, pl_proj, gains, head_gains, out_grad
):
    both = ("fsdp", "ctx")
    shard_height = w_attn.shape[0]
    laurel_first = 2 * KVH * HEAD + QH * HEAD
    row_pos = lax.all_gather(positions, "ctx", axis=0, tiled=True)
    row_total = row_pos.shape[0]
    w_laurel = lax.all_gather(
        w_attn[:, laurel_first : laurel_first + 2 * RANK], both, axis=0, tiled=True
    )

    def qk_prep(raw_heads, scale_vec):
        return rotary(rms_norm(raw_heads, scale_vec), row_pos)

    hidden = hidden_in.astype(jnp.float32)
    normed_in = rms_norm(hidden, gains[0])
    normed_low = normed_in.astype(jnp.bfloat16)
    w_qkv, w_out, row_normed = spread_weights(w_attn, (768, 256), ATTN_PIECES, 1, own=normed_low)
    latent = plain_dot(normed_low, w_laurel[:, :RANK]).astype(jnp.bfloat16)
    laurel_up = times_transposed(latent, w_laurel[:, RANK:])

    projected = plain_dot(row_normed, w_qkv)
    q_raw = projected[:, None, :HEAD]
    k_raw = projected[:, None, HEAD : 2 * HEAD]
    v_raw = projected[:, None, 2 * HEAD :]
    queries = qk_prep(q_raw, head_gains[0]).astype(jnp.bfloat16)[:, 0]
    keys = qk_prep(k_raw, head_gains[1]).astype(jnp.bfloat16)[:, 0]
    values = value_norm(v_raw).astype(jnp.bfloat16)[:, 0]
    index = jnp.arange(row_total, dtype=jnp.int32)
    distance = index[:, None] - index[None, :]
    allowed = (distance >= 0) & (distance <= jnp.minimum(row_pos, WINDOW - 1)[:, None])
    scores = jnp.where(allowed, times_transposed(queries, keys), NEG_LARGE)
    row_max = jnp.max(scores, axis=-1, keepdims=True)
    exp_scores = jnp.exp(scores - row_max)
    row_sum = jnp.sum(exp_scores, axis=-1, keepdims=True)
    probs = exp_scores / row_sum
    probs_low = probs.astype(jnp.bfloat16)
    mixed = plain_dot(probs_low, values).astype(jnp.bfloat16)
    attn_out = scatter_tokens(times_transposed(mixed, w_out).astype(jnp.bfloat16), 2)

    laurel_res = normed_in + rms_norm(laurel_up, gains[1])
    after_attn = hidden + rms_norm(attn_out, gains[2])
    joined = (after_attn + laurel_res) / math.sqrt(2.0)
    ffn_low = rms_norm(joined, gains[3]).astype(jnp.bfloat16)
    w_gate_up, w_down, row_ffn = spread_weights(w_mlp, (2048, 1024), MLP_PIECES, 3, own=ffn_low)
    gate_up = plain_dot(row_ffn, w_gate_up)
    activated = activate(gate_up).astype(jnp.bfloat16)
    ffn_out = scatter_tokens(times_transposed(activated, w_down).astype(jnp.bfloat16), 4)

    after_ffn = joined + rms_norm(ffn_out, gains[4])
    after_low = after_ffn.astype(jnp.bfloat16)
    vec_gate = plain_dot(after_low, pl_gate)
    vector_in = layer_vec.astype(jnp.float32)
    vec_mixed = vec_mix(vec_gate, vector_in).astype(jnp.bfloat16)
    vec_out = plain_dot(vec_mixed, pl_proj)
    result_out = after_ffn + rms_norm(vec_out, gains[5])
    upstream = out_grad.astype(jnp.float32)
    unused_out, vec_norm_back = jax.vjp(rms_norm, vec_out, gains[5])
    d_vec_out, d_gain_vec = vec_norm_back(upstream)
    d_vec_out_low = d_vec_out.astype(jnp.bfloat16)
    d_vec_mixed = times_transposed(d_vec_out_low, pl_proj)
    grad_pl_proj = contract_rows(vec_mixed, d_vec_out_low)
    unused_out, mix_back = jax.vjp(vec_mix, vec_gate, vector_in)
    d_vec_gate, d_vector_in = mix_back(d_vec_mixed)
    d_vec_gate_low = d_vec_gate.astype(jnp.bfloat16)
    grad_after = upstream + times_transposed(d_vec_gate_low, pl_gate)
    grad_pl_gate = contract_rows(after_low, d_vec_gate_low)
    unused_out, ffn_norm_back = jax.vjp(rms_norm, ffn_out, gains[4])
    d_ffn_out, d_gain_ffn = ffn_norm_back(grad_after)
    d_ffn_low = d_ffn_out.astype(jnp.bfloat16)

    row_d_ffn = gather_tokens(d_ffn_low, 5)
    unused_out, act_back = jax.vjp(activate, gate_up)
    d_gate_up = act_back(plain_dot(row_d_ffn, w_down))[0].astype(jnp.bfloat16)
    d_ffn_in = scatter_tokens(times_transposed(d_gate_up, w_gate_up).astype(jnp.bfloat16), 6)

    unused_out, pre_norm_back = jax.vjp(rms_norm, joined, gains[3])
    d_joined_part, d_gain_pre = pre_norm_back(d_ffn_in)
    d_half = (grad_after + d_joined_part) / math.sqrt(2.0)
    unused_out, laurel_norm_back = jax.vjp(rms_norm, laurel_up, gains[1])
    d_laurel_up, d_gain_laurel = laurel_norm_back(d_half)
    unused_out, attn_norm_back = jax.vjp(rms_norm, attn_out, gains[2])
    d_attn_out, d_gain_attn = attn_norm_back(d_half)
    d_laurel_low = d_laurel_up.astype(jnp.bfloat16)
    row_d_attn = gather_tokens(d_attn_out.astype(jnp.bfloat16), 7)
    mlp_land = drain_gradients(
        [
            contract_rows(row_ffn, d_gate_up).astype(jnp.bfloat16),
            contract_rows(row_d_ffn, activated).astype(jnp.bfloat16),
        ],
        shard_height,
        w_mlp.shape[1],
        MLP_PIECES,
        8,
    )

    d_latent_low = plain_dot(d_laurel_low, w_laurel[:, RANK:]).astype(jnp.bfloat16)
    d_mixed = plain_dot(row_d_attn, w_out).astype(jnp.bfloat16)
    d_probs = times_transposed(d_mixed, values)
    inner_sum = jnp.sum(probs * d_probs, axis=-1, keepdims=True)
    d_scores = (probs * (d_probs - inner_sum)).astype(jnp.bfloat16)
    d_queries = plain_dot(d_scores, keys)
    d_keys = contract_rows(d_scores, queries)
    d_values = contract_rows(probs_low, d_mixed)
    unused_out, query_back = jax.vjp(qk_prep, q_raw, head_gains[0])
    d_q_raw, d_head_query = query_back(d_queries[:, None])
    unused_out, key_back = jax.vjp(qk_prep, k_raw, head_gains[1])
    d_k_raw, d_head_key = key_back(d_keys[:, None])
    unused_out, value_back = jax.vjp(value_norm, v_raw)
    d_v_raw = value_back(d_values[:, None])[0]
    d_projected = jnp.concatenate([d_q_raw[:, 0], d_k_raw[:, 0], d_v_raw[:, 0]], axis=1).astype(
        jnp.bfloat16
    )
    d_normed_part = scatter_tokens(
        times_transposed(d_projected, w_qkv).astype(jnp.bfloat16), 9
    ) + times_transposed(d_latent_low, w_laurel[:, :RANK])
    unused_out, input_norm_back = jax.vjp(rms_norm, hidden, gains[0])
    d_hidden_part, d_gain_input = input_norm_back(d_half + d_normed_part)
    grad_hidden = d_half + d_hidden_part
    attn_land = drain_gradients(
        [
            contract_rows(row_normed, d_projected).astype(jnp.bfloat16),
            contract_rows(row_d_attn, mixed).astype(jnp.bfloat16),
        ],
        shard_height,
        QH * 4 * HEAD,
        ATTN_LAND,
        10,
    )
    laurel_grad = lax.psum_scatter(
        jnp.concatenate(
            [contract_rows(normed_low, d_latent_low), contract_rows(d_laurel_low, latent)], axis=1
        ),
        both,
        scatter_dimension=0,
        tiled=True,
    )
    landed = attn_land.astype(jnp.float32).reshape(shard_height, KVH, QH // KVH, 4, HEAD)
    grad_w_attn = jnp.concatenate(
        [
            landed[:, :, :, 0].reshape(shard_height, QH * HEAD),
            jnp.sum(landed[:, :, :, 1], axis=2).reshape(shard_height, KVH * HEAD),
            jnp.sum(landed[:, :, :, 2], axis=2).reshape(shard_height, KVH * HEAD),
            laurel_grad,
            landed[:, :, :, 3].reshape(shard_height, QH * HEAD),
        ],
        axis=1,
    )
    gain_rows = jnp.stack(
        [d_gain_input, d_gain_laurel, d_gain_attn, d_gain_pre, d_gain_ffn, d_gain_vec]
    )
    head_rows = jnp.stack([d_head_query, d_head_key])
    grad_gate_all, grad_proj_all = lax.psum((grad_pl_gate, grad_pl_proj), both)
    grad_gains, grad_heads = lax.psum((gain_rows, head_rows), both)
    return (
        result_out.astype(jnp.bfloat16),
        grad_hidden,
        d_vector_in,
        grad_w_attn,
        mlp_land.astype(jnp.float32),
        grad_gate_all,
        grad_proj_all,
        grad_gains,
        grad_heads,
    )


def solution(mesh):
    fits = mesh.shape["ctx"] == QH and mesh.shape["fsdp"] == 4
    body = per_device_split if fits else per_device
    return jax.shard_map(
        body,
        mesh=mesh,
        in_specs=(
            P(("fsdp", "ctx"), None),
            P(("fsdp", "ctx"), None),
            P(("fsdp", "ctx")),
            P(("fsdp", "ctx"), None),
            P(("fsdp", "ctx"), None),
            P(),
            P(),
            P(),
            P(),
            P(("fsdp", "ctx"), None),
        ),
        out_specs=(
            P(("fsdp", "ctx"), None),
            P(("fsdp", "ctx"), None),
            P(("fsdp", "ctx"), None),
            P(("fsdp", "ctx"), None),
            P(("fsdp", "ctx"), None),
            P(),
            P(),
            P(),
            P(),
        ),
        check_vma=False,
    )
```

```python
import math

import jax
import jax.numpy as jnp
from jax import lax
from jax.experimental import pallas as pl
from jax.experimental.pallas import tpu as pltpu
from jax.sharding import PartitionSpec as P

QH = 8
KVH = 2
HEAD = 256
RANK = 64
WINDOW = 512


EPSILON = 1e-06
THETA = 10000.0
NEG_LARGE = -1e30


def passed_along(block, axis, distance):
    devices = range(lax.axis_size(axis))
    route = [(i - distance, i) for i in devices if i - distance in devices]
    return lax.ppermute(block, axis, route)


def rms_norm(values, scale_vec):
    return (
        values * lax.rsqrt(jnp.mean(values * values, axis=-1, keepdims=True) + EPSILON) * scale_vec
    )


def value_norm(values):
    return rms_norm(values, 1.0)


def rotary(values, positions):
    half_size = values.shape[-1] // 2
    frequency = jnp.exp(
        jnp.arange(half_size, dtype=jnp.float32) * (-2.0 * math.log(THETA) / values.shape[-1])
    )
    angles = positions.astype(jnp.float32)[:, None] * frequency[None, :]
    cosine = jnp.cos(angles)[:, None, :]
    sine_part = jnp.sin(angles)[:, None, :]
    first_half = values[..., :half_size]
    second_half = values[..., half_size:]
    return jnp.concatenate(
        [
            first_half * cosine - second_half * sine_part,
            second_half * cosine + first_half * sine_part,
        ],
        axis=-1,
    )


def plain_dot(left_side, right_side):
    return jnp.dot(left_side, right_side, preferred_element_type=jnp.float32)


def times_transposed(left_side, right_side):
    return lax.dot_general(
        left_side, right_side, (((1,), (1,)), ((), ())), preferred_element_type=jnp.float32
    )


def contract_rows(left_side, right_side):
    return lax.dot_general(
        left_side, right_side, (((0,), (0,)), ((), ())), preferred_element_type=jnp.float32
    )


def activate(gate_up_val):
    half_cols = gate_up_val.shape[1] // 2
    return jax.nn.gelu(gate_up_val[:, :half_cols], approximate=True) * gate_up_val[:, half_cols:]


def vec_mix(gate_val, vector_val):
    return jax.nn.gelu(gate_val, approximate=True) * vector_val


def per_device(
    hidden_in, layer_vec, positions, w_attn, w_mlp, pl_gate, pl_proj, gains, head_gains, out_grad
):
    row_count = hidden_in.shape[0]
    model_width = hidden_in.shape[1]
    q_width = QH * HEAD
    kv_width = KVH * HEAD
    in_cols = q_width + 2 * kv_width + RANK
    group_size = QH // KVH
    ff_width = w_mlp.shape[1] // 3
    shard_height = w_mlp.shape[0]
    fsdp_count = lax.axis_size("fsdp")
    ctx_count = lax.axis_size("ctx")
    quarter = ff_width // fsdp_count

    def permute_cols(matrix):
        return (
            matrix.reshape(-1, fsdp_count, ctx_count, shard_height)
            .transpose(0, 2, 1, 3)
            .reshape(-1, model_width)
        )

    def restore_cols(matrix):
        return (
            matrix.reshape(-1, ctx_count, fsdp_count, shard_height)
            .transpose(0, 2, 1, 3)
            .reshape(-1, model_width)
        )

    def qk_prep(raw_heads, scale_vec):
        return rotary(rms_norm(raw_heads, scale_vec), positions)

    hidden = hidden_in.astype(jnp.float32)
    normed_in = rms_norm(hidden, gains[0])
    normed_low = normed_in.astype(jnp.bfloat16)
    projected = plain_dot(
        normed_low, lax.all_gather(w_attn[:, :in_cols], ("fsdp", "ctx"), axis=0, tiled=True)
    )
    q_raw = projected[:, :q_width].reshape(row_count, QH, HEAD)
    k_raw = projected[:, q_width : q_width + kv_width].reshape(row_count, KVH, HEAD)
    v_raw = projected[:, q_width + kv_width : q_width + 2 * kv_width].reshape(row_count, KVH, HEAD)
    latent = projected[:, q_width + 2 * kv_width :].astype(jnp.bfloat16)
    queries = qk_prep(q_raw, head_gains[0]).astype(jnp.bfloat16)
    keys_own = qk_prep(k_raw, head_gains[1]).astype(jnp.bfloat16)
    values_own = value_norm(v_raw).astype(jnp.bfloat16)
    kv_own = jnp.concatenate(
        [keys_own.reshape(row_count, kv_width), values_own.reshape(row_count, kv_width)], axis=1
    )
    hop_count = (WINDOW - 1) // row_count + 1
    earlier = []
    moving = kv_own
    for step_back in range(hop_count):
        moving = passed_along(moving, "ctx", 1)
        earlier.append(moving)
    kv_all = jnp.concatenate(earlier[::-1] + [kv_own], axis=0)
    span_rows = kv_all.shape[0]
    keys_all = kv_all[:, :kv_width].reshape(span_rows, KVH, HEAD)
    values_all = kv_all[:, kv_width:].reshape(span_rows, KVH, HEAD)
    grouped = queries.reshape(row_count, KVH, group_size, HEAD)
    distance = (
        jnp.arange(row_count, dtype=jnp.int32)[:, None]
        + hop_count * row_count
        - jnp.arange(span_rows, dtype=jnp.int32)[None, :]
    )
    allowed = (distance >= 0) & (distance <= jnp.minimum(positions, WINDOW - 1)[:, None])
    scores = jnp.einsum("qgrd,kgd->grqk", grouped, keys_all, preferred_element_type=jnp.float32)
    scores = jnp.where(allowed[None, None], scores, NEG_LARGE)
    row_max = jnp.max(scores, axis=-1, keepdims=True)
    exp_scores = jnp.exp(scores - row_max)
    row_sum = jnp.sum(exp_scores, axis=-1, keepdims=True)
    log_total = row_max + jnp.log(row_sum)
    probs_low = (exp_scores / row_sum).astype(jnp.bfloat16)
    mixed = jnp.einsum("grqk,kgd->qgrd", probs_low, values_all, preferred_element_type=jnp.float32)
    mixed = mixed.reshape(row_count, q_width).astype(jnp.bfloat16)
    shard_rows = lax.all_gather(w_attn[:, in_cols:], ("fsdp", "ctx"), axis=0, tiled=True)
    laurel_part = times_transposed(latent, shard_rows[:, :RANK])
    attn_part = times_transposed(mixed, shard_rows[:, RANK:])
    out_pair = jnp.stack([laurel_part, attn_part], axis=1)
    laurel_up = out_pair[:, 0]
    attn_out = out_pair[:, 1]
    laurel_res = normed_in + rms_norm(laurel_up, gains[1])
    after_attn = hidden + rms_norm(attn_out, gains[2])
    joined = (after_attn + laurel_res) / math.sqrt(2.0)
    ffn_low = rms_norm(joined, gains[3]).astype(jnp.bfloat16)
    sent_rows = w_mlp.reshape(shard_height, 3, fsdp_count, quarter)
    sent_tokens = jnp.broadcast_to(
        ffn_low[:, None, None, :], (row_count, 1, fsdp_count, model_width)
    )
    got_rows, got_tokens = (
        lax.all_to_all(sent_rows, "fsdp", split_axis=2, concat_axis=0, tiled=True),
        lax.all_to_all(sent_tokens, "fsdp", split_axis=2, concat_axis=0, tiled=True),
    )
    quarter_rows = lax.all_gather(got_rows, "ctx", axis=0, tiled=True).reshape(
        model_width, 3, quarter
    )
    w_gate_up = quarter_rows[:, :2].reshape(model_width, 2 * quarter)
    w_down = quarter_rows[:, 2]
    ffn_perm = permute_cols(got_tokens.reshape(fsdp_count * row_count, model_width))
    gate_up = plain_dot(ffn_perm, w_gate_up)
    activated = activate(gate_up).astype(jnp.bfloat16)
    ffn_out = lax.psum_scatter(
        restore_cols(times_transposed(activated, w_down)), "fsdp", scatter_dimension=0, tiled=True
    )
    after_ffn = joined + rms_norm(ffn_out, gains[4])
    after_low = after_ffn.astype(jnp.bfloat16)
    vec_gate = plain_dot(after_low, pl_gate)
    vector_in = layer_vec.astype(jnp.float32)
    vec_mixed = vec_mix(vec_gate, vector_in).astype(jnp.bfloat16)
    vec_out = plain_dot(vec_mixed, pl_proj)
    result_out = after_ffn + rms_norm(vec_out, gains[5])
    upstream = out_grad.astype(jnp.float32)
    unused_out, vec_norm_back = jax.vjp(rms_norm, vec_out, gains[5])
    d_vec_out, d_gain_vec = vec_norm_back(upstream)
    d_vec_out_low = d_vec_out.astype(jnp.bfloat16)
    d_vec_mixed = times_transposed(d_vec_out_low, pl_proj)
    grad_pl_proj = contract_rows(vec_mixed, d_vec_out_low)
    unused_out, mix_back = jax.vjp(vec_mix, vec_gate, vector_in)
    d_vec_gate, d_vector_in = mix_back(d_vec_mixed)
    d_vec_gate_low = d_vec_gate.astype(jnp.bfloat16)
    grad_after = upstream + times_transposed(d_vec_gate_low, pl_gate)
    grad_pl_gate = contract_rows(after_low, d_vec_gate_low)
    unused_out, ffn_norm_back = jax.vjp(rms_norm, ffn_out, gains[4])
    d_ffn_out, d_gain_ffn = ffn_norm_back(grad_after)
    d_ffn_low = d_ffn_out.astype(jnp.bfloat16)
    unused_out, act_back = jax.vjp(activate, gate_up)
    d_ffn_all = lax.all_gather(d_ffn_low, "fsdp", axis=0, tiled=True)
    d_ffn_perm = permute_cols(d_ffn_all)
    d_activated = plain_dot(d_ffn_perm, w_down)
    d_gate_up = act_back(d_activated)[0].astype(jnp.bfloat16)
    d_ffn_in = lax.psum_scatter(
        restore_cols(times_transposed(d_gate_up, w_gate_up)).astype(jnp.bfloat16),
        "fsdp",
        scatter_dimension=0,
        tiled=True,
    ).astype(jnp.float32)
    summed = lax.psum_scatter(
        jnp.concatenate(
            [contract_rows(ffn_perm, d_gate_up), contract_rows(d_ffn_perm, activated)], axis=1
        ).astype(jnp.bfloat16),
        "ctx",
        scatter_dimension=0,
        tiled=True,
    ).astype(jnp.float32)
    grad_w_mlp = (
        lax.all_to_all(
            summed.reshape(fsdp_count * shard_height, 3, 1, quarter).astype(jnp.bfloat16),
            "fsdp",
            split_axis=0,
            concat_axis=2,
            tiled=True,
        )
        .astype(jnp.float32)
        .reshape(shard_height, 3 * ff_width)
    )
    unused_out, pre_norm_back = jax.vjp(rms_norm, joined, gains[3])
    d_joined_part, d_gain_pre = pre_norm_back(d_ffn_in)
    d_joined = grad_after + d_joined_part
    d_half = d_joined / math.sqrt(2.0)
    unused_out, laurel_norm_back = jax.vjp(rms_norm, laurel_up, gains[1])
    d_laurel_up, d_gain_laurel = laurel_norm_back(d_half)
    unused_out, attn_norm_back = jax.vjp(rms_norm, attn_out, gains[2])
    d_attn_out, d_gain_attn = attn_norm_back(d_half)
    d_laurel_low = d_laurel_up.astype(jnp.bfloat16)
    d_attn_low = d_attn_out.astype(jnp.bfloat16)
    shard_rows = lax.all_gather(w_attn[:, in_cols:], ("fsdp", "ctx"), axis=0, tiled=True)
    d_latent = plain_dot(d_laurel_low, shard_rows[:, :RANK])
    d_mixed = plain_dot(d_attn_low, shard_rows[:, RANK:])
    d_grouped = d_mixed.astype(jnp.bfloat16).reshape(row_count, KVH, group_size, HEAD)
    again = jnp.einsum("qgrd,kgd->grqk", grouped, keys_all, preferred_element_type=jnp.float32)
    again = jnp.where(allowed[None, None], again, NEG_LARGE)
    probs = jnp.exp(again - log_total)
    d_probs = jnp.einsum(
        "qgrd,kgd->grqk", d_grouped, values_all, preferred_element_type=jnp.float32
    )
    inner_sum = jnp.sum(probs * d_probs, axis=-1, keepdims=True)
    d_scores = (probs * (d_probs - inner_sum)).astype(jnp.bfloat16)
    d_queries = jnp.einsum(
        "grqk,kgd->qgrd", d_scores, keys_all, preferred_element_type=jnp.float32
    ).reshape(row_count, QH, HEAD)
    d_keys_all = jnp.einsum("grqk,qgrd->kgd", d_scores, grouped, preferred_element_type=jnp.float32)
    d_values_all = jnp.einsum(
        "grqk,qgrd->kgd", probs.astype(jnp.bfloat16), d_grouped, preferred_element_type=jnp.float32
    )
    d_kv_all = jnp.concatenate(
        [d_keys_all.reshape(span_rows, kv_width), d_values_all.reshape(span_rows, kv_width)], axis=1
    )
    returned = d_kv_all[:row_count]
    for step_back in range(1, hop_count + 1):
        returned = (
            passed_along(returned.astype(jnp.bfloat16), "ctx", -1).astype(returned.dtype)
            + d_kv_all[step_back * row_count : (step_back + 1) * row_count]
        )
    d_keys_own = returned[:, :kv_width].reshape(row_count, KVH, HEAD)
    d_values_own = returned[:, kv_width:].reshape(row_count, KVH, HEAD)
    unused_out, query_back = jax.vjp(qk_prep, q_raw, head_gains[0])
    d_q_raw, d_head_query = query_back(d_queries)
    unused_out, key_back = jax.vjp(qk_prep, k_raw, head_gains[1])
    d_k_raw, d_head_key = key_back(d_keys_own)
    unused_out, value_back = jax.vjp(value_norm, v_raw)
    d_v_raw = value_back(d_values_own)[0]
    d_projected = jnp.concatenate(
        [
            d_q_raw.reshape(row_count, q_width),
            d_k_raw.reshape(row_count, kv_width),
            d_v_raw.reshape(row_count, kv_width),
            d_latent,
        ],
        axis=1,
    ).astype(jnp.bfloat16)
    d_normed_part = times_transposed(
        d_projected, lax.all_gather(w_attn[:, :in_cols], ("fsdp", "ctx"), axis=0, tiled=True)
    )
    unused_out, input_norm_back = jax.vjp(rms_norm, hidden, gains[0])
    d_hidden_part, d_gain_input = input_norm_back(d_half + d_normed_part)
    grad_hidden = d_half + d_hidden_part
    grad_w_attn = lax.psum_scatter(
        jnp.concatenate(
            [
                contract_rows(normed_low, d_projected),
                contract_rows(d_laurel_low, latent),
                contract_rows(d_attn_low, mixed),
            ],
            axis=1,
        ),
        ("fsdp", "ctx"),
        scatter_dimension=0,
        tiled=True,
    )
    gain_rows = jnp.stack(
        [d_gain_input, d_gain_laurel, d_gain_attn, d_gain_pre, d_gain_ffn, d_gain_vec]
    )
    head_rows = jnp.stack([d_head_query, d_head_key])
    grad_gains, grad_heads, grad_gate_all, grad_proj_all = lax.psum(
        (gain_rows, head_rows, grad_pl_gate, grad_pl_proj), ("fsdp", "ctx")
    )
    return (
        result_out.astype(jnp.bfloat16),
        grad_hidden,
        d_vector_in,
        grad_w_attn,
        grad_w_mlp,
        grad_gate_all,
        grad_proj_all,
        grad_gains,
        grad_heads,
    )

MESH = pl.DeviceIdType.MESH
VMEM_LIMIT = 60 * 1024 * 1024
ORDER = ((0, 0), (0, 1), (1, 0), (1, 1), (3, 0), (3, 1), (2, 0), (2, 1))


class Place:
    def __init__(self):
        self.f = lax.axis_index("fsdp")
        self.c = lax.axis_index("ctx")
        self.z = self.c // 2
        self.k = self.c % 2
        self.x_side = self.f + 1 - 2 * (self.f % 2)
        self.y_side = (self.f + 2) % 4
        self.diag = 3 - self.f
        self.sibling = (self.f, self.c + 1 - 2 * self.k)
        self.up = (self.f, self.c + 2)
        self.down = (self.f, self.c - 2)
        self.has_up = self.z < 3
        self.has_down = self.z > 0

    def peer(self, i):
        dz, dk = ORDER[i]
        return ((self.z + dz) % 4) * 2 + (self.k + dk) % 2

    def origin(self, i):
        dz, dk = ORDER[i]
        return ((self.z + 4 - dz) % 4) * 2 + (self.k + 2 - dk) % 2


def rows_at(start, count):
    return pl.ds(pl.multiple_of(start, 16), count)


def cols_at(start, count):
    if isinstance(start, int):
        return pl.ds(start, count)
    return pl.ds(pl.multiple_of(start, 128), count)


def remote(src, dst, send_sem, recv_sem, target):
    return pltpu.make_async_remote_copy(
        src_ref=src,
        dst_ref=dst,
        send_sem=send_sem,
        recv_sem=recv_sem,
        device_id=target,
        device_id_type=MESH,
    )


def greet(place, line, plane):
    barrier = pltpu.get_barrier_semaphore()
    count = 0

    def tell(target):
        pl.semaphore_signal(barrier, inc=1, device_id=target, device_id_type=MESH)

    if line == "all":
        for i in range(1, 8):
            tell((place.f, place.peer(i)))
        count += 7
    elif line == "chain":
        for i in (1, 2, 4):
            tell((place.f, place.peer(i)))
        count += 3
    if plane:
        tell((place.x_side, place.c))
        tell((place.y_side, place.c))
        count += 2
    pl.semaphore_wait(barrier, count)


class ChainGather:
    SEMS = [pltpu.SemaphoreType.DMA((2, 10)), pltpu.SemaphoreType.DMA((1,))]

    def __init__(self, place, own, out, sems):
        self.place, self.own, self.out = place, own, out
        self.sems, self.local_sem = sems
        self.rows = own.shape[0]

    def block(self, origin_z, core=None):
        core = self.place.k if core is None else core
        return self.out.at[rows_at((origin_z * 2 + core) * self.rows, self.rows)]

    def copy(self, src, dst, index, target):
        return remote(src, dst, self.sems.at[0, index], self.sems.at[1, index], target)

    def local(self):
        return pltpu.make_async_copy(self.own, self.block(self.place.z), self.local_sem.at[0])

    def upward(self, step):
        src = self.own if step == 0 else self.block(self.place.z - step)
        return self.copy(src, self.block(self.place.z - step), step, self.place.up)

    def downward(self, step):
        src = self.own if step == 0 else self.block(self.place.z + step)
        return self.copy(src, self.block(self.place.z + step), 3 + step, self.place.down)

    def across(self, origin_z, own=False):
        src = self.own if own else self.block(origin_z)
        return self.copy(src, self.block(origin_z), 6 + origin_z, self.place.sibling)

    def start(self):
        place = self.place

        @pl.when(place.has_up)
        def _():
            self.upward(0).start()

        @pl.when(place.has_down)
        def _():
            self.downward(0).start()

        self.across(place.z, True).start()
        self.local().start()

    def step(self, step):
        place = self.place

        @pl.when(place.z - step >= 0)
        def _():
            self.copy(self.own, self.block(place.z - step), step - 1, place.up).wait_recv()
            if step < 3:

                @pl.when(place.has_up)
                def _():
                    self.upward(step).start()

            self.across(place.z - step).start()

        @pl.when(place.z + step <= 3)
        def _():
            self.copy(self.own, self.block(place.z + step), 3 + step - 1, place.down).wait_recv()
            if step < 3:

                @pl.when(place.has_down)
                def _():
                    self.downward(step).start()

            self.across(place.z + step).start()

    def finish(self):
        place = self.place
        for origin in range(4):
            copy = self.copy(
                self.own, self.block(origin, 1 - place.k), 6 + origin, place.sibling
            )
            copy.wait_recv()
            copy.wait_send()
        for step in range(3):

            @pl.when((place.z - step >= 0) & place.has_up)
            def _(step=step):
                self.upward(step).wait_send()

            @pl.when((place.z + step <= 3) & place.has_down)
            def _(step=step):
                self.downward(step).wait_send()

        self.local().wait()


class ChainScatter:
    @staticmethod
    def scratch(rows, cols):
        return [
            pltpu.VMEM((4, rows, cols), jnp.bfloat16),
            pltpu.VMEM((6, rows, cols), jnp.bfloat16),
            pltpu.VMEM((6, rows, cols), jnp.bfloat16),
            pltpu.SemaphoreType.DMA((2, 10)),
        ]

    def __init__(self, place, partial, scratch):
        self.place, self.partial = place, partial
        self.from_sibling, self.arrived, self.going, self.sems = scratch
        self.rows = partial.shape[0] // 8

    def block(self, origin_z, core):
        return self.partial.at[rows_at((origin_z * 2 + core) * self.rows, self.rows)]

    def across(self, dest):
        return remote(
            self.block(dest, 1 - self.place.k),
            self.from_sibling.at[dest],
            self.sems.at[0, 6 + dest],
            self.sems.at[1, 6 + dest],
            self.place.sibling,
        )

    def moved(self, slot, target):
        return remote(
            self.going.at[slot],
            self.arrived.at[slot],
            self.sems.at[0, slot],
            self.sems.at[1, slot],
            target,
        )

    def start(self):
        for dest in (3, 0, 2, 1):
            self.across(dest).start()

    def pair_sum(self, dest):
        return self.block(dest, self.place.k)[...].astype(jnp.float32) + self.from_sibling[
            dest
        ].astype(jnp.float32)

    def pass_on(self, dest, upward, inner=False):
        place = self.place
        slot = dest - 1 if upward else 3 + dest
        target = place.up if upward else place.down
        self.across(dest).wait_recv()
        total = self.pair_sum(dest)
        if inner:
            self.moved(slot, target).wait_recv()
            total = total + self.arrived[slot].astype(jnp.float32)
        self.going[slot] = total.astype(jnp.bfloat16)
        self.moved(slot, target).start()

    def ends(self):
        z = self.place.z

        @pl.when(z == 0)
        def _():
            for dest in (3, 2, 1):
                self.pass_on(dest, True)

        @pl.when(z == 3)
        def _():
            for dest in (0, 1, 2):
                self.pass_on(dest, False)

    def inner(self, i):
        z = self.place.z

        @pl.when(z == 1)
        def _():
            if i == 0:
                self.pass_on(3, True, True)
            else:
                self.pass_on(0, False, True)
                self.pass_on(2, True, True)

        @pl.when(z == 2)
        def _():
            if i == 0:
                self.pass_on(0, False, True)
            else:
                self.pass_on(3, True, True)
                self.pass_on(1, False, True)

    def finish(self, out):
        place = self.place
        for dest in range(4):

            @pl.when(place.z == dest)
            def _(dest=dest):
                self.across(dest).wait_recv()
                total = self.pair_sum(dest)
                if dest > 0:
                    self.moved(dest - 1, place.up).wait_recv()
                    total = total + self.arrived[dest - 1].astype(jnp.float32)
                if dest < 3:
                    self.moved(3 + dest, place.down).wait_recv()
                    total = total + self.arrived[3 + dest].astype(jnp.float32)
                out[...] = total

        for dest in range(4):
            self.across(dest).wait_send()
        for i in range(3):
            top, bottom = 3 - i, i

            @pl.when(place.z < top)
            def _(top=top):
                self.moved(top - 1, place.up).wait_send()

            @pl.when(place.z > bottom)
            def _(bottom=bottom):
                self.moved(3 + bottom, place.down).wait_send()


class Spread:
    @staticmethod
    def sems(pieces, outs):
        return [
            pltpu.SemaphoreType.DMA((2, 8, pieces)),
            pltpu.SemaphoreType.DMA((2, 4, 8, outs)),
        ]

    def __init__(self, place, weight, outs, pieces, sems):
        self.place, self.weight, self.outs, self.pieces = place, weight, outs, pieces
        self.swap_sems, self.plane_sems = sems
        self.rows = weight.shape[0]

    def spot(self, f, c):
        return (f * 8 + c) * self.rows

    def swap(self, i, p, origin):
        column, width, out, out_column = self.pieces[p]
        peer = self.place.peer(i)
        src = self.weight.at[:, cols_at(column(peer), width)]
        dst = self.outs[out].at[
            rows_at(self.spot(self.place.f, origin), self.rows), pl.ds(out_column, width)
        ]
        if i == 0:
            return pltpu.make_async_copy(src, dst, self.swap_sems.at[0, 0, p])
        return remote(
            src,
            dst,
            self.swap_sems.at[0, i, p],
            self.swap_sems.at[1, i, p],
            (self.place.f, peer),
        )

    def whole(self, f, c, out):
        return self.outs[out].at[rows_at(self.spot(f, c), self.rows)]

    def part(self, f, c, out, half):
        count = self.rows // 2
        return self.outs[out].at[rows_at(self.spot(f, c) + half * count, count)]

    def plane(self, kind, i, out, ref, target):
        return remote(
            ref,
            ref,
            self.plane_sems.at[0, kind, i, out],
            self.plane_sems.at[1, kind, i, out],
            (target, self.place.c),
        )

    def start(self, first=0, last=8):
        for i in range(first, last):
            for p in range(len(self.pieces)):
                self.swap(i, p, self.place.c).start()

    def forward(self, i):
        place = self.place
        origin = place.origin(i)
        for p in range(len(self.pieces)):
            copy = self.swap(i, p, origin)
            if i == 0:
                copy.wait()
            else:
                copy.wait_recv()
        for out in range(len(self.outs)):
            ref = self.whole(place.f, origin, out)
            self.plane(0, i, out, ref, place.x_side).start()
            self.plane(1, i, out, ref, place.y_side).start()

    def relay(self, i):
        place = self.place
        origin = place.origin(i)
        for out in range(len(self.outs)):
            self.plane(0, i, out, self.whole(place.x_side, origin, out), place.x_side).wait_recv()
            self.plane(2, i, out, self.part(place.x_side, origin, out, 0), place.y_side).start()
            self.plane(1, i, out, self.whole(place.y_side, origin, out), place.y_side).wait_recv()
            self.plane(3, i, out, self.part(place.y_side, origin, out, 1), place.x_side).start()

    def finish(self, first=0, last=8):
        place = self.place
        for i in range(first, last):
            origin = place.origin(i)
            for out in range(len(self.outs)):
                self.plane(
                    2, i, out, self.part(place.diag, origin, out, 0), place.y_side
                ).wait_recv()
                self.plane(
                    3, i, out, self.part(place.diag, origin, out, 1), place.x_side
                ).wait_recv()
        for i in range(first, last):
            origin = place.origin(i)
            if i:
                for p in range(len(self.pieces)):
                    self.swap(i, p, place.c).wait_send()
            for out in range(len(self.outs)):
                own = self.whole(place.f, origin, out)
                self.plane(0, i, out, own, place.x_side).wait_send()
                self.plane(1, i, out, own, place.y_side).wait_send()
                half = self.part(place.f, origin, out, 0)
                self.plane(2, i, out, half, place.y_side).wait_send()
                self.plane(3, i, out, half, place.x_side).wait_send()


class Drain:
    @staticmethod
    def scratch(rows, widths, peers=8):
        half = rows // 2
        lists = []
        for width in widths:
            lists += [
                pltpu.VMEM((2, peers, 2, half, width), jnp.bfloat16),
                pltpu.VMEM((2, peers, half, width), jnp.bfloat16),
                pltpu.VMEM((2, peers, half, width), jnp.bfloat16),
                pltpu.VMEM((peers, rows, width), jnp.bfloat16),
            ]
        return lists

    @staticmethod
    def sems(pieces, outs, peers=8):
        return [
            pltpu.SemaphoreType.DMA((2, 2, peers, 2, outs)),
            pltpu.SemaphoreType.DMA((2, 2, peers, outs)),
            pltpu.SemaphoreType.DMA((2, peers, pieces)),
        ]

    def __init__(self, place, grads, land, pieces, scratch, sems, base=0, peers=8):
        self.place, self.grads, self.land, self.pieces = place, grads, land, pieces
        self.first = scratch[0::4]
        self.second = scratch[1::4]
        self.going = scratch[2::4]
        self.done = scratch[3::4]
        self.first_sems, self.second_sems, self.swap_sems = sems
        self.rows = land.shape[0]
        self.half = self.rows // 2
        self.units = len(grads[0].shape) == 4
        self.base, self.peers = base, peers

    def part(self, g, f, i, half):
        peer = self.place.peer(self.base + i)
        if self.units:
            start = (peer % 2) * self.rows + half * self.half
            return self.grads[g].at[i // 2, f, rows_at(start, self.half)]
        return self.grads[g].at[rows_at((f * 8 + peer) * self.rows + half * self.half, self.half)]

    def sides(self, axis):
        place = self.place
        return (place.x_side, place.y_side) if axis == 0 else (place.y_side, place.x_side)

    def first_copy(self, axis, i, which, g):
        near, _ = self.sides(axis)
        f = near if which == 0 else self.place.diag
        return remote(
            self.part(g, f, i, axis),
            self.first[g].at[axis, i, which],
            self.first_sems.at[0, axis, i, which, g],
            self.first_sems.at[1, axis, i, which, g],
            (near, self.place.c),
        )

    def second_copy(self, axis, i, g):
        _, far = self.sides(axis)
        return remote(
            self.going[g].at[axis, i],
            self.second[g].at[axis, i],
            self.second_sems.at[0, axis, i, g],
            self.second_sems.at[1, axis, i, g],
            (far, self.place.c),
        )

    def swap(self, i, p, origin):
        column, width, g, g_column = self.pieces[p]
        src = self.done[g].at[i, :, pl.ds(g_column, width)]
        dst = self.land.at[:, cols_at(column(origin), width)]
        if self.base + i == 0:
            return pltpu.make_async_copy(src, dst, self.swap_sems.at[0, i, p])
        return remote(
            src,
            dst,
            self.swap_sems.at[0, i, p],
            self.swap_sems.at[1, i, p],
            (self.place.f, self.place.peer(self.base + i)),
        )

    def start(self, i):
        for g in range(len(self.grads)):
            for which in (1, 0):
                for axis in range(2):
                    self.first_copy(axis, i, which, g).start()

    def middle(self, i):
        place = self.place
        for g in range(len(self.grads)):
            for axis in range(2):
                _, far = self.sides(axis)
                self.first_copy(axis, i, 1, g).wait_recv()
                mine = self.part(g, far, i, axis)
                self.going[g][axis, i] = (
                    mine[...].astype(jnp.float32) + self.first[g][axis, i, 1].astype(jnp.float32)
                ).astype(jnp.bfloat16)
                self.second_copy(axis, i, g).start()

    def last(self, i):
        place = self.place
        for g in range(len(self.grads)):
            for axis in range(2):
                self.first_copy(axis, i, 0, g).wait_recv()
                self.second_copy(axis, i, g).wait_recv()
                mine = self.part(g, place.f, i, axis)
                self.done[g][i, pl.ds(axis * self.half, self.half)] = (
                    mine[...].astype(jnp.float32)
                    + self.first[g][axis, i, 0].astype(jnp.float32)
                    + self.second[g][axis, i].astype(jnp.float32)
                ).astype(jnp.bfloat16)
        for p in range(len(self.pieces)):
            self.swap(i, p, place.c).start()

    def finish(self):
        place = self.place
        for i in range(self.peers):
            for p in range(len(self.pieces)):
                copy = self.swap(i, p, place.origin(self.base + i))
                if self.base + i == 0:
                    copy.wait()
                else:
                    copy.wait_recv()
                    copy.wait_send()
            for g in range(len(self.grads)):
                for axis in range(2):
                    for which in range(2):
                        self.first_copy(axis, i, which, g).wait_send()
                    self.second_copy(axis, i, g).wait_send()


ANY = pl.BlockSpec(memory_space=pl.ANY)
VMEM = pl.BlockSpec(memory_space=pltpu.VMEM)


def comm_call(kernel, ident, out_shape, in_specs, out_specs, scratch, aliases=None):
    return pl.pallas_call(
        kernel,
        input_output_aliases=aliases or {},
        out_shape=out_shape,
        in_specs=in_specs,
        out_specs=out_specs,
        scratch_shapes=scratch,
        compiler_params=pltpu.CompilerParams(
            collective_id=ident, has_side_effects=True, vmem_limit_bytes=VMEM_LIMIT
        ),
    )


def bf16(*shape):
    return jax.ShapeDtypeStruct(shape, jnp.bfloat16)


def gather_tokens(own, ident):
    def kernel(own_ref, out_ref, *sems):
        place = Place()
        greet(place, "chain", False)
        gather = ChainGather(place, own_ref, out_ref, sems)
        gather.start()
        for step in (1, 2, 3):
            gather.step(step)
        gather.finish()

    rows, cols = own.shape
    return comm_call(kernel, ident, bf16(8 * rows, cols), [ANY], ANY, ChainGather.SEMS)(own)


def scatter_tokens(partial, ident):
    rows, cols = partial.shape[0] // 8, partial.shape[1]

    def kernel(partial_ref, out_ref, *scratch):
        place = Place()
        greet(place, "chain", False)
        scatter = ChainScatter(place, partial_ref, scratch)
        scatter.start()
        scatter.ends()
        scatter.inner(0)
        scatter.inner(1)
        scatter.finish(out_ref)

    return comm_call(
        kernel,
        ident,
        jax.ShapeDtypeStruct((rows, cols), jnp.float32),
        [VMEM],
        VMEM,
        ChainScatter.scratch(rows, cols),
    )(partial)


ATTN_PIECES = (
    (lambda c: 256 * c, 256, 0, 0),
    (lambda c: 2048 + 256 * (c // 4), 256, 0, 256),
    (lambda c: 2560 + 256 * (c // 4), 256, 0, 512),
    (lambda c: 3200 + 256 * c, 256, 1, 0),
    (lambda c: 3072, 128, 2, 0),
)
ATTN_LAND = (
    (lambda c: 1152 * c, 896, 0, 0),
    (lambda c: 1152 * c + 896, 256, 1, 0),
)
MLP_PIECES = (
    (lambda c: 1024 * c, 1024, 0, 0),
    (lambda c: 8192 + 1024 * c, 1024, 0, 1024),
    (lambda c: 16384 + 1024 * c, 1024, 1, 0),
)
VEC_LAND = ((lambda c: 512 * c, 512, 0, 0),)
VEC_PIECES = ((lambda c: 0, 512, 0, 0),)


def attention_open(normed_low, own_pos, w_attn, w_mlp, ident):
    height = 32 * w_attn.shape[0]
    rows, width = normed_low.shape
    outs = [bf16(height, 768), bf16(height, 256), bf16(height, 128)]
    outs += [bf16(8 * rows, width), bf16(8 * rows, own_pos.shape[1])]
    outs += [bf16(height, 2048), bf16(height, 1024)]

    def kernel(
        own_ref, pos_ref, attn_ref, mlp_ref,
        qkv_ref, out_ref, laurel_ref, row_ref, row_pos_ref, gate_up_ref, down_ref, *sems
    ):
        place = Place()
        greet(place, "all", True)
        attn = Spread(place, attn_ref, [qkv_ref, out_ref, laurel_ref], ATTN_PIECES, sems[0:2])
        mlp = Spread(place, mlp_ref, [gate_up_ref, down_ref], MLP_PIECES, sems[2:4])
        gathers = [
            ChainGather(place, own_ref, row_ref, sems[4:6]),
            ChainGather(place, pos_ref, row_pos_ref, sems[6:8]),
        ]
        for gather in gathers:
            gather.start()
        attn.start()
        for i in range(8):
            attn.forward(i)
            if i:
                attn.relay(i - 1)
            if i == 0:
                mlp.start(0, 2)
            if i in (3, 5, 7):
                for gather in gathers:
                    gather.step((3, 5, 7).index(i) + 1)
            if i == 2:
                mlp.forward(0)
            if i == 4:
                mlp.forward(1)
                mlp.relay(0)
        attn.relay(7)
        mlp.relay(1)
        attn.finish()
        mlp.finish(0, 2)
        for gather in gathers:
            gather.finish()

    return comm_call(
        kernel,
        ident,
        outs,
        [ANY] * 4,
        [ANY] * 7,
        Spread.sems(len(ATTN_PIECES), 3) + Spread.sems(len(MLP_PIECES), 2) + ChainGather.SEMS * 2,
    )(normed_low, own_pos, w_attn, w_mlp)


def attention_close_ffn_open(
    partial, w_mlp, w_gate_up, w_down, hidden, normed_in, laurel_up, gains, ident
):
    rows, width = hidden.shape
    scratch = ChainScatter.scratch(rows, width)
    count = len(scratch)

    def kernel(
        partial_ref, w_ref, gate_up_in, down_in, hidden_ref, normed_ref, laurel_ref, gains_ref,
        attn_ref, joined_ref, gate_up_ref, down_ref, all_ref, own_ref, *refs
    ):
        place = Place()
        greet(place, "all", True)
        scatter = ChainScatter(place, partial_ref, refs[:count])
        spread = Spread(place, w_ref, [gate_up_ref, down_ref], MLP_PIECES, refs[count : count + 2])
        gather = ChainGather(place, own_ref, all_ref, refs[count + 2 :])
        scatter.start()
        scatter.ends()
        spread.start(2, 4)
        scatter.inner(0)
        spread.start(4, 6)
        scatter.inner(1)
        spread.start(6, 8)
        spread.forward(2)
        spread.forward(3)
        scatter.finish(attn_ref)
        laurel_res = normed_ref[...] + rms_norm(laurel_ref[...], gains_ref[1:2])
        after_attn = hidden_ref[...].astype(jnp.float32) + rms_norm(attn_ref[...], gains_ref[2:3])
        joined_ref[...] = (after_attn + laurel_res) / math.sqrt(2.0)
        own_ref[...] = rms_norm(joined_ref[...], gains_ref[3:4]).astype(jnp.bfloat16)
        gather.start()
        spread.relay(2)
        spread.forward(4)
        spread.relay(3)
        gather.step(1)
        spread.forward(5)
        spread.relay(4)
        gather.step(2)
        spread.forward(6)
        spread.relay(5)
        gather.step(3)
        spread.forward(7)
        spread.relay(6)
        spread.relay(7)
        spread.finish(2, 8)
        gather.finish()

    token_f32 = jax.ShapeDtypeStruct((rows, width), jnp.float32)
    return comm_call(
        kernel,
        ident,
        [
            token_f32,
            token_f32,
            bf16(*w_gate_up.shape),
            bf16(*w_down.shape),
            bf16(8 * rows, width),
        ],
        [VMEM, ANY, ANY, ANY, VMEM, VMEM, VMEM, VMEM],
        [VMEM, VMEM, ANY, ANY, ANY],
        [pltpu.VMEM((rows, width), jnp.bfloat16)]
        + scratch
        + Spread.sems(len(MLP_PIECES), 2)
        + ChainGather.SEMS,
        {2: 2, 3: 3},
    )(partial, w_mlp, w_gate_up, w_down, hidden, normed_in, laurel_up, gains)


def split_refs(refs, *counts):
    refs, parts = list(refs), []
    for count in counts:
        parts.append(refs[:count])
        refs = refs[count:]
    return parts


def unit_gradient(place, n, tokens_ref, grad_ref, out, turned_ref):
    zz = (place.z + ORDER[2 * n][0]) % 4
    count = turned_ref.shape[0] // 4
    for f in range(4):
        columns = cols_at((f * 4 + zz) * count, count)
        turned_ref[f * count : (f + 1) * count] = tokens_ref[:, columns].T
    step = 512

    @pl.loop(0, grad_ref.shape[1] // step)
    def _(t):
        columns = cols_at(t * step, step)
        block = plain_dot(turned_ref[...], grad_ref[:, columns]).astype(jnp.bfloat16)
        for f in range(4):
            out[f, :, columns] = block[f * count : (f + 1) * count]


def ffn_close_backward(
    partial, row_ffn, d_gate_up, row_d_ffn, activated, vec_grads, shard_height, mlp_cols, ident
):
    rows, width = partial.shape[0] // 8, partial.shape[1]
    wide, narrow = d_gate_up.shape[1], activated.shape[1]
    vec_width = vec_grads.shape[1]
    scatter_scratch = ChainScatter.scratch(rows, width)
    mlp_scratch = Drain.scratch(shard_height, (wide, narrow), 2)
    mlp_sems = Drain.sems(len(MLP_PIECES), 2, 2)
    vec_scratch = Drain.scratch(shard_height, (vec_width,))
    vec_sems = Drain.sems(1, 1)
    unit_rows = 2 * shard_height

    def kernel(*refs):
        (partial_ref, ffn_ref, dgu_ref, dffn_ref, act_ref, vec_ref), outs, held = split_refs(
            refs, 6, 7, len(refs) - 13
        )
        out_ref, mlp_land, vec_land, mid_wide, mid_narrow, end_wide, end_narrow = outs
        own, scat, mlp_s, mlp_m, vec_s, vec_m = split_refs(
            held, 3, len(scatter_scratch), len(mlp_scratch), 3, len(vec_scratch), 3
        )
        own_wide, own_narrow, turned = own
        place = Place()
        greet(place, "all", True)
        scatter = ChainScatter(place, partial_ref, scat)
        mlp = Drain(place, [own_wide, own_narrow], mlp_land, MLP_PIECES, mlp_s, mlp_m, 0, 2)
        vec = Drain(place, [vec_ref], vec_land, VEC_LAND, vec_s, vec_m)

        def unit(n, wide_ref, narrow_ref):
            unit_gradient(place, n, ffn_ref, dgu_ref, wide_ref, turned)
            unit_gradient(place, n, dffn_ref, act_ref, narrow_ref, turned)

        scatter.start()
        scatter.ends()
        unit(0, own_wide.at[0], own_narrow.at[0])
        mlp.start(0)
        mlp.start(1)
        for i in range(8):
            vec.start(i)
        unit(1, mid_wide.at[0], mid_narrow.at[0])
        scatter.inner(0)
        unit(2, mid_wide.at[1], mid_narrow.at[1])
        scatter.inner(1)
        unit(3, end_wide.at[0], end_narrow.at[0])
        mlp.middle(0)
        mlp.middle(1)
        scatter.finish(out_ref)
        for i in range(8):
            vec.middle(i)
        mlp.last(0)
        mlp.last(1)
        for i in range(8):
            vec.last(i)
        vec.finish()
        mlp.finish()

    def unit_shapes(count):
        return [bf16(count, 4, unit_rows, wide), bf16(count, 4, unit_rows, narrow)]

    return comm_call(
        kernel,
        ident,
        [
            jax.ShapeDtypeStruct((rows, width), jnp.float32),
            bf16(shard_height, mlp_cols),
            bf16(shard_height, 8 * vec_width),
        ]
        + unit_shapes(2)
        + unit_shapes(1),
        [VMEM] * 6,
        [VMEM, ANY, ANY] + [VMEM] * 4,
        [
            pltpu.VMEM((1, 4, unit_rows, wide), jnp.bfloat16),
            pltpu.VMEM((1, 4, unit_rows, narrow), jnp.bfloat16),
            pltpu.VMEM((4 * unit_rows, 8 * rows), jnp.bfloat16),
        ]
        + scatter_scratch
        + mlp_scratch
        + mlp_sems
        + vec_scratch
        + vec_sems,
    )(partial, row_ffn, d_gate_up, row_d_ffn, activated, vec_grads)


def attention_open_backward(d_attn_low, mid_wide, mid_narrow, mlp_land, vec_land, ident):
    rows, width = d_attn_low.shape
    shard_height, vec_width = vec_land.shape[0], vec_land.shape[1] // 8
    widths = (mid_wide.shape[3], mid_narrow.shape[3])
    mlp_scratch = Drain.scratch(shard_height, widths, 4)
    mlp_sems = Drain.sems(len(MLP_PIECES), 2, 4)
    vec_sems = Spread.sems(1, 1)

    def kernel(
        own_ref, wide_ref, narrow_ref, land_in, vec_ref, all_ref, land_ref, vec_all, *held
    ):
        (vec_own,), mlp_s, mlp_m, vec_m, gather_m = split_refs(held, 1, len(mlp_scratch), 3, 2, 2)
        place = Place()
        greet(place, "all", True)
        gather = ChainGather(place, own_ref, all_ref, gather_m)
        mlp = Drain(place, [wide_ref, narrow_ref], land_ref, MLP_PIECES, mlp_s, mlp_m, 2, 4)
        vec = Spread(place, vec_own, [vec_all], VEC_PIECES, vec_m)
        gather.start()
        mlp.start(0)
        mlp.start(1)
        total = vec_ref[:, 0:vec_width].astype(jnp.float32)
        for c in range(1, 8):
            total = total + vec_ref[:, c * vec_width : (c + 1) * vec_width].astype(jnp.float32)
        vec_own[...] = total.astype(jnp.bfloat16)
        gather.step(1)
        mlp.middle(0)
        mlp.start(2)
        vec.start()
        gather.step(2)
        mlp.middle(1)
        mlp.start(3)
        mlp.last(0)
        gather.step(3)
        mlp.middle(2)
        mlp.last(1)
        mlp.middle(3)
        mlp.last(2)
        for i in range(8):
            vec.forward(i)
            if i:
                vec.relay(i - 1)
        vec.relay(7)
        mlp.last(3)
        mlp.finish()
        gather.finish()
        vec.finish()

    return comm_call(
        kernel,
        ident,
        [bf16(8 * rows, width), bf16(*mlp_land.shape), bf16(32 * shard_height, vec_width)],
        [ANY, VMEM, VMEM, ANY, VMEM],
        [ANY, ANY, ANY],
        [pltpu.VMEM((shard_height, vec_width), jnp.bfloat16)]
        + mlp_scratch
        + mlp_sems
        + vec_sems
        + ChainGather.SEMS,
        {3: 1},
    )(d_attn_low, mid_wide, mid_narrow, mlp_land, vec_land)


def sum_everywhere(place, own, arrived, sems):
    z, k, f = place.z, place.k, place.f
    near = z + 1 - 2 * (z % 2)
    targets = [
        place.sibling,
        (place.x_side, place.c),
        (place.y_side, place.c),
        (f, near * 2 + k),
        (f, (3 - z) * 2 + k),
    ]
    return [
        remote(own.at[n], arrived.at[n], sems.at[0, n], sems.at[1, n], target)
        for n, target in enumerate(targets)
    ]


def close_backward(
    partial, base, hidden, gains, other_gains, mlp_grads, attn_grads, mlp_land, ident
):
    rows, width = base.shape
    shard_height = mlp_land.shape[0]
    scatter_scratch = ChainScatter.scratch(rows, width)
    mlp_scratch = Drain.scratch(shard_height, [grad.shape[3] for grad in mlp_grads], 2)
    mlp_sems = Drain.sems(len(MLP_PIECES), 2, 2)
    attn_scratch = Drain.scratch(shard_height, [grad.shape[1] for grad in attn_grads])
    attn_sems = Drain.sems(len(ATTN_LAND), 2)
    gain_rows = other_gains.shape[0]

    def kernel(*refs):
        ins, outs, held = split_refs(refs, 10, 4, len(refs) - 14)
        partial_ref, base_ref, hidden_ref, gains_ref, other_ref = ins[:5]
        out_ref, gain_ref, land_ref, attn_land = outs
        own_gains, scat, mlp_s, mlp_m, attn_s, attn_m = split_refs(
            held, 3, len(scatter_scratch), len(mlp_scratch), 3, len(attn_scratch), 3
        )
        place = Place()
        greet(place, "all", True)
        scatter = ChainScatter(place, partial_ref, scat)
        mlp = Drain(place, ins[5:7], land_ref, MLP_PIECES, mlp_s, mlp_m, 6, 2)
        attn = Drain(place, ins[7:9], attn_land, ATTN_LAND, attn_s, attn_m)
        held_gains, arrived_gains, gain_sems = own_gains
        rounds = sum_everywhere(place, held_gains, arrived_gains, gain_sems)

        def gain_round(n):
            rounds[n].wait_recv()
            held_gains[n + 1] = held_gains[n] + arrived_gains[n]
            if n < 4:
                rounds[n + 1].start()

        scatter.start()
        scatter.ends()
        mlp.start(0)
        mlp.start(1)
        attn.start(0)
        attn.start(1)
        scatter.inner(0)
        mlp.middle(0)
        scatter.inner(1)
        mlp.middle(1)
        attn.start(2)
        mlp.last(0)
        mlp.last(1)
        scatter.finish(out_ref)
        hidden_val = hidden_ref[...].astype(jnp.float32)
        inverse = lax.rsqrt(jnp.mean(hidden_val * hidden_val, axis=-1, keepdims=True) + EPSILON)
        unit = hidden_val * inverse
        d_normed = base_ref[...] + out_ref[...]
        scaled = d_normed * gains_ref[0:1]
        out_ref[...] = (
            scaled - unit * jnp.mean(unit * scaled, axis=-1, keepdims=True)
        ) * inverse
        held_gains[0] = other_ref[...]
        held_gains[0, 0:1] = jnp.sum(d_normed * unit, axis=0, keepdims=True)
        rounds[0].start()
        for i in range(8):
            attn.middle(i)
            if i < 5:
                attn.start(i + 3)
            if i:
                attn.last(i - 1)
            if i < 5:
                gain_round(i)
        attn.last(7)
        gain_ref[...] = held_gains[5]
        for copy in rounds:
            copy.wait_send()
        mlp.finish()
        attn.finish()

    attn_land_cols = 8 * sum(grad.shape[1] for grad in attn_grads)
    return comm_call(
        kernel,
        ident,
        [
            jax.ShapeDtypeStruct((rows, width), jnp.float32),
            jax.ShapeDtypeStruct((gain_rows, width), jnp.float32),
            bf16(*mlp_land.shape),
            bf16(shard_height, attn_land_cols),
        ],
        [VMEM] * 9 + [ANY],
        [VMEM, VMEM, ANY, ANY],
        [
            pltpu.VMEM((6, gain_rows, width), jnp.float32),
            pltpu.VMEM((5, gain_rows, width), jnp.float32),
            pltpu.SemaphoreType.DMA((2, 5)),
        ]
        + scatter_scratch
        + mlp_scratch
        + mlp_sems
        + attn_scratch
        + attn_sems,
        {9: 2},
    )(partial, base, hidden, gains, other_gains, *mlp_grads, *attn_grads, mlp_land)


def per_device_split(
    hidden_in, layer_vec, positions, w_attn, w_mlp, pl_gate, pl_proj, gains, head_gains, out_grad
):
    shard_height = w_attn.shape[0]
    row_total = QH * positions.shape[0]
    lanes = jnp.arange(128, dtype=jnp.int32)[None, :]
    own_pos = jnp.where(lanes == 0, positions[:, None] // 256, positions[:, None] % 256)

    def qk_prep(raw_heads, scale_vec):
        return rotary(rms_norm(raw_heads, scale_vec), row_pos)

    hidden = hidden_in.astype(jnp.float32)
    normed_in = rms_norm(hidden, gains[0])
    normed_low = normed_in.astype(jnp.bfloat16)
    w_qkv, w_out, w_laurel, row_normed, row_parts, w_gate_up, w_down = attention_open(
        normed_low, own_pos.astype(jnp.bfloat16), w_attn, w_mlp, 1
    )
    row_pos = row_parts[:, 0].astype(jnp.int32) * 256 + row_parts[:, 1].astype(jnp.int32)
    latent = plain_dot(normed_low, w_laurel[:, :RANK]).astype(jnp.bfloat16)
    laurel_up = times_transposed(latent, w_laurel[:, RANK:])

    projected = plain_dot(row_normed, w_qkv)
    q_raw = projected[:, None, :HEAD]
    k_raw = projected[:, None, HEAD : 2 * HEAD]
    v_raw = projected[:, None, 2 * HEAD :]
    queries = qk_prep(q_raw, head_gains[0]).astype(jnp.bfloat16)[:, 0]
    keys = qk_prep(k_raw, head_gains[1]).astype(jnp.bfloat16)[:, 0]
    values = value_norm(v_raw).astype(jnp.bfloat16)[:, 0]
    index = jnp.arange(row_total, dtype=jnp.int32)
    distance = index[:, None] - index[None, :]
    allowed = (distance >= 0) & (distance <= jnp.minimum(row_pos, WINDOW - 1)[:, None])
    scores = jnp.where(allowed, times_transposed(queries, keys), NEG_LARGE)
    row_max = jnp.max(scores, axis=-1, keepdims=True)
    exp_scores = jnp.exp(scores - row_max)
    row_sum = jnp.sum(exp_scores, axis=-1, keepdims=True)
    probs = exp_scores / row_sum
    probs_low = probs.astype(jnp.bfloat16)
    mixed = plain_dot(probs_low, values).astype(jnp.bfloat16)
    attn_partial = times_transposed(mixed, w_out).astype(jnp.bfloat16)
    attn_out, joined, w_gate_up, w_down, row_ffn = attention_close_ffn_open(
        attn_partial, w_mlp, w_gate_up, w_down, hidden_in, normed_in, laurel_up, gains, 2
    )
    gate_up = plain_dot(row_ffn, w_gate_up)
    activated = activate(gate_up).astype(jnp.bfloat16)
    ffn_out = scatter_tokens(times_transposed(activated, w_down).astype(jnp.bfloat16), 4)

    after_ffn = joined + rms_norm(ffn_out, gains[4])
    after_low = after_ffn.astype(jnp.bfloat16)
    vec_gate = plain_dot(after_low, pl_gate)
    vector_in = layer_vec.astype(jnp.float32)
    vec_mixed = vec_mix(vec_gate, vector_in).astype(jnp.bfloat16)
    vec_out = plain_dot(vec_mixed, pl_proj)
    result_out = after_ffn + rms_norm(vec_out, gains[5])
    upstream = out_grad.astype(jnp.float32)
    unused_out, vec_norm_back = jax.vjp(rms_norm, vec_out, gains[5])
    d_vec_out, d_gain_vec = vec_norm_back(upstream)
    d_vec_out_low = d_vec_out.astype(jnp.bfloat16)
    d_vec_mixed = times_transposed(d_vec_out_low, pl_proj)
    turned_pl_proj = contract_rows(d_vec_out_low, vec_mixed)
    unused_out, mix_back = jax.vjp(vec_mix, vec_gate, vector_in)
    d_vec_gate, d_vector_in = mix_back(d_vec_mixed)
    d_vec_gate_low = d_vec_gate.astype(jnp.bfloat16)
    grad_after = upstream + times_transposed(d_vec_gate_low, pl_gate)
    grad_pl_gate = contract_rows(after_low, d_vec_gate_low)
    unused_out, ffn_norm_back = jax.vjp(rms_norm, ffn_out, gains[4])
    d_ffn_out, d_gain_ffn = ffn_norm_back(grad_after)
    d_ffn_low = d_ffn_out.astype(jnp.bfloat16)

    row_d_ffn = gather_tokens(d_ffn_low, 5)
    unused_out, act_back = jax.vjp(activate, gate_up)
    d_gate_up = act_back(plain_dot(row_d_ffn, w_down))[0].astype(jnp.bfloat16)
    vec_grads = jnp.concatenate([grad_pl_gate, turned_pl_proj], axis=1).astype(jnp.bfloat16)
    d_ffn_in, mlp_land, vec_land, mid_wide, mid_narrow, end_wide, end_narrow = ffn_close_backward(
        times_transposed(d_gate_up, w_gate_up).astype(jnp.bfloat16),
        row_ffn,
        d_gate_up,
        row_d_ffn,
        activated,
        vec_grads,
        shard_height,
        w_mlp.shape[1],
        6,
    )

    unused_out, pre_norm_back = jax.vjp(rms_norm, joined, gains[3])
    d_joined_part, d_gain_pre = pre_norm_back(d_ffn_in)
    d_half = (grad_after + d_joined_part) / math.sqrt(2.0)
    unused_out, laurel_norm_back = jax.vjp(rms_norm, laurel_up, gains[1])
    d_laurel_up, d_gain_laurel = laurel_norm_back(d_half)
    unused_out, attn_norm_back = jax.vjp(rms_norm, attn_out, gains[2])
    d_attn_out, d_gain_attn = attn_norm_back(d_half)
    d_laurel_low = d_laurel_up.astype(jnp.bfloat16)
    row_d_attn, mlp_land, vec_all = attention_open_backward(
        d_attn_out.astype(jnp.bfloat16), mid_wide, mid_narrow, mlp_land, vec_land, 7
    )
    d_latent_low = plain_dot(d_laurel_low, w_laurel[:, RANK:]).astype(jnp.bfloat16)
    d_mixed = plain_dot(row_d_attn, w_out).astype(jnp.bfloat16)
    d_probs = times_transposed(d_mixed, values)
    inner_sum = jnp.sum(probs * d_probs, axis=-1, keepdims=True)
    d_scores = (probs * (d_probs - inner_sum)).astype(jnp.bfloat16)
    d_queries = plain_dot(d_scores, keys)
    d_keys = contract_rows(d_scores, queries)
    d_values = contract_rows(probs_low, d_mixed)
    unused_out, query_back = jax.vjp(qk_prep, q_raw, head_gains[0])
    d_q_raw, d_head_query = query_back(d_queries[:, None])
    unused_out, key_back = jax.vjp(qk_prep, k_raw, head_gains[1])
    d_k_raw, d_head_key = key_back(d_keys[:, None])
    unused_out, value_back = jax.vjp(value_norm, v_raw)
    d_v_raw = value_back(d_values[:, None])[0]
    d_projected = jnp.concatenate([d_q_raw[:, 0], d_k_raw[:, 0], d_v_raw[:, 0]], axis=1).astype(
        jnp.bfloat16
    )
    laurel_partial = jnp.concatenate(
        [contract_rows(normed_low, d_latent_low), contract_rows(d_laurel_low, latent)], axis=1
    )
    other_gains = jnp.concatenate(
        [
            jnp.zeros_like(gains[:1]),
            jnp.stack([d_gain_laurel, d_gain_attn, d_gain_pre, d_gain_ffn, d_gain_vec]),
            jnp.pad(
                jnp.concatenate([d_head_query, d_head_key])[None],
                ((0, 1), (0, gains.shape[1] - 2 * HEAD)),
            ),
        ],
        axis=0,
    )
    d_hidden_part, all_gains, mlp_land, attn_land = close_backward(
        times_transposed(d_projected, w_qkv).astype(jnp.bfloat16),
        d_half + times_transposed(d_latent_low, w_laurel[:, :RANK]),
        hidden_in,
        gains,
        other_gains,
        [end_wide, end_narrow],
        [
            jnp.concatenate(
                [
                    contract_rows(row_normed, d_projected).astype(jnp.bfloat16),
                    laurel_partial.astype(jnp.bfloat16),
                ],
                axis=1,
            ),
            contract_rows(row_d_attn, mixed).astype(jnp.bfloat16),
        ],
        mlp_land,
        9,
    )
    grad_hidden = d_half + d_hidden_part
    landed = attn_land.astype(jnp.float32).reshape(shard_height, KVH, QH // KVH, 1152)

    def heads_of(first):
        return landed[..., first : first + HEAD]

    grad_w_attn = jnp.concatenate(
        [
            heads_of(0).reshape(shard_height, QH * HEAD),
            jnp.sum(heads_of(HEAD), axis=2).reshape(shard_height, KVH * HEAD),
            jnp.sum(heads_of(2 * HEAD), axis=2).reshape(shard_height, KVH * HEAD),
            jnp.sum(landed[..., 3 * HEAD : 3 * HEAD + 2 * RANK], axis=(1, 2)),
            heads_of(896).reshape(shard_height, QH * HEAD),
        ],
        axis=1,
    )
    vec_sums = vec_all.astype(jnp.float32)
    grad_gate_all, grad_proj_all = vec_sums[:, : pl_gate.shape[1]], vec_sums[:, pl_gate.shape[1] :].T
    grad_gains, grad_heads = all_gains[:6], all_gains[6, : 2 * HEAD].reshape(2, HEAD)
    return (
        result_out.astype(jnp.bfloat16),
        grad_hidden,
        d_vector_in,
        grad_w_attn,
        mlp_land.astype(jnp.float32),
        grad_gate_all,
        grad_proj_all,
        grad_gains,
        grad_heads,
    )


def solution(mesh):
    fits = mesh.shape["ctx"] == QH and mesh.shape["fsdp"] == 4
    body = per_device_split if fits else per_device
    return jax.shard_map(
        body,
        mesh=mesh,
        in_specs=(
            P(("fsdp", "ctx"), None),
            P(("fsdp", "ctx"), None),
            P(("fsdp", "ctx")),
            P(("fsdp", "ctx"), None),
            P(("fsdp", "ctx"), None),
            P(),
            P(),
            P(),
            P(),
            P(("fsdp", "ctx"), None),
        ),
        out_specs=(
            P(("fsdp", "ctx"), None),
            P(("fsdp", "ctx"), None),
            P(("fsdp", "ctx"), None),
            P(("fsdp", "ctx"), None),
            P(("fsdp", "ctx"), None),
            P(),
            P(),
            P(),
            P(),
        ),
        check_vma=False,
    )
```

```python
import math

import jax
import jax.numpy as jnp
from jax import lax
from jax.experimental import pallas as pl
from jax.experimental.pallas import tpu as pltpu
from jax.sharding import PartitionSpec as P

QH = 8
KVH = 2
HEAD = 256
RANK = 64
WINDOW = 512


EPSILON = 1e-06
THETA = 10000.0
NEG_LARGE = -1e30


def passed_along(block, axis, distance):
    devices = range(lax.axis_size(axis))
    route = [(i - distance, i) for i in devices if i - distance in devices]
    return lax.ppermute(block, axis, route)


def rms_norm(values, scale_vec):
    return (
        values * lax.rsqrt(jnp.mean(values * values, axis=-1, keepdims=True) + EPSILON) * scale_vec
    )


def value_norm(values):
    return rms_norm(values, 1.0)


def rotary(values, positions):
    half_size = values.shape[-1] // 2
    frequency = jnp.exp(
        jnp.arange(half_size, dtype=jnp.float32) * (-2.0 * math.log(THETA) / values.shape[-1])
    )
    angles = positions.astype(jnp.float32)[:, None] * frequency[None, :]
    cosine = jnp.cos(angles)[:, None, :]
    sine_part = jnp.sin(angles)[:, None, :]
    first_half = values[..., :half_size]
    second_half = values[..., half_size:]
    return jnp.concatenate(
        [
            first_half * cosine - second_half * sine_part,
            second_half * cosine + first_half * sine_part,
        ],
        axis=-1,
    )


def plain_dot(left_side, right_side):
    return jnp.dot(left_side, right_side, preferred_element_type=jnp.float32)


def times_transposed(left_side, right_side):
    return lax.dot_general(
        left_side, right_side, (((1,), (1,)), ((), ())), preferred_element_type=jnp.float32
    )


def contract_rows(left_side, right_side):
    return lax.dot_general(
        left_side, right_side, (((0,), (0,)), ((), ())), preferred_element_type=jnp.float32
    )


def activate(gate_up_val):
    half_cols = gate_up_val.shape[1] // 2
    return jax.nn.gelu(gate_up_val[:, :half_cols], approximate=True) * gate_up_val[:, half_cols:]


def vec_mix(gate_val, vector_val):
    return jax.nn.gelu(gate_val, approximate=True) * vector_val


def per_device(
    hidden_in, layer_vec, positions, w_attn, w_mlp, pl_gate, pl_proj, gains, head_gains, out_grad
):
    row_count = hidden_in.shape[0]
    model_width = hidden_in.shape[1]
    q_width = QH * HEAD
    kv_width = KVH * HEAD
    in_cols = q_width + 2 * kv_width + RANK
    group_size = QH // KVH
    ff_width = w_mlp.shape[1] // 3
    shard_height = w_mlp.shape[0]
    fsdp_count = lax.axis_size("fsdp")
    ctx_count = lax.axis_size("ctx")
    quarter = ff_width // fsdp_count

    def permute_cols(matrix):
        return (
            matrix.reshape(-1, fsdp_count, ctx_count, shard_height)
            .transpose(0, 2, 1, 3)
            .reshape(-1, model_width)
        )

    def restore_cols(matrix):
        return (
            matrix.reshape(-1, ctx_count, fsdp_count, shard_height)
            .transpose(0, 2, 1, 3)
            .reshape(-1, model_width)
        )

    def qk_prep(raw_heads, scale_vec):
        return rotary(rms_norm(raw_heads, scale_vec), positions)

    hidden = hidden_in.astype(jnp.float32)
    normed_in = rms_norm(hidden, gains[0])
    normed_low = normed_in.astype(jnp.bfloat16)
    projected = plain_dot(
        normed_low, lax.all_gather(w_attn[:, :in_cols], ("fsdp", "ctx"), axis=0, tiled=True)
    )
    q_raw = projected[:, :q_width].reshape(row_count, QH, HEAD)
    k_raw = projected[:, q_width : q_width + kv_width].reshape(row_count, KVH, HEAD)
    v_raw = projected[:, q_width + kv_width : q_width + 2 * kv_width].reshape(row_count, KVH, HEAD)
    latent = projected[:, q_width + 2 * kv_width :].astype(jnp.bfloat16)
    queries = qk_prep(q_raw, head_gains[0]).astype(jnp.bfloat16)
    keys_own = qk_prep(k_raw, head_gains[1]).astype(jnp.bfloat16)
    values_own = value_norm(v_raw).astype(jnp.bfloat16)
    kv_own = jnp.concatenate(
        [keys_own.reshape(row_count, kv_width), values_own.reshape(row_count, kv_width)], axis=1
    )
    hop_count = (WINDOW - 1) // row_count + 1
    earlier = []
    moving = kv_own
    for step_back in range(hop_count):
        moving = passed_along(moving, "ctx", 1)
        earlier.append(moving)
    kv_all = jnp.concatenate(earlier[::-1] + [kv_own], axis=0)
    span_rows = kv_all.shape[0]
    keys_all = kv_all[:, :kv_width].reshape(span_rows, KVH, HEAD)
    values_all = kv_all[:, kv_width:].reshape(span_rows, KVH, HEAD)
    grouped = queries.reshape(row_count, KVH, group_size, HEAD)
    distance = (
        jnp.arange(row_count, dtype=jnp.int32)[:, None]
        + hop_count * row_count
        - jnp.arange(span_rows, dtype=jnp.int32)[None, :]
    )
    allowed = (distance >= 0) & (distance <= jnp.minimum(positions, WINDOW - 1)[:, None])
    scores = jnp.einsum("qgrd,kgd->grqk", grouped, keys_all, preferred_element_type=jnp.float32)
    scores = jnp.where(allowed[None, None], scores, NEG_LARGE)
    row_max = jnp.max(scores, axis=-1, keepdims=True)
    exp_scores = jnp.exp(scores - row_max)
    row_sum = jnp.sum(exp_scores, axis=-1, keepdims=True)
    log_total = row_max + jnp.log(row_sum)
    probs_low = (exp_scores / row_sum).astype(jnp.bfloat16)
    mixed = jnp.einsum("grqk,kgd->qgrd", probs_low, values_all, preferred_element_type=jnp.float32)
    mixed = mixed.reshape(row_count, q_width).astype(jnp.bfloat16)
    shard_rows = lax.all_gather(w_attn[:, in_cols:], ("fsdp", "ctx"), axis=0, tiled=True)
    laurel_part = times_transposed(latent, shard_rows[:, :RANK])
    attn_part = times_transposed(mixed, shard_rows[:, RANK:])
    out_pair = jnp.stack([laurel_part, attn_part], axis=1)
    laurel_up = out_pair[:, 0]
    attn_out = out_pair[:, 1]
    laurel_res = normed_in + rms_norm(laurel_up, gains[1])
    after_attn = hidden + rms_norm(attn_out, gains[2])
    joined = (after_attn + laurel_res) / math.sqrt(2.0)
    ffn_low = rms_norm(joined, gains[3]).astype(jnp.bfloat16)
    sent_rows = w_mlp.reshape(shard_height, 3, fsdp_count, quarter)
    sent_tokens = jnp.broadcast_to(
        ffn_low[:, None, None, :], (row_count, 1, fsdp_count, model_width)
    )
    got_rows, got_tokens = (
        lax.all_to_all(sent_rows, "fsdp", split_axis=2, concat_axis=0, tiled=True),
        lax.all_to_all(sent_tokens, "fsdp", split_axis=2, concat_axis=0, tiled=True),
    )
    quarter_rows = lax.all_gather(got_rows, "ctx", axis=0, tiled=True).reshape(
        model_width, 3, quarter
    )
    w_gate_up = quarter_rows[:, :2].reshape(model_width, 2 * quarter)
    w_down = quarter_rows[:, 2]
    ffn_perm = permute_cols(got_tokens.reshape(fsdp_count * row_count, model_width))
    gate_up = plain_dot(ffn_perm, w_gate_up)
    activated = activate(gate_up).astype(jnp.bfloat16)
    ffn_out = lax.psum_scatter(
        restore_cols(times_transposed(activated, w_down)), "fsdp", scatter_dimension=0, tiled=True
    )
    after_ffn = joined + rms_norm(ffn_out, gains[4])
    after_low = after_ffn.astype(jnp.bfloat16)
    vec_gate = plain_dot(after_low, pl_gate)
    vector_in = layer_vec.astype(jnp.float32)
    vec_mixed = vec_mix(vec_gate, vector_in).astype(jnp.bfloat16)
    vec_out = plain_dot(vec_mixed, pl_proj)
    result_out = after_ffn + rms_norm(vec_out, gains[5])
    upstream = out_grad.astype(jnp.float32)
    unused_out, vec_norm_back = jax.vjp(rms_norm, vec_out, gains[5])
    d_vec_out, d_gain_vec = vec_norm_back(upstream)
    d_vec_out_low = d_vec_out.astype(jnp.bfloat16)
    d_vec_mixed = times_transposed(d_vec_out_low, pl_proj)
    grad_pl_proj = contract_rows(vec_mixed, d_vec_out_low)
    unused_out, mix_back = jax.vjp(vec_mix, vec_gate, vector_in)
    d_vec_gate, d_vector_in = mix_back(d_vec_mixed)
    d_vec_gate_low = d_vec_gate.astype(jnp.bfloat16)
    grad_after = upstream + times_transposed(d_vec_gate_low, pl_gate)
    grad_pl_gate = contract_rows(after_low, d_vec_gate_low)
    unused_out, ffn_norm_back = jax.vjp(rms_norm, ffn_out, gains[4])
    d_ffn_out, d_gain_ffn = ffn_norm_back(grad_after)
    d_ffn_low = d_ffn_out.astype(jnp.bfloat16)
    unused_out, act_back = jax.vjp(activate, gate_up)
    d_ffn_all = lax.all_gather(d_ffn_low, "fsdp", axis=0, tiled=True)
    d_ffn_perm = permute_cols(d_ffn_all)
    d_activated = plain_dot(d_ffn_perm, w_down)
    d_gate_up = act_back(d_activated)[0].astype(jnp.bfloat16)
    d_ffn_in = lax.psum_scatter(
        restore_cols(times_transposed(d_gate_up, w_gate_up)).astype(jnp.bfloat16),
        "fsdp",
        scatter_dimension=0,
        tiled=True,
    ).astype(jnp.float32)
    summed = lax.psum_scatter(
        jnp.concatenate(
            [contract_rows(ffn_perm, d_gate_up), contract_rows(d_ffn_perm, activated)], axis=1
        ).astype(jnp.bfloat16),
        "ctx",
        scatter_dimension=0,
        tiled=True,
    ).astype(jnp.float32)
    grad_w_mlp = (
        lax.all_to_all(
            summed.reshape(fsdp_count * shard_height, 3, 1, quarter).astype(jnp.bfloat16),
            "fsdp",
            split_axis=0,
            concat_axis=2,
            tiled=True,
        )
        .astype(jnp.float32)
        .reshape(shard_height, 3 * ff_width)
    )
    unused_out, pre_norm_back = jax.vjp(rms_norm, joined, gains[3])
    d_joined_part, d_gain_pre = pre_norm_back(d_ffn_in)
    d_joined = grad_after + d_joined_part
    d_half = d_joined / math.sqrt(2.0)
    unused_out, laurel_norm_back = jax.vjp(rms_norm, laurel_up, gains[1])
    d_laurel_up, d_gain_laurel = laurel_norm_back(d_half)
    unused_out, attn_norm_back = jax.vjp(rms_norm, attn_out, gains[2])
    d_attn_out, d_gain_attn = attn_norm_back(d_half)
    d_laurel_low = d_laurel_up.astype(jnp.bfloat16)
    d_attn_low = d_attn_out.astype(jnp.bfloat16)
    shard_rows = lax.all_gather(w_attn[:, in_cols:], ("fsdp", "ctx"), axis=0, tiled=True)
    d_latent = plain_dot(d_laurel_low, shard_rows[:, :RANK])
    d_mixed = plain_dot(d_attn_low, shard_rows[:, RANK:])
    d_grouped = d_mixed.astype(jnp.bfloat16).reshape(row_count, KVH, group_size, HEAD)
    again = jnp.einsum("qgrd,kgd->grqk", grouped, keys_all, preferred_element_type=jnp.float32)
    again = jnp.where(allowed[None, None], again, NEG_LARGE)
    probs = jnp.exp(again - log_total)
    d_probs = jnp.einsum(
        "qgrd,kgd->grqk", d_grouped, values_all, preferred_element_type=jnp.float32
    )
    inner_sum = jnp.sum(probs * d_probs, axis=-1, keepdims=True)
    d_scores = (probs * (d_probs - inner_sum)).astype(jnp.bfloat16)
    d_queries = jnp.einsum(
        "grqk,kgd->qgrd", d_scores, keys_all, preferred_element_type=jnp.float32
    ).reshape(row_count, QH, HEAD)
    d_keys_all = jnp.einsum("grqk,qgrd->kgd", d_scores, grouped, preferred_element_type=jnp.float32)
    d_values_all = jnp.einsum(
        "grqk,qgrd->kgd", probs.astype(jnp.bfloat16), d_grouped, preferred_element_type=jnp.float32
    )
    d_kv_all = jnp.concatenate(
        [d_keys_all.reshape(span_rows, kv_width), d_values_all.reshape(span_rows, kv_width)], axis=1
    )
    returned = d_kv_all[:row_count]
    for step_back in range(1, hop_count + 1):
        returned = (
            passed_along(returned.astype(jnp.bfloat16), "ctx", -1).astype(returned.dtype)
            + d_kv_all[step_back * row_count : (step_back + 1) * row_count]
        )
    d_keys_own = returned[:, :kv_width].reshape(row_count, KVH, HEAD)
    d_values_own = returned[:, kv_width:].reshape(row_count, KVH, HEAD)
    unused_out, query_back = jax.vjp(qk_prep, q_raw, head_gains[0])
    d_q_raw, d_head_query = query_back(d_queries)
    unused_out, key_back = jax.vjp(qk_prep, k_raw, head_gains[1])
    d_k_raw, d_head_key = key_back(d_keys_own)
    unused_out, value_back = jax.vjp(value_norm, v_raw)
    d_v_raw = value_back(d_values_own)[0]
    d_projected = jnp.concatenate(
        [
            d_q_raw.reshape(row_count, q_width),
            d_k_raw.reshape(row_count, kv_width),
            d_v_raw.reshape(row_count, kv_width),
            d_latent,
        ],
        axis=1,
    ).astype(jnp.bfloat16)
    d_normed_part = times_transposed(
        d_projected, lax.all_gather(w_attn[:, :in_cols], ("fsdp", "ctx"), axis=0, tiled=True)
    )
    unused_out, input_norm_back = jax.vjp(rms_norm, hidden, gains[0])
    d_hidden_part, d_gain_input = input_norm_back(d_half + d_normed_part)
    grad_hidden = d_half + d_hidden_part
    grad_w_attn = lax.psum_scatter(
        jnp.concatenate(
            [
                contract_rows(normed_low, d_projected),
                contract_rows(d_laurel_low, latent),
                contract_rows(d_attn_low, mixed),
            ],
            axis=1,
        ),
        ("fsdp", "ctx"),
        scatter_dimension=0,
        tiled=True,
    )
    gain_rows = jnp.stack(
        [d_gain_input, d_gain_laurel, d_gain_attn, d_gain_pre, d_gain_ffn, d_gain_vec]
    )
    head_rows = jnp.stack([d_head_query, d_head_key])
    grad_gains, grad_heads, grad_gate_all, grad_proj_all = lax.psum(
        (gain_rows, head_rows, grad_pl_gate, grad_pl_proj), ("fsdp", "ctx")
    )
    return (
        result_out.astype(jnp.bfloat16),
        grad_hidden,
        d_vector_in,
        grad_w_attn,
        grad_w_mlp,
        grad_gate_all,
        grad_proj_all,
        grad_gains,
        grad_heads,
    )

MESH = pl.DeviceIdType.MESH
VMEM_LIMIT = 60 * 1024 * 1024
ORDER = ((0, 0), (0, 1), (1, 0), (1, 1), (2, 0), (2, 1), (3, 0), (3, 1))


class Place:
    def __init__(self):
        self.f = lax.axis_index("fsdp")
        self.c = lax.axis_index("ctx")
        self.z = self.c // 2
        self.k = self.c % 2
        self.x_side = self.f + 1 - 2 * (self.f % 2)
        self.y_side = (self.f + 2) % 4
        self.diag = 3 - self.f
        self.sibling = (self.f, self.c + 1 - 2 * self.k)
        self.up = (self.f, self.c + 2)
        self.down = (self.f, self.c - 2)
        self.has_up = self.z < 3
        self.has_down = self.z > 0

    def partner(self, which):
        z = self.z
        return (z, z + 1 - 2 * (z % 2), (z + 2) % 4, 3 - z)[which]

    def peer(self, i):
        which, other = ORDER[i]
        return self.partner(which) * 2 + (self.k + other) % 2


def rows_at(start, count):
    return pl.ds(pl.multiple_of(start, 16), count)


def cols_at(start, count):
    if isinstance(start, int):
        return pl.ds(start, count)
    return pl.ds(pl.multiple_of(start, 128), count)


def remote(src, dst, send_sem, recv_sem, target):
    return pltpu.make_async_remote_copy(
        src_ref=src,
        dst_ref=dst,
        send_sem=send_sem,
        recv_sem=recv_sem,
        device_id=target,
        device_id_type=MESH,
    )


def greet(place, line, plane):
    barrier = pltpu.get_barrier_semaphore()
    count = 0

    def tell(target):
        pl.semaphore_signal(barrier, inc=1, device_id=target, device_id_type=MESH)

    if line == "all":
        for i in range(1, 8):
            tell((place.f, place.peer(i)))
        count += 7
    elif line == "chain":
        tell(place.sibling)
        for distance in (1, 3):
            tell((place.f, (place.z + distance) % 4 * 2 + place.k))
        count += 3
    if plane:
        tell((place.x_side, place.c))
        tell((place.y_side, place.c))
        count += 2
    pl.semaphore_wait(barrier, count)


class ChainGather:
    SEMS = [pltpu.SemaphoreType.DMA((2, 10)), pltpu.SemaphoreType.DMA((1,))]

    def __init__(self, place, own, out, sems):
        self.place, self.own, self.out = place, own, out
        self.sems, self.local_sem = sems
        self.rows = own.shape[0]

    def block(self, origin_z, core=None):
        core = self.place.k if core is None else core
        return self.out.at[rows_at((origin_z * 2 + core) * self.rows, self.rows)]

    def copy(self, src, dst, index, target):
        return remote(src, dst, self.sems.at[0, index], self.sems.at[1, index], target)

    def local(self):
        return pltpu.make_async_copy(self.own, self.block(self.place.z), self.local_sem.at[0])

    def upward(self, step):
        src = self.own if step == 0 else self.block(self.place.z - step)
        return self.copy(src, self.block(self.place.z - step), step, self.place.up)

    def downward(self, step):
        src = self.own if step == 0 else self.block(self.place.z + step)
        return self.copy(src, self.block(self.place.z + step), 3 + step, self.place.down)

    def across(self, origin_z, own=False):
        src = self.own if own else self.block(origin_z)
        return self.copy(src, self.block(origin_z), 6 + origin_z, self.place.sibling)

    def start(self):
        place = self.place

        @pl.when(place.has_up)
        def _():
            self.upward(0).start()

        @pl.when(place.has_down)
        def _():
            self.downward(0).start()

        self.across(place.z, True).start()
        self.local().start()

    def step(self, step):
        place = self.place

        @pl.when(place.z - step >= 0)
        def _():
            self.copy(self.own, self.block(place.z - step), step - 1, place.up).wait_recv()
            if step < 3:

                @pl.when(place.has_up)
                def _():
                    self.upward(step).start()

            self.across(place.z - step).start()

        @pl.when(place.z + step <= 3)
        def _():
            self.copy(self.own, self.block(place.z + step), 3 + step - 1, place.down).wait_recv()
            if step < 3:

                @pl.when(place.has_down)
                def _():
                    self.downward(step).start()

            self.across(place.z + step).start()

    def finish(self):
        self.arrive()
        self.settle()

    def from_sibling(self, origin):
        return self.copy(
            self.own, self.block(origin, 1 - self.place.k), 6 + origin, self.place.sibling
        )

    def arrive(self):
        self.local().wait()
        for origin in range(4):
            self.from_sibling(origin).wait_recv()

    def settle(self):
        place = self.place
        for origin in range(4):
            self.from_sibling(origin).wait_send()
        for step in range(3):

            @pl.when((place.z - step >= 0) & place.has_up)
            def _(step=step):
                self.upward(step).wait_send()

            @pl.when((place.z + step <= 3) & place.has_down)
            def _(step=step):
                self.downward(step).wait_send()


class ChainScatter:
    @staticmethod
    def scratch(rows, cols):
        return [
            pltpu.VMEM((4, rows, cols), jnp.bfloat16),
            pltpu.VMEM((6, rows, cols), jnp.bfloat16),
            pltpu.VMEM((6, rows, cols), jnp.bfloat16),
            pltpu.SemaphoreType.DMA((2, 10)),
        ]

    def __init__(self, place, partial, scratch):
        self.place, self.partial = place, partial
        self.from_sibling, self.arrived, self.going, self.sems = scratch
        self.rows = partial.shape[0] // 8

    def block(self, origin_z, core):
        return self.partial.at[rows_at((origin_z * 2 + core) * self.rows, self.rows)]

    def across(self, dest):
        return remote(
            self.block(dest, 1 - self.place.k),
            self.from_sibling.at[dest],
            self.sems.at[0, 6 + dest],
            self.sems.at[1, 6 + dest],
            self.place.sibling,
        )

    def moved(self, slot, target):
        return remote(
            self.going.at[slot],
            self.arrived.at[slot],
            self.sems.at[0, slot],
            self.sems.at[1, slot],
            target,
        )

    def start(self):
        for dest in (3, 0, 2, 1):
            self.across(dest).start()

    def pair_sum(self, dest):
        return self.block(dest, self.place.k)[...].astype(jnp.float32) + self.from_sibling[
            dest
        ].astype(jnp.float32)

    def pass_on(self, dest, upward, inner=False):
        place = self.place
        slot = dest - 1 if upward else 3 + dest
        target = place.up if upward else place.down
        self.across(dest).wait_recv()
        total = self.pair_sum(dest)
        if inner:
            self.moved(slot, target).wait_recv()
            total = total + self.arrived[slot].astype(jnp.float32)
        self.going[slot] = total.astype(jnp.bfloat16)
        self.moved(slot, target).start()

    def ends(self):
        z = self.place.z

        @pl.when(z == 0)
        def _():
            for dest in (3, 2, 1):
                self.pass_on(dest, True)

        @pl.when(z == 3)
        def _():
            for dest in (0, 1, 2):
                self.pass_on(dest, False)

    def inner(self, i):
        z = self.place.z

        @pl.when(z == 1)
        def _():
            if i == 0:
                self.pass_on(3, True, True)
            else:
                self.pass_on(0, False, True)
                self.pass_on(2, True, True)

        @pl.when(z == 2)
        def _():
            if i == 0:
                self.pass_on(0, False, True)
            else:
                self.pass_on(3, True, True)
                self.pass_on(1, False, True)

    def finish(self, out):
        place = self.place
        for dest in range(4):

            @pl.when(place.z == dest)
            def _(dest=dest):
                self.across(dest).wait_recv()
                total = self.pair_sum(dest)
                if dest > 0:
                    self.moved(dest - 1, place.up).wait_recv()
                    total = total + self.arrived[dest - 1].astype(jnp.float32)
                if dest < 3:
                    self.moved(3 + dest, place.down).wait_recv()
                    total = total + self.arrived[3 + dest].astype(jnp.float32)
                out[...] = total

        for dest in range(4):
            self.across(dest).wait_send()
        for i in range(3):
            top, bottom = 3 - i, i

            @pl.when(place.z < top)
            def _(top=top):
                self.moved(top - 1, place.up).wait_send()

            @pl.when(place.z > bottom)
            def _(bottom=bottom):
                self.moved(3 + bottom, place.down).wait_send()


class Spread:
    @staticmethod
    def sems(pieces, outs):
        return [
            pltpu.SemaphoreType.DMA((2, 8, pieces)),
            pltpu.SemaphoreType.DMA((2, 4, 8, outs)),
        ]

    def __init__(self, place, weight, outs, pieces, sems):
        self.place, self.weight, self.outs, self.pieces = place, weight, outs, pieces
        self.swap_sems, self.plane_sems = sems
        self.rows = weight.shape[0]

    def spot(self, f, c):
        return (f * 8 + c) * self.rows

    def swap(self, i, p, origin):
        column, width, out, out_column = self.pieces[p]
        peer = self.place.peer(i)
        src = self.weight.at[:, cols_at(column(peer), width)]
        dst = self.outs[out].at[
            rows_at(self.spot(self.place.f, origin), self.rows), pl.ds(out_column, width)
        ]
        if i == 0:
            return pltpu.make_async_copy(src, dst, self.swap_sems.at[0, 0, p])
        return remote(
            src,
            dst,
            self.swap_sems.at[0, i, p],
            self.swap_sems.at[1, i, p],
            (self.place.f, peer),
        )

    def whole(self, f, c, out):
        return self.outs[out].at[rows_at(self.spot(f, c), self.rows)]

    def part(self, f, c, out, half):
        count = self.rows // 2
        return self.outs[out].at[rows_at(self.spot(f, c) + half * count, count)]

    def plane(self, kind, i, out, ref, target):
        return remote(
            ref,
            ref,
            self.plane_sems.at[0, kind, i, out],
            self.plane_sems.at[1, kind, i, out],
            (target, self.place.c),
        )

    def start(self, first=0, last=8):
        for i in range(first, last):
            for p in range(len(self.pieces)):
                self.swap(i, p, self.place.c).start()

    def forward(self, i):
        place = self.place
        origin = place.peer(i)
        for p in range(len(self.pieces)):
            copy = self.swap(i, p, origin)
            if i == 0:
                copy.wait()
            else:
                copy.wait_recv()
        for out in range(len(self.outs)):
            ref = self.whole(place.f, origin, out)
            self.plane(0, i, out, ref, place.x_side).start()
            self.plane(1, i, out, ref, place.y_side).start()

    def relay(self, i):
        place = self.place
        origin = place.peer(i)
        for out in range(len(self.outs)):
            self.plane(0, i, out, self.whole(place.x_side, origin, out), place.x_side).wait_recv()
            self.plane(2, i, out, self.part(place.x_side, origin, out, 0), place.y_side).start()
            self.plane(1, i, out, self.whole(place.y_side, origin, out), place.y_side).wait_recv()
            self.plane(3, i, out, self.part(place.y_side, origin, out, 1), place.x_side).start()

    def finish(self, first=0, last=8):
        self.arrive(first, last)
        self.settle(first, last)

    def arrive(self, first=0, last=8):
        place = self.place
        for i in range(first, last):
            origin = place.peer(i)
            for out in range(len(self.outs)):
                self.plane(
                    2, i, out, self.part(place.diag, origin, out, 0), place.y_side
                ).wait_recv()
                self.plane(
                    3, i, out, self.part(place.diag, origin, out, 1), place.x_side
                ).wait_recv()

    def settle(self, first=0, last=8):
        place = self.place
        for i in range(first, last):
            origin = place.peer(i)
            if i:
                for p in range(len(self.pieces)):
                    self.swap(i, p, place.c).wait_send()
            for out in range(len(self.outs)):
                own = self.whole(place.f, origin, out)
                self.plane(0, i, out, own, place.x_side).wait_send()
                self.plane(1, i, out, own, place.y_side).wait_send()
                half = self.part(place.f, origin, out, 0)
                self.plane(2, i, out, half, place.y_side).wait_send()
                self.plane(3, i, out, half, place.x_side).wait_send()


class Drain:
    @staticmethod
    def scratch(rows, widths, peers=8):
        half = rows // 2
        lists = []
        for width in widths:
            lists += [
                pltpu.VMEM((2, peers, 2, half, width), jnp.bfloat16),
                pltpu.VMEM((2, peers, half, width), jnp.bfloat16),
                pltpu.VMEM((2, peers, half, width), jnp.bfloat16),
                pltpu.VMEM((peers, rows, width), jnp.bfloat16),
            ]
        return lists

    @staticmethod
    def sems(pieces, outs, peers=8):
        return [
            pltpu.SemaphoreType.DMA((2, 2, peers, 2, outs)),
            pltpu.SemaphoreType.DMA((2, 2, peers, outs)),
            pltpu.SemaphoreType.DMA((2, peers, pieces)),
        ]

    def __init__(self, place, grads, land, pieces, scratch, sems, base=0, peers=8):
        self.place, self.grads, self.land, self.pieces = place, grads, land, pieces
        self.first = scratch[0::4]
        self.second = scratch[1::4]
        self.going = scratch[2::4]
        self.done = scratch[3::4]
        self.first_sems, self.second_sems, self.swap_sems = sems
        self.rows = land.shape[0]
        self.half = self.rows // 2
        self.units = len(grads[0].shape) == 4
        self.base, self.peers = base, peers

    def part(self, g, f, i, half):
        peer = self.place.peer(self.base + i)
        if self.units:
            start = (peer % 2) * self.rows + half * self.half
            return self.grads[g].at[i // 2, f, rows_at(start, self.half)]
        return self.grads[g].at[rows_at((f * 8 + peer) * self.rows + half * self.half, self.half)]

    def sides(self, axis):
        place = self.place
        return (place.x_side, place.y_side) if axis == 0 else (place.y_side, place.x_side)

    def first_copy(self, axis, i, which, g):
        near, _ = self.sides(axis)
        f = near if which == 0 else self.place.diag
        return remote(
            self.part(g, f, i, axis),
            self.first[g].at[axis, i, which],
            self.first_sems.at[0, axis, i, which, g],
            self.first_sems.at[1, axis, i, which, g],
            (near, self.place.c),
        )

    def second_copy(self, axis, i, g):
        _, far = self.sides(axis)
        return remote(
            self.going[g].at[axis, i],
            self.second[g].at[axis, i],
            self.second_sems.at[0, axis, i, g],
            self.second_sems.at[1, axis, i, g],
            (far, self.place.c),
        )

    def swap(self, i, p, origin):
        column, width, g, g_column = self.pieces[p]
        src = self.done[g].at[i, :, pl.ds(g_column, width)]
        dst = self.land.at[:, cols_at(column(origin), width)]
        if self.base + i == 0:
            return pltpu.make_async_copy(src, dst, self.swap_sems.at[0, i, p])
        return remote(
            src,
            dst,
            self.swap_sems.at[0, i, p],
            self.swap_sems.at[1, i, p],
            (self.place.f, self.place.peer(self.base + i)),
        )

    def start(self, i):
        for g in range(len(self.grads)):
            for which in (1, 0):
                for axis in range(2):
                    self.first_copy(axis, i, which, g).start()

    def middle(self, i):
        place = self.place
        for g in range(len(self.grads)):
            for axis in range(2):
                _, far = self.sides(axis)
                self.first_copy(axis, i, 1, g).wait_recv()
                mine = self.part(g, far, i, axis)
                self.going[g][axis, i] = (
                    mine[...].astype(jnp.float32) + self.first[g][axis, i, 1].astype(jnp.float32)
                ).astype(jnp.bfloat16)
                self.second_copy(axis, i, g).start()

    def last(self, i):
        place = self.place
        for g in range(len(self.grads)):
            for axis in range(2):
                self.first_copy(axis, i, 0, g).wait_recv()
                self.second_copy(axis, i, g).wait_recv()
                mine = self.part(g, place.f, i, axis)
                self.done[g][i, pl.ds(axis * self.half, self.half)] = (
                    mine[...].astype(jnp.float32)
                    + self.first[g][axis, i, 0].astype(jnp.float32)
                    + self.second[g][axis, i].astype(jnp.float32)
                ).astype(jnp.bfloat16)
        for p in range(len(self.pieces)):
            self.swap(i, p, place.c).start()

    def finish(self):
        place = self.place
        for i in range(self.peers):
            for p in range(len(self.pieces)):
                copy = self.swap(i, p, place.peer(self.base + i))
                if self.base + i == 0:
                    copy.wait()
                else:
                    copy.wait_recv()
                    copy.wait_send()
            for g in range(len(self.grads)):
                for axis in range(2):
                    for which in range(2):
                        self.first_copy(axis, i, which, g).wait_send()
                    self.second_copy(axis, i, g).wait_send()


ANY = pl.BlockSpec(memory_space=pl.ANY)
VMEM = pl.BlockSpec(memory_space=pltpu.VMEM)


def comm_call(kernel, ident, out_shape, in_specs, out_specs, scratch, aliases=None):
    return pl.pallas_call(
        kernel,
        input_output_aliases=aliases or {},
        out_shape=out_shape,
        in_specs=in_specs,
        out_specs=out_specs,
        scratch_shapes=scratch,
        compiler_params=pltpu.CompilerParams(
            collective_id=ident, has_side_effects=True, vmem_limit_bytes=VMEM_LIMIT
        ),
    )


def bf16(*shape):
    return jax.ShapeDtypeStruct(shape, jnp.bfloat16)


def gather_tokens(own, ident):
    def kernel(own_ref, out_ref, *sems):
        place = Place()
        greet(place, "chain", False)
        gather = ChainGather(place, own_ref, out_ref, sems)
        gather.start()
        for step in (1, 2, 3):
            gather.step(step)
        gather.finish()

    rows, cols = own.shape
    return comm_call(kernel, ident, bf16(8 * rows, cols), [ANY], ANY, ChainGather.SEMS)(own)


def scatter_tokens(partial, ident):
    rows, cols = partial.shape[0] // 8, partial.shape[1]

    def kernel(partial_ref, out_ref, *scratch):
        place = Place()
        greet(place, "chain", False)
        scatter = ChainScatter(place, partial_ref, scratch)
        scatter.start()
        scatter.ends()
        scatter.inner(0)
        scatter.inner(1)
        scatter.finish(out_ref)

    return comm_call(
        kernel,
        ident,
        jax.ShapeDtypeStruct((rows, cols), jnp.float32),
        [VMEM],
        VMEM,
        ChainScatter.scratch(rows, cols),
    )(partial)


ATTN_PIECES = (
    (lambda c: 256 * c, 256, 0, 0),
    (lambda c: 2048 + 256 * (c // 4), 256, 0, 256),
    (lambda c: 2560 + 256 * (c // 4), 256, 0, 512),
    (lambda c: 3200 + 256 * c, 256, 1, 0),
    (lambda c: 3072, 128, 2, 0),
)
ATTN_LAND = (
    (lambda c: 1152 * c, 896, 0, 0),
    (lambda c: 1152 * c + 896, 256, 1, 0),
)
MLP_PIECES = (
    (lambda c: 1024 * c, 1024, 0, 0),
    (lambda c: 8192 + 1024 * c, 1024, 0, 1024),
    (lambda c: 16384 + 1024 * c, 1024, 1, 0),
)
VEC_LAND = ((lambda c: 512 * c, 512, 0, 0),)
VEC_PIECES = ((lambda c: 0, 512, 0, 0),)


def turn(values, cosine, sine):
    half = HEAD // 2
    first, second = values[:, :half], values[:, half:]
    return jnp.concatenate(
        [first * cosine - second * sine, second * cosine + first * sine], axis=1
    )


def allowed_pairs(first_query, first_key, positions):
    shape = (positions.shape[0], 768)
    distance = (
        lax.broadcasted_iota(jnp.int32, shape, 0)
        - lax.broadcasted_iota(jnp.int32, shape, 1)
        + (first_query - first_key)
    )
    return (distance >= 0) & (distance <= jnp.minimum(positions, WINDOW - 1))


def positions_of(parts):
    return (parts[:, 0:1].astype(jnp.float32) * 256.0 + parts[:, 1:2].astype(jnp.float32)).astype(
        jnp.int32
    )


def attention_forward(
    normed_low, own_pos, w_attn, w_mlp, hidden, normed_in, gains, head_gains, tables, ident
):
    height = 32 * w_attn.shape[0]
    rows, width = hidden.shape
    total = 8 * rows
    query_block, key_span = 2 * rows, 768
    scatter_scratch = ChainScatter.scratch(rows, width)

    def kernel(*refs):
        ins, outs, held = split_refs(refs, 9, 17, len(refs) - 26)
        (own_ref, pos_ref, attn_ref, mlp_ref, hidden_ref, normed_ref, gains_ref, head_ref,
         tables_ref) = ins
        (row_ref, qkv_ref, out_ref, laurel_ref, row_pos, gate_up_ref, down_ref, row_ffn,
         projected, q_low, k_low, v_low, mixed, latent_ref, laurel_up, attn_out, joined) = outs
        scratch, scat, attn_m, mlp_m, gather_m = split_refs(held, 2, len(scatter_scratch), 2, 2, 6)
        own_ffn, partial = scratch
        place = Place()
        greet(place, "all", True)
        attn = Spread(place, attn_ref, [qkv_ref, out_ref, laurel_ref], ATTN_PIECES, attn_m)
        mlp = Spread(place, mlp_ref, [gate_up_ref, down_ref], MLP_PIECES, mlp_m)
        gathers = [
            ChainGather(place, own_ref, row_ref, gather_m[0:2]),
            ChainGather(place, pos_ref, row_pos, gather_m[2:4]),
        ]
        last = ChainGather(place, own_ffn, row_ffn, gather_m[4:6])
        scatter = ChainScatter(place, partial, scat)

        def step(n):
            for gather in gathers:
                gather.step(n)

        for gather in gathers:
            gather.start()
        attn.start(0, 2)
        attn.start(4, 6)
        attn.start(2, 4)
        attn.start(6, 8)
        mlp.start(0, 2)
        attn.forward(0)
        attn.forward(1)
        mlp.forward(0)
        step(1)
        attn.forward(2)
        attn.forward(3)
        attn.relay(0)
        attn.relay(1)
        step(2)
        attn.forward(4)
        attn.forward(5)
        attn.relay(2)
        attn.relay(3)
        mlp.forward(1)
        step(3)
        attn.forward(6)
        attn.forward(7)
        mlp.start(4, 6)
        mlp.start(2, 4)
        attn.relay(4)
        attn.relay(5)
        mlp.relay(0)
        attn.relay(6)
        attn.relay(7)
        for gather in gathers:
            gather.arrive()
        attn.arrive()
        mlp.relay(1)
        mlp.start(6, 8)

        @pl.loop(0, total // query_block)
        def _(n):
            here = rows_at(n * query_block, query_block)
            block = plain_dot(row_ref[here], qkv_ref[...])
            projected[here] = block
            cosine, sine = tables_ref[here, : HEAD // 2], tables_ref[here, HEAD // 2 :]
            q_low[here] = turn(
                rms_norm(block[:, :HEAD], head_ref[0:1]), cosine, sine
            ).astype(jnp.bfloat16)
            k_low[here] = turn(
                rms_norm(block[:, HEAD : 2 * HEAD], head_ref[1:2]), cosine, sine
            ).astype(jnp.bfloat16)
            v_low[here] = value_norm(block[:, 2 * HEAD :]).astype(jnp.bfloat16)

        upper = place.z // 2

        @pl.loop(0, total // query_block)
        def _(n):
            d = n * upper + (3 - n) * (1 - upper)
            here = rows_at(d * query_block, query_block)
            first_key = (d // 2) * (d - 2) * query_block
            there = rows_at(first_key, key_span)
            scores = jnp.where(
                allowed_pairs(d * query_block, first_key, positions_of(row_pos[here])),
                times_transposed(q_low[here], k_low[there]),
                NEG_LARGE,
            )
            weights = jnp.exp(scores - jnp.max(scores, axis=-1, keepdims=True))
            probs = (weights / jnp.sum(weights, axis=-1, keepdims=True)).astype(jnp.bfloat16)
            block = plain_dot(probs, v_low[there]).astype(jnp.bfloat16)
            mixed[here] = block
            partial[here] = times_transposed(block, out_ref[...]).astype(jnp.bfloat16)
            scatter.across(d).start()

        scatter.ends()
        mlp.forward(2)
        mlp.forward(3)
        scatter.inner(0)
        low = plain_dot(own_ref[...], laurel_ref[...])
        latent_ref[...] = low.astype(jnp.bfloat16)
        lanes = lax.broadcasted_iota(jnp.int32, low.shape, 1)
        shifted = jnp.where(lanes >= RANK, pltpu.roll(low, RANK, 1), 0.0).astype(jnp.bfloat16)
        laurel_up[...] = times_transposed(shifted, laurel_ref[...])
        scatter.inner(1)
        mlp.relay(2)
        mlp.relay(3)
        mlp.forward(4)
        mlp.forward(5)
        scatter.finish(attn_out)
        laurel_res = normed_ref[...] + rms_norm(laurel_up[...], gains_ref[1:2])
        after_attn = hidden_ref[...].astype(jnp.float32) + rms_norm(attn_out[...], gains_ref[2:3])
        joined[...] = (after_attn + laurel_res) / math.sqrt(2.0)
        own_ffn[...] = rms_norm(joined[...], gains_ref[3:4]).astype(jnp.bfloat16)
        last.start()
        mlp.relay(4)
        mlp.relay(5)
        last.step(1)
        mlp.forward(6)
        mlp.forward(7)
        last.step(2)
        mlp.relay(6)
        mlp.relay(7)
        last.step(3)
        mlp.arrive()
        last.arrive()
        attn.settle()
        mlp.settle()
        for gather in gathers:
            gather.settle()
        last.settle()

    def f32(*shape):
        return jax.ShapeDtypeStruct(shape, jnp.float32)

    token_f32 = f32(rows, width)
    head = bf16(total, HEAD)
    outs = [bf16(total, width), bf16(height, 768), bf16(height, 256), bf16(height, 128)]
    outs += [bf16(total, 128), bf16(height, 2048), bf16(height, 1024), bf16(total, width)]
    outs += [f32(total, 768), head, head, head, head, bf16(rows, 128)]
    outs += [token_f32, token_f32, token_f32]
    return comm_call(
        kernel,
        ident,
        outs,
        [VMEM, VMEM, ANY, ANY] + [VMEM] * 5,
        [VMEM] * 5 + [ANY] * 3 + [VMEM] * 9,
        [pltpu.VMEM((rows, width), jnp.bfloat16), pltpu.VMEM((total, width), jnp.bfloat16)]
        + scatter_scratch
        + Spread.sems(len(ATTN_PIECES), 3)
        + Spread.sems(len(MLP_PIECES), 2)
        + ChainGather.SEMS * 3,
    )(normed_low, own_pos, w_attn, w_mlp, hidden, normed_in, gains, head_gains, tables)


def split_refs(refs, *counts):
    refs, parts = list(refs), []
    for count in counts:
        parts.append(refs[:count])
        refs = refs[count:]
    return parts


def unit_gradient(place, n, tokens_ref, grad_ref, out, turned_ref):
    zz = place.partner(n)
    count = turned_ref.shape[0] // 4
    for f in range(4):
        columns = cols_at((f * 4 + zz) * count, count)
        turned_ref[f * count : (f + 1) * count] = tokens_ref[:, columns].T
    step = 512

    @pl.loop(0, grad_ref.shape[1] // step)
    def _(t):
        columns = cols_at(t * step, step)
        block = plain_dot(turned_ref[...], grad_ref[:, columns]).astype(jnp.bfloat16)
        for f in range(4):
            out[f, :, columns] = block[f * count : (f + 1) * count]


def ffn_close_backward(
    partial, row_ffn, d_gate_up, row_d_ffn, activated, vec_grads, shard_height, mlp_cols, ident
):
    rows, width = partial.shape[0] // 8, partial.shape[1]
    wide, narrow = d_gate_up.shape[1], activated.shape[1]
    vec_width = vec_grads.shape[1]
    scatter_scratch = ChainScatter.scratch(rows, width)
    mlp_scratch = Drain.scratch(shard_height, (wide, narrow), 2)
    mlp_sems = Drain.sems(len(MLP_PIECES), 2, 2)
    vec_scratch = Drain.scratch(shard_height, (vec_width,))
    vec_sems = Drain.sems(1, 1)
    unit_rows = 2 * shard_height

    def kernel(*refs):
        (partial_ref, ffn_ref, dgu_ref, dffn_ref, act_ref, vec_ref), outs, held = split_refs(
            refs, 6, 7, len(refs) - 13
        )
        out_ref, mlp_land, vec_land, mid_wide, mid_narrow, end_wide, end_narrow = outs
        own, scat, mlp_s, mlp_m, vec_s, vec_m = split_refs(
            held, 3, len(scatter_scratch), len(mlp_scratch), 3, len(vec_scratch), 3
        )
        own_wide, own_narrow, turned = own
        place = Place()
        greet(place, "all", True)
        scatter = ChainScatter(place, partial_ref, scat)
        mlp = Drain(place, [own_wide, own_narrow], mlp_land, MLP_PIECES, mlp_s, mlp_m, 0, 2)
        vec = Drain(place, [vec_ref], vec_land, VEC_LAND, vec_s, vec_m)

        def unit(n, wide_ref, narrow_ref):
            unit_gradient(place, n, ffn_ref, dgu_ref, wide_ref, turned)
            unit_gradient(place, n, dffn_ref, act_ref, narrow_ref, turned)

        scatter.start()
        scatter.ends()
        unit(0, own_wide.at[0], own_narrow.at[0])
        mlp.start(0)
        mlp.start(1)
        for i in range(8):
            vec.start(i)
        unit(1, mid_wide.at[0], mid_narrow.at[0])
        scatter.inner(0)
        unit(2, mid_wide.at[1], mid_narrow.at[1])
        scatter.inner(1)
        unit(3, end_wide.at[0], end_narrow.at[0])
        mlp.middle(0)
        mlp.middle(1)
        scatter.finish(out_ref)
        for i in range(8):
            vec.middle(i)
        mlp.last(0)
        mlp.last(1)
        for i in range(8):
            vec.last(i)
        vec.finish()
        mlp.finish()

    def unit_shapes(count):
        return [bf16(count, 4, unit_rows, wide), bf16(count, 4, unit_rows, narrow)]

    return comm_call(
        kernel,
        ident,
        [
            jax.ShapeDtypeStruct((rows, width), jnp.float32),
            bf16(shard_height, mlp_cols),
            bf16(shard_height, 8 * vec_width),
        ]
        + unit_shapes(2)
        + unit_shapes(1),
        [VMEM] * 6,
        [VMEM, ANY, ANY] + [VMEM] * 4,
        [
            pltpu.VMEM((1, 4, unit_rows, wide), jnp.bfloat16),
            pltpu.VMEM((1, 4, unit_rows, narrow), jnp.bfloat16),
            pltpu.VMEM((4 * unit_rows, 8 * rows), jnp.bfloat16),
        ]
        + scatter_scratch
        + mlp_scratch
        + mlp_sems
        + vec_scratch
        + vec_sems,
    )(partial, row_ffn, d_gate_up, row_d_ffn, activated, vec_grads)


def attention_open_backward(d_attn_low, mid_wide, mid_narrow, mlp_land, vec_land, ident):
    rows, width = d_attn_low.shape
    shard_height, vec_width = vec_land.shape[0], vec_land.shape[1] // 8
    widths = (mid_wide.shape[3], mid_narrow.shape[3])
    mlp_scratch = Drain.scratch(shard_height, widths, 4)
    mlp_sems = Drain.sems(len(MLP_PIECES), 2, 4)
    vec_sems = Spread.sems(1, 1)

    def kernel(
        own_ref, wide_ref, narrow_ref, land_in, vec_ref, all_ref, land_ref, vec_all, *held
    ):
        (vec_own,), mlp_s, mlp_m, vec_m, gather_m = split_refs(held, 1, len(mlp_scratch), 3, 2, 2)
        place = Place()
        greet(place, "all", True)
        gather = ChainGather(place, own_ref, all_ref, gather_m)
        mlp = Drain(place, [wide_ref, narrow_ref], land_ref, MLP_PIECES, mlp_s, mlp_m, 2, 4)
        vec = Spread(place, vec_own, [vec_all], VEC_PIECES, vec_m)
        gather.start()
        mlp.start(0)
        mlp.start(1)
        total = vec_ref[:, 0:vec_width].astype(jnp.float32)
        for c in range(1, 8):
            total = total + vec_ref[:, c * vec_width : (c + 1) * vec_width].astype(jnp.float32)
        vec_own[...] = total.astype(jnp.bfloat16)
        gather.step(1)
        mlp.middle(0)
        mlp.start(2)
        vec.start()
        gather.step(2)
        mlp.middle(1)
        mlp.start(3)
        mlp.last(0)
        gather.step(3)
        mlp.middle(2)
        mlp.last(1)
        mlp.middle(3)
        mlp.last(2)
        for i in range(8):
            vec.forward(i)
            if i:
                vec.relay(i - 1)
        vec.relay(7)
        mlp.last(3)
        mlp.finish()
        gather.finish()
        vec.finish()

    return comm_call(
        kernel,
        ident,
        [bf16(8 * rows, width), bf16(*mlp_land.shape), bf16(32 * shard_height, vec_width)],
        [ANY, VMEM, VMEM, ANY, VMEM],
        [ANY, ANY, ANY],
        [pltpu.VMEM((shard_height, vec_width), jnp.bfloat16)]
        + mlp_scratch
        + mlp_sems
        + vec_sems
        + ChainGather.SEMS,
        {3: 1},
    )(d_attn_low, mid_wide, mid_narrow, mlp_land, vec_land)


def sum_everywhere(place, own, arrived, sems):
    k, f = place.k, place.f
    targets = [
        place.sibling,
        (place.x_side, place.c),
        (place.y_side, place.c),
        (f, place.partner(1) * 2 + k),
        (f, place.partner(3) * 2 + k),
    ]
    return [
        remote(own.at[n], arrived.at[n], sems.at[0, n], sems.at[1, n], target)
        for n, target in enumerate(targets)
    ]


def close_backward(
    partial, base, hidden, gains, other_gains, mlp_grads, attn_grads, mlp_land, ident
):
    rows, width = base.shape
    shard_height = mlp_land.shape[0]
    scatter_scratch = ChainScatter.scratch(rows, width)
    mlp_scratch = Drain.scratch(shard_height, [grad.shape[3] for grad in mlp_grads], 2)
    mlp_sems = Drain.sems(len(MLP_PIECES), 2, 2)
    attn_scratch = Drain.scratch(shard_height, [grad.shape[1] for grad in attn_grads])
    attn_sems = Drain.sems(len(ATTN_LAND), 2)
    gain_rows = other_gains.shape[0]

    def kernel(*refs):
        ins, outs, held = split_refs(refs, 10, 4, len(refs) - 14)
        partial_ref, base_ref, hidden_ref, gains_ref, other_ref = ins[:5]
        out_ref, gain_ref, land_ref, attn_land = outs
        own_gains, scat, mlp_s, mlp_m, attn_s, attn_m = split_refs(
            held, 3, len(scatter_scratch), len(mlp_scratch), 3, len(attn_scratch), 3
        )
        place = Place()
        greet(place, "all", True)
        scatter = ChainScatter(place, partial_ref, scat)
        mlp = Drain(place, ins[5:7], land_ref, MLP_PIECES, mlp_s, mlp_m, 6, 2)
        attn = Drain(place, ins[7:9], attn_land, ATTN_LAND, attn_s, attn_m)
        held_gains, arrived_gains, gain_sems = own_gains
        rounds = sum_everywhere(place, held_gains, arrived_gains, gain_sems)

        def gain_round(n):
            rounds[n].wait_recv()
            held_gains[n + 1] = held_gains[n] + arrived_gains[n]
            if n < 4:
                rounds[n + 1].start()

        scatter.start()
        scatter.ends()
        mlp.start(0)
        mlp.start(1)
        attn.start(0)
        attn.start(1)
        scatter.inner(0)
        mlp.middle(0)
        scatter.inner(1)
        mlp.middle(1)
        attn.start(2)
        mlp.last(0)
        mlp.last(1)
        scatter.finish(out_ref)
        hidden_val = hidden_ref[...].astype(jnp.float32)
        inverse = lax.rsqrt(jnp.mean(hidden_val * hidden_val, axis=-1, keepdims=True) + EPSILON)
        unit = hidden_val * inverse
        d_normed = base_ref[...] + out_ref[...]
        scaled = d_normed * gains_ref[0:1]
        out_ref[...] = (
            scaled - unit * jnp.mean(unit * scaled, axis=-1, keepdims=True)
        ) * inverse
        held_gains[0] = other_ref[...]
        held_gains[0, 0:1] = jnp.sum(d_normed * unit, axis=0, keepdims=True)
        rounds[0].start()
        for i in range(8):
            attn.middle(i)
            if i < 5:
                attn.start(i + 3)
            if i:
                attn.last(i - 1)
            if i < 5:
                gain_round(i)
        attn.last(7)
        gain_ref[...] = held_gains[5]
        for copy in rounds:
            copy.wait_send()
        mlp.finish()
        attn.finish()

    attn_land_cols = 8 * sum(grad.shape[1] for grad in attn_grads)
    return comm_call(
        kernel,
        ident,
        [
            jax.ShapeDtypeStruct((rows, width), jnp.float32),
            jax.ShapeDtypeStruct((gain_rows, width), jnp.float32),
            bf16(*mlp_land.shape),
            bf16(shard_height, attn_land_cols),
        ],
        [VMEM] * 9 + [ANY],
        [VMEM, VMEM, ANY, ANY],
        [
            pltpu.VMEM((6, gain_rows, width), jnp.float32),
            pltpu.VMEM((5, gain_rows, width), jnp.float32),
            pltpu.SemaphoreType.DMA((2, 5)),
        ]
        + scatter_scratch
        + mlp_scratch
        + mlp_sems
        + attn_scratch
        + attn_sems,
        {9: 2},
    )(partial, base, hidden, gains, other_gains, *mlp_grads, *attn_grads, mlp_land)


def per_device_split(
    hidden_in, layer_vec, positions, w_attn, w_mlp, pl_gate, pl_proj, gains, head_gains, out_grad
):
    shard_height = w_attn.shape[0]
    row_total = QH * positions.shape[0]
    lanes = jnp.arange(128, dtype=jnp.int32)[None, :]
    own_pos = jnp.where(lanes == 0, positions[:, None] // 256, positions[:, None] % 256)

    index = jnp.arange(row_total, dtype=jnp.int32)
    frequency = jnp.exp(
        jnp.arange(HEAD // 2, dtype=jnp.float32) * (-2.0 * math.log(THETA) / HEAD)
    )
    angles = index.astype(jnp.float32)[:, None] * frequency[None, :]
    tables = jnp.concatenate([jnp.cos(angles), jnp.sin(angles)], axis=1)

    def qk_prep(raw_heads, scale_vec):
        return turn(rms_norm(raw_heads, scale_vec), tables[:, : HEAD // 2], tables[:, HEAD // 2 :])

    hidden = hidden_in.astype(jnp.float32)
    normed_in = rms_norm(hidden, gains[0])
    normed_low = normed_in.astype(jnp.bfloat16)
    (
        row_normed, w_qkv, w_out, w_laurel, row_parts, w_gate_up, w_down, row_ffn, projected,
        queries, keys, values, mixed, latent, laurel_up, attn_out, joined,
    ) = attention_forward(
        normed_low, own_pos.astype(jnp.bfloat16), w_attn, w_mlp, hidden_in, normed_in, gains,
        head_gains, tables, 1,
    )
    latent = latent[:, :RANK]
    q_raw, k_raw, v_raw = jnp.split(projected, 3, axis=1)
    gate_up = plain_dot(row_ffn, w_gate_up)
    activated = activate(gate_up).astype(jnp.bfloat16)
    ffn_out = scatter_tokens(times_transposed(activated, w_down).astype(jnp.bfloat16), 4)

    after_ffn = joined + rms_norm(ffn_out, gains[4])
    after_low = after_ffn.astype(jnp.bfloat16)
    vec_gate = plain_dot(after_low, pl_gate)
    vector_in = layer_vec.astype(jnp.float32)
    vec_mixed = vec_mix(vec_gate, vector_in).astype(jnp.bfloat16)
    vec_out = plain_dot(vec_mixed, pl_proj)
    result_out = after_ffn + rms_norm(vec_out, gains[5])
    upstream = out_grad.astype(jnp.float32)
    unused_out, vec_norm_back = jax.vjp(rms_norm, vec_out, gains[5])
    d_vec_out, d_gain_vec = vec_norm_back(upstream)
    d_vec_out_low = d_vec_out.astype(jnp.bfloat16)
    d_vec_mixed = times_transposed(d_vec_out_low, pl_proj)
    turned_pl_proj = contract_rows(d_vec_out_low, vec_mixed)
    unused_out, mix_back = jax.vjp(vec_mix, vec_gate, vector_in)
    d_vec_gate, d_vector_in = mix_back(d_vec_mixed)
    d_vec_gate_low = d_vec_gate.astype(jnp.bfloat16)
    grad_after = upstream + times_transposed(d_vec_gate_low, pl_gate)
    grad_pl_gate = contract_rows(after_low, d_vec_gate_low)
    unused_out, ffn_norm_back = jax.vjp(rms_norm, ffn_out, gains[4])
    d_ffn_out, d_gain_ffn = ffn_norm_back(grad_after)
    d_ffn_low = d_ffn_out.astype(jnp.bfloat16)

    row_d_ffn = gather_tokens(d_ffn_low, 5)
    unused_out, act_back = jax.vjp(activate, gate_up)
    d_gate_up = act_back(plain_dot(row_d_ffn, w_down))[0].astype(jnp.bfloat16)
    vec_grads = jnp.concatenate([grad_pl_gate, turned_pl_proj], axis=1).astype(jnp.bfloat16)
    d_ffn_in, mlp_land, vec_land, mid_wide, mid_narrow, end_wide, end_narrow = ffn_close_backward(
        times_transposed(d_gate_up, w_gate_up).astype(jnp.bfloat16),
        row_ffn,
        d_gate_up,
        row_d_ffn,
        activated,
        vec_grads,
        shard_height,
        w_mlp.shape[1],
        6,
    )

    unused_out, pre_norm_back = jax.vjp(rms_norm, joined, gains[3])
    d_joined_part, d_gain_pre = pre_norm_back(d_ffn_in)
    d_half = (grad_after + d_joined_part) / math.sqrt(2.0)
    unused_out, laurel_norm_back = jax.vjp(rms_norm, laurel_up, gains[1])
    d_laurel_up, d_gain_laurel = laurel_norm_back(d_half)
    unused_out, attn_norm_back = jax.vjp(rms_norm, attn_out, gains[2])
    d_attn_out, d_gain_attn = attn_norm_back(d_half)
    d_laurel_low = d_laurel_up.astype(jnp.bfloat16)
    row_d_attn, mlp_land, vec_all = attention_open_backward(
        d_attn_out.astype(jnp.bfloat16), mid_wide, mid_narrow, mlp_land, vec_land, 7
    )
    d_latent_low = plain_dot(d_laurel_low, w_laurel[:, RANK:]).astype(jnp.bfloat16)
    d_mixed = plain_dot(row_d_attn, w_out).astype(jnp.bfloat16)
    row_pos = positions_of(row_parts)
    distance = index[:, None] - index[None, :]
    allowed = (distance >= 0) & (distance <= jnp.minimum(row_pos, WINDOW - 1))
    probs = jax.nn.softmax(
        jnp.where(allowed, times_transposed(queries, keys), NEG_LARGE), axis=-1
    )
    probs_low = probs.astype(jnp.bfloat16)
    d_probs = times_transposed(d_mixed, values)
    inner_sum = jnp.sum(probs * d_probs, axis=-1, keepdims=True)
    d_scores = (probs * (d_probs - inner_sum)).astype(jnp.bfloat16)
    d_queries = plain_dot(d_scores, keys)
    d_keys = contract_rows(d_scores, queries)
    d_values = contract_rows(probs_low, d_mixed)
    unused_out, query_back = jax.vjp(qk_prep, q_raw, head_gains[0])
    d_q_raw, d_head_query = query_back(d_queries)
    unused_out, key_back = jax.vjp(qk_prep, k_raw, head_gains[1])
    d_k_raw, d_head_key = key_back(d_keys)
    unused_out, value_back = jax.vjp(value_norm, v_raw)
    d_v_raw = value_back(d_values)[0]
    d_projected = jnp.concatenate([d_q_raw, d_k_raw, d_v_raw], axis=1).astype(jnp.bfloat16)
    laurel_partial = jnp.concatenate(
        [contract_rows(normed_low, d_latent_low), contract_rows(d_laurel_low, latent)], axis=1
    )
    other_gains = jnp.concatenate(
        [
            jnp.zeros_like(gains[:1]),
            jnp.stack([d_gain_laurel, d_gain_attn, d_gain_pre, d_gain_ffn, d_gain_vec]),
            jnp.pad(
                jnp.concatenate([d_head_query, d_head_key])[None],
                ((0, 1), (0, gains.shape[1] - 2 * HEAD)),
            ),
        ],
        axis=0,
    )
    d_hidden_part, all_gains, mlp_land, attn_land = close_backward(
        times_transposed(d_projected, w_qkv).astype(jnp.bfloat16),
        d_half + times_transposed(d_latent_low, w_laurel[:, :RANK]),
        hidden_in,
        gains,
        other_gains,
        [end_wide, end_narrow],
        [
            jnp.concatenate(
                [
                    contract_rows(row_normed, d_projected).astype(jnp.bfloat16),
                    laurel_partial.astype(jnp.bfloat16),
                ],
                axis=1,
            ),
            contract_rows(row_d_attn, mixed).astype(jnp.bfloat16),
        ],
        mlp_land,
        9,
    )
    grad_hidden = d_half + d_hidden_part
    landed = attn_land.astype(jnp.float32).reshape(shard_height, KVH, QH // KVH, 1152)

    def heads_of(first):
        return landed[..., first : first + HEAD]

    grad_w_attn = jnp.concatenate(
        [
            heads_of(0).reshape(shard_height, QH * HEAD),
            jnp.sum(heads_of(HEAD), axis=2).reshape(shard_height, KVH * HEAD),
            jnp.sum(heads_of(2 * HEAD), axis=2).reshape(shard_height, KVH * HEAD),
            jnp.sum(landed[..., 3 * HEAD : 3 * HEAD + 2 * RANK], axis=(1, 2)),
            heads_of(896).reshape(shard_height, QH * HEAD),
        ],
        axis=1,
    )
    vec_sums = vec_all.astype(jnp.float32)
    grad_gate_all, grad_proj_all = vec_sums[:, : pl_gate.shape[1]], vec_sums[:, pl_gate.shape[1] :].T
    grad_gains, grad_heads = all_gains[:6], all_gains[6, : 2 * HEAD].reshape(2, HEAD)
    return (
        result_out.astype(jnp.bfloat16),
        grad_hidden,
        d_vector_in,
        grad_w_attn,
        mlp_land.astype(jnp.float32),
        grad_gate_all,
        grad_proj_all,
        grad_gains,
        grad_heads,
    )


def solution(mesh):
    fits = mesh.shape["ctx"] == QH and mesh.shape["fsdp"] == 4
    body = per_device_split if fits else per_device
    return jax.shard_map(
        body,
        mesh=mesh,
        in_specs=(
            P(("fsdp", "ctx"), None),
            P(("fsdp", "ctx"), None),
            P(("fsdp", "ctx")),
            P(("fsdp", "ctx"), None),
            P(("fsdp", "ctx"), None),
            P(),
            P(),
            P(),
            P(),
            P(("fsdp", "ctx"), None),
        ),
        out_specs=(
            P(("fsdp", "ctx"), None),
            P(("fsdp", "ctx"), None),
            P(("fsdp", "ctx"), None),
            P(("fsdp", "ctx"), None),
            P(("fsdp", "ctx"), None),
            P(),
            P(),
            P(),
            P(),
        ),
        check_vma=False,
    )
```

```python
import math

import jax
import jax.numpy as jnp
from jax import lax
from jax.experimental import pallas as pl
from jax.experimental.pallas import tpu as pltpu
from jax.sharding import PartitionSpec as P

QH = 8
KVH = 2
HEAD = 256
RANK = 64
WINDOW = 512


EPSILON = 1e-06
THETA = 10000.0
NEG_LARGE = -1e30


def passed_along(block, axis, distance):
    devices = range(lax.axis_size(axis))
    route = [(i - distance, i) for i in devices if i - distance in devices]
    return lax.ppermute(block, axis, route)


def rms_norm(values, scale_vec):
    return (
        values * lax.rsqrt(jnp.mean(values * values, axis=-1, keepdims=True) + EPSILON) * scale_vec
    )


def value_norm(values):
    return rms_norm(values, 1.0)


def rotary(values, positions):
    half_size = values.shape[-1] // 2
    frequency = jnp.exp(
        jnp.arange(half_size, dtype=jnp.float32) * (-2.0 * math.log(THETA) / values.shape[-1])
    )
    angles = positions.astype(jnp.float32)[:, None] * frequency[None, :]
    cosine = jnp.cos(angles)[:, None, :]
    sine_part = jnp.sin(angles)[:, None, :]
    first_half = values[..., :half_size]
    second_half = values[..., half_size:]
    return jnp.concatenate(
        [
            first_half * cosine - second_half * sine_part,
            second_half * cosine + first_half * sine_part,
        ],
        axis=-1,
    )


def plain_dot(left_side, right_side):
    return jnp.dot(left_side, right_side, preferred_element_type=jnp.float32)


def times_transposed(left_side, right_side):
    return lax.dot_general(
        left_side, right_side, (((1,), (1,)), ((), ())), preferred_element_type=jnp.float32
    )


def contract_rows(left_side, right_side):
    return lax.dot_general(
        left_side, right_side, (((0,), (0,)), ((), ())), preferred_element_type=jnp.float32
    )


def activate(gate_up_val):
    half_cols = gate_up_val.shape[1] // 2
    return jax.nn.gelu(gate_up_val[:, :half_cols], approximate=True) * gate_up_val[:, half_cols:]


def vec_mix(gate_val, vector_val):
    return jax.nn.gelu(gate_val, approximate=True) * vector_val


def per_device(
    hidden_in, layer_vec, positions, w_attn, w_mlp, pl_gate, pl_proj, gains, head_gains, out_grad
):
    row_count = hidden_in.shape[0]
    model_width = hidden_in.shape[1]
    q_width = QH * HEAD
    kv_width = KVH * HEAD
    in_cols = q_width + 2 * kv_width + RANK
    group_size = QH // KVH
    ff_width = w_mlp.shape[1] // 3
    shard_height = w_mlp.shape[0]
    fsdp_count = lax.axis_size("fsdp")
    ctx_count = lax.axis_size("ctx")
    quarter = ff_width // fsdp_count

    def permute_cols(matrix):
        return (
            matrix.reshape(-1, fsdp_count, ctx_count, shard_height)
            .transpose(0, 2, 1, 3)
            .reshape(-1, model_width)
        )

    def restore_cols(matrix):
        return (
            matrix.reshape(-1, ctx_count, fsdp_count, shard_height)
            .transpose(0, 2, 1, 3)
            .reshape(-1, model_width)
        )

    def qk_prep(raw_heads, scale_vec):
        return rotary(rms_norm(raw_heads, scale_vec), positions)

    hidden = hidden_in.astype(jnp.float32)
    normed_in = rms_norm(hidden, gains[0])
    normed_low = normed_in.astype(jnp.bfloat16)
    projected = plain_dot(
        normed_low, lax.all_gather(w_attn[:, :in_cols], ("fsdp", "ctx"), axis=0, tiled=True)
    )
    q_raw = projected[:, :q_width].reshape(row_count, QH, HEAD)
    k_raw = projected[:, q_width : q_width + kv_width].reshape(row_count, KVH, HEAD)
    v_raw = projected[:, q_width + kv_width : q_width + 2 * kv_width].reshape(row_count, KVH, HEAD)
    latent = projected[:, q_width + 2 * kv_width :].astype(jnp.bfloat16)
    queries = qk_prep(q_raw, head_gains[0]).astype(jnp.bfloat16)
    keys_own = qk_prep(k_raw, head_gains[1]).astype(jnp.bfloat16)
    values_own = value_norm(v_raw).astype(jnp.bfloat16)
    kv_own = jnp.concatenate(
        [keys_own.reshape(row_count, kv_width), values_own.reshape(row_count, kv_width)], axis=1
    )
    hop_count = (WINDOW - 1) // row_count + 1
    earlier = []
    moving = kv_own
    for step_back in range(hop_count):
        moving = passed_along(moving, "ctx", 1)
        earlier.append(moving)
    kv_all = jnp.concatenate(earlier[::-1] + [kv_own], axis=0)
    span_rows = kv_all.shape[0]
    keys_all = kv_all[:, :kv_width].reshape(span_rows, KVH, HEAD)
    values_all = kv_all[:, kv_width:].reshape(span_rows, KVH, HEAD)
    grouped = queries.reshape(row_count, KVH, group_size, HEAD)
    distance = (
        jnp.arange(row_count, dtype=jnp.int32)[:, None]
        + hop_count * row_count
        - jnp.arange(span_rows, dtype=jnp.int32)[None, :]
    )
    allowed = (distance >= 0) & (distance <= jnp.minimum(positions, WINDOW - 1)[:, None])
    scores = jnp.einsum("qgrd,kgd->grqk", grouped, keys_all, preferred_element_type=jnp.float32)
    scores = jnp.where(allowed[None, None], scores, NEG_LARGE)
    row_max = jnp.max(scores, axis=-1, keepdims=True)
    exp_scores = jnp.exp(scores - row_max)
    row_sum = jnp.sum(exp_scores, axis=-1, keepdims=True)
    log_total = row_max + jnp.log(row_sum)
    probs_low = (exp_scores / row_sum).astype(jnp.bfloat16)
    mixed = jnp.einsum("grqk,kgd->qgrd", probs_low, values_all, preferred_element_type=jnp.float32)
    mixed = mixed.reshape(row_count, q_width).astype(jnp.bfloat16)
    shard_rows = lax.all_gather(w_attn[:, in_cols:], ("fsdp", "ctx"), axis=0, tiled=True)
    laurel_part = times_transposed(latent, shard_rows[:, :RANK])
    attn_part = times_transposed(mixed, shard_rows[:, RANK:])
    out_pair = jnp.stack([laurel_part, attn_part], axis=1)
    laurel_up = out_pair[:, 0]
    attn_out = out_pair[:, 1]
    laurel_res = normed_in + rms_norm(laurel_up, gains[1])
    after_attn = hidden + rms_norm(attn_out, gains[2])
    joined = (after_attn + laurel_res) / math.sqrt(2.0)
    ffn_low = rms_norm(joined, gains[3]).astype(jnp.bfloat16)
    sent_rows = w_mlp.reshape(shard_height, 3, fsdp_count, quarter)
    sent_tokens = jnp.broadcast_to(
        ffn_low[:, None, None, :], (row_count, 1, fsdp_count, model_width)
    )
    got_rows, got_tokens = (
        lax.all_to_all(sent_rows, "fsdp", split_axis=2, concat_axis=0, tiled=True),
        lax.all_to_all(sent_tokens, "fsdp", split_axis=2, concat_axis=0, tiled=True),
    )
    quarter_rows = lax.all_gather(got_rows, "ctx", axis=0, tiled=True).reshape(
        model_width, 3, quarter
    )
    w_gate_up = quarter_rows[:, :2].reshape(model_width, 2 * quarter)
    w_down = quarter_rows[:, 2]
    ffn_perm = permute_cols(got_tokens.reshape(fsdp_count * row_count, model_width))
    gate_up = plain_dot(ffn_perm, w_gate_up)
    activated = activate(gate_up).astype(jnp.bfloat16)
    ffn_out = lax.psum_scatter(
        restore_cols(times_transposed(activated, w_down)), "fsdp", scatter_dimension=0, tiled=True
    )
    after_ffn = joined + rms_norm(ffn_out, gains[4])
    after_low = after_ffn.astype(jnp.bfloat16)
    vec_gate = plain_dot(after_low, pl_gate)
    vector_in = layer_vec.astype(jnp.float32)
    vec_mixed = vec_mix(vec_gate, vector_in).astype(jnp.bfloat16)
    vec_out = plain_dot(vec_mixed, pl_proj)
    result_out = after_ffn + rms_norm(vec_out, gains[5])
    upstream = out_grad.astype(jnp.float32)
    unused_out, vec_norm_back = jax.vjp(rms_norm, vec_out, gains[5])
    d_vec_out, d_gain_vec = vec_norm_back(upstream)
    d_vec_out_low = d_vec_out.astype(jnp.bfloat16)
    d_vec_mixed = times_transposed(d_vec_out_low, pl_proj)
    grad_pl_proj = contract_rows(vec_mixed, d_vec_out_low)
    unused_out, mix_back = jax.vjp(vec_mix, vec_gate, vector_in)
    d_vec_gate, d_vector_in = mix_back(d_vec_mixed)
    d_vec_gate_low = d_vec_gate.astype(jnp.bfloat16)
    grad_after = upstream + times_transposed(d_vec_gate_low, pl_gate)
    grad_pl_gate = contract_rows(after_low, d_vec_gate_low)
    unused_out, ffn_norm_back = jax.vjp(rms_norm, ffn_out, gains[4])
    d_ffn_out, d_gain_ffn = ffn_norm_back(grad_after)
    d_ffn_low = d_ffn_out.astype(jnp.bfloat16)
    unused_out, act_back = jax.vjp(activate, gate_up)
    d_ffn_all = lax.all_gather(d_ffn_low, "fsdp", axis=0, tiled=True)
    d_ffn_perm = permute_cols(d_ffn_all)
    d_activated = plain_dot(d_ffn_perm, w_down)
    d_gate_up = act_back(d_activated)[0].astype(jnp.bfloat16)
    d_ffn_in = lax.psum_scatter(
        restore_cols(times_transposed(d_gate_up, w_gate_up)).astype(jnp.bfloat16),
        "fsdp",
        scatter_dimension=0,
        tiled=True,
    ).astype(jnp.float32)
    summed = lax.psum_scatter(
        jnp.concatenate(
            [contract_rows(ffn_perm, d_gate_up), contract_rows(d_ffn_perm, activated)], axis=1
        ).astype(jnp.bfloat16),
        "ctx",
        scatter_dimension=0,
        tiled=True,
    ).astype(jnp.float32)
    grad_w_mlp = (
        lax.all_to_all(
            summed.reshape(fsdp_count * shard_height, 3, 1, quarter).astype(jnp.bfloat16),
            "fsdp",
            split_axis=0,
            concat_axis=2,
            tiled=True,
        )
        .astype(jnp.float32)
        .reshape(shard_height, 3 * ff_width)
    )
    unused_out, pre_norm_back = jax.vjp(rms_norm, joined, gains[3])
    d_joined_part, d_gain_pre = pre_norm_back(d_ffn_in)
    d_joined = grad_after + d_joined_part
    d_half = d_joined / math.sqrt(2.0)
    unused_out, laurel_norm_back = jax.vjp(rms_norm, laurel_up, gains[1])
    d_laurel_up, d_gain_laurel = laurel_norm_back(d_half)
    unused_out, attn_norm_back = jax.vjp(rms_norm, attn_out, gains[2])
    d_attn_out, d_gain_attn = attn_norm_back(d_half)
    d_laurel_low = d_laurel_up.astype(jnp.bfloat16)
    d_attn_low = d_attn_out.astype(jnp.bfloat16)
    shard_rows = lax.all_gather(w_attn[:, in_cols:], ("fsdp", "ctx"), axis=0, tiled=True)
    d_latent = plain_dot(d_laurel_low, shard_rows[:, :RANK])
    d_mixed = plain_dot(d_attn_low, shard_rows[:, RANK:])
    d_grouped = d_mixed.astype(jnp.bfloat16).reshape(row_count, KVH, group_size, HEAD)
    again = jnp.einsum("qgrd,kgd->grqk", grouped, keys_all, preferred_element_type=jnp.float32)
    again = jnp.where(allowed[None, None], again, NEG_LARGE)
    probs = jnp.exp(again - log_total)
    d_probs = jnp.einsum(
        "qgrd,kgd->grqk", d_grouped, values_all, preferred_element_type=jnp.float32
    )
    inner_sum = jnp.sum(probs * d_probs, axis=-1, keepdims=True)
    d_scores = (probs * (d_probs - inner_sum)).astype(jnp.bfloat16)
    d_queries = jnp.einsum(
        "grqk,kgd->qgrd", d_scores, keys_all, preferred_element_type=jnp.float32
    ).reshape(row_count, QH, HEAD)
    d_keys_all = jnp.einsum("grqk,qgrd->kgd", d_scores, grouped, preferred_element_type=jnp.float32)
    d_values_all = jnp.einsum(
        "grqk,qgrd->kgd", probs.astype(jnp.bfloat16), d_grouped, preferred_element_type=jnp.float32
    )
    d_kv_all = jnp.concatenate(
        [d_keys_all.reshape(span_rows, kv_width), d_values_all.reshape(span_rows, kv_width)], axis=1
    )
    returned = d_kv_all[:row_count]
    for step_back in range(1, hop_count + 1):
        returned = (
            passed_along(returned.astype(jnp.bfloat16), "ctx", -1).astype(returned.dtype)
            + d_kv_all[step_back * row_count : (step_back + 1) * row_count]
        )
    d_keys_own = returned[:, :kv_width].reshape(row_count, KVH, HEAD)
    d_values_own = returned[:, kv_width:].reshape(row_count, KVH, HEAD)
    unused_out, query_back = jax.vjp(qk_prep, q_raw, head_gains[0])
    d_q_raw, d_head_query = query_back(d_queries)
    unused_out, key_back = jax.vjp(qk_prep, k_raw, head_gains[1])
    d_k_raw, d_head_key = key_back(d_keys_own)
    unused_out, value_back = jax.vjp(value_norm, v_raw)
    d_v_raw = value_back(d_values_own)[0]
    d_projected = jnp.concatenate(
        [
            d_q_raw.reshape(row_count, q_width),
            d_k_raw.reshape(row_count, kv_width),
            d_v_raw.reshape(row_count, kv_width),
            d_latent,
        ],
        axis=1,
    ).astype(jnp.bfloat16)
    d_normed_part = times_transposed(
        d_projected, lax.all_gather(w_attn[:, :in_cols], ("fsdp", "ctx"), axis=0, tiled=True)
    )
    unused_out, input_norm_back = jax.vjp(rms_norm, hidden, gains[0])
    d_hidden_part, d_gain_input = input_norm_back(d_half + d_normed_part)
    grad_hidden = d_half + d_hidden_part
    grad_w_attn = lax.psum_scatter(
        jnp.concatenate(
            [
                contract_rows(normed_low, d_projected),
                contract_rows(d_laurel_low, latent),
                contract_rows(d_attn_low, mixed),
            ],
            axis=1,
        ),
        ("fsdp", "ctx"),
        scatter_dimension=0,
        tiled=True,
    )
    gain_rows = jnp.stack(
        [d_gain_input, d_gain_laurel, d_gain_attn, d_gain_pre, d_gain_ffn, d_gain_vec]
    )
    head_rows = jnp.stack([d_head_query, d_head_key])
    grad_gains, grad_heads, grad_gate_all, grad_proj_all = lax.psum(
        (gain_rows, head_rows, grad_pl_gate, grad_pl_proj), ("fsdp", "ctx")
    )
    return (
        result_out.astype(jnp.bfloat16),
        grad_hidden,
        d_vector_in,
        grad_w_attn,
        grad_w_mlp,
        grad_gate_all,
        grad_proj_all,
        grad_gains,
        grad_heads,
    )

MESH = pl.DeviceIdType.MESH
VMEM_LIMIT = 60 * 1024 * 1024
ORDER = ((0, 0), (0, 1), (1, 0), (1, 1), (2, 0), (2, 1), (3, 0), (3, 1))


class Place:
    def __init__(self):
        self.f = lax.axis_index("fsdp")
        self.c = lax.axis_index("ctx")
        self.z = self.c // 2
        self.k = self.c % 2
        self.x_side = self.f + 1 - 2 * (self.f % 2)
        self.y_side = (self.f + 2) % 4
        self.diag = 3 - self.f
        self.sibling = (self.f, self.c + 1 - 2 * self.k)
        self.up = (self.f, self.c + 2)
        self.down = (self.f, self.c - 2)
        self.has_up = self.z < 3
        self.has_down = self.z > 0

    def partner(self, which):
        z = self.z
        return (z, z + 1 - 2 * (z % 2), (z + 2) % 4, 3 - z)[which]

    def peer(self, i):
        which, other = ORDER[i]
        return self.partner(which) * 2 + (self.k + other) % 2


def rows_at(start, count):
    return pl.ds(pl.multiple_of(start, 16), count)


def cols_at(start, count):
    if isinstance(start, int):
        return pl.ds(start, count)
    return pl.ds(pl.multiple_of(start, 128), count)


def remote(src, dst, send_sem, recv_sem, target):
    return pltpu.make_async_remote_copy(
        src_ref=src,
        dst_ref=dst,
        send_sem=send_sem,
        recv_sem=recv_sem,
        device_id=target,
        device_id_type=MESH,
    )


def greet(place, line, plane):
    barrier = pltpu.get_barrier_semaphore()
    count = 0

    def tell(target):
        pl.semaphore_signal(barrier, inc=1, device_id=target, device_id_type=MESH)

    if line == "all":
        for i in range(1, 8):
            tell((place.f, place.peer(i)))
        count += 7
    elif line == "chain":
        tell(place.sibling)
        for distance in (1, 3):
            tell((place.f, (place.z + distance) % 4 * 2 + place.k))
        count += 3
    if plane:
        tell((place.x_side, place.c))
        tell((place.y_side, place.c))
        count += 2
    pl.semaphore_wait(barrier, count)


class ChainGather:
    SEMS = [pltpu.SemaphoreType.DMA((2, 10)), pltpu.SemaphoreType.DMA((1,))]

    def __init__(self, place, own, out, sems):
        self.place, self.own, self.out = place, own, out
        self.sems, self.local_sem = sems
        self.rows = own.shape[0]

    def block(self, origin_z, core=None):
        core = self.place.k if core is None else core
        return self.out.at[rows_at((origin_z * 2 + core) * self.rows, self.rows)]

    def copy(self, src, dst, index, target):
        return remote(src, dst, self.sems.at[0, index], self.sems.at[1, index], target)

    def local(self):
        return pltpu.make_async_copy(self.own, self.block(self.place.z), self.local_sem.at[0])

    def upward(self, step):
        src = self.own if step == 0 else self.block(self.place.z - step)
        return self.copy(src, self.block(self.place.z - step), step, self.place.up)

    def downward(self, step):
        src = self.own if step == 0 else self.block(self.place.z + step)
        return self.copy(src, self.block(self.place.z + step), 3 + step, self.place.down)

    def across(self, origin_z, own=False):
        src = self.own if own else self.block(origin_z)
        return self.copy(src, self.block(origin_z), 6 + origin_z, self.place.sibling)

    def start(self):
        place = self.place

        @pl.when(place.has_up)
        def _():
            self.upward(0).start()

        @pl.when(place.has_down)
        def _():
            self.downward(0).start()

        self.across(place.z, True).start()
        self.local().start()

    def step(self, step):
        place = self.place

        @pl.when(place.z - step >= 0)
        def _():
            self.copy(self.own, self.block(place.z - step), step - 1, place.up).wait_recv()
            if step < 3:

                @pl.when(place.has_up)
                def _():
                    self.upward(step).start()

            self.across(place.z - step).start()

        @pl.when(place.z + step <= 3)
        def _():
            self.copy(self.own, self.block(place.z + step), 3 + step - 1, place.down).wait_recv()
            if step < 3:

                @pl.when(place.has_down)
                def _():
                    self.downward(step).start()

            self.across(place.z + step).start()

    def finish(self):
        self.arrive()
        self.settle()

    def from_sibling(self, origin):
        return self.copy(
            self.own, self.block(origin, 1 - self.place.k), 6 + origin, self.place.sibling
        )

    def arrive(self):
        self.local().wait()
        for origin in range(4):
            self.from_sibling(origin).wait_recv()

    def settle(self):
        place = self.place
        for origin in range(4):
            self.from_sibling(origin).wait_send()
        for step in range(3):

            @pl.when((place.z - step >= 0) & place.has_up)
            def _(step=step):
                self.upward(step).wait_send()

            @pl.when((place.z + step <= 3) & place.has_down)
            def _(step=step):
                self.downward(step).wait_send()


class ChainScatter:
    @staticmethod
    def scratch(rows, cols):
        return [
            pltpu.VMEM((4, rows, cols), jnp.bfloat16),
            pltpu.VMEM((6, rows, cols), jnp.bfloat16),
            pltpu.SemaphoreType.DMA((2, 10)),
        ]

    def __init__(self, place, partial, scratch):
        self.place, self.partial = place, partial
        self.from_sibling, self.moving, self.sems = scratch
        self.rows = partial.shape[0] // 8

    def block(self, origin_z, core):
        return self.partial.at[rows_at((origin_z * 2 + core) * self.rows, self.rows)]

    def across(self, dest):
        return remote(
            self.block(dest, 1 - self.place.k),
            self.from_sibling.at[dest],
            self.sems.at[0, 6 + dest],
            self.sems.at[1, 6 + dest],
            self.place.sibling,
        )

    def moved(self, slot, target):
        return remote(
            self.moving.at[slot],
            self.moving.at[slot],
            self.sems.at[0, slot],
            self.sems.at[1, slot],
            target,
        )

    def start(self):
        for dest in (3, 0, 2, 1):
            self.across(dest).start()

    def pair_sum(self, dest):
        return self.block(dest, self.place.k)[...].astype(jnp.float32) + self.from_sibling[
            dest
        ].astype(jnp.float32)

    def pass_on(self, dest, upward, inner=False):
        place = self.place
        slot = dest - 1 if upward else 3 + dest
        target = place.up if upward else place.down
        self.across(dest).wait_recv()
        total = self.pair_sum(dest)
        if inner:
            self.moved(slot, target).wait_recv()
            total = total + self.moving[slot].astype(jnp.float32)
        self.moving[slot] = total.astype(jnp.bfloat16)
        self.moved(slot, target).start()

    def ends(self):
        z = self.place.z

        @pl.when(z == 0)
        def _():
            for dest in (3, 2, 1):
                self.pass_on(dest, True)

        @pl.when(z == 3)
        def _():
            for dest in (0, 1, 2):
                self.pass_on(dest, False)

    def inner(self, i):
        z = self.place.z

        @pl.when(z == 1)
        def _():
            if i == 0:
                self.pass_on(3, True, True)
            else:
                self.pass_on(0, False, True)
                self.pass_on(2, True, True)

        @pl.when(z == 2)
        def _():
            if i == 0:
                self.pass_on(0, False, True)
            else:
                self.pass_on(3, True, True)
                self.pass_on(1, False, True)

    def finish(self, out):
        place = self.place
        for dest in range(4):

            @pl.when(place.z == dest)
            def _(dest=dest):
                self.across(dest).wait_recv()
                total = self.pair_sum(dest)
                if dest > 0:
                    self.moved(dest - 1, place.up).wait_recv()
                    total = total + self.moving[dest - 1].astype(jnp.float32)
                if dest < 3:
                    self.moved(3 + dest, place.down).wait_recv()
                    total = total + self.moving[3 + dest].astype(jnp.float32)
                out[...] = total

        for dest in range(4):
            self.across(dest).wait_send()
        for i in range(3):
            top, bottom = 3 - i, i

            @pl.when(place.z < top)
            def _(top=top):
                self.moved(top - 1, place.up).wait_send()

            @pl.when(place.z > bottom)
            def _(bottom=bottom):
                self.moved(3 + bottom, place.down).wait_send()


class Spread:
    @staticmethod
    def sems(pieces, outs):
        return [
            pltpu.SemaphoreType.DMA((2, 8, pieces)),
            pltpu.SemaphoreType.DMA((2, 4, 8, outs)),
        ]

    def __init__(self, place, weight, outs, pieces, sems):
        self.place, self.weight, self.outs, self.pieces = place, weight, outs, pieces
        self.swap_sems, self.plane_sems = sems
        self.rows = weight.shape[0]

    def spot(self, f, c):
        return (f * 8 + c) * self.rows

    def swap(self, i, p, origin):
        column, width, out, out_column = self.pieces[p]
        peer = self.place.peer(i)
        src = self.weight.at[:, cols_at(column(peer), width)]
        dst = self.outs[out].at[
            rows_at(self.spot(self.place.f, origin), self.rows), pl.ds(out_column, width)
        ]
        if i == 0:
            return pltpu.make_async_copy(src, dst, self.swap_sems.at[0, 0, p])
        return remote(
            src,
            dst,
            self.swap_sems.at[0, i, p],
            self.swap_sems.at[1, i, p],
            (self.place.f, peer),
        )

    def whole(self, f, c, out):
        return self.outs[out].at[rows_at(self.spot(f, c), self.rows)]

    def part(self, f, c, out, half):
        count = self.rows // 2
        return self.outs[out].at[rows_at(self.spot(f, c) + half * count, count)]

    def plane(self, kind, i, out, ref, target):
        return remote(
            ref,
            ref,
            self.plane_sems.at[0, kind, i, out],
            self.plane_sems.at[1, kind, i, out],
            (target, self.place.c),
        )

    def start(self, first=0, last=8):
        for i in range(first, last):
            for p in range(len(self.pieces)):
                self.swap(i, p, self.place.c).start()

    def forward(self, i):
        place = self.place
        origin = place.peer(i)
        for p in range(len(self.pieces)):
            copy = self.swap(i, p, origin)
            if i == 0:
                copy.wait()
            else:
                copy.wait_recv()
        for out in range(len(self.outs)):
            ref = self.whole(place.f, origin, out)
            self.plane(0, i, out, ref, place.x_side).start()
            self.plane(1, i, out, ref, place.y_side).start()

    def relay(self, i):
        place = self.place
        origin = place.peer(i)
        for out in range(len(self.outs)):
            self.plane(0, i, out, self.whole(place.x_side, origin, out), place.x_side).wait_recv()
            self.plane(2, i, out, self.part(place.x_side, origin, out, 0), place.y_side).start()
            self.plane(1, i, out, self.whole(place.y_side, origin, out), place.y_side).wait_recv()
            self.plane(3, i, out, self.part(place.y_side, origin, out, 1), place.x_side).start()

    def finish(self, first=0, last=8):
        self.arrive(first, last)
        self.settle(first, last)

    def arrive(self, first=0, last=8):
        place = self.place
        for i in range(first, last):
            origin = place.peer(i)
            for out in range(len(self.outs)):
                self.plane(
                    2, i, out, self.part(place.diag, origin, out, 0), place.y_side
                ).wait_recv()
                self.plane(
                    3, i, out, self.part(place.diag, origin, out, 1), place.x_side
                ).wait_recv()

    def settle(self, first=0, last=8):
        place = self.place
        for i in range(first, last):
            origin = place.peer(i)
            if i:
                for p in range(len(self.pieces)):
                    self.swap(i, p, place.c).wait_send()
            for out in range(len(self.outs)):
                own = self.whole(place.f, origin, out)
                self.plane(0, i, out, own, place.x_side).wait_send()
                self.plane(1, i, out, own, place.y_side).wait_send()
                half = self.part(place.f, origin, out, 0)
                self.plane(2, i, out, half, place.y_side).wait_send()
                self.plane(3, i, out, half, place.x_side).wait_send()


class PlaneGather:
    SEMS = [pltpu.SemaphoreType.DMA((2, 4))]

    def __init__(self, place, out, sems):
        self.place, self.out = place, out
        self.sems = sems[0]
        self.rows = out.shape[0] // 4

    def copy(self, kind, f, target):
        count = self.rows // 2 if kind > 1 else self.rows
        start = f * self.rows + (count if kind == 3 else 0)
        ref = self.out.at[rows_at(start, count)]
        return remote(
            ref, ref, self.sems.at[0, kind], self.sems.at[1, kind], (target, self.place.c)
        )

    def start(self):
        place = self.place
        self.copy(0, place.f, place.x_side).start()
        self.copy(1, place.f, place.y_side).start()

    def relay(self):
        place = self.place
        self.copy(0, place.x_side, place.x_side).wait_recv()
        self.copy(2, place.x_side, place.y_side).start()
        self.copy(1, place.y_side, place.y_side).wait_recv()
        self.copy(3, place.y_side, place.x_side).start()

    def finish(self):
        place = self.place
        self.copy(2, place.diag, place.y_side).wait_recv()
        self.copy(3, place.diag, place.x_side).wait_recv()
        self.copy(0, place.f, place.x_side).wait_send()
        self.copy(1, place.f, place.y_side).wait_send()
        self.copy(2, place.x_side, place.y_side).wait_send()
        self.copy(3, place.y_side, place.x_side).wait_send()


class Drain:
    @staticmethod
    def scratch(rows, widths, peers=8):
        half = rows // 2
        lists = []
        for width in widths:
            lists += [
                pltpu.VMEM((2, peers, 2, half, width), jnp.bfloat16),
                pltpu.VMEM((2, peers, half, width), jnp.bfloat16),
            ]
        return lists

    @staticmethod
    def sems(pieces, outs, peers=8):
        return [
            pltpu.SemaphoreType.DMA((2, 2, peers, 2, outs)),
            pltpu.SemaphoreType.DMA((2, 2, peers, outs)),
            pltpu.SemaphoreType.DMA((2, peers, pieces, 2)),
        ]

    def __init__(self, place, grads, land, pieces, scratch, sems, base=0, peers=8, adds=None):
        self.place, self.grads, self.land, self.pieces = place, grads, land, pieces
        self.adds = adds or grads
        self.first = scratch[0::2]
        self.second = scratch[1::2]
        self.first_sems, self.second_sems, self.swap_sems = sems
        self.rows = land.shape[0]
        self.half = self.rows // 2
        self.units = len(grads[0].shape) == 4
        self.base, self.peers = base, peers

    def part(self, g, f, i, half, adds=False):
        refs = self.adds if adds else self.grads
        peer = self.place.peer(self.base + i)
        if self.units:
            start = (peer % 2) * self.rows + half * self.half
            return refs[g].at[i // 2, f, rows_at(start, self.half)]
        return refs[g].at[rows_at((f * 8 + peer) * self.rows + half * self.half, self.half)]

    def sides(self, axis):
        place = self.place
        return (place.x_side, place.y_side) if axis == 0 else (place.y_side, place.x_side)

    def first_copy(self, axis, i, which, g):
        near, _ = self.sides(axis)
        f = near if which == 0 else self.place.diag
        return remote(
            self.part(g, f, i, axis),
            self.first[g].at[axis, i, which],
            self.first_sems.at[0, axis, i, which, g],
            self.first_sems.at[1, axis, i, which, g],
            (near, self.place.c),
        )

    def second_copy(self, axis, i, g):
        _, far = self.sides(axis)
        return remote(
            self.first[g].at[axis, i, 1],
            self.second[g].at[axis, i],
            self.second_sems.at[0, axis, i, g],
            self.second_sems.at[1, axis, i, g],
            (far, self.place.c),
        )

    def swap(self, i, p, half, origin):
        column, width, g, g_column = self.pieces[p]
        src = self.first[g].at[half, i, 0, :, pl.ds(g_column, width)]
        dst = self.land.at[pl.ds(half * self.half, self.half), cols_at(column(origin), width)]
        if self.base + i == 0:
            return pltpu.make_async_copy(src, dst, self.swap_sems.at[0, i, p, half])
        return remote(
            src,
            dst,
            self.swap_sems.at[0, i, p, half],
            self.swap_sems.at[1, i, p, half],
            (self.place.f, self.place.peer(self.base + i)),
        )

    def start(self, i):
        for g in range(len(self.grads)):
            for which in (1, 0):
                for axis in range(2):
                    self.first_copy(axis, i, which, g).start()

    def middle(self, i):
        place = self.place
        for g in range(len(self.grads)):
            for axis in range(2):
                _, far = self.sides(axis)
                self.first_copy(axis, i, 1, g).wait_recv()
                mine = self.part(g, far, i, axis, True)
                self.first[g][axis, i, 1] = (
                    mine[...].astype(jnp.float32) + self.first[g][axis, i, 1].astype(jnp.float32)
                ).astype(jnp.bfloat16)
                self.second_copy(axis, i, g).start()

    def last(self, i):
        place = self.place
        for g in range(len(self.grads)):
            for axis in range(2):
                self.first_copy(axis, i, 0, g).wait_recv()
                self.second_copy(axis, i, g).wait_recv()
                mine = self.part(g, place.f, i, axis, True)
                self.first[g][axis, i, 0] = (
                    mine[...].astype(jnp.float32)
                    + self.first[g][axis, i, 0].astype(jnp.float32)
                    + self.second[g][axis, i].astype(jnp.float32)
                ).astype(jnp.bfloat16)
        for p in range(len(self.pieces)):
            for half in range(2):
                self.swap(i, p, half, place.c).start()

    def finish(self):
        place = self.place
        for i in range(self.peers):
            for p in range(len(self.pieces)):
                for half in range(2):
                    copy = self.swap(i, p, half, place.peer(self.base + i))
                    if self.base + i == 0:
                        copy.wait()
                    else:
                        copy.wait_recv()
                        copy.wait_send()
            for g in range(len(self.grads)):
                for axis in range(2):
                    for which in range(2):
                        self.first_copy(axis, i, which, g).wait_send()
                    self.second_copy(axis, i, g).wait_send()


ANY = pl.BlockSpec(memory_space=pl.ANY)
VMEM = pl.BlockSpec(memory_space=pltpu.VMEM)


def comm_call(kernel, ident, out_shape, in_specs, out_specs, scratch, aliases=None):
    return pl.pallas_call(
        kernel,
        input_output_aliases=aliases or {},
        out_shape=out_shape,
        in_specs=in_specs,
        out_specs=out_specs,
        scratch_shapes=scratch,
        compiler_params=pltpu.CompilerParams(
            collective_id=ident, has_side_effects=True, vmem_limit_bytes=VMEM_LIMIT
        ),
    )


class Local:
    def __init__(self, sems):
        self.sems, self.copies = sems, []

    def start(self, src, dst):
        self.copies.append(pltpu.make_async_copy(src, dst, self.sems.at[len(self.copies)]))
        self.copies[-1].start()
        return len(self.copies) - 1

    def wait(self, *indices):
        for index in indices:
            self.copies[index].wait()


def bf16(*shape):
    return jax.ShapeDtypeStruct(shape, jnp.bfloat16)


def scatter_tokens(partial, ident):
    rows, cols = partial.shape[0] // 8, partial.shape[1]

    def kernel(partial_ref, out_ref, *scratch):
        place = Place()
        greet(place, "chain", False)
        scatter = ChainScatter(place, partial_ref, scratch)
        scatter.start()
        scatter.ends()
        scatter.inner(0)
        scatter.inner(1)
        scatter.finish(out_ref)

    return comm_call(
        kernel,
        ident,
        jax.ShapeDtypeStruct((rows, cols), jnp.float32),
        [VMEM],
        VMEM,
        ChainScatter.scratch(rows, cols),
    )(partial)


ATTN_PIECES = (
    (lambda c: 256 * c, 256, 0, 0),
    (lambda c: 2048 + 256 * (c // 4), 256, 0, 256),
    (lambda c: 2560 + 256 * (c // 4), 256, 0, 512),
    (lambda c: 3200 + 256 * c, 256, 1, 0),
    (lambda c: 3072, 128, 2, 0),
)
ATTN_LAND = (
    (lambda c: 1152 * c, 896, 0, 0),
    (lambda c: 1152 * c + 896, 256, 1, 0),
)
MLP_PIECES = (
    (lambda c: 1024 * c, 1024, 0, 0),
    (lambda c: 8192 + 1024 * c, 1024, 0, 1024),
    (lambda c: 16384 + 1024 * c, 1024, 1, 0),
)
VEC_LAND = ((lambda c: 512 * c, 512, 0, 0),)
EARLY_UNITS = 2


def turn(values, cosine, sine):
    half = HEAD // 2
    first, second = values[:, :half], values[:, half:]
    return jnp.concatenate(
        [first * cosine - second * sine, second * cosine + first * sine], axis=1
    )


def allowed_pairs(first_query, first_key, positions):
    shape = (positions.shape[0], 768)
    distance = (
        lax.broadcasted_iota(jnp.int32, shape, 0)
        - lax.broadcasted_iota(jnp.int32, shape, 1)
        + (first_query - first_key)
    )
    return (distance >= 0) & (distance <= jnp.minimum(positions, WINDOW - 1))


def positions_of(parts):
    return (parts[:, 0:1].astype(jnp.float32) * 256.0 + parts[:, 1:2].astype(jnp.float32)).astype(
        jnp.int32
    )


def attention_forward(
    normed_low, own_pos, w_attn, w_mlp, hidden, normed_in, gains, head_gains, tables, ident
):
    height = 32 * w_attn.shape[0]
    rows, width = hidden.shape
    total = 8 * rows
    query_block, key_span = 2 * rows, 768
    scatter_scratch = ChainScatter.scratch(rows, width)

    def kernel(*refs):
        ins, outs, held = split_refs(refs, 9, 17, len(refs) - 26)
        (own_ref, pos_ref, attn_ref, mlp_ref, hidden_ref, normed_ref, gains_ref, head_ref,
         tables_ref) = ins
        (row_ref, qkv_ref, out_ref, laurel_ref, row_pos, gate_up_ref, down_ref, row_ffn,
         projected, q_low, k_low, v_low, mixed, latent_ref, laurel_up, attn_out, joined) = outs
        scratch, scat, attn_m, mlp_m, gather_m = split_refs(held, 2, len(scatter_scratch), 2, 2, 6)
        own_ffn, partial = scratch
        place = Place()
        greet(place, "all", True)
        attn = Spread(place, attn_ref, [qkv_ref, out_ref, laurel_ref], ATTN_PIECES, attn_m)
        mlp = Spread(place, mlp_ref, [gate_up_ref, down_ref], MLP_PIECES, mlp_m)
        gathers = [
            ChainGather(place, own_ref, row_ref, gather_m[0:2]),
            ChainGather(place, pos_ref, row_pos, gather_m[2:4]),
        ]
        last = ChainGather(place, own_ffn, row_ffn, gather_m[4:6])
        scatter = ChainScatter(place, partial, scat)

        def step(n):
            for gather in gathers:
                gather.step(n)

        for gather in gathers:
            gather.start()
        attn.start(0, 2)
        attn.start(4, 6)
        attn.start(2, 4)
        attn.start(6, 8)
        mlp.start(0, 2)
        attn.forward(0)
        attn.forward(1)
        mlp.forward(0)
        step(1)
        attn.forward(2)
        attn.forward(3)
        attn.relay(0)
        attn.relay(1)
        step(2)
        attn.forward(4)
        attn.forward(5)
        attn.relay(2)
        attn.relay(3)
        mlp.forward(1)
        step(3)
        attn.forward(6)
        attn.forward(7)
        mlp.start(4, 6)
        mlp.start(2, 4)
        attn.relay(4)
        attn.relay(5)
        mlp.relay(0)
        attn.relay(6)
        attn.relay(7)
        for gather in gathers:
            gather.arrive()
        attn.arrive()
        mlp.relay(1)
        mlp.start(6, 8)

        @pl.loop(0, total // query_block)
        def _(n):
            here = rows_at(n * query_block, query_block)
            block = plain_dot(row_ref[here], qkv_ref[...])
            projected[here] = block
            cosine, sine = tables_ref[here, : HEAD // 2], tables_ref[here, HEAD // 2 :]
            q_low[here] = turn(
                rms_norm(block[:, :HEAD], head_ref[0:1]), cosine, sine
            ).astype(jnp.bfloat16)
            k_low[here] = turn(
                rms_norm(block[:, HEAD : 2 * HEAD], head_ref[1:2]), cosine, sine
            ).astype(jnp.bfloat16)
            v_low[here] = value_norm(block[:, 2 * HEAD :]).astype(jnp.bfloat16)

        upper = place.z // 2

        @pl.loop(0, total // query_block)
        def _(n):
            d = n * upper + (3 - n) * (1 - upper)
            here = rows_at(d * query_block, query_block)
            first_key = (d // 2) * (d - 2) * query_block
            there = rows_at(first_key, key_span)
            scores = jnp.where(
                allowed_pairs(d * query_block, first_key, positions_of(row_pos[here])),
                times_transposed(q_low[here], k_low[there]),
                NEG_LARGE,
            )
            weights = jnp.exp(scores - jnp.max(scores, axis=-1, keepdims=True))
            probs = (weights / jnp.sum(weights, axis=-1, keepdims=True)).astype(jnp.bfloat16)
            block = plain_dot(probs, v_low[there]).astype(jnp.bfloat16)
            mixed[here] = block
            partial[here] = times_transposed(block, out_ref[...]).astype(jnp.bfloat16)
            scatter.across(d).start()

        scatter.ends()
        mlp.forward(2)
        mlp.forward(3)
        scatter.inner(0)
        low = plain_dot(own_ref[...], laurel_ref[...])
        latent_ref[...] = low.astype(jnp.bfloat16)
        lanes = lax.broadcasted_iota(jnp.int32, low.shape, 1)
        shifted = jnp.where(lanes >= RANK, pltpu.roll(low, RANK, 1), 0.0).astype(jnp.bfloat16)
        laurel_up[...] = times_transposed(shifted, laurel_ref[...])
        scatter.inner(1)
        mlp.relay(2)
        mlp.relay(3)
        mlp.forward(4)
        mlp.forward(5)
        scatter.finish(attn_out)
        laurel_res = normed_ref[...] + rms_norm(laurel_up[...], gains_ref[1:2])
        after_attn = hidden_ref[...].astype(jnp.float32) + rms_norm(attn_out[...], gains_ref[2:3])
        joined[...] = (after_attn + laurel_res) / math.sqrt(2.0)
        own_ffn[...] = rms_norm(joined[...], gains_ref[3:4]).astype(jnp.bfloat16)
        last.start()
        mlp.relay(4)
        mlp.relay(5)
        last.step(1)
        mlp.forward(6)
        mlp.forward(7)
        last.step(2)
        mlp.relay(6)
        mlp.relay(7)
        last.step(3)
        mlp.arrive()
        last.arrive()
        attn.settle()
        mlp.settle()
        for gather in gathers:
            gather.settle()
        last.settle()

    def f32(*shape):
        return jax.ShapeDtypeStruct(shape, jnp.float32)

    token_f32 = f32(rows, width)
    head = bf16(total, HEAD)
    outs = [bf16(total, width), bf16(height, 768), bf16(height, 256), bf16(height, 128)]
    outs += [bf16(total, 128), bf16(height, 2048), bf16(height, 1024), bf16(total, width)]
    outs += [f32(total, 768), head, head, head, head, bf16(rows, 128)]
    outs += [token_f32, token_f32, token_f32]
    return comm_call(
        kernel,
        ident,
        outs,
        [VMEM, VMEM, ANY, ANY] + [VMEM] * 5,
        [VMEM] * 5 + [ANY] * 3 + [VMEM] * 9,
        [pltpu.VMEM((rows, width), jnp.bfloat16), pltpu.VMEM((total, width), jnp.bfloat16)]
        + scatter_scratch
        + Spread.sems(len(ATTN_PIECES), 3)
        + Spread.sems(len(MLP_PIECES), 2)
        + ChainGather.SEMS * 3,
    )(normed_low, own_pos, w_attn, w_mlp, hidden, normed_in, gains, head_gains, tables)


def split_refs(refs, *counts):
    refs, parts = list(refs), []
    for count in counts:
        parts.append(refs[:count])
        refs = refs[count:]
    return parts


def unit_gradient(place, n, tokens_ref, grad_ref, out, turned_ref):
    zz = place.partner(n)
    count = turned_ref.shape[0] // 4
    for f in range(4):
        columns = cols_at((f * 4 + zz) * count, count)
        turned_ref[f * count : (f + 1) * count] = tokens_ref[:, columns].T
    step = 512

    @pl.loop(0, grad_ref.shape[1] // step)
    def _(t):
        columns = cols_at(t * step, step)
        block = plain_dot(turned_ref[...], grad_ref[:, columns]).astype(jnp.bfloat16)
        for f in range(4):
            out[f, :, columns] = block[f * count : (f + 1) * count]


def ffn_open_backward(d_ffn_low, vec_grads, shard_height, ident):
    rows, width = d_ffn_low.shape
    vec_width = vec_grads.shape[1]
    vec_scratch = Drain.scratch(shard_height, (vec_width,))

    def kernel(own_ref, vec_ref, all_ref, vec_land, *held):
        gather_m, vec_s, vec_m = split_refs(held, 2, len(vec_scratch), 3)
        place = Place()
        greet(place, "all", True)
        gather = ChainGather(place, own_ref, all_ref, gather_m)
        vec = Drain(place, [vec_ref], vec_land, VEC_LAND, vec_s, vec_m)
        gather.start()
        for i in range(8):
            vec.start(i)
        gather.step(1)
        for i in range(4):
            vec.middle(i)
        gather.step(2)
        for i in range(4, 8):
            vec.middle(i)
        for i in range(8):
            vec.last(i)
        gather.step(3)
        gather.finish()
        vec.finish()

    return comm_call(
        kernel,
        ident,
        [bf16(8 * rows, width), bf16(shard_height, 8 * vec_width)],
        [VMEM, VMEM],
        [ANY, ANY],
        ChainGather.SEMS + vec_scratch + Drain.sems(1, 1),
    )(d_ffn_low, vec_grads)


def ffn_close_backward(
    partial, row_ffn, d_gate_up, row_d_ffn, activated, shard_height, mlp_cols, ident
):
    rows, width = partial.shape[0] // 8, partial.shape[1]
    wide, narrow = d_gate_up.shape[1], activated.shape[1]
    scatter_scratch = ChainScatter.scratch(rows, width)
    mlp_scratch = Drain.scratch(shard_height, (wide, narrow), 2 * EARLY_UNITS)
    mlp_sems = Drain.sems(len(MLP_PIECES), 2, 2 * EARLY_UNITS)
    unit_rows = 2 * shard_height
    late = 4 - EARLY_UNITS

    def kernel(*refs):
        (partial_ref, ffn_hbm, dgu_ref, dffn_hbm, act_ref), outs, held = split_refs(
            refs, 5, 4, len(refs) - 9
        )
        out_ref, mlp_land, late_wide, late_narrow = outs
        own, scat, mlp_s, mlp_m = split_refs(held, 6, len(scatter_scratch), len(mlp_scratch), 3)
        own_wide, own_narrow, turned, ffn_ref, dffn_ref, local_sems = own
        place = Place()
        local = Local(local_sems)
        ffn_copy = local.start(ffn_hbm, ffn_ref)
        dffn_copy = local.start(dffn_hbm, dffn_ref)
        greet(place, "all", True)
        scatter = ChainScatter(place, partial_ref, scat)
        mlp = Drain(
            place, [own_wide, own_narrow], mlp_land, MLP_PIECES, mlp_s, mlp_m, 0, 2 * EARLY_UNITS
        )

        def unit(n):
            unit_gradient(place, n, ffn_ref, dgu_ref, own_wide.at[n], turned)
            unit_gradient(place, n, dffn_ref, act_ref, own_narrow.at[n], turned)

        def kept(n):
            return (
                local.start(own_wide.at[n], late_wide.at[n - EARLY_UNITS]),
                local.start(own_narrow.at[n], late_narrow.at[n - EARLY_UNITS]),
            )

        scatter.start()
        scatter.ends()
        local.wait(ffn_copy, dffn_copy)
        unit(1)
        mlp.start(2)
        mlp.start(3)
        unit(0)
        scatter.inner(0)
        unit(2)
        mlp.middle(2)
        mlp.start(0)
        mlp.middle(3)
        mlp.start(1)
        scatter.inner(1)
        unit(3)
        out_copies = []
        for n in range(EARLY_UNITS, 4):
            out_copies += kept(n)
        mlp.last(2)
        mlp.last(3)
        mlp.middle(0)
        if EARLY_UNITS > 2:
            mlp.start(4)
        mlp.middle(1)
        if EARLY_UNITS > 2:
            mlp.start(5)
        scatter.finish(out_ref)
        mlp.last(0)
        mlp.last(1)
        if EARLY_UNITS > 2:
            mlp.middle(4)
            mlp.middle(5)
            mlp.last(4)
            mlp.last(5)
        local.wait(*out_copies)
        mlp.finish()

    return comm_call(
        kernel,
        ident,
        [
            jax.ShapeDtypeStruct((rows, width), jnp.float32),
            bf16(shard_height, mlp_cols),
            bf16(late, 4, unit_rows, wide),
            bf16(late, 4, unit_rows, narrow),
        ],
        [VMEM, ANY, VMEM, ANY, VMEM],
        [VMEM, ANY, ANY, ANY],
        [
            pltpu.VMEM((4, 4, unit_rows, wide), jnp.bfloat16),
            pltpu.VMEM((4, 4, unit_rows, narrow), jnp.bfloat16),
            pltpu.VMEM((4 * unit_rows, 8 * rows), jnp.bfloat16),
            pltpu.VMEM(row_ffn.shape, jnp.bfloat16),
            pltpu.VMEM(row_d_ffn.shape, jnp.bfloat16),
            pltpu.SemaphoreType.DMA((2 + 2 * late,)),
        ]
        + scatter_scratch
        + mlp_scratch
        + mlp_sems,
    )(partial, row_ffn, d_gate_up, row_d_ffn, activated)


def sum_everywhere(place, own, arrived, sems):
    k, f = place.k, place.f
    targets = [
        place.sibling,
        (place.x_side, place.c),
        (place.y_side, place.c),
        (f, place.partner(1) * 2 + k),
        (f, place.partner(3) * 2 + k),
    ]
    return [
        remote(own.at[n], arrived.at[n], sems.at[0, n], sems.at[1, n], target)
        for n, target in enumerate(targets)
    ]


def turn_back(grads, cosine, sine):
    half = HEAD // 2
    first, second = grads[:, :half], grads[:, half:]
    return jnp.concatenate(
        [first * cosine + second * sine, second * cosine - first * sine], axis=1
    )


def norm_back(values, scale_vec, grads):
    inverse = lax.rsqrt(jnp.mean(values * values, axis=-1, keepdims=True) + EPSILON)
    unit = values * inverse
    scaled = grads * scale_vec
    back = (scaled - unit * jnp.mean(unit * scaled, axis=-1, keepdims=True)) * inverse
    return back, jnp.sum(grads * unit, axis=0, keepdims=True)


def attention_backward(
    d_attn_low, weights, kept, tables, head_gains, hidden, gains, base, other_gains,
    laurel_partial, mlp_grads, mlp_land, vec_land, ident
):
    w_qkv, w_out = weights
    queries, keys, values, mixed, projected, row_normed, row_parts = kept
    rows, width = base.shape
    total = 8 * rows
    query_block, key_span = 2 * rows, 768
    shard_height, vec_width = vec_land.shape[0], vec_land.shape[1] // 8
    qkv_width, laurel_width = w_qkv.shape[1], laurel_partial.shape[1]
    attn_widths = (qkv_width + laurel_width, w_out.shape[1])
    scatter_scratch = ChainScatter.scratch(rows, width)
    first_late, late = 2 * EARLY_UNITS, 2 * (4 - EARLY_UNITS)
    mlp_scratch = Drain.scratch(shard_height, [grad.shape[3] for grad in mlp_grads], late)
    mlp_sems = Drain.sems(len(MLP_PIECES), 2, late)
    loads = [*mlp_grads, w_out, queries, keys, values, tables, projected, w_qkv, mixed, row_normed]
    attn_scratch = Drain.scratch(shard_height, attn_widths)
    attn_sems = Drain.sems(len(ATTN_LAND), 2)
    gain_rows = other_gains.shape[0]

    def kernel(*refs):
        ins, outs, held = split_refs(refs, 21, 5, len(refs) - 26)
        (own_ref, row_pos, head_ref, hidden_ref, gains_ref, base_ref, other_ref, laurel_ref,
         vec_ref) = ins[:9]
        wide_hbm, narrow_hbm = ins[9:11]
        out_ref, gain_ref, land_ref, attn_land, vec_all = outs
        (scratch, loaded, local_sems, gain_s, scat, mlp_s, mlp_m, attn_s, attn_m, vec_m, gather_m) = (
            split_refs(
                held, 8, 11, 1, 3, len(scatter_scratch), len(mlp_scratch), 3, len(attn_scratch), 3,
                3, 2,
            )
        )
        vec_own, row_grad, d_mixed, d_keys, d_values, d_projected, qkv_grad, out_grad = scratch
        (wide_ref, narrow_ref, w_out_ref, q_low, k_low, v_low, tables_ref, projected_ref, qkv_ref,
         mixed_ref, row_ref) = loaded
        held_gains, arrived_gains, gain_sems = gain_s
        place = Place()
        local = Local(local_sems[0])
        for src, dst in zip(ins[9:20], loaded):
            local.start(src, dst)
        greet(place, "all", True)
        gather = ChainGather(place, own_ref, row_grad, gather_m)
        scatter = ChainScatter(place, row_grad, scat)
        mlp = Drain(
            place, [wide_hbm, narrow_hbm], land_ref, MLP_PIECES, mlp_s, mlp_m, first_late, late,
            [wide_ref, narrow_ref],
        )
        attn = Drain(place, [qkv_grad, out_grad], attn_land, ATTN_LAND, attn_s, attn_m)
        vec = ChainGather(
            place, vec_own, vec_all.at[rows_at(place.f * 8 * shard_height, 8 * shard_height)],
            vec_m[:2],
        )
        plane = PlaneGather(place, vec_all, vec_m[2:])
        rounds = sum_everywhere(place, held_gains, arrived_gains, gain_sems)

        def gain_round(n):
            rounds[n].wait_recv()
            held_gains[n + 1] = held_gains[n] + arrived_gains[n]
            if n < 4:
                rounds[n + 1].start()

        gather.start()
        mlp.start(0)
        mlp.start(1)
        vec_sum = vec_ref[:, 0:vec_width].astype(jnp.float32)
        for c in range(1, 8):
            vec_sum = vec_sum + vec_ref[:, c * vec_width : (c + 1) * vec_width].astype(jnp.float32)
        vec_own[...] = vec_sum.astype(jnp.bfloat16)
        vec.start()
        d_keys[...] = jnp.zeros_like(d_keys)
        d_values[...] = jnp.zeros_like(d_values)
        held_gains[0] = other_ref[...]
        qkv_grad[:, qkv_width:] = laurel_ref[...]
        local.wait(0, 1)
        gather.step(1)
        vec.step(1)
        mlp.middle(0)
        mlp.middle(1)
        for i in range(2, late):
            mlp.start(i)
        gather.step(2)
        vec.step(2)
        mlp.last(0)
        mlp.last(1)
        gather.step(3)
        vec.step(3)
        gather.arrive()
        vec.arrive()
        plane.start()
        local.wait(2, 3, 4, 5, 6, 7)

        @pl.loop(0, total // query_block)
        def _(n):
            here = rows_at(n * query_block, query_block)
            d_mixed[here] = plain_dot(row_grad[here], w_out_ref[...]).astype(jnp.bfloat16)

        for i in range(2, late):
            mlp.middle(i)

        @pl.loop(0, total // query_block)
        def _(d):
            here = rows_at(d * query_block, query_block)
            first_key = (d // 2) * (d - 2) * query_block
            there = rows_at(first_key, key_span)
            query, key, value, d_mix = q_low[here], k_low[there], v_low[there], d_mixed[here]
            scores = jnp.where(
                allowed_pairs(d * query_block, first_key, positions_of(row_pos[here])),
                times_transposed(query, key),
                NEG_LARGE,
            )
            exps = jnp.exp(scores - jnp.max(scores, axis=-1, keepdims=True))
            probs = exps / jnp.sum(exps, axis=-1, keepdims=True)
            d_probs = times_transposed(d_mix, value)
            inner_sum = jnp.sum(probs * d_probs, axis=-1, keepdims=True)
            d_scores = (probs * (d_probs - inner_sum)).astype(jnp.bfloat16)
            d_keys[there] += contract_rows(d_scores, query)
            d_values[there] += contract_rows(probs.astype(jnp.bfloat16), d_mix)
            cosine, sine = tables_ref[here, : HEAD // 2], tables_ref[here, HEAD // 2 :]
            d_query, d_scale = norm_back(
                projected_ref[here, :HEAD],
                head_ref[0:1],
                turn_back(plain_dot(d_scores, key), cosine, sine),
            )
            d_projected[here, :HEAD] = d_query.astype(jnp.bfloat16)
            held_gains[0, 6:7, :HEAD] += d_scale

        for i in range(2, late):
            mlp.last(i)

        @pl.loop(0, total // query_block)
        def _(n):
            here = rows_at(n * query_block, query_block)
            cosine, sine = tables_ref[here, : HEAD // 2], tables_ref[here, HEAD // 2 :]
            d_key, d_scale = norm_back(
                projected_ref[here, HEAD : 2 * HEAD],
                head_ref[1:2],
                turn_back(d_keys[here], cosine, sine),
            )
            d_projected[here, HEAD : 2 * HEAD] = d_key.astype(jnp.bfloat16)
            held_gains[0, 6:7, HEAD : 2 * HEAD] += d_scale
            d_value, _ = norm_back(projected_ref[here, 2 * HEAD :], 1.0, d_values[here])
            d_projected[here, 2 * HEAD :] = d_value.astype(jnp.bfloat16)

        quarter = width // 4
        local.wait(8, 9, 10)

        @pl.loop(0, 4)
        def _(n):
            columns = cols_at(n * quarter, quarter)
            out_grad[rows_at(n * quarter, quarter)] = contract_rows(
                row_grad[:, columns], mixed_ref[...]
            ).astype(jnp.bfloat16)

        gather.settle()
        upper = place.z // 2

        @pl.loop(0, total // query_block)
        def _(n):
            d = n * upper + (3 - n) * (1 - upper)
            here = rows_at(d * query_block, query_block)
            row_grad[here] = times_transposed(d_projected[here], qkv_ref[...]).astype(jnp.bfloat16)
            scatter.across(d).start()

        scatter.ends()

        @pl.loop(0, 4)
        def _(n):
            columns = cols_at(n * quarter, quarter)
            qkv_grad[rows_at(n * quarter, quarter), :qkv_width] = contract_rows(
                row_ref[:, columns], d_projected[...]
            ).astype(jnp.bfloat16)

        attn.start(0)
        attn.start(1)
        attn.start(2)
        attn.start(3)
        scatter.inner(0)
        plane.relay()
        attn.middle(0)
        attn.start(4)
        scatter.inner(1)
        attn.middle(1)
        attn.start(5)
        attn.last(0)
        attn.middle(2)
        attn.start(6)
        attn.last(1)
        scatter.finish(out_ref)
        d_normed = base_ref[...] + out_ref[...]
        d_hidden, d_scale = norm_back(
            hidden_ref[...].astype(jnp.float32), gains_ref[0:1], d_normed
        )
        out_ref[...] = d_hidden
        held_gains[0, 0:1] = d_scale
        rounds[0].start()
        attn.start(7)
        for i in range(3, 8):
            attn.middle(i)
            attn.last(i - 1)
            gain_round(i - 3)
        attn.last(7)
        gain_ref[...] = held_gains[5]
        for copy in rounds:
            copy.wait_send()
        vec.settle()
        plane.finish()
        mlp.finish()
        attn.finish()

    return comm_call(
        kernel,
        ident,
        [
            jax.ShapeDtypeStruct((rows, width), jnp.float32),
            jax.ShapeDtypeStruct((gain_rows, width), jnp.float32),
            bf16(*mlp_land.shape),
            bf16(shard_height, 8 * sum(attn_widths)),
            bf16(32 * shard_height, vec_width),
        ],
        [VMEM] * 9 + [ANY] * 12,
        [VMEM, VMEM, ANY, ANY, ANY],
        [
            pltpu.VMEM((shard_height, vec_width), jnp.bfloat16),
            pltpu.VMEM((total, width), jnp.bfloat16),
            pltpu.VMEM((total, HEAD), jnp.bfloat16),
            pltpu.VMEM((total, HEAD), jnp.float32),
            pltpu.VMEM((total, HEAD), jnp.float32),
            pltpu.VMEM((total, qkv_width), jnp.bfloat16),
            pltpu.VMEM((width, attn_widths[0]), jnp.bfloat16),
            pltpu.VMEM((width, attn_widths[1]), jnp.bfloat16),
        ]
        + [pltpu.VMEM(array.shape, array.dtype) for array in loads]
        + [
            pltpu.SemaphoreType.DMA((len(loads),)),
            pltpu.VMEM((6, gain_rows, width), jnp.float32),
            pltpu.VMEM((5, gain_rows, width), jnp.float32),
            pltpu.SemaphoreType.DMA((2, 5)),
        ]
        + scatter_scratch
        + mlp_scratch
        + mlp_sems
        + attn_scratch
        + attn_sems
        + ChainGather.SEMS
        + PlaneGather.SEMS
        + ChainGather.SEMS,
        {20: 2},
    )(
        d_attn_low, row_parts, head_gains, hidden, gains, base, other_gains, laurel_partial,
        vec_land, *loads, mlp_land,
    )


def per_device_split(
    hidden_in, layer_vec, positions, w_attn, w_mlp, pl_gate, pl_proj, gains, head_gains, out_grad
):
    shard_height = w_attn.shape[0]
    row_total = QH * positions.shape[0]
    lanes = jnp.arange(128, dtype=jnp.int32)[None, :]
    own_pos = jnp.where(lanes == 0, positions[:, None] // 256, positions[:, None] % 256)

    index = jnp.arange(row_total, dtype=jnp.int32)
    frequency = jnp.exp(
        jnp.arange(HEAD // 2, dtype=jnp.float32) * (-2.0 * math.log(THETA) / HEAD)
    )
    angles = index.astype(jnp.float32)[:, None] * frequency[None, :]
    tables = jnp.concatenate([jnp.cos(angles), jnp.sin(angles)], axis=1)

    hidden = hidden_in.astype(jnp.float32)
    normed_in = rms_norm(hidden, gains[0])
    normed_low = normed_in.astype(jnp.bfloat16)
    (
        row_normed, w_qkv, w_out, w_laurel, row_parts, w_gate_up, w_down, row_ffn, projected,
        queries, keys, values, mixed, latent, laurel_up, attn_out, joined,
    ) = attention_forward(
        normed_low, own_pos.astype(jnp.bfloat16), w_attn, w_mlp, hidden_in, normed_in, gains,
        head_gains, tables, 1,
    )
    latent = latent[:, :RANK]
    gate_up = plain_dot(row_ffn, w_gate_up)
    activated = activate(gate_up).astype(jnp.bfloat16)
    ffn_out = scatter_tokens(times_transposed(activated, w_down).astype(jnp.bfloat16), 4)

    after_ffn = joined + rms_norm(ffn_out, gains[4])
    after_low = after_ffn.astype(jnp.bfloat16)
    vec_gate = plain_dot(after_low, pl_gate)
    vector_in = layer_vec.astype(jnp.float32)
    vec_mixed = vec_mix(vec_gate, vector_in).astype(jnp.bfloat16)
    vec_out = plain_dot(vec_mixed, pl_proj)
    result_out = after_ffn + rms_norm(vec_out, gains[5])
    upstream = out_grad.astype(jnp.float32)
    unused_out, vec_norm_back = jax.vjp(rms_norm, vec_out, gains[5])
    d_vec_out, d_gain_vec = vec_norm_back(upstream)
    d_vec_out_low = d_vec_out.astype(jnp.bfloat16)
    d_vec_mixed = times_transposed(d_vec_out_low, pl_proj)
    turned_pl_proj = contract_rows(d_vec_out_low, vec_mixed)
    unused_out, mix_back = jax.vjp(vec_mix, vec_gate, vector_in)
    d_vec_gate, d_vector_in = mix_back(d_vec_mixed)
    d_vec_gate_low = d_vec_gate.astype(jnp.bfloat16)
    grad_after = upstream + times_transposed(d_vec_gate_low, pl_gate)
    grad_pl_gate = contract_rows(after_low, d_vec_gate_low)
    unused_out, ffn_norm_back = jax.vjp(rms_norm, ffn_out, gains[4])
    d_ffn_out, d_gain_ffn = ffn_norm_back(grad_after)
    d_ffn_low = d_ffn_out.astype(jnp.bfloat16)

    vec_grads = jnp.concatenate([grad_pl_gate, turned_pl_proj], axis=1).astype(jnp.bfloat16)
    row_d_ffn, vec_land = ffn_open_backward(d_ffn_low, vec_grads, shard_height, 5)
    unused_out, act_back = jax.vjp(activate, gate_up)
    d_gate_up = act_back(plain_dot(row_d_ffn, w_down))[0].astype(jnp.bfloat16)
    d_ffn_in, mlp_land, late_wide, late_narrow = ffn_close_backward(
        times_transposed(d_gate_up, w_gate_up).astype(jnp.bfloat16),
        row_ffn,
        d_gate_up,
        row_d_ffn,
        activated,
        shard_height,
        w_mlp.shape[1],
        6,
    )

    unused_out, pre_norm_back = jax.vjp(rms_norm, joined, gains[3])
    d_joined_part, d_gain_pre = pre_norm_back(d_ffn_in)
    d_half = (grad_after + d_joined_part) / math.sqrt(2.0)
    unused_out, laurel_norm_back = jax.vjp(rms_norm, laurel_up, gains[1])
    d_laurel_up, d_gain_laurel = laurel_norm_back(d_half)
    unused_out, attn_norm_back = jax.vjp(rms_norm, attn_out, gains[2])
    d_attn_out, d_gain_attn = attn_norm_back(d_half)
    d_laurel_low = d_laurel_up.astype(jnp.bfloat16)
    d_latent_low = plain_dot(d_laurel_low, w_laurel[:, RANK:]).astype(jnp.bfloat16)
    laurel_partial = jnp.concatenate(
        [contract_rows(normed_low, d_latent_low), contract_rows(d_laurel_low, latent)], axis=1
    ).astype(jnp.bfloat16)
    other_gains = jnp.stack(
        [
            jnp.zeros_like(d_gain_vec), d_gain_laurel, d_gain_attn, d_gain_pre, d_gain_ffn,
            d_gain_vec, jnp.zeros_like(d_gain_vec), jnp.zeros_like(d_gain_vec),
        ]
    )
    d_hidden_part, all_gains, mlp_land, attn_land, vec_all = attention_backward(
        d_attn_out.astype(jnp.bfloat16),
        (w_qkv, w_out),
        (queries, keys, values, mixed, projected, row_normed, row_parts),
        tables,
        head_gains,
        hidden_in,
        gains,
        d_half + times_transposed(d_latent_low, w_laurel[:, :RANK]),
        other_gains,
        laurel_partial,
        (late_wide, late_narrow),
        mlp_land,
        vec_land,
        9,
    )
    grad_hidden = d_half + d_hidden_part
    landed = attn_land.astype(jnp.float32).reshape(shard_height, KVH, QH // KVH, 1152)

    def heads_of(first):
        return landed[..., first : first + HEAD]

    grad_w_attn = jnp.concatenate(
        [
            heads_of(0).reshape(shard_height, QH * HEAD),
            jnp.sum(heads_of(HEAD), axis=2).reshape(shard_height, KVH * HEAD),
            jnp.sum(heads_of(2 * HEAD), axis=2).reshape(shard_height, KVH * HEAD),
            jnp.sum(landed[..., 3 * HEAD : 3 * HEAD + 2 * RANK], axis=(1, 2)),
            heads_of(896).reshape(shard_height, QH * HEAD),
        ],
        axis=1,
    )
    vec_sums = vec_all.astype(jnp.float32)
    grad_gate_all, grad_proj_all = vec_sums[:, : pl_gate.shape[1]], vec_sums[:, pl_gate.shape[1] :].T
    grad_gains, grad_heads = all_gains[:6], all_gains[6, : 2 * HEAD].reshape(2, HEAD)
    return (
        result_out.astype(jnp.bfloat16),
        grad_hidden,
        d_vector_in,
        grad_w_attn,
        mlp_land.astype(jnp.float32),
        grad_gate_all,
        grad_proj_all,
        grad_gains,
        grad_heads,
    )


def solution(mesh):
    fits = mesh.shape["ctx"] == QH and mesh.shape["fsdp"] == 4
    body = per_device_split if fits else per_device
    return jax.shard_map(
        body,
        mesh=mesh,
        in_specs=(
            P(("fsdp", "ctx"), None),
            P(("fsdp", "ctx"), None),
            P(("fsdp", "ctx")),
            P(("fsdp", "ctx"), None),
            P(("fsdp", "ctx"), None),
            P(),
            P(),
            P(),
            P(),
            P(("fsdp", "ctx"), None),
        ),
        out_specs=(
            P(("fsdp", "ctx"), None),
            P(("fsdp", "ctx"), None),
            P(("fsdp", "ctx"), None),
            P(("fsdp", "ctx"), None),
            P(("fsdp", "ctx"), None),
            P(),
            P(),
            P(),
            P(),
        ),
        check_vma=False,
    )
```

```python
import math

import jax
import jax.numpy as jnp
import numpy as np
from jax import lax
from jax.experimental import pallas as pl
from jax.experimental.pallas import tpu as pltpu
from jax.sharding import PartitionSpec as P

QH = 8
KVH = 2
HEAD = 256
RANK = 64
WINDOW = 512


EPSILON = 1e-06
THETA = 10000.0
NEG_LARGE = -1e30


def passed_along(block, axis, distance):
    devices = range(lax.axis_size(axis))
    route = [(i - distance, i) for i in devices if i - distance in devices]
    return lax.ppermute(block, axis, route)


def rms_norm(values, scale_vec):
    return (
        values * lax.rsqrt(jnp.mean(values * values, axis=-1, keepdims=True) + EPSILON) * scale_vec
    )


def value_norm(values):
    return rms_norm(values, 1.0)


def rotary(values, positions):
    half_size = values.shape[-1] // 2
    frequency = jnp.exp(
        jnp.arange(half_size, dtype=jnp.float32) * (-2.0 * math.log(THETA) / values.shape[-1])
    )
    angles = positions.astype(jnp.float32)[:, None] * frequency[None, :]
    cosine = jnp.cos(angles)[:, None, :]
    sine_part = jnp.sin(angles)[:, None, :]
    first_half = values[..., :half_size]
    second_half = values[..., half_size:]
    return jnp.concatenate(
        [
            first_half * cosine - second_half * sine_part,
            second_half * cosine + first_half * sine_part,
        ],
        axis=-1,
    )


def plain_dot(left_side, right_side):
    return jnp.dot(left_side, right_side, preferred_element_type=jnp.float32)


def times_transposed(left_side, right_side):
    return lax.dot_general(
        left_side, right_side, (((1,), (1,)), ((), ())), preferred_element_type=jnp.float32
    )


def contract_rows(left_side, right_side):
    return lax.dot_general(
        left_side, right_side, (((0,), (0,)), ((), ())), preferred_element_type=jnp.float32
    )


def activate(gate_up_val):
    half_cols = gate_up_val.shape[1] // 2
    return jax.nn.gelu(gate_up_val[:, :half_cols], approximate=True) * gate_up_val[:, half_cols:]


def vec_mix(gate_val, vector_val):
    return jax.nn.gelu(gate_val, approximate=True) * vector_val


def per_device(
    hidden_in, layer_vec, positions, w_attn, w_mlp, pl_gate, pl_proj, gains, head_gains, out_grad
):
    row_count = hidden_in.shape[0]
    model_width = hidden_in.shape[1]
    q_width = QH * HEAD
    kv_width = KVH * HEAD
    in_cols = q_width + 2 * kv_width + RANK
    group_size = QH // KVH
    ff_width = w_mlp.shape[1] // 3
    shard_height = w_mlp.shape[0]
    fsdp_count = lax.axis_size("fsdp")
    ctx_count = lax.axis_size("ctx")
    quarter = ff_width // fsdp_count

    def permute_cols(matrix):
        return (
            matrix.reshape(-1, fsdp_count, ctx_count, shard_height)
            .transpose(0, 2, 1, 3)
            .reshape(-1, model_width)
        )

    def restore_cols(matrix):
        return (
            matrix.reshape(-1, ctx_count, fsdp_count, shard_height)
            .transpose(0, 2, 1, 3)
            .reshape(-1, model_width)
        )

    def qk_prep(raw_heads, scale_vec):
        return rotary(rms_norm(raw_heads, scale_vec), positions)

    hidden = hidden_in.astype(jnp.float32)
    normed_in = rms_norm(hidden, gains[0])
    normed_low = normed_in.astype(jnp.bfloat16)
    projected = plain_dot(
        normed_low, lax.all_gather(w_attn[:, :in_cols], ("fsdp", "ctx"), axis=0, tiled=True)
    )
    q_raw = projected[:, :q_width].reshape(row_count, QH, HEAD)
    k_raw = projected[:, q_width : q_width + kv_width].reshape(row_count, KVH, HEAD)
    v_raw = projected[:, q_width + kv_width : q_width + 2 * kv_width].reshape(row_count, KVH, HEAD)
    latent = projected[:, q_width + 2 * kv_width :].astype(jnp.bfloat16)
    queries = qk_prep(q_raw, head_gains[0]).astype(jnp.bfloat16)
    keys_own = qk_prep(k_raw, head_gains[1]).astype(jnp.bfloat16)
    values_own = value_norm(v_raw).astype(jnp.bfloat16)
    kv_own = jnp.concatenate(
        [keys_own.reshape(row_count, kv_width), values_own.reshape(row_count, kv_width)], axis=1
    )
    hop_count = (WINDOW - 1) // row_count + 1
    earlier = []
    moving = kv_own
    for step_back in range(hop_count):
        moving = passed_along(moving, "ctx", 1)
        earlier.append(moving)
    kv_all = jnp.concatenate(earlier[::-1] + [kv_own], axis=0)
    span_rows = kv_all.shape[0]
    keys_all = kv_all[:, :kv_width].reshape(span_rows, KVH, HEAD)
    values_all = kv_all[:, kv_width:].reshape(span_rows, KVH, HEAD)
    grouped = queries.reshape(row_count, KVH, group_size, HEAD)
    distance = (
        jnp.arange(row_count, dtype=jnp.int32)[:, None]
        + hop_count * row_count
        - jnp.arange(span_rows, dtype=jnp.int32)[None, :]
    )
    allowed = (distance >= 0) & (distance <= jnp.minimum(positions, WINDOW - 1)[:, None])
    scores = jnp.einsum("qgrd,kgd->grqk", grouped, keys_all, preferred_element_type=jnp.float32)
    scores = jnp.where(allowed[None, None], scores, NEG_LARGE)
    row_max = jnp.max(scores, axis=-1, keepdims=True)
    exp_scores = jnp.exp(scores - row_max)
    row_sum = jnp.sum(exp_scores, axis=-1, keepdims=True)
    log_total = row_max + jnp.log(row_sum)
    probs_low = (exp_scores / row_sum).astype(jnp.bfloat16)
    mixed = jnp.einsum("grqk,kgd->qgrd", probs_low, values_all, preferred_element_type=jnp.float32)
    mixed = mixed.reshape(row_count, q_width).astype(jnp.bfloat16)
    shard_rows = lax.all_gather(w_attn[:, in_cols:], ("fsdp", "ctx"), axis=0, tiled=True)
    laurel_part = times_transposed(latent, shard_rows[:, :RANK])
    attn_part = times_transposed(mixed, shard_rows[:, RANK:])
    out_pair = jnp.stack([laurel_part, attn_part], axis=1)
    laurel_up = out_pair[:, 0]
    attn_out = out_pair[:, 1]
    laurel_res = normed_in + rms_norm(laurel_up, gains[1])
    after_attn = hidden + rms_norm(attn_out, gains[2])
    joined = (after_attn + laurel_res) / math.sqrt(2.0)
    ffn_low = rms_norm(joined, gains[3]).astype(jnp.bfloat16)
    sent_rows = w_mlp.reshape(shard_height, 3, fsdp_count, quarter)
    sent_tokens = jnp.broadcast_to(
        ffn_low[:, None, None, :], (row_count, 1, fsdp_count, model_width)
    )
    got_rows, got_tokens = (
        lax.all_to_all(sent_rows, "fsdp", split_axis=2, concat_axis=0, tiled=True),
        lax.all_to_all(sent_tokens, "fsdp", split_axis=2, concat_axis=0, tiled=True),
    )
    quarter_rows = lax.all_gather(got_rows, "ctx", axis=0, tiled=True).reshape(
        model_width, 3, quarter
    )
    w_gate_up = quarter_rows[:, :2].reshape(model_width, 2 * quarter)
    w_down = quarter_rows[:, 2]
    ffn_perm = permute_cols(got_tokens.reshape(fsdp_count * row_count, model_width))
    gate_up = plain_dot(ffn_perm, w_gate_up)
    activated = activate(gate_up).astype(jnp.bfloat16)
    ffn_out = lax.psum_scatter(
        restore_cols(times_transposed(activated, w_down)), "fsdp", scatter_dimension=0, tiled=True
    )
    after_ffn = joined + rms_norm(ffn_out, gains[4])
    after_low = after_ffn.astype(jnp.bfloat16)
    vec_gate = plain_dot(after_low, pl_gate)
    vector_in = layer_vec.astype(jnp.float32)
    vec_mixed = vec_mix(vec_gate, vector_in).astype(jnp.bfloat16)
    vec_out = plain_dot(vec_mixed, pl_proj)
    result_out = after_ffn + rms_norm(vec_out, gains[5])
    upstream = out_grad.astype(jnp.float32)
    unused_out, vec_norm_back = jax.vjp(rms_norm, vec_out, gains[5])
    d_vec_out, d_gain_vec = vec_norm_back(upstream)
    d_vec_out_low = d_vec_out.astype(jnp.bfloat16)
    d_vec_mixed = times_transposed(d_vec_out_low, pl_proj)
    grad_pl_proj = contract_rows(vec_mixed, d_vec_out_low)
    unused_out, mix_back = jax.vjp(vec_mix, vec_gate, vector_in)
    d_vec_gate, d_vector_in = mix_back(d_vec_mixed)
    d_vec_gate_low = d_vec_gate.astype(jnp.bfloat16)
    grad_after = upstream + times_transposed(d_vec_gate_low, pl_gate)
    grad_pl_gate = contract_rows(after_low, d_vec_gate_low)
    unused_out, ffn_norm_back = jax.vjp(rms_norm, ffn_out, gains[4])
    d_ffn_out, d_gain_ffn = ffn_norm_back(grad_after)
    d_ffn_low = d_ffn_out.astype(jnp.bfloat16)
    unused_out, act_back = jax.vjp(activate, gate_up)
    d_ffn_all = lax.all_gather(d_ffn_low, "fsdp", axis=0, tiled=True)
    d_ffn_perm = permute_cols(d_ffn_all)
    d_activated = plain_dot(d_ffn_perm, w_down)
    d_gate_up = act_back(d_activated)[0].astype(jnp.bfloat16)
    d_ffn_in = lax.psum_scatter(
        restore_cols(times_transposed(d_gate_up, w_gate_up)).astype(jnp.bfloat16),
        "fsdp",
        scatter_dimension=0,
        tiled=True,
    ).astype(jnp.float32)
    summed = lax.psum_scatter(
        jnp.concatenate(
            [contract_rows(ffn_perm, d_gate_up), contract_rows(d_ffn_perm, activated)], axis=1
        ).astype(jnp.bfloat16),
        "ctx",
        scatter_dimension=0,
        tiled=True,
    ).astype(jnp.float32)
    grad_w_mlp = (
        lax.all_to_all(
            summed.reshape(fsdp_count * shard_height, 3, 1, quarter).astype(jnp.bfloat16),
            "fsdp",
            split_axis=0,
            concat_axis=2,
            tiled=True,
        )
        .astype(jnp.float32)
        .reshape(shard_height, 3 * ff_width)
    )
    unused_out, pre_norm_back = jax.vjp(rms_norm, joined, gains[3])
    d_joined_part, d_gain_pre = pre_norm_back(d_ffn_in)
    d_joined = grad_after + d_joined_part
    d_half = d_joined / math.sqrt(2.0)
    unused_out, laurel_norm_back = jax.vjp(rms_norm, laurel_up, gains[1])
    d_laurel_up, d_gain_laurel = laurel_norm_back(d_half)
    unused_out, attn_norm_back = jax.vjp(rms_norm, attn_out, gains[2])
    d_attn_out, d_gain_attn = attn_norm_back(d_half)
    d_laurel_low = d_laurel_up.astype(jnp.bfloat16)
    d_attn_low = d_attn_out.astype(jnp.bfloat16)
    shard_rows = lax.all_gather(w_attn[:, in_cols:], ("fsdp", "ctx"), axis=0, tiled=True)
    d_latent = plain_dot(d_laurel_low, shard_rows[:, :RANK])
    d_mixed = plain_dot(d_attn_low, shard_rows[:, RANK:])
    d_grouped = d_mixed.astype(jnp.bfloat16).reshape(row_count, KVH, group_size, HEAD)
    again = jnp.einsum("qgrd,kgd->grqk", grouped, keys_all, preferred_element_type=jnp.float32)
    again = jnp.where(allowed[None, None], again, NEG_LARGE)
    probs = jnp.exp(again - log_total)
    d_probs = jnp.einsum(
        "qgrd,kgd->grqk", d_grouped, values_all, preferred_element_type=jnp.float32
    )
    inner_sum = jnp.sum(probs * d_probs, axis=-1, keepdims=True)
    d_scores = (probs * (d_probs - inner_sum)).astype(jnp.bfloat16)
    d_queries = jnp.einsum(
        "grqk,kgd->qgrd", d_scores, keys_all, preferred_element_type=jnp.float32
    ).reshape(row_count, QH, HEAD)
    d_keys_all = jnp.einsum("grqk,qgrd->kgd", d_scores, grouped, preferred_element_type=jnp.float32)
    d_values_all = jnp.einsum(
        "grqk,qgrd->kgd", probs.astype(jnp.bfloat16), d_grouped, preferred_element_type=jnp.float32
    )
    d_kv_all = jnp.concatenate(
        [d_keys_all.reshape(span_rows, kv_width), d_values_all.reshape(span_rows, kv_width)], axis=1
    )
    returned = d_kv_all[:row_count]
    for step_back in range(1, hop_count + 1):
        returned = (
            passed_along(returned.astype(jnp.bfloat16), "ctx", -1).astype(returned.dtype)
            + d_kv_all[step_back * row_count : (step_back + 1) * row_count]
        )
    d_keys_own = returned[:, :kv_width].reshape(row_count, KVH, HEAD)
    d_values_own = returned[:, kv_width:].reshape(row_count, KVH, HEAD)
    unused_out, query_back = jax.vjp(qk_prep, q_raw, head_gains[0])
    d_q_raw, d_head_query = query_back(d_queries)
    unused_out, key_back = jax.vjp(qk_prep, k_raw, head_gains[1])
    d_k_raw, d_head_key = key_back(d_keys_own)
    unused_out, value_back = jax.vjp(value_norm, v_raw)
    d_v_raw = value_back(d_values_own)[0]
    d_projected = jnp.concatenate(
        [
            d_q_raw.reshape(row_count, q_width),
            d_k_raw.reshape(row_count, kv_width),
            d_v_raw.reshape(row_count, kv_width),
            d_latent,
        ],
        axis=1,
    ).astype(jnp.bfloat16)
    d_normed_part = times_transposed(
        d_projected, lax.all_gather(w_attn[:, :in_cols], ("fsdp", "ctx"), axis=0, tiled=True)
    )
    unused_out, input_norm_back = jax.vjp(rms_norm, hidden, gains[0])
    d_hidden_part, d_gain_input = input_norm_back(d_half + d_normed_part)
    grad_hidden = d_half + d_hidden_part
    grad_w_attn = lax.psum_scatter(
        jnp.concatenate(
            [
                contract_rows(normed_low, d_projected),
                contract_rows(d_laurel_low, latent),
                contract_rows(d_attn_low, mixed),
            ],
            axis=1,
        ),
        ("fsdp", "ctx"),
        scatter_dimension=0,
        tiled=True,
    )
    gain_rows = jnp.stack(
        [d_gain_input, d_gain_laurel, d_gain_attn, d_gain_pre, d_gain_ffn, d_gain_vec]
    )
    head_rows = jnp.stack([d_head_query, d_head_key])
    grad_gains, grad_heads, grad_gate_all, grad_proj_all = lax.psum(
        (gain_rows, head_rows, grad_pl_gate, grad_pl_proj), ("fsdp", "ctx")
    )
    return (
        result_out.astype(jnp.bfloat16),
        grad_hidden,
        d_vector_in,
        grad_w_attn,
        grad_w_mlp,
        grad_gate_all,
        grad_proj_all,
        grad_gains,
        grad_heads,
    )

MESH = pl.DeviceIdType.MESH
VMEM_LIMIT = 63 * 1024 * 1024
ORDER = ((0, 0), (0, 1), (1, 0), (1, 1), (2, 0), (2, 1), (3, 0), (3, 1))


class Place:
    def __init__(self):
        self.f = lax.axis_index("fsdp")
        self.c = lax.axis_index("ctx")
        self.z = self.c // 2
        self.k = self.c % 2
        self.x_side = self.f + 1 - 2 * (self.f % 2)
        self.y_side = (self.f + 2) % 4
        self.diag = 3 - self.f
        self.sibling = (self.f, self.c + 1 - 2 * self.k)
        self.up = (self.f, self.c + 2)
        self.down = (self.f, self.c - 2)
        self.has_up = self.z < 3
        self.has_down = self.z > 0

    def partner(self, which):
        z = self.z
        return (z, z + 1 - 2 * (z % 2), (z + 2) % 4, 3 - z)[which]

    def peer(self, i):
        which, other = ORDER[i]
        return self.partner(which) * 2 + (self.k + other) % 2


def rows_at(start, count):
    return pl.ds(pl.multiple_of(start, 16), count)


def cols_at(start, count):
    if isinstance(start, int):
        return pl.ds(start, count)
    return pl.ds(pl.multiple_of(start, 128), count)


def remote(src, dst, send_sem, recv_sem, target):
    return pltpu.make_async_remote_copy(
        src_ref=src,
        dst_ref=dst,
        send_sem=send_sem,
        recv_sem=recv_sem,
        device_id=target,
        device_id_type=MESH,
    )


def greet(place, line, plane):
    barrier = pltpu.get_barrier_semaphore()
    count = 0

    def tell(target):
        pl.semaphore_signal(barrier, inc=1, device_id=target, device_id_type=MESH)

    if line == "all":
        for i in range(1, 8):
            tell((place.f, place.peer(i)))
        count += 7
    elif line == "chain":
        tell(place.sibling)
        for distance in (1, 3):
            tell((place.f, (place.z + distance) % 4 * 2 + place.k))
        count += 3
    if plane:
        tell((place.x_side, place.c))
        tell((place.y_side, place.c))
        count += 2
    pl.semaphore_wait(barrier, count)


class ChainGather:
    SEMS = [pltpu.SemaphoreType.DMA((2, 10)), pltpu.SemaphoreType.DMA((1,))]

    def __init__(self, place, own, out, sems):
        self.place, self.own, self.out = place, own, out
        self.sems, self.local_sem = sems
        self.rows = own.shape[0]

    def block(self, origin_z, core=None):
        core = self.place.k if core is None else core
        return self.out.at[rows_at((origin_z * 2 + core) * self.rows, self.rows)]

    def copy(self, src, dst, index, target):
        return remote(src, dst, self.sems.at[0, index], self.sems.at[1, index], target)

    def local(self):
        return pltpu.make_async_copy(self.own, self.block(self.place.z), self.local_sem.at[0])

    def upward(self, step):
        src = self.own if step == 0 else self.block(self.place.z - step)
        return self.copy(src, self.block(self.place.z - step), step, self.place.up)

    def downward(self, step):
        src = self.own if step == 0 else self.block(self.place.z + step)
        return self.copy(src, self.block(self.place.z + step), 3 + step, self.place.down)

    def across(self, origin_z, own=False):
        src = self.own if own else self.block(origin_z)
        return self.copy(src, self.block(origin_z), 6 + origin_z, self.place.sibling)

    def start(self):
        place = self.place

        @pl.when(place.has_up)
        def _():
            self.upward(0).start()

        @pl.when(place.has_down)
        def _():
            self.downward(0).start()

        self.across(place.z, True).start()
        self.local().start()

    def step(self, step):
        place = self.place

        @pl.when(place.z - step >= 0)
        def _():
            self.copy(self.own, self.block(place.z - step), step - 1, place.up).wait_recv()
            if step < 3:

                @pl.when(place.has_up)
                def _():
                    self.upward(step).start()

            self.across(place.z - step).start()

        @pl.when(place.z + step <= 3)
        def _():
            self.copy(self.own, self.block(place.z + step), 3 + step - 1, place.down).wait_recv()
            if step < 3:

                @pl.when(place.has_down)
                def _():
                    self.downward(step).start()

            self.across(place.z + step).start()

    def finish(self):
        self.arrive()
        self.settle()

    def from_sibling(self, origin):
        return self.copy(
            self.own, self.block(origin, 1 - self.place.k), 6 + origin, self.place.sibling
        )

    def arrive(self):
        self.local().wait()
        for origin in range(4):
            self.from_sibling(origin).wait_recv()

    def settle(self):
        place = self.place
        for origin in range(4):
            self.from_sibling(origin).wait_send()
        for step in range(3):

            @pl.when((place.z - step >= 0) & place.has_up)
            def _(step=step):
                self.upward(step).wait_send()

            @pl.when((place.z + step <= 3) & place.has_down)
            def _(step=step):
                self.downward(step).wait_send()


class ChainScatter:
    @staticmethod
    def scratch(rows, cols):
        return [
            pltpu.VMEM((4, rows, cols), jnp.bfloat16),
            pltpu.VMEM((6, rows, cols), jnp.bfloat16),
            pltpu.SemaphoreType.DMA((2, 10)),
        ]

    def __init__(self, place, partial, scratch):
        self.place, self.partial = place, partial
        self.from_sibling, self.moving, self.sems = scratch
        self.rows = partial.shape[0] // 8

    def block(self, origin_z, core):
        return self.partial.at[rows_at((origin_z * 2 + core) * self.rows, self.rows)]

    def across(self, dest):
        return remote(
            self.block(dest, 1 - self.place.k),
            self.from_sibling.at[dest],
            self.sems.at[0, 6 + dest],
            self.sems.at[1, 6 + dest],
            self.place.sibling,
        )

    def moved(self, slot, target):
        return remote(
            self.moving.at[slot],
            self.moving.at[slot],
            self.sems.at[0, slot],
            self.sems.at[1, slot],
            target,
        )

    def start(self):
        for dest in (3, 0, 2, 1):
            self.across(dest).start()

    def pair_sum(self, dest):
        return self.block(dest, self.place.k)[...].astype(jnp.float32) + self.from_sibling[
            dest
        ].astype(jnp.float32)

    def pass_on(self, dest, upward, inner=False):
        place = self.place
        slot = dest - 1 if upward else 3 + dest
        target = place.up if upward else place.down
        self.across(dest).wait_recv()
        total = self.pair_sum(dest)
        if inner:
            self.moved(slot, target).wait_recv()
            total = total + self.moving[slot].astype(jnp.float32)
        self.moving[slot] = total.astype(jnp.bfloat16)
        self.moved(slot, target).start()

    def ends_after(self, n):
        z = self.place.z

        @pl.when((n > 0) & (z == 0))
        def _():
            self.pass_on(4 - n, True)

        @pl.when((n > 0) & (z == 3))
        def _():
            self.pass_on(n - 1, False)

    def ends(self):
        z = self.place.z

        @pl.when(z == 0)
        def _():
            for dest in (3, 2, 1):
                self.pass_on(dest, True)

        @pl.when(z == 3)
        def _():
            for dest in (0, 1, 2):
                self.pass_on(dest, False)

    def inner(self, i):
        z = self.place.z

        @pl.when(z == 1)
        def _():
            if i == 0:
                self.pass_on(3, True, True)
            else:
                self.pass_on(0, False, True)
                self.pass_on(2, True, True)

        @pl.when(z == 2)
        def _():
            if i == 0:
                self.pass_on(0, False, True)
            else:
                self.pass_on(3, True, True)
                self.pass_on(1, False, True)

    def finish(self, out):
        place = self.place
        for dest in range(4):

            @pl.when(place.z == dest)
            def _(dest=dest):
                self.across(dest).wait_recv()
                total = self.pair_sum(dest)
                if dest > 0:
                    self.moved(dest - 1, place.up).wait_recv()
                    total = total + self.moving[dest - 1].astype(jnp.float32)
                if dest < 3:
                    self.moved(3 + dest, place.down).wait_recv()
                    total = total + self.moving[3 + dest].astype(jnp.float32)
                out[...] = total

        for dest in range(4):
            self.across(dest).wait_send()
        for i in range(3):
            top, bottom = 3 - i, i

            @pl.when(place.z < top)
            def _(top=top):
                self.moved(top - 1, place.up).wait_send()

            @pl.when(place.z > bottom)
            def _(bottom=bottom):
                self.moved(3 + bottom, place.down).wait_send()


class Spread:
    @staticmethod
    def sems(pieces, outs):
        return [
            pltpu.SemaphoreType.DMA((2, 8, pieces)),
            pltpu.SemaphoreType.DMA((2, 4, 8, outs)),
        ]

    def __init__(self, place, weight, outs, pieces, sems):
        self.place, self.weight, self.outs, self.pieces = place, weight, outs, pieces
        self.swap_sems, self.plane_sems = sems
        self.rows = weight.shape[0]

    def spot(self, f, c):
        return (f * 8 + c) * self.rows

    def swap(self, i, p, origin):
        column, width, out, out_column = self.pieces[p]
        peer = self.place.peer(i)
        src = self.weight.at[:, cols_at(column(peer), width)]
        dst = self.outs[out].at[
            rows_at(self.spot(self.place.f, origin), self.rows), pl.ds(out_column, width)
        ]
        if i == 0:
            return pltpu.make_async_copy(src, dst, self.swap_sems.at[0, 0, p])
        return remote(
            src,
            dst,
            self.swap_sems.at[0, i, p],
            self.swap_sems.at[1, i, p],
            (self.place.f, peer),
        )

    def whole(self, f, c, out):
        return self.outs[out].at[rows_at(self.spot(f, c), self.rows)]

    def part(self, f, c, out, half):
        count = self.rows // 2
        return self.outs[out].at[rows_at(self.spot(f, c) + half * count, count)]

    def plane(self, kind, i, out, ref, target):
        return remote(
            ref,
            ref,
            self.plane_sems.at[0, kind, i, out],
            self.plane_sems.at[1, kind, i, out],
            (target, self.place.c),
        )

    def start(self, first=0, last=8):
        for i in range(first, last):
            for p in range(len(self.pieces)):
                self.swap(i, p, self.place.c).start()

    def forward(self, i):
        place = self.place
        origin = place.peer(i)
        for p in range(len(self.pieces)):
            copy = self.swap(i, p, origin)
            if i == 0:
                copy.wait()
            else:
                copy.wait_recv()
        for out in range(len(self.outs)):
            ref = self.whole(place.f, origin, out)
            self.plane(0, i, out, ref, place.x_side).start()
            self.plane(1, i, out, ref, place.y_side).start()

    def relay(self, i):
        place = self.place
        origin = place.peer(i)
        for out in range(len(self.outs)):
            self.plane(0, i, out, self.whole(place.x_side, origin, out), place.x_side).wait_recv()
            self.plane(2, i, out, self.part(place.x_side, origin, out, 0), place.y_side).start()
            self.plane(1, i, out, self.whole(place.y_side, origin, out), place.y_side).wait_recv()
            self.plane(3, i, out, self.part(place.y_side, origin, out, 1), place.x_side).start()

    def finish(self, first=0, last=8):
        self.arrive(first, last)
        self.settle(first, last)

    def arrive(self, first=0, last=8):
        place = self.place
        for i in range(first, last):
            origin = place.peer(i)
            for out in range(len(self.outs)):
                self.plane(
                    2, i, out, self.part(place.diag, origin, out, 0), place.y_side
                ).wait_recv()
                self.plane(
                    3, i, out, self.part(place.diag, origin, out, 1), place.x_side
                ).wait_recv()

    def settle(self, first=0, last=8):
        place = self.place
        for i in range(first, last):
            origin = place.peer(i)
            if i:
                for p in range(len(self.pieces)):
                    self.swap(i, p, place.c).wait_send()
            for out in range(len(self.outs)):
                own = self.whole(place.f, origin, out)
                self.plane(0, i, out, own, place.x_side).wait_send()
                self.plane(1, i, out, own, place.y_side).wait_send()
                half = self.part(place.f, origin, out, 0)
                self.plane(2, i, out, half, place.y_side).wait_send()
                self.plane(3, i, out, half, place.x_side).wait_send()


class PlaneGather:
    SEMS = [pltpu.SemaphoreType.DMA((2, 4))]

    def __init__(self, place, out, sems):
        self.place, self.out = place, out
        self.sems = sems[0]
        self.rows = out.shape[0] // 4

    def copy(self, kind, f, target):
        count = self.rows // 2 if kind > 1 else self.rows
        start = f * self.rows + (count if kind == 3 else 0)
        ref = self.out.at[rows_at(start, count)]
        return remote(
            ref, ref, self.sems.at[0, kind], self.sems.at[1, kind], (target, self.place.c)
        )

    def start(self):
        place = self.place
        self.copy(0, place.f, place.x_side).start()
        self.copy(1, place.f, place.y_side).start()

    def relay(self):
        place = self.place
        self.copy(0, place.x_side, place.x_side).wait_recv()
        self.copy(2, place.x_side, place.y_side).start()
        self.copy(1, place.y_side, place.y_side).wait_recv()
        self.copy(3, place.y_side, place.x_side).start()

    def finish(self):
        place = self.place
        self.copy(2, place.diag, place.y_side).wait_recv()
        self.copy(3, place.diag, place.x_side).wait_recv()
        self.copy(0, place.f, place.x_side).wait_send()
        self.copy(1, place.f, place.y_side).wait_send()
        self.copy(2, place.x_side, place.y_side).wait_send()
        self.copy(3, place.y_side, place.x_side).wait_send()


class Drain:
    @staticmethod
    def scratch(rows, widths, peers=8):
        half = rows // 2
        lists = []
        for width in widths:
            lists += [
                pltpu.VMEM((2, peers, 2, half, width), jnp.bfloat16),
                pltpu.VMEM((2, peers, half, width), jnp.bfloat16),
            ]
        return lists

    @staticmethod
    def sems(pieces, outs, peers=8):
        return [
            pltpu.SemaphoreType.DMA((2, 2, peers, 2, outs)),
            pltpu.SemaphoreType.DMA((2, 2, peers, outs)),
            pltpu.SemaphoreType.DMA((2, peers, pieces, 2)),
        ]

    def __init__(self, place, grads, land, pieces, scratch, sems, base=0, peers=8, adds=None):
        self.place, self.grads, self.land, self.pieces = place, grads, land, pieces
        self.adds = adds or grads
        self.first = scratch[0::2]
        self.second = scratch[1::2]
        self.first_sems, self.second_sems, self.swap_sems = sems
        self.rows = land.shape[0]
        self.half = self.rows // 2
        self.units = grads[0].shape[0] < 32 * self.rows or peers < 8
        self.base, self.peers = base, peers

    def part(self, g, f, i, half, adds=False):
        refs = self.adds if adds else self.grads
        peer = self.place.peer(self.base + i)
        if self.units:
            start = (i // 2 * 8 + f * 2 + peer % 2) * self.rows + half * self.half
            return refs[g].at[rows_at(start, self.half)]
        return refs[g].at[rows_at((f * 8 + peer) * self.rows + half * self.half, self.half)]

    def sides(self, axis):
        place = self.place
        return (place.x_side, place.y_side) if axis == 0 else (place.y_side, place.x_side)

    def first_copy(self, axis, i, which, g):
        near, _ = self.sides(axis)
        f = near if which == 0 else self.place.diag
        return remote(
            self.part(g, f, i, axis),
            self.first[g].at[axis, i, which],
            self.first_sems.at[0, axis, i, which, g],
            self.first_sems.at[1, axis, i, which, g],
            (near, self.place.c),
        )

    def second_copy(self, axis, i, g):
        _, far = self.sides(axis)
        return remote(
            self.first[g].at[axis, i, 1],
            self.second[g].at[axis, i],
            self.second_sems.at[0, axis, i, g],
            self.second_sems.at[1, axis, i, g],
            (far, self.place.c),
        )

    def swap(self, i, p, half, origin):
        column, width, g, g_column = self.pieces[p]
        src = self.first[g].at[half, i, 0, :, pl.ds(g_column, width)]
        dst = self.land.at[pl.ds(half * self.half, self.half), cols_at(column(origin), width)]
        if self.base + i == 0:
            return pltpu.make_async_copy(src, dst, self.swap_sems.at[0, i, p, half])
        return remote(
            src,
            dst,
            self.swap_sems.at[0, i, p, half],
            self.swap_sems.at[1, i, p, half],
            (self.place.f, self.place.peer(self.base + i)),
        )

    def start(self, i):
        for g in range(len(self.grads)):
            for which in (1, 0):
                for axis in range(2):
                    self.first_copy(axis, i, which, g).start()

    def middle(self, i):
        place = self.place
        for g in range(len(self.grads)):
            for axis in range(2):
                _, far = self.sides(axis)
                self.first_copy(axis, i, 1, g).wait_recv()
                mine = self.part(g, far, i, axis, True)
                self.first[g][axis, i, 1] = (
                    mine[...].astype(jnp.float32) + self.first[g][axis, i, 1].astype(jnp.float32)
                ).astype(jnp.bfloat16)
                self.second_copy(axis, i, g).start()

    def last(self, i):
        place = self.place
        for g in range(len(self.grads)):
            for axis in range(2):
                self.first_copy(axis, i, 0, g).wait_recv()
                self.second_copy(axis, i, g).wait_recv()
                mine = self.part(g, place.f, i, axis, True)
                self.first[g][axis, i, 0] = (
                    mine[...].astype(jnp.float32)
                    + self.first[g][axis, i, 0].astype(jnp.float32)
                    + self.second[g][axis, i].astype(jnp.float32)
                ).astype(jnp.bfloat16)
        for p in range(len(self.pieces)):
            for half in range(2):
                self.swap(i, p, half, place.c).start()

    def finish(self):
        place = self.place
        for i in range(self.peers):
            for p in range(len(self.pieces)):
                for half in range(2):
                    copy = self.swap(i, p, half, place.peer(self.base + i))
                    if self.base + i == 0:
                        copy.wait()
                    else:
                        copy.wait_recv()
                        copy.wait_send()
            for g in range(len(self.grads)):
                for axis in range(2):
                    for which in range(2):
                        self.first_copy(axis, i, which, g).wait_send()
                    self.second_copy(axis, i, g).wait_send()


ANY = pl.BlockSpec(memory_space=pl.ANY)
VMEM = pl.BlockSpec(memory_space=pltpu.VMEM)


def comm_call(kernel, ident, out_shape, in_specs, out_specs, scratch, aliases=None):
    return pl.pallas_call(
        kernel,
        input_output_aliases=aliases or {},
        out_shape=out_shape,
        in_specs=in_specs,
        out_specs=out_specs,
        scratch_shapes=scratch,
        compiler_params=pltpu.CompilerParams(
            collective_id=ident, has_side_effects=True, vmem_limit_bytes=VMEM_LIMIT
        ),
    )


class Local:
    def __init__(self, sems):
        self.sems, self.copies = sems, []

    def start(self, src, dst):
        self.copies.append(pltpu.make_async_copy(src, dst, self.sems.at[len(self.copies)]))
        self.copies[-1].start()
        return len(self.copies) - 1

    def wait(self, *indices):
        for index in indices:
            self.copies[index].wait()


def bf16(*shape):
    return jax.ShapeDtypeStruct(shape, jnp.bfloat16)


ATTN_PIECES = (
    (lambda c: 256 * c, 256, 0, 0),
    (lambda c: 2048 + 256 * (c // 4), 256, 0, 256),
    (lambda c: 2560 + 256 * (c // 4), 256, 0, 512),
    (lambda c: 3200 + 256 * c, 256, 1, 0),
    (lambda c: 3072, 128, 2, 0),
)
ATTN_LAND = (
    (lambda c: 1152 * c, 896, 0, 0),
    (lambda c: 1152 * c + 896, 256, 1, 0),
)
MLP_PIECES = (
    (lambda c: 1024 * c, 1024, 0, 0),
    (lambda c: 8192 + 1024 * c, 1024, 0, 1024),
    (lambda c: 16384 + 1024 * c, 1024, 1, 0),
)
VEC_LAND = ((lambda c: 512 * c, 512, 0, 0),)


def turn(values, cosine, sine):
    half = HEAD // 2
    first, second = values[:, :half], values[:, half:]
    return jnp.concatenate(
        [first * cosine - second * sine, second * cosine + first * sine], axis=1
    )


def allowed_pairs(first_query, first_key, positions):
    shape = (positions.shape[0], 768)
    distance = (
        lax.broadcasted_iota(jnp.int32, shape, 0)
        - lax.broadcasted_iota(jnp.int32, shape, 1)
        + (first_query - first_key)
    )
    return (distance >= 0) & (distance <= jnp.minimum(positions, WINDOW - 1))


def positions_of(parts):
    return (parts[:, 0:1].astype(jnp.float32) * 256.0 + parts[:, 1:2].astype(jnp.float32)).astype(
        jnp.int32
    )


def attention_forward(own_pos, w_attn, w_mlp, hidden, gains, head_gains, tables, ident):
    height = 32 * w_attn.shape[0]
    rows, width = hidden.shape
    total = 8 * rows
    query_block, key_span = 2 * rows, 768
    scatter_scratch = ChainScatter.scratch(rows, width)

    def kernel(*refs):
        ins, outs, held = split_refs(refs, 7, 17, len(refs) - 24)
        pos_ref, attn_ref, mlp_ref, hidden_ref, gains_ref, head_ref, tables_ref = ins
        (row_ref, qkv_ref, out_ref, laurel_ref, row_pos, gate_up_ref, down_ref, row_ffn,
         projected, q_low, k_low, v_low, mixed, latent_ref, laurel_up, attn_out, joined) = outs
        scratch, scat, attn_m, mlp_m, gather_m = split_refs(held, 4, len(scatter_scratch), 2, 2, 6)
        own_ffn, partial, own_ref, normed_ref = scratch
        place = Place()
        normed_ref[...] = rms_norm(hidden_ref[...].astype(jnp.float32), gains_ref[0:1])
        own_ref[...] = normed_ref[...].astype(jnp.bfloat16)
        greet(place, "all", True)
        attn = Spread(place, attn_ref, [qkv_ref, out_ref, laurel_ref], ATTN_PIECES, attn_m)
        mlp = Spread(place, mlp_ref, [gate_up_ref, down_ref], MLP_PIECES, mlp_m)
        gathers = [
            ChainGather(place, own_ref, row_ref, gather_m[0:2]),
            ChainGather(place, pos_ref, row_pos, gather_m[2:4]),
        ]
        last = ChainGather(place, own_ffn, row_ffn, gather_m[4:6])
        scatter = ChainScatter(place, partial, scat)

        def step(n):
            for gather in gathers:
                gather.step(n)

        for gather in gathers:
            gather.start()
        attn.start(0, 2)
        attn.start(4, 6)
        attn.start(2, 4)
        attn.start(6, 8)
        mlp.start(0, 2)
        attn.forward(0)
        attn.forward(1)
        mlp.forward(0)
        step(1)
        attn.forward(2)
        attn.forward(3)
        attn.relay(0)
        attn.relay(1)
        step(2)
        attn.forward(4)
        attn.forward(5)
        attn.relay(2)
        attn.relay(3)
        mlp.forward(1)
        step(3)
        attn.forward(6)
        attn.forward(7)
        mlp.start(4, 6)
        mlp.start(2, 4)
        attn.relay(4)
        attn.relay(5)
        mlp.relay(0)
        attn.relay(6)
        attn.relay(7)
        for gather in gathers:
            gather.arrive()
        attn.arrive()
        mlp.relay(1)
        mlp.start(6, 8)

        @pl.loop(0, total // query_block)
        def _(n):
            here = rows_at(n * query_block, query_block)
            block = plain_dot(row_ref[here], qkv_ref[...])
            projected[here] = block
            cosine, sine = tables_ref[here, : HEAD // 2], tables_ref[here, HEAD // 2 :]
            q_low[here] = turn(
                rms_norm(block[:, :HEAD], head_ref[0:1]), cosine, sine
            ).astype(jnp.bfloat16)
            k_low[here] = turn(
                rms_norm(block[:, HEAD : 2 * HEAD], head_ref[1:2]), cosine, sine
            ).astype(jnp.bfloat16)
            v_low[here] = value_norm(block[:, 2 * HEAD :]).astype(jnp.bfloat16)

        upper = place.z // 2

        @pl.loop(0, total // query_block)
        def _(n):
            d = n * upper + (3 - n) * (1 - upper)
            here = rows_at(d * query_block, query_block)
            first_key = (d // 2) * (d - 2) * query_block
            there = rows_at(first_key, key_span)
            scores = jnp.where(
                allowed_pairs(d * query_block, first_key, positions_of(row_pos[here])),
                times_transposed(q_low[here], k_low[there]),
                NEG_LARGE,
            )
            weights = jnp.exp(scores - jnp.max(scores, axis=-1, keepdims=True))
            probs = (weights / jnp.sum(weights, axis=-1, keepdims=True)).astype(jnp.bfloat16)
            block = plain_dot(probs, v_low[there]).astype(jnp.bfloat16)
            mixed[here] = block
            partial[here] = times_transposed(block, out_ref[...]).astype(jnp.bfloat16)
            scatter.across(d).start()

        scatter.ends()
        mlp.forward(2)
        mlp.forward(3)
        scatter.inner(0)
        low = plain_dot(own_ref[...], laurel_ref[...])
        latent_ref[...] = low.astype(jnp.bfloat16)
        lanes = lax.broadcasted_iota(jnp.int32, low.shape, 1)
        shifted = jnp.where(lanes >= RANK, pltpu.roll(low, RANK, 1), 0.0).astype(jnp.bfloat16)
        laurel_up[...] = times_transposed(shifted, laurel_ref[...])
        scatter.inner(1)
        mlp.relay(2)
        mlp.relay(3)
        mlp.forward(4)
        mlp.forward(5)
        scatter.finish(attn_out)
        laurel_res = normed_ref[...] + rms_norm(laurel_up[...], gains_ref[1:2])
        after_attn = hidden_ref[...].astype(jnp.float32) + rms_norm(attn_out[...], gains_ref[2:3])
        joined[...] = (after_attn + laurel_res) / math.sqrt(2.0)
        own_ffn[...] = rms_norm(joined[...], gains_ref[3:4]).astype(jnp.bfloat16)
        last.start()
        mlp.relay(4)
        mlp.relay(5)
        last.step(1)
        mlp.forward(6)
        mlp.forward(7)
        last.step(2)
        mlp.relay(6)
        mlp.relay(7)
        last.step(3)
        mlp.arrive()
        last.arrive()
        attn.settle()
        mlp.settle()
        for gather in gathers:
            gather.settle()
        last.settle()

    def f32(*shape):
        return jax.ShapeDtypeStruct(shape, jnp.float32)

    token_f32 = f32(rows, width)
    head = bf16(total, HEAD)
    outs = [bf16(total, width), bf16(height, 768), bf16(height, 256), bf16(height, 128)]
    outs += [bf16(total, 128), bf16(height, 2048), bf16(height, 1024), bf16(total, width)]
    outs += [f32(total, 768), head, head, head, head, bf16(rows, 128)]
    outs += [token_f32, token_f32, token_f32]
    return comm_call(
        kernel,
        ident,
        outs,
        [VMEM, ANY, ANY] + [VMEM] * 4,
        [VMEM] * 5 + [ANY] * 3 + [VMEM] * 9,
        [
            pltpu.VMEM((rows, width), jnp.bfloat16),
            pltpu.VMEM((total, width), jnp.bfloat16),
            pltpu.VMEM((rows, width), jnp.bfloat16),
            pltpu.VMEM((rows, width), jnp.float32),
        ]
        + scatter_scratch
        + Spread.sems(len(ATTN_PIECES), 3)
        + Spread.sems(len(MLP_PIECES), 2)
        + ChainGather.SEMS * 3,
    )(own_pos, w_attn, w_mlp, hidden, gains, head_gains, tables)


def split_refs(refs, *counts):
    refs, parts = list(refs), []
    for count in counts:
        parts.append(refs[:count])
        refs = refs[count:]
    return parts


def turn_back(grads, cosine, sine):
    half = HEAD // 2
    first, second = grads[:, :half], grads[:, half:]
    return jnp.concatenate(
        [first * cosine + second * sine, second * cosine - first * sine], axis=1
    )


def norm_back(values, scale_vec, grads):
    inverse = lax.rsqrt(jnp.mean(values * values, axis=-1, keepdims=True) + EPSILON)
    unit = values * inverse
    scaled = grads * scale_vec
    back = (scaled - unit * jnp.mean(unit * scaled, axis=-1, keepdims=True)) * inverse
    return back, jnp.sum(grads * unit, axis=0, keepdims=True)


def unit_gradient(place, n, tokens_ref, grad_ref, out, turned_ref):
    zz = place.partner(n)
    unit_rows = turned_ref.shape[0]
    count = unit_rows // 4
    for f in range(4):
        columns = cols_at((f * 4 + zz) * count, count)
        turned_ref[f * count : (f + 1) * count] = tokens_ref[:, columns].T
    step = 512

    @pl.loop(0, grad_ref.shape[1] // step)
    def _(t):
        columns = cols_at(t * step, step)
        out[n * unit_rows : (n + 1) * unit_rows, columns] = plain_dot(
            turned_ref[...], grad_ref[:, columns]
        ).astype(jnp.bfloat16)


def gelu_pair(values):
    scale = math.sqrt(2.0 / math.pi)
    squares = values * values
    bend = jnp.tanh(scale * values * (1.0 + 0.044715 * squares))
    half = 0.5 * (1.0 + bend)
    slope = half + 0.5 * values * (1.0 - bend * bend) * scale * (1.0 + 3.0 * 0.044715 * squares)
    return values * half, slope


def ffn_layer(
    row_ffn, w_gate_up, w_down, joined, attn_out, laurel_up, gains, layer_vec, pl_gate, pl_proj,
    out_grad, shard_height, mlp_cols, ident
):
    rows, width = joined.shape
    total, hidden_units = 8 * rows, w_down.shape[1]
    block, chunk = 2 * rows, 256
    vec_width = 2 * pl_gate.shape[1]
    unit_rows = 8 * shard_height
    scatter_scratch = ChainScatter.scratch(rows, width)
    mlp_scratch = Drain.scratch(shard_height, (2 * hidden_units, hidden_units), 4)
    mlp_sems = Drain.sems(len(MLP_PIECES), 2, 4)
    vec_scratch = Drain.scratch(shard_height, (vec_width,))
    vec_sems = Drain.sems(1, 1)
    chunks = hidden_units // chunk

    def kernel(*refs):
        ins, outs, held = split_refs(refs, 11, 10, len(refs) - 21)
        ffn_hbm, gate_up_hbm, down_hbm = ins[:3]
        (joined_ref, attn_ref, laurel_ref, gains_ref, vector_ref, pl_gate_ref, pl_proj_ref,
         out_grad_ref) = ins[3:]
        (result_ref, d_vector_ref, d_half_ref, d_attn_ref, d_laurel_ref, gain_ref, mlp_land,
         vec_land, late_wide, late_narrow) = outs
        scratch, scat, mlp_s, mlp_m, vec_s, vec_m, gather_m, last = split_refs(
            held, 12, len(scatter_scratch), len(mlp_scratch), 3, len(vec_scratch), 3, 2, 1
        )
        (ffn_ref, gate_up_ref, down_ref, slopes, active, row_grad, partial, turned, vec_grad,
         own_grad, ffn_out, grad_after) = scratch
        place = Place()
        local = Local(last[0])
        local.start(ffn_hbm, ffn_ref)
        for t in range(chunks):
            for first in (0, hidden_units):
                columns = pl.ds(first + t * chunk, chunk)
                local.start(gate_up_hbm.at[:, columns], gate_up_ref.at[:, columns])
        down_copy = local.start(down_hbm, down_ref)
        greet(place, "all", True)
        scatter = ChainScatter(place, partial, scat)
        gather = ChainGather(place, own_grad, row_grad, gather_m)
        mlp = Drain(place, [gate_up_ref, down_ref], mlp_land, MLP_PIECES, mlp_s, mlp_m, 0, 4)
        vec = Drain(place, [vec_grad], vec_land, VEC_LAND, vec_s, vec_m)
        upper = place.z // 2

        local.wait(0)
        for t in range(chunks):
            local.wait(1 + 2 * t, 2 + 2 * t)
            gates = pl.ds(t * chunk, chunk)
            ups = pl.ds(hidden_units + t * chunk, chunk)

            @pl.loop(0, total // (2 * block))
            def _(n, gates=gates, ups=ups):
                here = rows_at(n * 2 * block, 2 * block)
                gate = plain_dot(ffn_ref[here], gate_up_ref[:, gates])
                up = plain_dot(ffn_ref[here], gate_up_ref[:, ups])
                value, slope = gelu_pair(gate)
                active[here, gates] = (value * up).astype(jnp.bfloat16)
                slopes[here, gates] = (slope * up).astype(jnp.bfloat16)
                slopes[here, ups] = value.astype(jnp.bfloat16)

        local.wait(down_copy)

        @pl.loop(0, total // block)
        def _(n):
            d = n * upper + (3 - n) * (1 - upper)
            here = rows_at(d * block, block)
            partial[here] = times_transposed(active[here], down_ref[...]).astype(jnp.bfloat16)
            scatter.across(d).start()
            scatter.ends_after(n)

        scatter.inner(0)
        scatter.inner(1)
        scatter.finish(ffn_out)

        after = joined_ref[...] + rms_norm(ffn_out[...], gains_ref[4:5])
        after_low = after.astype(jnp.bfloat16)
        vec_gate = plain_dot(after_low, pl_gate_ref[...])
        vector = vector_ref[...].astype(jnp.float32)
        value, slope = gelu_pair(vec_gate)
        vec_mixed = (value * vector).astype(jnp.bfloat16)
        vec_out = plain_dot(vec_mixed, pl_proj_ref[...])
        result_ref[...] = (after + rms_norm(vec_out, gains_ref[5:6])).astype(jnp.bfloat16)
        upstream = out_grad_ref[...].astype(jnp.float32)
        d_vec_out, d_scale = norm_back(vec_out, gains_ref[5:6], upstream)
        gain_ref[...] = jnp.zeros_like(gain_ref)
        gain_ref[5:6] = d_scale
        d_vec_out_low = d_vec_out.astype(jnp.bfloat16)
        d_vec_mixed = times_transposed(d_vec_out_low, pl_proj_ref[...])
        d_vector_ref[...] = d_vec_mixed * value
        d_vec_gate_low = (d_vec_mixed * vector * slope).astype(jnp.bfloat16)
        grad_after[...] = upstream + times_transposed(d_vec_gate_low, pl_gate_ref[...])
        d_ffn_out, d_scale = norm_back(ffn_out[...], gains_ref[4:5], grad_after[...])
        gain_ref[4:5] = d_scale
        own_grad[...] = d_ffn_out.astype(jnp.bfloat16)
        gather.start()
        half = vec_width // 2
        vec_grad[:, :half] = contract_rows(after_low, d_vec_gate_low).astype(jnp.bfloat16)
        vec_grad[:, half:] = contract_rows(d_vec_out_low, vec_mixed).astype(jnp.bfloat16)
        for i in range(8):
            vec.start(i)
        gather.step(1)
        for i in range(4):
            vec.middle(i)
        gather.step(2)
        for i in range(4, 8):
            vec.middle(i)
        for i in range(8):
            vec.last(i)
        gather.step(3)
        gather.arrive()

        @pl.loop(0, total // block)
        def _(n):
            d = n * upper + (3 - n) * (1 - upper)
            here = rows_at(d * block, block)
            for t in range(2):
                gates = pl.ds(t * (hidden_units // 2), hidden_units // 2)
                ups = pl.ds(hidden_units + t * (hidden_units // 2), hidden_units // 2)
                d_active = plain_dot(row_grad[here], down_ref[:, gates])
                slopes[here, gates] = (d_active * slopes[here, gates].astype(jnp.float32)).astype(
                    jnp.bfloat16
                )
                slopes[here, ups] = (d_active * slopes[here, ups].astype(jnp.float32)).astype(
                    jnp.bfloat16
                )
            partial[here] = times_transposed(slopes[here], gate_up_ref[...]).astype(jnp.bfloat16)
            scatter.across(d).start()
            scatter.ends_after(n)

        def unit(n):
            unit_gradient(place, n, ffn_ref, slopes, gate_up_ref, turned)
            unit_gradient(place, n, row_grad, active, down_ref, turned)

        unit(1)
        mlp.start(2)
        mlp.start(3)
        scatter.inner(0)
        unit(0)
        mlp.middle(2)
        mlp.start(0)
        mlp.middle(3)
        mlp.start(1)
        scatter.inner(1)
        unit(2)
        mlp.last(2)
        mlp.last(3)
        unit(3)
        kept = [
            local.start(ref.at[pl.ds(2 * unit_rows, 2 * unit_rows)], out)
            for ref, out in ((gate_up_ref, late_wide), (down_ref, late_narrow))
        ]
        mlp.middle(0)
        mlp.middle(1)
        scatter.finish(ffn_out)
        d_joined, d_scale = norm_back(joined_ref[...], gains_ref[3:4], ffn_out[...])
        gain_ref[3:4] = d_scale
        d_half = (grad_after[...] + d_joined) / math.sqrt(2.0)
        d_half_ref[...] = d_half
        d_attn, d_scale = norm_back(attn_ref[...], gains_ref[2:3], d_half)
        gain_ref[2:3] = d_scale
        d_attn_ref[...] = d_attn.astype(jnp.bfloat16)
        d_laurel, d_scale = norm_back(laurel_ref[...], gains_ref[1:2], d_half)
        gain_ref[1:2] = d_scale
        d_laurel_ref[...] = d_laurel.astype(jnp.bfloat16)
        mlp.last(0)
        mlp.last(1)
        gather.settle()
        vec.finish()
        local.wait(*kept)
        mlp.finish()

    def f32(*shape):
        return jax.ShapeDtypeStruct(shape, jnp.float32)

    def held_bf16(*shape):
        return pltpu.VMEM(shape, jnp.bfloat16)

    return comm_call(
        kernel,
        ident,
        [
            bf16(rows, width),
            f32(rows, vec_width // 2),
            f32(rows, width),
            bf16(rows, width),
            bf16(rows, width),
            f32(8, width),
            bf16(shard_height, mlp_cols),
            bf16(shard_height, 8 * vec_width),
            bf16(2 * unit_rows, 2 * hidden_units),
            bf16(2 * unit_rows, hidden_units),
        ],
        [ANY] * 3 + [VMEM] * 8,
        [VMEM] * 6 + [ANY] * 4,
        [
            held_bf16(total, width),
            held_bf16(*w_gate_up.shape),
            held_bf16(*w_down.shape),
            held_bf16(total, 2 * hidden_units),
            held_bf16(total, hidden_units),
            held_bf16(total, width),
            held_bf16(total, width),
            held_bf16(unit_rows, total),
            held_bf16(width, vec_width),
            held_bf16(rows, width),
            pltpu.VMEM((rows, width), jnp.float32),
            pltpu.VMEM((rows, width), jnp.float32),
        ]
        + scatter_scratch
        + mlp_scratch
        + mlp_sems
        + vec_scratch
        + vec_sems
        + ChainGather.SEMS
        + [pltpu.SemaphoreType.DMA((2 * chunks + 4,))],
    )(
        row_ffn, w_gate_up, w_down, joined, attn_out, laurel_up, gains, layer_vec, pl_gate,
        pl_proj, out_grad,
    )


def sum_everywhere(place, own, arrived, sems):
    k, f = place.k, place.f
    targets = [
        place.sibling,
        (place.x_side, place.c),
        (place.y_side, place.c),
        (f, place.partner(1) * 2 + k),
        (f, place.partner(3) * 2 + k),
    ]
    return [
        remote(own.at[n], arrived.at[n], sems.at[0, n], sems.at[1, n], target)
        for n, target in enumerate(targets)
    ]


def attention_backward(
    d_attn_low, d_laurel_low, d_half, weights, kept, tables, head_gains, hidden, gains,
    other_gains, mlp_grads, mlp_land, vec_land, ident
):
    w_qkv, w_out, w_laurel = weights
    queries, keys, values, mixed, latent, projected, row_normed, row_parts = kept
    rows, width = d_half.shape
    total = 8 * rows
    query_block, key_span = 2 * rows, 768
    shard_height, vec_width = vec_land.shape[0], vec_land.shape[1] // 8
    qkv_width, laurel_width = w_qkv.shape[1], w_laurel.shape[1]
    attn_widths = (qkv_width + laurel_width, w_out.shape[1])
    scatter_scratch = ChainScatter.scratch(rows, width)
    first_late, late = 4, 4
    mlp_scratch = Drain.scratch(shard_height, [grad.shape[1] for grad in mlp_grads], late)
    mlp_sems = Drain.sems(len(MLP_PIECES), 2, late)
    loads = [*mlp_grads, w_out, queries, keys, values, tables, projected, w_qkv, mixed, row_normed]
    attn_scratch = Drain.scratch(shard_height, attn_widths)
    attn_sems = Drain.sems(len(ATTN_LAND), 2)
    gain_rows = other_gains.shape[0]

    def kernel(*refs):
        ins, outs, held = split_refs(refs, 23, 5, len(refs) - 28)
        (own_ref, row_pos, head_ref, hidden_ref, gains_ref, base_ref, other_ref, laurel_ref,
         vec_ref, w_laurel_ref, latent_ref) = ins[:11]
        wide_hbm, narrow_hbm = ins[11:13]
        out_ref, gain_ref, land_ref, attn_land, vec_all = outs
        (scratch, loaded, local_sems, gain_s, scat, mlp_s, mlp_m, attn_s, attn_m, vec_m, gather_m) = (
            split_refs(
                held, 9, 11, 1, 3, len(scatter_scratch), len(mlp_scratch), 3, len(attn_scratch), 3,
                3, 2,
            )
        )
        (vec_own, row_grad, d_mixed, d_keys, d_values, d_projected, qkv_grad, out_grad,
         laurel_back) = scratch
        (wide_ref, narrow_ref, w_out_ref, q_low, k_low, v_low, tables_ref, projected_ref, qkv_ref,
         mixed_ref, row_ref) = loaded
        held_gains, arrived_gains, gain_sems = gain_s
        place = Place()
        local = Local(local_sems[0])
        for src, dst in zip(ins[11:22], loaded):
            local.start(src, dst)
        greet(place, "all", True)
        gather = ChainGather(place, own_ref, row_grad, gather_m)
        scatter = ChainScatter(place, row_grad, scat)
        mlp = Drain(
            place, [wide_hbm, narrow_hbm], land_ref, MLP_PIECES, mlp_s, mlp_m, first_late, late,
            [wide_ref, narrow_ref],
        )
        attn = Drain(place, [qkv_grad, out_grad], attn_land, ATTN_LAND, attn_s, attn_m)
        vec = ChainGather(
            place, vec_own, vec_all.at[rows_at(place.f * 8 * shard_height, 8 * shard_height)],
            vec_m[:2],
        )
        plane = PlaneGather(place, vec_all, vec_m[2:])
        rounds = sum_everywhere(place, held_gains, arrived_gains, gain_sems)

        def gain_round(n):
            rounds[n].wait_recv()
            held_gains[n + 1] = held_gains[n] + arrived_gains[n]
            if n < 4:
                rounds[n + 1].start()

        gather.start()
        mlp.start(0)
        mlp.start(1)
        vec_sum = vec_ref[:, 0:vec_width].astype(jnp.float32)
        for c in range(1, 8):
            vec_sum = vec_sum + vec_ref[:, c * vec_width : (c + 1) * vec_width].astype(jnp.float32)
        vec_own[...] = vec_sum.astype(jnp.bfloat16)
        vec.start()
        d_keys[...] = jnp.zeros_like(d_keys)
        d_values[...] = jnp.zeros_like(d_values)
        held_gains[0] = other_ref[...]
        low = plain_dot(laurel_ref[...], w_laurel_ref[...])
        lanes = lax.broadcasted_iota(jnp.int32, low.shape, 1)
        d_latent = jnp.where(lanes < RANK, pltpu.roll(low, RANK, 1), 0.0).astype(jnp.bfloat16)
        laurel_back[...] = base_ref[...] + times_transposed(d_latent, w_laurel_ref[...])
        normed_low = rms_norm(hidden_ref[...].astype(jnp.float32), gains_ref[0:1]).astype(
            jnp.bfloat16
        )
        shifted = pltpu.roll(latent_ref[...].astype(jnp.float32), RANK, 1)
        up_side = jnp.where(lanes >= RANK, shifted, 0.0).astype(jnp.bfloat16)
        qkv_grad[:, qkv_width:] = (
            contract_rows(normed_low, d_latent) + contract_rows(laurel_ref[...], up_side)
        ).astype(jnp.bfloat16)
        local.wait(0, 1)
        gather.step(1)
        vec.step(1)
        mlp.middle(0)
        mlp.middle(1)
        for i in range(2, late):
            mlp.start(i)
        gather.step(2)
        vec.step(2)
        mlp.last(0)
        mlp.last(1)
        gather.step(3)
        vec.step(3)
        gather.arrive()
        vec.arrive()
        plane.start()
        local.wait(2, 3, 4, 5, 6, 7)

        @pl.loop(0, total // query_block)
        def _(n):
            here = rows_at(n * query_block, query_block)
            d_mixed[here] = plain_dot(row_grad[here], w_out_ref[...]).astype(jnp.bfloat16)

        for i in range(2, late):
            mlp.middle(i)

        @pl.loop(0, total // query_block)
        def _(d):
            here = rows_at(d * query_block, query_block)
            first_key = (d // 2) * (d - 2) * query_block
            there = rows_at(first_key, key_span)
            query, key, value, d_mix = q_low[here], k_low[there], v_low[there], d_mixed[here]
            scores = jnp.where(
                allowed_pairs(d * query_block, first_key, positions_of(row_pos[here])),
                times_transposed(query, key),
                NEG_LARGE,
            )
            exps = jnp.exp(scores - jnp.max(scores, axis=-1, keepdims=True))
            probs = exps / jnp.sum(exps, axis=-1, keepdims=True)
            d_probs = times_transposed(d_mix, value)
            inner_sum = jnp.sum(probs * d_probs, axis=-1, keepdims=True)
            d_scores = (probs * (d_probs - inner_sum)).astype(jnp.bfloat16)
            d_keys[there] += contract_rows(d_scores, query)
            d_values[there] += contract_rows(probs.astype(jnp.bfloat16), d_mix)
            cosine, sine = tables_ref[here, : HEAD // 2], tables_ref[here, HEAD // 2 :]
            d_query, d_scale = norm_back(
                projected_ref[here, :HEAD],
                head_ref[0:1],
                turn_back(plain_dot(d_scores, key), cosine, sine),
            )
            d_projected[here, :HEAD] = d_query.astype(jnp.bfloat16)
            held_gains[0, 6:7, :HEAD] += d_scale

        for i in range(2, late):
            mlp.last(i)

        @pl.loop(0, total // query_block)
        def _(n):
            here = rows_at(n * query_block, query_block)
            cosine, sine = tables_ref[here, : HEAD // 2], tables_ref[here, HEAD // 2 :]
            d_key, d_scale = norm_back(
                projected_ref[here, HEAD : 2 * HEAD],
                head_ref[1:2],
                turn_back(d_keys[here], cosine, sine),
            )
            d_projected[here, HEAD : 2 * HEAD] = d_key.astype(jnp.bfloat16)
            held_gains[0, 6:7, HEAD : 2 * HEAD] += d_scale
            d_value, _ = norm_back(projected_ref[here, 2 * HEAD :], 1.0, d_values[here])
            d_projected[here, 2 * HEAD :] = d_value.astype(jnp.bfloat16)

        quarter = width // 4
        local.wait(8, 9, 10)

        @pl.loop(0, 4)
        def _(n):
            columns = cols_at(n * quarter, quarter)
            out_grad[rows_at(n * quarter, quarter)] = contract_rows(
                row_grad[:, columns], mixed_ref[...]
            ).astype(jnp.bfloat16)

        gather.settle()
        upper = place.z // 2

        @pl.loop(0, total // query_block)
        def _(n):
            d = n * upper + (3 - n) * (1 - upper)
            here = rows_at(d * query_block, query_block)
            row_grad[here] = times_transposed(d_projected[here], qkv_ref[...]).astype(jnp.bfloat16)
            scatter.across(d).start()

        scatter.ends()

        @pl.loop(0, 4)
        def _(n):
            columns = cols_at(n * quarter, quarter)
            qkv_grad[rows_at(n * quarter, quarter), :qkv_width] = contract_rows(
                row_ref[:, columns], d_projected[...]
            ).astype(jnp.bfloat16)

        attn.start(0)
        attn.start(1)
        attn.start(2)
        attn.start(3)
        scatter.inner(0)
        plane.relay()
        attn.middle(0)
        attn.start(4)
        scatter.inner(1)
        attn.middle(1)
        attn.start(5)
        attn.last(0)
        attn.middle(2)
        attn.start(6)
        attn.last(1)
        scatter.finish(out_ref)
        d_normed = laurel_back[...] + out_ref[...]
        d_hidden, d_scale = norm_back(
            hidden_ref[...].astype(jnp.float32), gains_ref[0:1], d_normed
        )
        out_ref[...] = d_hidden
        held_gains[0, 0:1] = d_scale
        rounds[0].start()
        attn.start(7)
        for i in range(3, 8):
            attn.middle(i)
            attn.last(i - 1)
            gain_round(i - 3)
        attn.last(7)
        gain_ref[...] = held_gains[5]
        for copy in rounds:
            copy.wait_send()
        vec.settle()
        plane.finish()
        mlp.finish()
        attn.finish()

    return comm_call(
        kernel,
        ident,
        [
            jax.ShapeDtypeStruct((rows, width), jnp.float32),
            jax.ShapeDtypeStruct((gain_rows, width), jnp.float32),
            bf16(*mlp_land.shape),
            bf16(shard_height, 8 * sum(attn_widths)),
            bf16(32 * shard_height, vec_width),
        ],
        [VMEM] * 11 + [ANY] * 12,
        [VMEM, VMEM, ANY, ANY, ANY],
        [
            pltpu.VMEM((shard_height, vec_width), jnp.bfloat16),
            pltpu.VMEM((total, width), jnp.bfloat16),
            pltpu.VMEM((total, HEAD), jnp.bfloat16),
            pltpu.VMEM((total, HEAD), jnp.float32),
            pltpu.VMEM((total, HEAD), jnp.float32),
            pltpu.VMEM((total, qkv_width), jnp.bfloat16),
            pltpu.VMEM((width, attn_widths[0]), jnp.bfloat16),
            pltpu.VMEM((width, attn_widths[1]), jnp.bfloat16),
            pltpu.VMEM((rows, width), jnp.float32),
        ]
        + [pltpu.VMEM(array.shape, array.dtype) for array in loads]
        + [
            pltpu.SemaphoreType.DMA((len(loads),)),
            pltpu.VMEM((6, gain_rows, width), jnp.float32),
            pltpu.VMEM((5, gain_rows, width), jnp.float32),
            pltpu.SemaphoreType.DMA((2, 5)),
        ]
        + scatter_scratch
        + mlp_scratch
        + mlp_sems
        + attn_scratch
        + attn_sems
        + ChainGather.SEMS
        + PlaneGather.SEMS
        + ChainGather.SEMS,
        {22: 2},
    )(
        d_attn_low, row_parts, head_gains, hidden, gains, d_half, other_gains, d_laurel_low,
        vec_land, w_laurel, latent, *loads, mlp_land,
    )


def finish_outputs(mlp_land, attn_land, vec_all, d_half, d_hidden_part, attn_cols):
    height, mlp_cols = mlp_land.shape
    rows, width = d_half.shape
    model, vec_width = vec_all.shape
    per_source = attn_land.shape[1] // 8
    half = vec_width // 2
    group = QH // KVH
    kv_first, laurel_first, out_first = QH * HEAD, (QH + 2 * KVH) * HEAD, 3200

    def kernel(mlp_ref, attn_ref, vec_ref, half_ref, part_ref, *outs):
        mlp_out, attn_out, gate_out, proj_out, hidden_out = outs
        c = pl.program_id(0)
        mlp_out[...] = mlp_ref[...].astype(jnp.float32)
        gate_out[...] = vec_ref[:, :half].astype(jnp.float32)
        proj_out[...] = vec_ref[:, half:].astype(jnp.float32).T
        hidden_out[...] = half_ref[...] + part_ref[...]
        landed = attn_ref[...].astype(jnp.float32)
        attn_out[:, cols_at(c * HEAD, HEAD)] = landed[:, :HEAD]
        attn_out[:, cols_at(out_first + c * HEAD, HEAD)] = landed[:, per_source - HEAD :]

        def add(first, count, start, fresh):
            columns = cols_at(first, count)
            value = landed[:, start : start + count]

            @pl.when(fresh)
            def _():
                attn_out[:, columns] = value

            @pl.when(jnp.logical_not(fresh))
            def _():
                attn_out[:, columns] += value

        add(kv_first + c // group * HEAD, HEAD, HEAD, c % group == 0)
        add(kv_first + (KVH + c // group) * HEAD, HEAD, 2 * HEAD, c % group == 0)
        add(laurel_first, 2 * RANK, 3 * HEAD, c == 0)

    def spec(block, by_column):
        return pl.BlockSpec(block, (lambda c: (0, c)) if by_column else (lambda c: (c, 0)))

    f32 = jnp.float32
    return pl.pallas_call(
        kernel,
        grid=(8,),
        out_shape=[
            jax.ShapeDtypeStruct((height, mlp_cols), f32),
            jax.ShapeDtypeStruct((height, attn_cols), f32),
            jax.ShapeDtypeStruct((model, half), f32),
            jax.ShapeDtypeStruct((half, model), f32),
            jax.ShapeDtypeStruct((rows, width), f32),
        ],
        in_specs=[
            spec((height, mlp_cols // 8), True),
            spec((height, per_source), True),
            spec((model // 8, vec_width), False),
            spec((rows // 8, width), False),
            spec((rows // 8, width), False),
        ],
        out_specs=[
            spec((height, mlp_cols // 8), True),
            pl.BlockSpec((height, attn_cols), lambda c: (0, 0)),
            spec((model // 8, half), False),
            spec((half, model // 8), True),
            spec((rows // 8, width), False),
        ],
    )(mlp_land, attn_land, vec_all, d_half, d_hidden_part)


def per_device_split(
    hidden_in, layer_vec, positions, w_attn, w_mlp, pl_gate, pl_proj, gains, head_gains, out_grad
):
    shard_height = w_attn.shape[0]
    row_total = QH * positions.shape[0]
    lanes = jnp.arange(128, dtype=jnp.int32)[None, :]
    own_pos = jnp.where(lanes == 0, positions[:, None] // 256, positions[:, None] % 256)

    frequency = np.exp(np.arange(HEAD // 2) * (-2.0 * math.log(THETA) / HEAD))
    angles = np.arange(row_total)[:, None] * frequency[None, :]
    tables = jnp.asarray(np.concatenate([np.cos(angles), np.sin(angles)], axis=1), jnp.float32)

    (
        row_normed, w_qkv, w_out, w_laurel, row_parts, w_gate_up, w_down, row_ffn, projected,
        queries, keys, values, mixed, latent, laurel_up, attn_out, joined,
    ) = attention_forward(
        own_pos.astype(jnp.bfloat16), w_attn, w_mlp, hidden_in, gains, head_gains, tables, 1
    )
    (
        result_out, d_vector_in, d_half, d_attn_low, d_laurel_low, other_gains, mlp_land,
        vec_land, late_wide, late_narrow,
    ) = ffn_layer(
        row_ffn, w_gate_up, w_down, joined, attn_out, laurel_up, gains, layer_vec, pl_gate,
        pl_proj, out_grad, shard_height, w_mlp.shape[1], 2,
    )
    d_hidden_part, all_gains, mlp_land, attn_land, vec_all = attention_backward(
        d_attn_low,
        d_laurel_low,
        d_half,
        (w_qkv, w_out, w_laurel),
        (queries, keys, values, mixed, latent, projected, row_normed, row_parts),
        tables,
        head_gains,
        hidden_in,
        gains,
        other_gains,
        (late_wide, late_narrow),
        mlp_land,
        vec_land,
        3,
    )
    grad_w_mlp, grad_w_attn, grad_gate_all, grad_proj_all, grad_hidden = finish_outputs(
        mlp_land, attn_land, vec_all, d_half, d_hidden_part, w_attn.shape[1]
    )
    grad_gains, grad_heads = all_gains[:6], all_gains[6, : 2 * HEAD].reshape(2, HEAD)
    return (
        result_out,
        grad_hidden,
        d_vector_in,
        grad_w_attn,
        grad_w_mlp,
        grad_gate_all,
        grad_proj_all,
        grad_gains,
        grad_heads,
    )


def solution(mesh):
    fits = mesh.shape["ctx"] == QH and mesh.shape["fsdp"] == 4
    body = per_device_split if fits else per_device
    return jax.shard_map(
        body,
        mesh=mesh,
        in_specs=(
            P(("fsdp", "ctx"), None),
            P(("fsdp", "ctx"), None),
            P(("fsdp", "ctx")),
            P(("fsdp", "ctx"), None),
            P(("fsdp", "ctx"), None),
            P(),
            P(),
            P(),
            P(),
            P(("fsdp", "ctx"), None),
        ),
        out_specs=(
            P(("fsdp", "ctx"), None),
            P(("fsdp", "ctx"), None),
            P(("fsdp", "ctx"), None),
            P(("fsdp", "ctx"), None),
            P(("fsdp", "ctx"), None),
            P(),
            P(),
            P(),
            P(),
        ),
        check_vma=False,
    )
```

```python
import math

import jax
import jax.numpy as jnp
import numpy as np
from jax import lax
from jax.experimental import pallas as pl
from jax.experimental.pallas import tpu as pltpu
from jax.sharding import PartitionSpec as P

QH = 8
KVH = 2
HEAD = 256
RANK = 64
WINDOW = 512


EPSILON = 1e-06
THETA = 10000.0
NEG_LARGE = -1e30


def passed_along(block, axis, distance):
    devices = range(lax.axis_size(axis))
    route = [(i - distance, i) for i in devices if i - distance in devices]
    return lax.ppermute(block, axis, route)


def rms_norm(values, scale_vec):
    return (
        values * lax.rsqrt(jnp.mean(values * values, axis=-1, keepdims=True) + EPSILON) * scale_vec
    )


def value_norm(values):
    return rms_norm(values, 1.0)


def rotary(values, positions):
    half_size = values.shape[-1] // 2
    frequency = jnp.exp(
        jnp.arange(half_size, dtype=jnp.float32) * (-2.0 * math.log(THETA) / values.shape[-1])
    )
    angles = positions.astype(jnp.float32)[:, None] * frequency[None, :]
    cosine = jnp.cos(angles)[:, None, :]
    sine_part = jnp.sin(angles)[:, None, :]
    first_half = values[..., :half_size]
    second_half = values[..., half_size:]
    return jnp.concatenate(
        [
            first_half * cosine - second_half * sine_part,
            second_half * cosine + first_half * sine_part,
        ],
        axis=-1,
    )


def plain_dot(left_side, right_side):
    return jnp.dot(left_side, right_side, preferred_element_type=jnp.float32)


def times_transposed(left_side, right_side):
    return lax.dot_general(
        left_side, right_side, (((1,), (1,)), ((), ())), preferred_element_type=jnp.float32
    )


def contract_rows(left_side, right_side):
    return lax.dot_general(
        left_side, right_side, (((0,), (0,)), ((), ())), preferred_element_type=jnp.float32
    )


def activate(gate_up_val):
    half_cols = gate_up_val.shape[1] // 2
    return jax.nn.gelu(gate_up_val[:, :half_cols], approximate=True) * gate_up_val[:, half_cols:]


def vec_mix(gate_val, vector_val):
    return jax.nn.gelu(gate_val, approximate=True) * vector_val


def per_device(
    hidden_in, layer_vec, positions, w_attn, w_mlp, pl_gate, pl_proj, gains, head_gains, out_grad
):
    row_count = hidden_in.shape[0]
    model_width = hidden_in.shape[1]
    q_width = QH * HEAD
    kv_width = KVH * HEAD
    in_cols = q_width + 2 * kv_width + RANK
    group_size = QH // KVH
    ff_width = w_mlp.shape[1] // 3
    shard_height = w_mlp.shape[0]
    fsdp_count = lax.axis_size("fsdp")
    ctx_count = lax.axis_size("ctx")
    quarter = ff_width // fsdp_count

    def permute_cols(matrix):
        return (
            matrix.reshape(-1, fsdp_count, ctx_count, shard_height)
            .transpose(0, 2, 1, 3)
            .reshape(-1, model_width)
        )

    def restore_cols(matrix):
        return (
            matrix.reshape(-1, ctx_count, fsdp_count, shard_height)
            .transpose(0, 2, 1, 3)
            .reshape(-1, model_width)
        )

    def qk_prep(raw_heads, scale_vec):
        return rotary(rms_norm(raw_heads, scale_vec), positions)

    hidden = hidden_in.astype(jnp.float32)
    normed_in = rms_norm(hidden, gains[0])
    normed_low = normed_in.astype(jnp.bfloat16)
    projected = plain_dot(
        normed_low, lax.all_gather(w_attn[:, :in_cols], ("fsdp", "ctx"), axis=0, tiled=True)
    )
    q_raw = projected[:, :q_width].reshape(row_count, QH, HEAD)
    k_raw = projected[:, q_width : q_width + kv_width].reshape(row_count, KVH, HEAD)
    v_raw = projected[:, q_width + kv_width : q_width + 2 * kv_width].reshape(row_count, KVH, HEAD)
    latent = projected[:, q_width + 2 * kv_width :].astype(jnp.bfloat16)
    queries = qk_prep(q_raw, head_gains[0]).astype(jnp.bfloat16)
    keys_own = qk_prep(k_raw, head_gains[1]).astype(jnp.bfloat16)
    values_own = value_norm(v_raw).astype(jnp.bfloat16)
    kv_own = jnp.concatenate(
        [keys_own.reshape(row_count, kv_width), values_own.reshape(row_count, kv_width)], axis=1
    )
    hop_count = (WINDOW - 1) // row_count + 1
    earlier = []
    moving = kv_own
    for step_back in range(hop_count):
        moving = passed_along(moving, "ctx", 1)
        earlier.append(moving)
    kv_all = jnp.concatenate(earlier[::-1] + [kv_own], axis=0)
    span_rows = kv_all.shape[0]
    keys_all = kv_all[:, :kv_width].reshape(span_rows, KVH, HEAD)
    values_all = kv_all[:, kv_width:].reshape(span_rows, KVH, HEAD)
    grouped = queries.reshape(row_count, KVH, group_size, HEAD)
    distance = (
        jnp.arange(row_count, dtype=jnp.int32)[:, None]
        + hop_count * row_count
        - jnp.arange(span_rows, dtype=jnp.int32)[None, :]
    )
    allowed = (distance >= 0) & (distance <= jnp.minimum(positions, WINDOW - 1)[:, None])
    scores = jnp.einsum("qgrd,kgd->grqk", grouped, keys_all, preferred_element_type=jnp.float32)
    scores = jnp.where(allowed[None, None], scores, NEG_LARGE)
    row_max = jnp.max(scores, axis=-1, keepdims=True)
    exp_scores = jnp.exp(scores - row_max)
    row_sum = jnp.sum(exp_scores, axis=-1, keepdims=True)
    log_total = row_max + jnp.log(row_sum)
    probs_low = (exp_scores / row_sum).astype(jnp.bfloat16)
    mixed = jnp.einsum("grqk,kgd->qgrd", probs_low, values_all, preferred_element_type=jnp.float32)
    mixed = mixed.reshape(row_count, q_width).astype(jnp.bfloat16)
    shard_rows = lax.all_gather(w_attn[:, in_cols:], ("fsdp", "ctx"), axis=0, tiled=True)
    laurel_part = times_transposed(latent, shard_rows[:, :RANK])
    attn_part = times_transposed(mixed, shard_rows[:, RANK:])
    out_pair = jnp.stack([laurel_part, attn_part], axis=1)
    laurel_up = out_pair[:, 0]
    attn_out = out_pair[:, 1]
    laurel_res = normed_in + rms_norm(laurel_up, gains[1])
    after_attn = hidden + rms_norm(attn_out, gains[2])
    joined = (after_attn + laurel_res) / math.sqrt(2.0)
    ffn_low = rms_norm(joined, gains[3]).astype(jnp.bfloat16)
    sent_rows = w_mlp.reshape(shard_height, 3, fsdp_count, quarter)
    sent_tokens = jnp.broadcast_to(
        ffn_low[:, None, None, :], (row_count, 1, fsdp_count, model_width)
    )
    got_rows, got_tokens = (
        lax.all_to_all(sent_rows, "fsdp", split_axis=2, concat_axis=0, tiled=True),
        lax.all_to_all(sent_tokens, "fsdp", split_axis=2, concat_axis=0, tiled=True),
    )
    quarter_rows = lax.all_gather(got_rows, "ctx", axis=0, tiled=True).reshape(
        model_width, 3, quarter
    )
    w_gate_up = quarter_rows[:, :2].reshape(model_width, 2 * quarter)
    w_down = quarter_rows[:, 2]
    ffn_perm = permute_cols(got_tokens.reshape(fsdp_count * row_count, model_width))
    gate_up = plain_dot(ffn_perm, w_gate_up)
    activated = activate(gate_up).astype(jnp.bfloat16)
    ffn_out = lax.psum_scatter(
        restore_cols(times_transposed(activated, w_down)), "fsdp", scatter_dimension=0, tiled=True
    )
    after_ffn = joined + rms_norm(ffn_out, gains[4])
    after_low = after_ffn.astype(jnp.bfloat16)
    vec_gate = plain_dot(after_low, pl_gate)
    vector_in = layer_vec.astype(jnp.float32)
    vec_mixed = vec_mix(vec_gate, vector_in).astype(jnp.bfloat16)
    vec_out = plain_dot(vec_mixed, pl_proj)
    result_out = after_ffn + rms_norm(vec_out, gains[5])
    upstream = out_grad.astype(jnp.float32)
    unused_out, vec_norm_back = jax.vjp(rms_norm, vec_out, gains[5])
    d_vec_out, d_gain_vec = vec_norm_back(upstream)
    d_vec_out_low = d_vec_out.astype(jnp.bfloat16)
    d_vec_mixed = times_transposed(d_vec_out_low, pl_proj)
    grad_pl_proj = contract_rows(vec_mixed, d_vec_out_low)
    unused_out, mix_back = jax.vjp(vec_mix, vec_gate, vector_in)
    d_vec_gate, d_vector_in = mix_back(d_vec_mixed)
    d_vec_gate_low = d_vec_gate.astype(jnp.bfloat16)
    grad_after = upstream + times_transposed(d_vec_gate_low, pl_gate)
    grad_pl_gate = contract_rows(after_low, d_vec_gate_low)
    unused_out, ffn_norm_back = jax.vjp(rms_norm, ffn_out, gains[4])
    d_ffn_out, d_gain_ffn = ffn_norm_back(grad_after)
    d_ffn_low = d_ffn_out.astype(jnp.bfloat16)
    unused_out, act_back = jax.vjp(activate, gate_up)
    d_ffn_all = lax.all_gather(d_ffn_low, "fsdp", axis=0, tiled=True)
    d_ffn_perm = permute_cols(d_ffn_all)
    d_activated = plain_dot(d_ffn_perm, w_down)
    d_gate_up = act_back(d_activated)[0].astype(jnp.bfloat16)
    d_ffn_in = lax.psum_scatter(
        restore_cols(times_transposed(d_gate_up, w_gate_up)).astype(jnp.bfloat16),
        "fsdp",
        scatter_dimension=0,
        tiled=True,
    ).astype(jnp.float32)
    summed = lax.psum_scatter(
        jnp.concatenate(
            [contract_rows(ffn_perm, d_gate_up), contract_rows(d_ffn_perm, activated)], axis=1
        ).astype(jnp.bfloat16),
        "ctx",
        scatter_dimension=0,
        tiled=True,
    ).astype(jnp.float32)
    grad_w_mlp = (
        lax.all_to_all(
            summed.reshape(fsdp_count * shard_height, 3, 1, quarter).astype(jnp.bfloat16),
            "fsdp",
            split_axis=0,
            concat_axis=2,
            tiled=True,
        )
        .astype(jnp.float32)
        .reshape(shard_height, 3 * ff_width)
    )
    unused_out, pre_norm_back = jax.vjp(rms_norm, joined, gains[3])
    d_joined_part, d_gain_pre = pre_norm_back(d_ffn_in)
    d_joined = grad_after + d_joined_part
    d_half = d_joined / math.sqrt(2.0)
    unused_out, laurel_norm_back = jax.vjp(rms_norm, laurel_up, gains[1])
    d_laurel_up, d_gain_laurel = laurel_norm_back(d_half)
    unused_out, attn_norm_back = jax.vjp(rms_norm, attn_out, gains[2])
    d_attn_out, d_gain_attn = attn_norm_back(d_half)
    d_laurel_low = d_laurel_up.astype(jnp.bfloat16)
    d_attn_low = d_attn_out.astype(jnp.bfloat16)
    shard_rows = lax.all_gather(w_attn[:, in_cols:], ("fsdp", "ctx"), axis=0, tiled=True)
    d_latent = plain_dot(d_laurel_low, shard_rows[:, :RANK])
    d_mixed = plain_dot(d_attn_low, shard_rows[:, RANK:])
    d_grouped = d_mixed.astype(jnp.bfloat16).reshape(row_count, KVH, group_size, HEAD)
    again = jnp.einsum("qgrd,kgd->grqk", grouped, keys_all, preferred_element_type=jnp.float32)
    again = jnp.where(allowed[None, None], again, NEG_LARGE)
    probs = jnp.exp(again - log_total)
    d_probs = jnp.einsum(
        "qgrd,kgd->grqk", d_grouped, values_all, preferred_element_type=jnp.float32
    )
    inner_sum = jnp.sum(probs * d_probs, axis=-1, keepdims=True)
    d_scores = (probs * (d_probs - inner_sum)).astype(jnp.bfloat16)
    d_queries = jnp.einsum(
        "grqk,kgd->qgrd", d_scores, keys_all, preferred_element_type=jnp.float32
    ).reshape(row_count, QH, HEAD)
    d_keys_all = jnp.einsum("grqk,qgrd->kgd", d_scores, grouped, preferred_element_type=jnp.float32)
    d_values_all = jnp.einsum(
        "grqk,qgrd->kgd", probs.astype(jnp.bfloat16), d_grouped, preferred_element_type=jnp.float32
    )
    d_kv_all = jnp.concatenate(
        [d_keys_all.reshape(span_rows, kv_width), d_values_all.reshape(span_rows, kv_width)], axis=1
    )
    returned = d_kv_all[:row_count]
    for step_back in range(1, hop_count + 1):
        returned = (
            passed_along(returned.astype(jnp.bfloat16), "ctx", -1).astype(returned.dtype)
            + d_kv_all[step_back * row_count : (step_back + 1) * row_count]
        )
    d_keys_own = returned[:, :kv_width].reshape(row_count, KVH, HEAD)
    d_values_own = returned[:, kv_width:].reshape(row_count, KVH, HEAD)
    unused_out, query_back = jax.vjp(qk_prep, q_raw, head_gains[0])
    d_q_raw, d_head_query = query_back(d_queries)
    unused_out, key_back = jax.vjp(qk_prep, k_raw, head_gains[1])
    d_k_raw, d_head_key = key_back(d_keys_own)
    unused_out, value_back = jax.vjp(value_norm, v_raw)
    d_v_raw = value_back(d_values_own)[0]
    d_projected = jnp.concatenate(
        [
            d_q_raw.reshape(row_count, q_width),
            d_k_raw.reshape(row_count, kv_width),
            d_v_raw.reshape(row_count, kv_width),
            d_latent,
        ],
        axis=1,
    ).astype(jnp.bfloat16)
    d_normed_part = times_transposed(
        d_projected, lax.all_gather(w_attn[:, :in_cols], ("fsdp", "ctx"), axis=0, tiled=True)
    )
    unused_out, input_norm_back = jax.vjp(rms_norm, hidden, gains[0])
    d_hidden_part, d_gain_input = input_norm_back(d_half + d_normed_part)
    grad_hidden = d_half + d_hidden_part
    grad_w_attn = lax.psum_scatter(
        jnp.concatenate(
            [
                contract_rows(normed_low, d_projected),
                contract_rows(d_laurel_low, latent),
                contract_rows(d_attn_low, mixed),
            ],
            axis=1,
        ),
        ("fsdp", "ctx"),
        scatter_dimension=0,
        tiled=True,
    )
    gain_rows = jnp.stack(
        [d_gain_input, d_gain_laurel, d_gain_attn, d_gain_pre, d_gain_ffn, d_gain_vec]
    )
    head_rows = jnp.stack([d_head_query, d_head_key])
    grad_gains, grad_heads, grad_gate_all, grad_proj_all = lax.psum(
        (gain_rows, head_rows, grad_pl_gate, grad_pl_proj), ("fsdp", "ctx")
    )
    return (
        result_out.astype(jnp.bfloat16),
        grad_hidden,
        d_vector_in,
        grad_w_attn,
        grad_w_mlp,
        grad_gate_all,
        grad_proj_all,
        grad_gains,
        grad_heads,
    )

MESH = pl.DeviceIdType.MESH
VMEM_LIMIT = 63 * 1024 * 1024
ORDER = ((0, 0), (0, 1), (1, 0), (1, 1), (2, 0), (2, 1), (3, 0), (3, 1))


class Place:
    def __init__(self):
        self.f = lax.axis_index("fsdp")
        self.c = lax.axis_index("ctx")
        self.z = self.c // 2
        self.k = self.c % 2
        self.x_side = self.f + 1 - 2 * (self.f % 2)
        self.y_side = (self.f + 2) % 4
        self.diag = 3 - self.f
        self.sibling = (self.f, self.c + 1 - 2 * self.k)
        self.up = (self.f, self.c + 2)
        self.down = (self.f, self.c - 2)
        self.has_up = self.z < 3
        self.has_down = self.z > 0

    def partner(self, which):
        z = self.z
        return (z, z + 1 - 2 * (z % 2), (z + 2) % 4, 3 - z)[which]

    def peer(self, i):
        which, other = ORDER[i]
        return self.partner(which) * 2 + (self.k + other) % 2


def rows_at(start, count):
    return pl.ds(pl.multiple_of(start, 16), count)


def cols_at(start, count):
    if isinstance(start, int):
        return pl.ds(start, count)
    return pl.ds(pl.multiple_of(start, 128), count)


def remote(src, dst, send_sem, recv_sem, target):
    return pltpu.make_async_remote_copy(
        src_ref=src,
        dst_ref=dst,
        send_sem=send_sem,
        recv_sem=recv_sem,
        device_id=target,
        device_id_type=MESH,
    )


def greet(place, line, plane):
    barrier = pltpu.get_barrier_semaphore()
    count = 0

    def tell(target):
        pl.semaphore_signal(barrier, inc=1, device_id=target, device_id_type=MESH)

    if line == "all":
        for i in range(1, 8):
            tell((place.f, place.peer(i)))
        count += 7
    elif line == "chain":
        tell(place.sibling)
        for distance in (1, 3):
            tell((place.f, (place.z + distance) % 4 * 2 + place.k))
        count += 3
    if plane:
        tell((place.x_side, place.c))
        tell((place.y_side, place.c))
        count += 2
    pl.semaphore_wait(barrier, count)


class ChainGather:
    SEMS = [pltpu.SemaphoreType.DMA((2, 10)), pltpu.SemaphoreType.DMA((1,))]

    def __init__(self, place, own, out, sems, stride=None, offset=0):
        self.place, self.own, self.out = place, own, out
        self.sems, self.local_sem = sems
        self.rows = own.shape[0]
        self.stride, self.offset = stride or self.rows, offset

    def block(self, origin_z, core=None):
        core = self.place.k if core is None else core
        return self.out.at[
            rows_at((origin_z * 2 + core) * self.stride + self.offset, self.rows)
        ]

    def copy(self, src, dst, index, target):
        return remote(src, dst, self.sems.at[0, index], self.sems.at[1, index], target)

    def local(self):
        return pltpu.make_async_copy(self.own, self.block(self.place.z), self.local_sem.at[0])

    def upward(self, step):
        src = self.own if step == 0 else self.block(self.place.z - step)
        return self.copy(src, self.block(self.place.z - step), step, self.place.up)

    def downward(self, step):
        src = self.own if step == 0 else self.block(self.place.z + step)
        return self.copy(src, self.block(self.place.z + step), 3 + step, self.place.down)

    def across(self, origin_z, own=False):
        src = self.own if own else self.block(origin_z)
        return self.copy(src, self.block(origin_z), 6 + origin_z, self.place.sibling)

    def start(self):
        place = self.place

        @pl.when(place.has_up)
        def _():
            self.upward(0).start()

        @pl.when(place.has_down)
        def _():
            self.downward(0).start()

        self.across(place.z, True).start()
        self.local().start()

    def step(self, step):
        place = self.place

        @pl.when(place.z - step >= 0)
        def _():
            self.copy(self.own, self.block(place.z - step), step - 1, place.up).wait_recv()
            if step < 3:

                @pl.when(place.has_up)
                def _():
                    self.upward(step).start()

            self.across(place.z - step).start()

        @pl.when(place.z + step <= 3)
        def _():
            self.copy(self.own, self.block(place.z + step), 3 + step - 1, place.down).wait_recv()
            if step < 3:

                @pl.when(place.has_down)
                def _():
                    self.downward(step).start()

            self.across(place.z + step).start()

    def finish(self):
        self.arrive()
        self.settle()

    def from_sibling(self, origin):
        return self.copy(
            self.own, self.block(origin, 1 - self.place.k), 6 + origin, self.place.sibling
        )

    def near_first(self, n):
        upper = self.place.z // 2
        near = (1 - upper) * self.place.z + upper * (3 - self.place.z)
        late = n // 2
        chip = late * n + (1 - late) * ((near + n) % 2)
        return (1 - upper) * chip + upper * (3 - chip)

    def arrive(self):
        self.local().wait()
        for origin in range(4):
            self.from_sibling(origin).wait_recv()

    def settle(self):
        place = self.place
        for origin in range(4):
            self.from_sibling(origin).wait_send()
        for step in range(3):

            @pl.when((place.z - step >= 0) & place.has_up)
            def _(step=step):
                self.upward(step).wait_send()

            @pl.when((place.z + step <= 3) & place.has_down)
            def _(step=step):
                self.downward(step).wait_send()


class ChainScatter:
    PARTS = 2

    @staticmethod
    def scratch(rows, cols):
        return [
            pltpu.VMEM((4, rows, cols), jnp.bfloat16),
            pltpu.VMEM((6, rows, cols), jnp.bfloat16),
            pltpu.SemaphoreType.DMA((2, 4 + 6 * ChainScatter.PARTS)),
        ]

    def __init__(self, place, partial, scratch):
        self.place, self.partial = place, partial
        self.from_sibling, self.moving, self.sems = scratch
        self.rows = partial.shape[0] // 8

    def block(self, origin_z, core):
        return self.partial.at[rows_at((origin_z * 2 + core) * self.rows, self.rows)]

    def across(self, dest):
        return remote(
            self.block(dest, 1 - self.place.k),
            self.from_sibling.at[dest],
            self.sems.at[0, dest],
            self.sems.at[1, dest],
            self.place.sibling,
        )

    def moved(self, slot, part, target):
        count = self.rows // self.PARTS
        ref = self.moving.at[slot, pl.ds(part * count, count)]
        index = 4 + slot * self.PARTS + part
        return remote(ref, ref, self.sems.at[0, index], self.sems.at[1, index], target)

    def start(self):
        for dest in (3, 0, 2, 1):
            self.across(dest).start()

    def pair_sum(self, dest, part):
        count = self.rows // self.PARTS
        start = (dest * 2 + self.place.k) * self.rows + part * count
        return self.partial[rows_at(start, count)].astype(jnp.float32) + self.from_sibling[
            dest, part * count : (part + 1) * count
        ].astype(jnp.float32)

    def pass_on(self, dest, upward, inner=False, parts=(0, 1)):
        place = self.place
        slot = dest - 1 if upward else 3 + dest
        target = place.up if upward else place.down
        count = self.rows // self.PARTS
        if parts[0] == 0:
            self.across(dest).wait_recv()
        for part in parts:
            rows = slice(part * count, (part + 1) * count)
            total = self.pair_sum(dest, part)
            if inner:
                self.moved(slot, part, target).wait_recv()
                total = total + self.moving[slot, rows].astype(jnp.float32)
            self.moving[slot, rows] = total.astype(jnp.bfloat16)
            self.moved(slot, part, target).start()

    def ends_after(self, n):
        z = self.place.z

        @pl.when((n > 0) & (z == 0))
        def _():
            self.pass_on(4 - n, True)

        @pl.when((n > 0) & (z == 3))
        def _():
            self.pass_on(n - 1, False)

    def ends(self, parts=(0, 1)):
        z = self.place.z

        @pl.when(z == 0)
        def _():
            for dest in (3, 2, 1):
                self.pass_on(dest, True, False, parts)

        @pl.when(z == 3)
        def _():
            for dest in (0, 1, 2):
                self.pass_on(dest, False, False, parts)

    def inner(self, i, parts=(0, 1)):
        z = self.place.z

        @pl.when(z == 1)
        def _():
            if i == 0:
                self.pass_on(3, True, True, parts)
            else:
                self.pass_on(0, False, True, parts)
                self.pass_on(2, True, True, parts)

        @pl.when(z == 2)
        def _():
            if i == 0:
                self.pass_on(0, False, True, parts)
            else:
                self.pass_on(3, True, True, parts)
                self.pass_on(1, False, True, parts)

    def late_ends_after(self, n):
        z = self.place.z

        @pl.when((n > 1) & (z == 0))
        def _():
            self.pass_on(n - 1, True)

        @pl.when((n > 1) & (z == 3))
        def _():
            self.pass_on(4 - n, False)

    def late_inner(self, i):
        z = self.place.z

        @pl.when(z == 1)
        def _():
            dest = (2, 3, 0)[i]
            self.pass_on(dest, dest > 1, True)

        @pl.when(z == 2)
        def _():
            dest = (1, 0, 3)[i]
            self.pass_on(dest, dest > 1, True)

    def finish(self, out):
        self.total(out)
        self.settle()

    def total(self, out, parts=(0, 1)):
        place = self.place
        count = self.rows // self.PARTS
        for dest in range(4):

            @pl.when(place.z == dest)
            def _(dest=dest):
                if parts[0] == 0:
                    self.across(dest).wait_recv()
                for part in parts:
                    rows = slice(part * count, (part + 1) * count)
                    total = self.pair_sum(dest, part)
                    if dest > 0:
                        self.moved(dest - 1, part, place.up).wait_recv()
                        total = total + self.moving[dest - 1, rows].astype(jnp.float32)
                    if dest < 3:
                        self.moved(3 + dest, part, place.down).wait_recv()
                        total = total + self.moving[3 + dest, rows].astype(jnp.float32)
                    out[rows] = total

    def settle(self):
        place = self.place
        for dest in range(4):
            self.across(dest).wait_send()
        for i in range(3):
            top, bottom = 3 - i, i
            for part in range(self.PARTS):

                @pl.when(place.z < top)
                def _(top=top, part=part):
                    self.moved(top - 1, part, place.up).wait_send()

                @pl.when(place.z > bottom)
                def _(bottom=bottom, part=part):
                    self.moved(3 + bottom, part, place.down).wait_send()


class Spread:
    @staticmethod
    def sems(pieces, outs):
        return [
            pltpu.SemaphoreType.DMA((2, 8, pieces)),
            pltpu.SemaphoreType.DMA((2, 4, 8, outs)),
        ]

    def __init__(self, place, weight, outs, pieces, sems):
        self.place, self.weight, self.outs, self.pieces = place, weight, outs, pieces
        self.swap_sems, self.plane_sems = sems
        self.rows = weight.shape[0]

    def spot(self, f, c):
        return (f * 8 + c) * self.rows

    def swap(self, i, p, origin):
        column, width, out, out_column = self.pieces[p]
        peer = self.place.peer(i)
        src = self.weight.at[:, cols_at(column(peer), width)]
        dst = self.outs[out].at[
            rows_at(self.spot(self.place.f, origin), self.rows), pl.ds(out_column, width)
        ]
        if i == 0:
            return pltpu.make_async_copy(src, dst, self.swap_sems.at[0, 0, p])
        return remote(
            src,
            dst,
            self.swap_sems.at[0, i, p],
            self.swap_sems.at[1, i, p],
            (self.place.f, peer),
        )

    def whole(self, f, c, out):
        return self.outs[out].at[rows_at(self.spot(f, c), self.rows)]

    def part(self, f, c, out, half):
        count = self.rows // 2
        return self.outs[out].at[rows_at(self.spot(f, c) + half * count, count)]

    def plane(self, kind, i, out, ref, target):
        return remote(
            ref,
            ref,
            self.plane_sems.at[0, kind, i, out],
            self.plane_sems.at[1, kind, i, out],
            (target, self.place.c),
        )

    def start(self, first=0, last=8):
        for i in range(first, last):
            for p in range(len(self.pieces)):
                self.swap(i, p, self.place.c).start()

    def forward(self, i):
        place = self.place
        origin = place.peer(i)
        for p in range(len(self.pieces)):
            copy = self.swap(i, p, origin)
            if i == 0:
                copy.wait()
            else:
                copy.wait_recv()
        for out in range(len(self.outs)):
            ref = self.whole(place.f, origin, out)
            self.plane(0, i, out, ref, place.x_side).start()
            self.plane(1, i, out, ref, place.y_side).start()

    def relay(self, i):
        place = self.place
        origin = place.peer(i)
        for out in range(len(self.outs)):
            self.plane(0, i, out, self.whole(place.x_side, origin, out), place.x_side).wait_recv()
            self.plane(2, i, out, self.part(place.x_side, origin, out, 0), place.y_side).start()
            self.plane(1, i, out, self.whole(place.y_side, origin, out), place.y_side).wait_recv()
            self.plane(3, i, out, self.part(place.y_side, origin, out, 1), place.x_side).start()

    def finish(self, first=0, last=8):
        self.arrive(first, last)
        self.settle(first, last)

    def arrive(self, first=0, last=8):
        place = self.place
        for i in range(first, last):
            origin = place.peer(i)
            for out in range(len(self.outs)):
                self.plane(
                    2, i, out, self.part(place.diag, origin, out, 0), place.y_side
                ).wait_recv()
                self.plane(
                    3, i, out, self.part(place.diag, origin, out, 1), place.x_side
                ).wait_recv()

    def settle(self, first=0, last=8):
        place = self.place
        for i in range(first, last):
            origin = place.peer(i)
            if i:
                for p in range(len(self.pieces)):
                    self.swap(i, p, place.c).wait_send()
            for out in range(len(self.outs)):
                own = self.whole(place.f, origin, out)
                self.plane(0, i, out, own, place.x_side).wait_send()
                self.plane(1, i, out, own, place.y_side).wait_send()
                half = self.part(place.f, origin, out, 0)
                self.plane(2, i, out, half, place.y_side).wait_send()
                self.plane(3, i, out, half, place.x_side).wait_send()


class PlaneGather:
    SEMS = [pltpu.SemaphoreType.DMA((2, 4))]

    def __init__(self, place, out, sems):
        self.place, self.out = place, out
        self.sems = sems[0]
        self.rows = out.shape[0] // 4

    def copy(self, kind, f, target):
        count = self.rows // 2 if kind > 1 else self.rows
        start = f * self.rows + (count if kind == 3 else 0)
        ref = self.out.at[rows_at(start, count)]
        return remote(
            ref, ref, self.sems.at[0, kind], self.sems.at[1, kind], (target, self.place.c)
        )

    def start(self):
        place = self.place
        self.copy(0, place.f, place.x_side).start()
        self.copy(1, place.f, place.y_side).start()

    def relay(self):
        place = self.place
        self.copy(0, place.x_side, place.x_side).wait_recv()
        self.copy(2, place.x_side, place.y_side).start()
        self.copy(1, place.y_side, place.y_side).wait_recv()
        self.copy(3, place.y_side, place.x_side).start()

    def finish(self):
        place = self.place
        self.copy(2, place.diag, place.y_side).wait_recv()
        self.copy(3, place.diag, place.x_side).wait_recv()
        self.copy(0, place.f, place.x_side).wait_send()
        self.copy(1, place.f, place.y_side).wait_send()
        self.copy(2, place.x_side, place.y_side).wait_send()
        self.copy(3, place.y_side, place.x_side).wait_send()


DRAIN_ORDER = (0, 1, 4, 5, 2, 3, 6, 7)


class Drain:
    @staticmethod
    def scratch(rows, widths, peers=8):
        half = rows // 2
        lists = []
        for width in widths:
            lists += [
                pltpu.VMEM((2, peers, 2, half, width), jnp.bfloat16),
                pltpu.VMEM((2, peers, half, width), jnp.bfloat16),
            ]
        return lists

    @staticmethod
    def sems(pieces, outs, peers=8):
        return [
            pltpu.SemaphoreType.DMA((2, 2, peers, 2, outs)),
            pltpu.SemaphoreType.DMA((2, 2, peers, outs)),
            pltpu.SemaphoreType.DMA((2, peers, pieces, 2)),
        ]

    def __init__(self, place, grads, land, pieces, scratch, sems, base=0, peers=8, adds=None):
        self.place, self.grads, self.land, self.pieces = place, grads, land, pieces
        self.adds = adds or grads
        self.first = scratch[0::2]
        self.second = scratch[1::2]
        self.first_sems, self.second_sems, self.swap_sems = sems
        self.rows = land.shape[0]
        self.half = self.rows // 2
        self.units = grads[0].shape[0] < 32 * self.rows or peers < 8
        self.base, self.peers = base, peers

    def peer(self, i):
        return self.place.peer(DRAIN_ORDER[self.base + i])

    def part(self, g, f, i, half, adds=False):
        refs = self.adds if adds else self.grads
        peer = self.peer(i)
        if self.units:
            start = (i // 2 * 8 + f * 2 + peer % 2) * self.rows + half * self.half
            return refs[g].at[rows_at(start, self.half)]
        return refs[g].at[rows_at((f * 8 + peer) * self.rows + half * self.half, self.half)]

    def sides(self, axis):
        place = self.place
        return (place.x_side, place.y_side) if axis == 0 else (place.y_side, place.x_side)

    def first_copy(self, axis, i, which, g):
        near, _ = self.sides(axis)
        f = near if which == 0 else self.place.diag
        return remote(
            self.part(g, f, i, axis),
            self.first[g].at[axis, i, which],
            self.first_sems.at[0, axis, i, which, g],
            self.first_sems.at[1, axis, i, which, g],
            (near, self.place.c),
        )

    def second_copy(self, axis, i, g):
        _, far = self.sides(axis)
        return remote(
            self.first[g].at[axis, i, 1],
            self.second[g].at[axis, i],
            self.second_sems.at[0, axis, i, g],
            self.second_sems.at[1, axis, i, g],
            (far, self.place.c),
        )

    def swap(self, i, p, half, origin):
        column, width, g, g_column = self.pieces[p]
        src = self.first[g].at[half, i, 0, :, pl.ds(g_column, width)]
        dst = self.land.at[pl.ds(half * self.half, self.half), cols_at(column(origin), width)]
        if self.base + i == 0:
            return pltpu.make_async_copy(src, dst, self.swap_sems.at[0, i, p, half])
        return remote(
            src,
            dst,
            self.swap_sems.at[0, i, p, half],
            self.swap_sems.at[1, i, p, half],
            (self.place.f, self.peer(i)),
        )

    def start(self, i):
        for g in range(len(self.grads)):
            for which in (1, 0):
                for axis in range(2):
                    self.first_copy(axis, i, which, g).start()

    def middle(self, i):
        place = self.place
        for g in range(len(self.grads)):
            for axis in range(2):
                _, far = self.sides(axis)
                self.first_copy(axis, i, 1, g).wait_recv()
                mine = self.part(g, far, i, axis, True)
                self.first[g][axis, i, 1] = (
                    mine[...].astype(jnp.float32) + self.first[g][axis, i, 1].astype(jnp.float32)
                ).astype(jnp.bfloat16)
                self.second_copy(axis, i, g).start()

    def last(self, i):
        place = self.place
        for g in range(len(self.grads)):
            for axis in range(2):
                self.first_copy(axis, i, 0, g).wait_recv()
                self.second_copy(axis, i, g).wait_recv()
                mine = self.part(g, place.f, i, axis, True)
                self.first[g][axis, i, 0] = (
                    mine[...].astype(jnp.float32)
                    + self.first[g][axis, i, 0].astype(jnp.float32)
                    + self.second[g][axis, i].astype(jnp.float32)
                ).astype(jnp.bfloat16)
        for p in range(len(self.pieces)):
            for half in range(2):
                self.swap(i, p, half, place.c).start()

    def finish(self):
        place = self.place
        for i in range(self.peers):
            for p in range(len(self.pieces)):
                for half in range(2):
                    copy = self.swap(i, p, half, self.peer(i))
                    if self.base + i == 0:
                        copy.wait()
                    else:
                        copy.wait_recv()
                        copy.wait_send()
            for g in range(len(self.grads)):
                for axis in range(2):
                    for which in range(2):
                        self.first_copy(axis, i, which, g).wait_send()
                    self.second_copy(axis, i, g).wait_send()


ANY = pl.BlockSpec(memory_space=pl.ANY)
VMEM = pl.BlockSpec(memory_space=pltpu.VMEM)


def comm_call(kernel, ident, out_shape, in_specs, out_specs, scratch, aliases=None):
    return pl.pallas_call(
        kernel,
        input_output_aliases=aliases or {},
        out_shape=out_shape,
        in_specs=in_specs,
        out_specs=out_specs,
        scratch_shapes=scratch,
        compiler_params=pltpu.CompilerParams(
            collective_id=ident, has_side_effects=True, vmem_limit_bytes=VMEM_LIMIT
        ),
    )


class Local:
    def __init__(self, sems):
        self.sems, self.copies = sems, []

    def start(self, src, dst):
        self.copies.append(pltpu.make_async_copy(src, dst, self.sems.at[len(self.copies)]))
        self.copies[-1].start()
        return len(self.copies) - 1

    def wait(self, *indices):
        for index in indices:
            self.copies[index].wait()


def bf16(*shape):
    return jax.ShapeDtypeStruct(shape, jnp.bfloat16)


ATTN_PIECES = (
    (lambda c: 256 * c, 256, 0, 0),
    (lambda c: 2048 + 256 * (c // 4), 256, 0, 256),
    (lambda c: 2560 + 256 * (c // 4), 256, 0, 512),
    (lambda c: 3200 + 256 * c, 256, 1, 0),
    (lambda c: 3072, 128, 2, 0),
)
ATTN_LAND = (
    (lambda c: 1152 * c, 896, 0, 0),
    (lambda c: 1152 * c + 896, 256, 1, 0),
)
MLP_PIECES = (
    (lambda c: 1024 * c, 1024, 0, 0),
    (lambda c: 8192 + 1024 * c, 1024, 0, 1024),
    (lambda c: 16384 + 1024 * c, 1024, 1, 0),
)
EARLY_UNITS = 2
VEC_LAND = ((lambda c: 512 * c, 512, 0, 0),)


def turn(values, cosine, sine):
    half = HEAD // 2
    first, second = values[:, :half], values[:, half:]
    return jnp.concatenate(
        [first * cosine - second * sine, second * cosine + first * sine], axis=1
    )


def allowed_pairs(first_query, first_key, positions):
    shape = (positions.shape[0], 768)
    distance = (
        lax.broadcasted_iota(jnp.int32, shape, 0)
        - lax.broadcasted_iota(jnp.int32, shape, 1)
        + (first_query - first_key)
    )
    return (distance >= 0) & (distance <= jnp.minimum(positions, WINDOW - 1))


def positions_of(parts):
    return (parts[:, 0:1].astype(jnp.float32) * 256.0 + parts[:, 1:2].astype(jnp.float32)).astype(
        jnp.int32
    )


def attention_forward(own_pos, w_attn, w_mlp, hidden, gains, head_gains, tables, ident):
    height = 32 * w_attn.shape[0]
    rows, width = hidden.shape
    total = 8 * rows
    query_block, key_span = 2 * rows, 768
    scatter_scratch = ChainScatter.scratch(rows, width)

    def kernel(*refs):
        ins, outs, held = split_refs(refs, 7, 17, len(refs) - 24)
        pos_ref, attn_ref, mlp_ref, hidden_ref, gains_ref, head_ref, tables_ref = ins
        (row_ref, qkv_ref, out_ref, laurel_ref, row_pos, gate_up_ref, down_ref, row_ffn,
         projected, q_low, k_low, v_low, mixed, latent_ref, laurel_up, attn_out, joined) = outs
        scratch, scat, attn_m, mlp_m, gather_m = split_refs(held, 4, len(scatter_scratch), 2, 2, 8)
        own_ffn, partial, own_ref, normed_ref = scratch
        place = Place()
        normed_ref[...] = rms_norm(hidden_ref[...].astype(jnp.float32), gains_ref[0:1])
        own_ref[...] = normed_ref[...].astype(jnp.bfloat16)
        greet(place, "all", True)
        attn = Spread(place, attn_ref, [qkv_ref, out_ref, laurel_ref], ATTN_PIECES, attn_m)
        mlp = Spread(place, mlp_ref, [gate_up_ref, down_ref], MLP_PIECES, mlp_m)
        gathers = [
            ChainGather(place, own_ref, row_ref, gather_m[0:2]),
            ChainGather(place, pos_ref, row_pos, gather_m[2:4]),
        ]
        last = [
            ChainGather(
                place, own_ffn.at[pl.ds(part * (rows // 2), rows // 2)], row_ffn,
                gather_m[4 + 2 * part : 6 + 2 * part], rows, part * (rows // 2),
            )
            for part in range(2)
        ]
        scatter = ChainScatter(place, partial, scat)

        def step(n):
            for gather in gathers:
                gather.step(n)

        for gather in gathers:
            gather.start()
        attn.start(0, 4)
        mlp.start(0, 2)
        attn.forward(0)
        attn.forward(1)
        mlp.forward(0)
        step(1)
        attn.start(4, 6)
        mlp.start(4, 5)
        attn.forward(2)
        attn.forward(3)
        attn.relay(0)
        attn.relay(1)
        step(2)
        attn.start(6, 8)
        mlp.start(5, 6)
        attn.forward(4)
        attn.forward(5)
        attn.relay(2)
        attn.relay(3)
        step(3)
        attn.forward(6)
        attn.forward(7)
        mlp.start(2, 4)
        attn.relay(4)
        attn.relay(5)
        mlp.relay(0)
        attn.relay(6)
        attn.relay(7)
        for gather in gathers:
            gather.arrive()
        attn.arrive()
        mlp.forward(1)
        mlp.start(6, 7)

        @pl.loop(0, total // query_block)
        def _(n):
            here = rows_at(n * query_block, query_block)
            block = plain_dot(row_ref[here], qkv_ref[...])
            projected[here] = block
            cosine, sine = tables_ref[here, : HEAD // 2], tables_ref[here, HEAD // 2 :]
            q_low[here] = turn(
                rms_norm(block[:, :HEAD], head_ref[0:1]), cosine, sine
            ).astype(jnp.bfloat16)
            k_low[here] = turn(
                rms_norm(block[:, HEAD : 2 * HEAD], head_ref[1:2]), cosine, sine
            ).astype(jnp.bfloat16)
            v_low[here] = value_norm(block[:, 2 * HEAD :]).astype(jnp.bfloat16)

        mlp.start(7, 8)
        upper = place.z // 2

        @pl.loop(0, total // query_block)
        def _(n):
            d = n * upper + (3 - n) * (1 - upper)
            here = rows_at(d * query_block, query_block)
            first_key = (d // 2) * (d - 2) * query_block
            there = rows_at(first_key, key_span)
            scores = jnp.where(
                allowed_pairs(d * query_block, first_key, positions_of(row_pos[here])),
                times_transposed(q_low[here], k_low[there]),
                NEG_LARGE,
            )
            weights = jnp.exp(scores - jnp.max(scores, axis=-1, keepdims=True))
            probs = (weights / jnp.sum(weights, axis=-1, keepdims=True)).astype(jnp.bfloat16)
            block = plain_dot(probs, v_low[there]).astype(jnp.bfloat16)
            mixed[here] = block
            partial[here] = times_transposed(block, out_ref[...]).astype(jnp.bfloat16)
            scatter.across(d).start()

        scatter.ends((0,))
        scatter.ends((1,))
        mlp.relay(1)
        mlp.forward(2)
        mlp.forward(3)
        scatter.inner(0, (0,))
        mlp.forward(4)
        low = plain_dot(own_ref[...], laurel_ref[...])
        latent_ref[...] = low.astype(jnp.bfloat16)
        lanes = lax.broadcasted_iota(jnp.int32, low.shape, 1)
        shifted = jnp.where(lanes >= RANK, pltpu.roll(low, RANK, 1), 0.0).astype(jnp.bfloat16)
        laurel_up[...] = times_transposed(shifted, laurel_ref[...])
        scatter.inner(1, (0,))
        mlp.forward(5)

        def close(part):
            here = slice(part * (rows // 2), (part + 1) * (rows // 2))
            laurel_res = normed_ref[here] + rms_norm(laurel_up[here], gains_ref[1:2])
            after_attn = hidden_ref[here].astype(jnp.float32) + rms_norm(
                attn_out[here], gains_ref[2:3]
            )
            joined[here] = (after_attn + laurel_res) / math.sqrt(2.0)
            own_ffn[here] = rms_norm(joined[here], gains_ref[3:4]).astype(jnp.bfloat16)

        scatter.total(attn_out, (0,))
        close(0)
        last[0].start()
        scatter.inner(0, (1,))
        scatter.inner(1, (1,))
        mlp.relay(2)
        mlp.relay(3)
        last[0].step(1)
        scatter.total(attn_out, (1,))
        close(1)
        last[1].start()
        mlp.relay(4)
        mlp.forward(6)
        mlp.forward(7)
        last[0].step(2)
        last[1].step(1)
        mlp.relay(5)
        last[0].step(3)
        mlp.relay(6)
        last[1].step(2)
        mlp.relay(7)
        last[1].step(3)
        scatter.settle()
        mlp.arrive()
        for gather in last:
            gather.arrive()
        attn.settle()
        mlp.settle()
        for gather in gathers + last:
            gather.settle()

    def f32(*shape):
        return jax.ShapeDtypeStruct(shape, jnp.float32)

    token_f32 = f32(rows, width)
    head = bf16(total, HEAD)
    outs = [bf16(total, width), bf16(height, 768), bf16(height, 256), bf16(height, 128)]
    outs += [bf16(total, 128), bf16(height, 2048), bf16(height, 1024), bf16(total, width)]
    outs += [f32(total, 768), head, head, head, head, bf16(rows, 128)]
    outs += [token_f32, token_f32, token_f32]
    return comm_call(
        kernel,
        ident,
        outs,
        [VMEM, ANY, ANY] + [VMEM] * 4,
        [VMEM] * 5 + [ANY] * 3 + [VMEM] * 9,
        [
            pltpu.VMEM((rows, width), jnp.bfloat16),
            pltpu.VMEM((total, width), jnp.bfloat16),
            pltpu.VMEM((rows, width), jnp.bfloat16),
            pltpu.VMEM((rows, width), jnp.float32),
        ]
        + scatter_scratch
        + Spread.sems(len(ATTN_PIECES), 3)
        + Spread.sems(len(MLP_PIECES), 2)
        + ChainGather.SEMS * 4,
    )(own_pos, w_attn, w_mlp, hidden, gains, head_gains, tables)


def split_refs(refs, *counts):
    refs, parts = list(refs), []
    for count in counts:
        parts.append(refs[:count])
        refs = refs[count:]
    return parts


def turn_back(grads, cosine, sine):
    half = HEAD // 2
    first, second = grads[:, :half], grads[:, half:]
    return jnp.concatenate(
        [first * cosine + second * sine, second * cosine - first * sine], axis=1
    )


def norm_back(values, scale_vec, grads):
    inverse = lax.rsqrt(jnp.mean(values * values, axis=-1, keepdims=True) + EPSILON)
    unit = values * inverse
    scaled = grads * scale_vec
    back = (scaled - unit * jnp.mean(unit * scaled, axis=-1, keepdims=True)) * inverse
    return back, jnp.sum(grads * unit, axis=0, keepdims=True)


def unit_gradient(place, n, tokens_ref, grad_ref, out, turned_ref):
    zz = place.partner(ORDER[DRAIN_ORDER[2 * n]][0])
    unit_rows = turned_ref.shape[0]
    count = unit_rows // 4
    for f in range(4):
        columns = cols_at((f * 4 + zz) * count, count)
        turned_ref[f * count : (f + 1) * count] = tokens_ref[:, columns].T
    step = 512

    @pl.loop(0, grad_ref.shape[1] // step)
    def _(t):
        columns = cols_at(t * step, step)
        out[n * unit_rows : (n + 1) * unit_rows, columns] = plain_dot(
            turned_ref[...], grad_ref[:, columns]
        ).astype(jnp.bfloat16)


def gelu_pair(values):
    scale = math.sqrt(2.0 / math.pi)
    squares = values * values
    bend = jnp.tanh(scale * values * (1.0 + 0.044715 * squares))
    half = 0.5 * (1.0 + bend)
    slope = half + 0.5 * values * (1.0 - bend * bend) * scale * (1.0 + 3.0 * 0.044715 * squares)
    return values * half, slope


def ffn_layer(
    row_ffn, w_gate_up, w_down, joined, attn_out, laurel_up, gains, layer_vec, pl_gate, pl_proj,
    out_grad, shard_height, mlp_cols, ident
):
    rows, width = joined.shape
    total, hidden_units = 8 * rows, w_down.shape[1]
    block, chunk = 2 * rows, hidden_units // 2
    vec_width = 2 * pl_gate.shape[1]
    unit_rows = 8 * shard_height
    scatter_scratch = ChainScatter.scratch(rows, width)
    early, late = 2 * EARLY_UNITS, 4 - EARLY_UNITS
    mlp_scratch = Drain.scratch(shard_height, (2 * hidden_units, hidden_units), early)
    mlp_sems = Drain.sems(len(MLP_PIECES), 2, early)
    vec_scratch = Drain.scratch(shard_height, (vec_width,))
    vec_sems = Drain.sems(1, 1)

    def kernel(*refs):
        ins, outs, held = split_refs(refs, 11, 10, len(refs) - 21)
        ffn_hbm, gate_up_hbm, down_hbm = ins[:3]
        (joined_ref, attn_ref, laurel_ref, gains_ref, vector_ref, pl_gate_ref, pl_proj_ref,
         out_grad_ref) = ins[3:]
        (result_ref, d_vector_ref, d_half_ref, d_attn_ref, d_laurel_ref, gain_ref, mlp_land,
         vec_land, late_wide, late_narrow) = outs
        scratch, scat, mlp_s, mlp_m, vec_s, vec_m, gather_m, last = split_refs(
            held, 12, len(scatter_scratch), len(mlp_scratch), 3, len(vec_scratch), 3, 2, 1
        )
        (ffn_ref, gate_up_ref, down_ref, slopes, active, row_grad, partial, turned, vec_grad,
         own_grad, ffn_out, grad_after) = scratch
        place = Place()
        local = Local(last[0])
        local.start(ffn_hbm, ffn_ref)
        local.start(gate_up_hbm, gate_up_ref)
        down_copy = local.start(down_hbm, down_ref)
        greet(place, "all", True)
        scatter = ChainScatter(place, partial, scat)
        gather = ChainGather(place, own_grad, row_grad, gather_m)
        mlp = Drain(
            place, [gate_up_ref, down_ref], mlp_land, MLP_PIECES, mlp_s, mlp_m, 0, early
        )
        vec = Drain(place, [vec_grad], vec_land, VEC_LAND, vec_s, vec_m)
        upper = place.z // 2

        local.wait(0, 1, down_copy)

        @pl.loop(0, total // block)
        def _(n):
            d = n * upper + (3 - n) * (1 - upper)
            here = rows_at(d * block, block)
            for t in range(2):
                gates = pl.ds(t * chunk, chunk)
                ups = pl.ds(hidden_units + t * chunk, chunk)
                gate = plain_dot(ffn_ref[here], gate_up_ref[:, gates])
                up = plain_dot(ffn_ref[here], gate_up_ref[:, ups])
                value, slope = gelu_pair(gate)
                active[here, gates] = (value * up).astype(jnp.bfloat16)
                slopes[here, gates] = (slope * up).astype(jnp.bfloat16)
                slopes[here, ups] = value.astype(jnp.bfloat16)
            partial[here] = times_transposed(active[here], down_ref[...]).astype(jnp.bfloat16)
            scatter.across(d).start()
            scatter.ends_after(n)

        scatter.inner(0)
        scatter.inner(1)
        scatter.finish(ffn_out)

        after = joined_ref[...] + rms_norm(ffn_out[...], gains_ref[4:5])
        after_low = after.astype(jnp.bfloat16)
        vec_gate = plain_dot(after_low, pl_gate_ref[...])
        vector = vector_ref[...].astype(jnp.float32)
        value, slope = gelu_pair(vec_gate)
        vec_mixed = (value * vector).astype(jnp.bfloat16)
        vec_out = plain_dot(vec_mixed, pl_proj_ref[...])
        result_ref[...] = (after + rms_norm(vec_out, gains_ref[5:6])).astype(jnp.bfloat16)
        upstream = out_grad_ref[...].astype(jnp.float32)
        d_vec_out, d_scale = norm_back(vec_out, gains_ref[5:6], upstream)
        gain_ref[...] = jnp.zeros_like(gain_ref)
        gain_ref[5:6] = d_scale
        d_vec_out_low = d_vec_out.astype(jnp.bfloat16)
        d_vec_mixed = times_transposed(d_vec_out_low, pl_proj_ref[...])
        d_vector_ref[...] = d_vec_mixed * value
        d_vec_gate_low = (d_vec_mixed * vector * slope).astype(jnp.bfloat16)
        grad_after[...] = upstream + times_transposed(d_vec_gate_low, pl_gate_ref[...])
        d_ffn_out, d_scale = norm_back(ffn_out[...], gains_ref[4:5], grad_after[...])
        gain_ref[4:5] = d_scale
        own_grad[...] = d_ffn_out.astype(jnp.bfloat16)
        gather.start()
        half = vec_width // 2
        vec_grad[:, :half] = contract_rows(after_low, d_vec_gate_low).astype(jnp.bfloat16)
        vec_grad[:, half:] = contract_rows(d_vec_out_low, vec_mixed).astype(jnp.bfloat16)
        for i in range(8):
            vec.start(i)
        gather.local().wait()

        @pl.loop(0, total // block)
        def _(n):
            for step in (1, 2, 3):

                @pl.when(n == step)
                def _(step=step):
                    gather.step(step)
                    for i in ((), range(4), range(4, 8), ())[step]:
                        vec.middle(i)
                    for i in ((), (), range(4), range(4, 8))[step]:
                        vec.last(i)

            d = gather.near_first(n)
            gather.from_sibling(d).wait_recv()
            here = rows_at(d * block, block)
            for t in range(2):
                gates = pl.ds(t * chunk, chunk)
                ups = pl.ds(hidden_units + t * chunk, chunk)
                d_active = plain_dot(row_grad[here], down_ref[:, gates])
                slopes[here, gates] = (d_active * slopes[here, gates].astype(jnp.float32)).astype(
                    jnp.bfloat16
                )
                slopes[here, ups] = (d_active * slopes[here, ups].astype(jnp.float32)).astype(
                    jnp.bfloat16
                )
            partial[here] = times_transposed(slopes[here], gate_up_ref[...]).astype(jnp.bfloat16)
            scatter.across(d).start()
            scatter.late_ends_after(n)

        scatter.late_ends_after(4)

        def unit(n):
            unit_gradient(place, n, ffn_ref, slopes, gate_up_ref, turned)
            unit_gradient(place, n, row_grad, active, down_ref, turned)

        first = EARLY_UNITS - 1
        scatter.late_inner(0)
        unit(first)
        mlp.start(2 * first)
        mlp.start(2 * first + 1)
        scatter.late_inner(1)
        unit(1 - first)
        scatter.late_inner(2)
        for i in range(2 * first):
            mlp.start(i)
        mlp.middle(2 * first)
        mlp.middle(2 * first + 1)
        unit(2)
        mlp.last(2 * first)
        mlp.last(2 * first + 1)
        unit(3)
        kept = [
            local.start(ref.at[pl.ds(EARLY_UNITS * unit_rows, late * unit_rows)], out)
            for ref, out in ((gate_up_ref, late_wide), (down_ref, late_narrow))
        ]
        for i in range(2 * first):
            mlp.middle(i)
        scatter.finish(ffn_out)
        d_joined, d_scale = norm_back(joined_ref[...], gains_ref[3:4], ffn_out[...])
        gain_ref[3:4] = d_scale
        d_half = (grad_after[...] + d_joined) / math.sqrt(2.0)
        d_half_ref[...] = d_half
        d_attn, d_scale = norm_back(attn_ref[...], gains_ref[2:3], d_half)
        gain_ref[2:3] = d_scale
        d_attn_ref[...] = d_attn.astype(jnp.bfloat16)
        d_laurel, d_scale = norm_back(laurel_ref[...], gains_ref[1:2], d_half)
        gain_ref[1:2] = d_scale
        d_laurel_ref[...] = d_laurel.astype(jnp.bfloat16)
        for i in range(2 * first):
            mlp.last(i)
        gather.settle()
        vec.finish()
        local.wait(*kept)
        mlp.finish()

    def f32(*shape):
        return jax.ShapeDtypeStruct(shape, jnp.float32)

    def held_bf16(*shape):
        return pltpu.VMEM(shape, jnp.bfloat16)

    return comm_call(
        kernel,
        ident,
        [
            bf16(rows, width),
            f32(rows, vec_width // 2),
            f32(rows, width),
            bf16(rows, width),
            bf16(rows, width),
            f32(8, width),
            bf16(shard_height, mlp_cols),
            bf16(shard_height, 8 * vec_width),
            bf16(late * unit_rows, 2 * hidden_units),
            bf16(late * unit_rows, hidden_units),
        ],
        [ANY] * 3 + [VMEM] * 8,
        [VMEM] * 6 + [ANY] * 4,
        [
            held_bf16(total, width),
            held_bf16(*w_gate_up.shape),
            held_bf16(*w_down.shape),
            held_bf16(total, 2 * hidden_units),
            held_bf16(total, hidden_units),
            held_bf16(total, width),
            held_bf16(total, width),
            held_bf16(unit_rows, total),
            held_bf16(width, vec_width),
            held_bf16(rows, width),
            pltpu.VMEM((rows, width), jnp.float32),
            pltpu.VMEM((rows, width), jnp.float32),
        ]
        + scatter_scratch
        + mlp_scratch
        + mlp_sems
        + vec_scratch
        + vec_sems
        + ChainGather.SEMS
        + [pltpu.SemaphoreType.DMA((5,))],
    )(
        row_ffn, w_gate_up, w_down, joined, attn_out, laurel_up, gains, layer_vec, pl_gate,
        pl_proj, out_grad,
    )


def sum_everywhere(place, own, arrived, sems):
    k, f = place.k, place.f
    targets = [
        place.sibling,
        (place.x_side, place.c),
        (place.y_side, place.c),
        (f, place.partner(1) * 2 + k),
        (f, place.partner(3) * 2 + k),
    ]
    return [
        remote(own.at[n], arrived.at[n], sems.at[0, n], sems.at[1, n], target)
        for n, target in enumerate(targets)
    ]


def attention_backward(
    d_attn_low, d_laurel_low, d_half, weights, kept, tables, head_gains, hidden, gains,
    other_gains, mlp_grads, mlp_land, vec_land, ident
):
    w_qkv, w_out, w_laurel = weights
    queries, keys, values, mixed, latent, projected, row_normed, row_parts = kept
    rows, width = d_half.shape
    total = 8 * rows
    query_block, key_span = 2 * rows, 768
    shard_height, vec_width = vec_land.shape[0], vec_land.shape[1] // 8
    qkv_width, laurel_width = w_qkv.shape[1], w_laurel.shape[1]
    attn_widths = (qkv_width + laurel_width, w_out.shape[1])
    scatter_scratch = ChainScatter.scratch(rows, width)
    first_late, late = 2 * EARLY_UNITS, 8 - 2 * EARLY_UNITS
    mlp_scratch = Drain.scratch(shard_height, [grad.shape[1] for grad in mlp_grads], late)
    mlp_sems = Drain.sems(len(MLP_PIECES), 2, late)
    loads = [*mlp_grads, w_out, queries, keys, values, tables, projected, w_qkv, mixed, row_normed]
    attn_scratch = Drain.scratch(shard_height, attn_widths)
    attn_sems = Drain.sems(len(ATTN_LAND), 2)
    gain_rows = other_gains.shape[0]

    def kernel(*refs):
        ins, outs, held = split_refs(refs, 23, 5, len(refs) - 28)
        (own_ref, row_pos, head_ref, hidden_ref, gains_ref, base_ref, other_ref, laurel_ref,
         vec_ref, w_laurel_ref, latent_ref) = ins[:11]
        wide_hbm, narrow_hbm = ins[11:13]
        out_ref, gain_ref, land_ref, attn_land, vec_all = outs
        (scratch, loaded, local_sems, gain_s, scat, mlp_s, mlp_m, attn_s, attn_m, vec_m, gather_m) = (
            split_refs(
                held, 9, 11, 1, 3, len(scatter_scratch), len(mlp_scratch), 3, len(attn_scratch), 3,
                3, 2,
            )
        )
        (vec_own, row_grad, d_mixed, d_keys, d_values, d_projected, qkv_grad, out_grad,
         laurel_back) = scratch
        (wide_ref, narrow_ref, w_out_ref, q_low, k_low, v_low, tables_ref, projected_ref, qkv_ref,
         mixed_ref, row_ref) = loaded
        held_gains, arrived_gains, gain_sems = gain_s
        place = Place()
        local = Local(local_sems[0])
        for src, dst in zip(ins[11:22], loaded):
            local.start(src, dst)
        greet(place, "all", True)
        gather = ChainGather(place, own_ref, row_grad, gather_m)
        scatter = ChainScatter(place, row_grad, scat)
        mlp = Drain(
            place, [wide_hbm, narrow_hbm], land_ref, MLP_PIECES, mlp_s, mlp_m, first_late, late,
            [wide_ref, narrow_ref],
        )
        attn = Drain(place, [qkv_grad, out_grad], attn_land, ATTN_LAND, attn_s, attn_m)
        vec = ChainGather(
            place, vec_own, vec_all.at[rows_at(place.f * 8 * shard_height, 8 * shard_height)],
            vec_m[:2],
        )
        plane = PlaneGather(place, vec_all, vec_m[2:])
        rounds = sum_everywhere(place, held_gains, arrived_gains, gain_sems)

        def gain_round(n):
            rounds[n].wait_recv()
            held_gains[n + 1] = held_gains[n] + arrived_gains[n]
            if n < 4:
                rounds[n + 1].start()

        gather.start()
        mlp.start(0)
        mlp.start(1)
        vec_sum = vec_ref[:, 0:vec_width].astype(jnp.float32)
        for c in range(1, 8):
            vec_sum = vec_sum + vec_ref[:, c * vec_width : (c + 1) * vec_width].astype(jnp.float32)
        vec_own[...] = vec_sum.astype(jnp.bfloat16)
        vec.start()
        d_keys[...] = jnp.zeros_like(d_keys)
        d_values[...] = jnp.zeros_like(d_values)
        held_gains[0] = other_ref[...]
        low = plain_dot(laurel_ref[...], w_laurel_ref[...])
        lanes = lax.broadcasted_iota(jnp.int32, low.shape, 1)
        d_latent = jnp.where(lanes < RANK, pltpu.roll(low, RANK, 1), 0.0).astype(jnp.bfloat16)
        laurel_back[...] = base_ref[...] + times_transposed(d_latent, w_laurel_ref[...])
        normed_low = rms_norm(hidden_ref[...].astype(jnp.float32), gains_ref[0:1]).astype(
            jnp.bfloat16
        )
        shifted = pltpu.roll(latent_ref[...].astype(jnp.float32), RANK, 1)
        up_side = jnp.where(lanes >= RANK, shifted, 0.0).astype(jnp.bfloat16)
        qkv_grad[:, qkv_width:] = (
            contract_rows(normed_low, d_latent) + contract_rows(laurel_ref[...], up_side)
        ).astype(jnp.bfloat16)
        local.wait(0, 1)
        gather.step(1)
        vec.step(1)
        mlp.middle(0)
        mlp.middle(1)
        for i in range(2, late):
            mlp.start(i)
        gather.step(2)
        vec.step(2)
        mlp.last(0)
        mlp.last(1)
        gather.step(3)
        vec.step(3)
        gather.arrive()
        vec.arrive()
        plane.start()
        local.wait(2, 3, 4, 5, 6, 7)

        @pl.loop(0, total // query_block)
        def _(n):
            here = rows_at(n * query_block, query_block)
            d_mixed[here] = plain_dot(row_grad[here], w_out_ref[...]).astype(jnp.bfloat16)

        for i in range(2, late):
            mlp.middle(i)

        @pl.loop(0, total // query_block)
        def _(d):
            here = rows_at(d * query_block, query_block)
            first_key = (d // 2) * (d - 2) * query_block
            there = rows_at(first_key, key_span)
            query, key, value, d_mix = q_low[here], k_low[there], v_low[there], d_mixed[here]
            scores = jnp.where(
                allowed_pairs(d * query_block, first_key, positions_of(row_pos[here])),
                times_transposed(query, key),
                NEG_LARGE,
            )
            exps = jnp.exp(scores - jnp.max(scores, axis=-1, keepdims=True))
            probs = exps / jnp.sum(exps, axis=-1, keepdims=True)
            d_probs = times_transposed(d_mix, value)
            inner_sum = jnp.sum(probs * d_probs, axis=-1, keepdims=True)
            d_scores = (probs * (d_probs - inner_sum)).astype(jnp.bfloat16)
            d_keys[there] += contract_rows(d_scores, query)
            d_values[there] += contract_rows(probs.astype(jnp.bfloat16), d_mix)
            cosine, sine = tables_ref[here, : HEAD // 2], tables_ref[here, HEAD // 2 :]
            d_query, d_scale = norm_back(
                projected_ref[here, :HEAD],
                head_ref[0:1],
                turn_back(plain_dot(d_scores, key), cosine, sine),
            )
            d_projected[here, :HEAD] = d_query.astype(jnp.bfloat16)
            held_gains[0, 6:7, :HEAD] += d_scale

        for i in range(2, late):
            mlp.last(i)

        @pl.loop(0, total // query_block)
        def _(n):
            here = rows_at(n * query_block, query_block)
            cosine, sine = tables_ref[here, : HEAD // 2], tables_ref[here, HEAD // 2 :]
            d_key, d_scale = norm_back(
                projected_ref[here, HEAD : 2 * HEAD],
                head_ref[1:2],
                turn_back(d_keys[here], cosine, sine),
            )
            d_projected[here, HEAD : 2 * HEAD] = d_key.astype(jnp.bfloat16)
            held_gains[0, 6:7, HEAD : 2 * HEAD] += d_scale
            d_value, _ = norm_back(projected_ref[here, 2 * HEAD :], 1.0, d_values[here])
            d_projected[here, 2 * HEAD :] = d_value.astype(jnp.bfloat16)

        quarter = width // 4
        local.wait(8, 9, 10)

        @pl.loop(0, 4)
        def _(n):
            columns = cols_at(n * quarter, quarter)
            out_grad[rows_at(n * quarter, quarter)] = contract_rows(
                row_grad[:, columns], mixed_ref[...]
            ).astype(jnp.bfloat16)

        gather.settle()
        upper = place.z // 2

        @pl.loop(0, total // query_block)
        def _(n):
            d = n * upper + (3 - n) * (1 - upper)
            here = rows_at(d * query_block, query_block)
            row_grad[here] = times_transposed(d_projected[here], qkv_ref[...]).astype(jnp.bfloat16)
            scatter.across(d).start()

        scatter.ends()

        @pl.loop(0, 4)
        def _(n):
            columns = cols_at(n * quarter, quarter)
            qkv_grad[rows_at(n * quarter, quarter), :qkv_width] = contract_rows(
                row_ref[:, columns], d_projected[...]
            ).astype(jnp.bfloat16)

        attn.start(0)
        attn.start(1)
        attn.start(2)
        attn.start(3)
        scatter.inner(0)
        plane.relay()
        attn.middle(0)
        attn.start(4)
        scatter.inner(1)
        attn.middle(1)
        attn.start(5)
        attn.last(0)
        attn.middle(2)
        attn.start(6)
        attn.last(1)
        scatter.finish(out_ref)
        d_normed = laurel_back[...] + out_ref[...]
        d_hidden, d_scale = norm_back(
            hidden_ref[...].astype(jnp.float32), gains_ref[0:1], d_normed
        )
        out_ref[...] = d_hidden
        held_gains[0, 0:1] = d_scale
        rounds[0].start()
        attn.start(7)
        for i in range(3, 8):
            attn.middle(i)
            attn.last(i - 1)
            gain_round(i - 3)
        attn.last(7)
        gain_ref[...] = held_gains[5]
        for copy in rounds:
            copy.wait_send()
        vec.settle()
        plane.finish()
        mlp.finish()
        attn.finish()

    return comm_call(
        kernel,
        ident,
        [
            jax.ShapeDtypeStruct((rows, width), jnp.float32),
            jax.ShapeDtypeStruct((gain_rows, width), jnp.float32),
            bf16(*mlp_land.shape),
            bf16(shard_height, 8 * sum(attn_widths)),
            bf16(32 * shard_height, vec_width),
        ],
        [VMEM] * 11 + [ANY] * 12,
        [VMEM, VMEM, ANY, ANY, ANY],
        [
            pltpu.VMEM((shard_height, vec_width), jnp.bfloat16),
            pltpu.VMEM((total, width), jnp.bfloat16),
            pltpu.VMEM((total, HEAD), jnp.bfloat16),
            pltpu.VMEM((total, HEAD), jnp.float32),
            pltpu.VMEM((total, HEAD), jnp.float32),
            pltpu.VMEM((total, qkv_width), jnp.bfloat16),
            pltpu.VMEM((width, attn_widths[0]), jnp.bfloat16),
            pltpu.VMEM((width, attn_widths[1]), jnp.bfloat16),
            pltpu.VMEM((rows, width), jnp.float32),
        ]
        + [pltpu.VMEM(array.shape, array.dtype) for array in loads]
        + [
            pltpu.SemaphoreType.DMA((len(loads),)),
            pltpu.VMEM((6, gain_rows, width), jnp.float32),
            pltpu.VMEM((5, gain_rows, width), jnp.float32),
            pltpu.SemaphoreType.DMA((2, 5)),
        ]
        + scatter_scratch
        + mlp_scratch
        + mlp_sems
        + attn_scratch
        + attn_sems
        + ChainGather.SEMS
        + PlaneGather.SEMS
        + ChainGather.SEMS,
        {22: 2},
    )(
        d_attn_low, row_parts, head_gains, hidden, gains, d_half, other_gains, d_laurel_low,
        vec_land, w_laurel, latent, *loads, mlp_land,
    )


def finish_outputs(mlp_land, attn_land, vec_all, d_half, d_hidden_part, attn_cols):
    height, mlp_cols = mlp_land.shape
    rows, width = d_half.shape
    model, vec_width = vec_all.shape
    per_source = attn_land.shape[1] // 8
    half = vec_width // 2
    group = QH // KVH
    kv_first, laurel_first, out_first = QH * HEAD, (QH + 2 * KVH) * HEAD, 3200

    def kernel(mlp_ref, attn_ref, vec_ref, half_ref, part_ref, *outs):
        mlp_out, attn_out, gate_out, proj_out, hidden_out = outs
        c = pl.program_id(0)
        mlp_out[...] = mlp_ref[...].astype(jnp.float32)
        gate_out[...] = vec_ref[:, :half].astype(jnp.float32)
        proj_out[...] = vec_ref[:, half:].astype(jnp.float32).T
        hidden_out[...] = half_ref[...] + part_ref[...]
        landed = attn_ref[...].astype(jnp.float32)
        attn_out[:, cols_at(c * HEAD, HEAD)] = landed[:, :HEAD]
        attn_out[:, cols_at(out_first + c * HEAD, HEAD)] = landed[:, per_source - HEAD :]

        def add(first, count, start, fresh):
            columns = cols_at(first, count)
            value = landed[:, start : start + count]

            @pl.when(fresh)
            def _():
                attn_out[:, columns] = value

            @pl.when(jnp.logical_not(fresh))
            def _():
                attn_out[:, columns] += value

        add(kv_first + c // group * HEAD, HEAD, HEAD, c % group == 0)
        add(kv_first + (KVH + c // group) * HEAD, HEAD, 2 * HEAD, c % group == 0)
        add(laurel_first, 2 * RANK, 3 * HEAD, c == 0)

    def spec(block, by_column):
        return pl.BlockSpec(block, (lambda c: (0, c)) if by_column else (lambda c: (c, 0)))

    f32 = jnp.float32
    return pl.pallas_call(
        kernel,
        grid=(8,),
        out_shape=[
            jax.ShapeDtypeStruct((height, mlp_cols), f32),
            jax.ShapeDtypeStruct((height, attn_cols), f32),
            jax.ShapeDtypeStruct((model, half), f32),
            jax.ShapeDtypeStruct((half, model), f32),
            jax.ShapeDtypeStruct((rows, width), f32),
        ],
        in_specs=[
            spec((height, mlp_cols // 8), True),
            spec((height, per_source), True),
            spec((model // 8, vec_width), False),
            spec((rows // 8, width), False),
            spec((rows // 8, width), False),
        ],
        out_specs=[
            spec((height, mlp_cols // 8), True),
            pl.BlockSpec((height, attn_cols), lambda c: (0, 0)),
            spec((model // 8, half), False),
            spec((half, model // 8), True),
            spec((rows // 8, width), False),
        ],
    )(mlp_land, attn_land, vec_all, d_half, d_hidden_part)


def per_device_split(
    hidden_in, layer_vec, positions, w_attn, w_mlp, pl_gate, pl_proj, gains, head_gains, out_grad
):
    shard_height = w_attn.shape[0]
    row_total = QH * positions.shape[0]
    lanes = jnp.arange(128, dtype=jnp.int32)[None, :]
    own_pos = jnp.where(lanes == 0, positions[:, None] // 256, positions[:, None] % 256)

    frequency = np.exp(np.arange(HEAD // 2) * (-2.0 * math.log(THETA) / HEAD))
    angles = np.arange(row_total)[:, None] * frequency[None, :]
    tables = jnp.asarray(np.concatenate([np.cos(angles), np.sin(angles)], axis=1), jnp.float32)

    (
        row_normed, w_qkv, w_out, w_laurel, row_parts, w_gate_up, w_down, row_ffn, projected,
        queries, keys, values, mixed, latent, laurel_up, attn_out, joined,
    ) = attention_forward(
        own_pos.astype(jnp.bfloat16), w_attn, w_mlp, hidden_in, gains, head_gains, tables, 1
    )
    (
        result_out, d_vector_in, d_half, d_attn_low, d_laurel_low, other_gains, mlp_land,
        vec_land, late_wide, late_narrow,
    ) = ffn_layer(
        row_ffn, w_gate_up, w_down, joined, attn_out, laurel_up, gains, layer_vec, pl_gate,
        pl_proj, out_grad, shard_height, w_mlp.shape[1], 2,
    )
    d_hidden_part, all_gains, mlp_land, attn_land, vec_all = attention_backward(
        d_attn_low,
        d_laurel_low,
        d_half,
        (w_qkv, w_out, w_laurel),
        (queries, keys, values, mixed, latent, projected, row_normed, row_parts),
        tables,
        head_gains,
        hidden_in,
        gains,
        other_gains,
        (late_wide, late_narrow),
        mlp_land,
        vec_land,
        3,
    )
    grad_w_mlp, grad_w_attn, grad_gate_all, grad_proj_all, grad_hidden = finish_outputs(
        mlp_land, attn_land, vec_all, d_half, d_hidden_part, w_attn.shape[1]
    )
    grad_gains, grad_heads = all_gains[:6], all_gains[6, : 2 * HEAD].reshape(2, HEAD)
    return (
        result_out,
        grad_hidden,
        d_vector_in,
        grad_w_attn,
        grad_w_mlp,
        grad_gate_all,
        grad_proj_all,
        grad_gains,
        grad_heads,
    )


def solution(mesh):
    fits = mesh.shape["ctx"] == QH and mesh.shape["fsdp"] == 4
    body = per_device_split if fits else per_device
    return jax.shard_map(
        body,
        mesh=mesh,
        in_specs=(
            P(("fsdp", "ctx"), None),
            P(("fsdp", "ctx"), None),
            P(("fsdp", "ctx")),
            P(("fsdp", "ctx"), None),
            P(("fsdp", "ctx"), None),
            P(),
            P(),
            P(),
            P(),
            P(("fsdp", "ctx"), None),
        ),
        out_specs=(
            P(("fsdp", "ctx"), None),
            P(("fsdp", "ctx"), None),
            P(("fsdp", "ctx"), None),
            P(("fsdp", "ctx"), None),
            P(("fsdp", "ctx"), None),
            P(),
            P(),
            P(),
            P(),
        ),
        check_vma=False,
    )
```

```python
import math

import jax
import jax.numpy as jnp
import numpy as np
from jax import lax
from jax.experimental import pallas as pl
from jax.experimental.pallas import tpu as pltpu
from jax.sharding import PartitionSpec as P

QH = 8
KVH = 2
HEAD = 256
RANK = 64
WINDOW = 512


EPSILON = 1e-06
THETA = 10000.0
NEG_LARGE = -1e30


def passed_along(block, axis, distance):
    devices = range(lax.axis_size(axis))
    route = [(i - distance, i) for i in devices if i - distance in devices]
    return lax.ppermute(block, axis, route)


def rms_norm(values, scale_vec):
    return (
        values * lax.rsqrt(jnp.mean(values * values, axis=-1, keepdims=True) + EPSILON) * scale_vec
    )


def value_norm(values):
    return rms_norm(values, 1.0)


def rotary(values, positions):
    half_size = values.shape[-1] // 2
    frequency = jnp.exp(
        jnp.arange(half_size, dtype=jnp.float32) * (-2.0 * math.log(THETA) / values.shape[-1])
    )
    angles = positions.astype(jnp.float32)[:, None] * frequency[None, :]
    cosine = jnp.cos(angles)[:, None, :]
    sine_part = jnp.sin(angles)[:, None, :]
    first_half = values[..., :half_size]
    second_half = values[..., half_size:]
    return jnp.concatenate(
        [
            first_half * cosine - second_half * sine_part,
            second_half * cosine + first_half * sine_part,
        ],
        axis=-1,
    )


def plain_dot(left_side, right_side):
    return jnp.dot(left_side, right_side, preferred_element_type=jnp.float32)


def times_transposed(left_side, right_side):
    return lax.dot_general(
        left_side, right_side, (((1,), (1,)), ((), ())), preferred_element_type=jnp.float32
    )


def contract_rows(left_side, right_side):
    return lax.dot_general(
        left_side, right_side, (((0,), (0,)), ((), ())), preferred_element_type=jnp.float32
    )


def activate(gate_up_val):
    half_cols = gate_up_val.shape[1] // 2
    return jax.nn.gelu(gate_up_val[:, :half_cols], approximate=True) * gate_up_val[:, half_cols:]


def vec_mix(gate_val, vector_val):
    return jax.nn.gelu(gate_val, approximate=True) * vector_val


def per_device(
    hidden_in, layer_vec, positions, w_attn, w_mlp, pl_gate, pl_proj, gains, head_gains, out_grad
):
    row_count = hidden_in.shape[0]
    model_width = hidden_in.shape[1]
    q_width = QH * HEAD
    kv_width = KVH * HEAD
    in_cols = q_width + 2 * kv_width + RANK
    group_size = QH // KVH
    ff_width = w_mlp.shape[1] // 3
    shard_height = w_mlp.shape[0]
    fsdp_count = lax.axis_size("fsdp")
    ctx_count = lax.axis_size("ctx")
    quarter = ff_width // fsdp_count

    def permute_cols(matrix):
        return (
            matrix.reshape(-1, fsdp_count, ctx_count, shard_height)
            .transpose(0, 2, 1, 3)
            .reshape(-1, model_width)
        )

    def restore_cols(matrix):
        return (
            matrix.reshape(-1, ctx_count, fsdp_count, shard_height)
            .transpose(0, 2, 1, 3)
            .reshape(-1, model_width)
        )

    def qk_prep(raw_heads, scale_vec):
        return rotary(rms_norm(raw_heads, scale_vec), positions)

    hidden = hidden_in.astype(jnp.float32)
    normed_in = rms_norm(hidden, gains[0])
    normed_low = normed_in.astype(jnp.bfloat16)
    projected = plain_dot(
        normed_low, lax.all_gather(w_attn[:, :in_cols], ("fsdp", "ctx"), axis=0, tiled=True)
    )
    q_raw = projected[:, :q_width].reshape(row_count, QH, HEAD)
    k_raw = projected[:, q_width : q_width + kv_width].reshape(row_count, KVH, HEAD)
    v_raw = projected[:, q_width + kv_width : q_width + 2 * kv_width].reshape(row_count, KVH, HEAD)
    latent = projected[:, q_width + 2 * kv_width :].astype(jnp.bfloat16)
    queries = qk_prep(q_raw, head_gains[0]).astype(jnp.bfloat16)
    keys_own = qk_prep(k_raw, head_gains[1]).astype(jnp.bfloat16)
    values_own = value_norm(v_raw).astype(jnp.bfloat16)
    kv_own = jnp.concatenate(
        [keys_own.reshape(row_count, kv_width), values_own.reshape(row_count, kv_width)], axis=1
    )
    hop_count = (WINDOW - 1) // row_count + 1
    earlier = []
    moving = kv_own
    for step_back in range(hop_count):
        moving = passed_along(moving, "ctx", 1)
        earlier.append(moving)
    kv_all = jnp.concatenate(earlier[::-1] + [kv_own], axis=0)
    span_rows = kv_all.shape[0]
    keys_all = kv_all[:, :kv_width].reshape(span_rows, KVH, HEAD)
    values_all = kv_all[:, kv_width:].reshape(span_rows, KVH, HEAD)
    grouped = queries.reshape(row_count, KVH, group_size, HEAD)
    distance = (
        jnp.arange(row_count, dtype=jnp.int32)[:, None]
        + hop_count * row_count
        - jnp.arange(span_rows, dtype=jnp.int32)[None, :]
    )
    allowed = (distance >= 0) & (distance <= jnp.minimum(positions, WINDOW - 1)[:, None])
    scores = jnp.einsum("qgrd,kgd->grqk", grouped, keys_all, preferred_element_type=jnp.float32)
    scores = jnp.where(allowed[None, None], scores, NEG_LARGE)
    row_max = jnp.max(scores, axis=-1, keepdims=True)
    exp_scores = jnp.exp(scores - row_max)
    row_sum = jnp.sum(exp_scores, axis=-1, keepdims=True)
    log_total = row_max + jnp.log(row_sum)
    probs_low = (exp_scores / row_sum).astype(jnp.bfloat16)
    mixed = jnp.einsum("grqk,kgd->qgrd", probs_low, values_all, preferred_element_type=jnp.float32)
    mixed = mixed.reshape(row_count, q_width).astype(jnp.bfloat16)
    shard_rows = lax.all_gather(w_attn[:, in_cols:], ("fsdp", "ctx"), axis=0, tiled=True)
    laurel_part = times_transposed(latent, shard_rows[:, :RANK])
    attn_part = times_transposed(mixed, shard_rows[:, RANK:])
    out_pair = jnp.stack([laurel_part, attn_part], axis=1)
    laurel_up = out_pair[:, 0]
    attn_out = out_pair[:, 1]
    laurel_res = normed_in + rms_norm(laurel_up, gains[1])
    after_attn = hidden + rms_norm(attn_out, gains[2])
    joined = (after_attn + laurel_res) / math.sqrt(2.0)
    ffn_low = rms_norm(joined, gains[3]).astype(jnp.bfloat16)
    sent_rows = w_mlp.reshape(shard_height, 3, fsdp_count, quarter)
    sent_tokens = jnp.broadcast_to(
        ffn_low[:, None, None, :], (row_count, 1, fsdp_count, model_width)
    )
    got_rows, got_tokens = (
        lax.all_to_all(sent_rows, "fsdp", split_axis=2, concat_axis=0, tiled=True),
        lax.all_to_all(sent_tokens, "fsdp", split_axis=2, concat_axis=0, tiled=True),
    )
    quarter_rows = lax.all_gather(got_rows, "ctx", axis=0, tiled=True).reshape(
        model_width, 3, quarter
    )
    w_gate_up = quarter_rows[:, :2].reshape(model_width, 2 * quarter)
    w_down = quarter_rows[:, 2]
    ffn_perm = permute_cols(got_tokens.reshape(fsdp_count * row_count, model_width))
    gate_up = plain_dot(ffn_perm, w_gate_up)
    activated = activate(gate_up).astype(jnp.bfloat16)
    ffn_out = lax.psum_scatter(
        restore_cols(times_transposed(activated, w_down)), "fsdp", scatter_dimension=0, tiled=True
    )
    after_ffn = joined + rms_norm(ffn_out, gains[4])
    after_low = after_ffn.astype(jnp.bfloat16)
    vec_gate = plain_dot(after_low, pl_gate)
    vector_in = layer_vec.astype(jnp.float32)
    vec_mixed = vec_mix(vec_gate, vector_in).astype(jnp.bfloat16)
    vec_out = plain_dot(vec_mixed, pl_proj)
    result_out = after_ffn + rms_norm(vec_out, gains[5])
    upstream = out_grad.astype(jnp.float32)
    unused_out, vec_norm_back = jax.vjp(rms_norm, vec_out, gains[5])
    d_vec_out, d_gain_vec = vec_norm_back(upstream)
    d_vec_out_low = d_vec_out.astype(jnp.bfloat16)
    d_vec_mixed = times_transposed(d_vec_out_low, pl_proj)
    grad_pl_proj = contract_rows(vec_mixed, d_vec_out_low)
    unused_out, mix_back = jax.vjp(vec_mix, vec_gate, vector_in)
    d_vec_gate, d_vector_in = mix_back(d_vec_mixed)
    d_vec_gate_low = d_vec_gate.astype(jnp.bfloat16)
    grad_after = upstream + times_transposed(d_vec_gate_low, pl_gate)
    grad_pl_gate = contract_rows(after_low, d_vec_gate_low)
    unused_out, ffn_norm_back = jax.vjp(rms_norm, ffn_out, gains[4])
    d_ffn_out, d_gain_ffn = ffn_norm_back(grad_after)
    d_ffn_low = d_ffn_out.astype(jnp.bfloat16)
    unused_out, act_back = jax.vjp(activate, gate_up)
    d_ffn_all = lax.all_gather(d_ffn_low, "fsdp", axis=0, tiled=True)
    d_ffn_perm = permute_cols(d_ffn_all)
    d_activated = plain_dot(d_ffn_perm, w_down)
    d_gate_up = act_back(d_activated)[0].astype(jnp.bfloat16)
    d_ffn_in = lax.psum_scatter(
        restore_cols(times_transposed(d_gate_up, w_gate_up)).astype(jnp.bfloat16),
        "fsdp",
        scatter_dimension=0,
        tiled=True,
    ).astype(jnp.float32)
    summed = lax.psum_scatter(
        jnp.concatenate(
            [contract_rows(ffn_perm, d_gate_up), contract_rows(d_ffn_perm, activated)], axis=1
        ).astype(jnp.bfloat16),
        "ctx",
        scatter_dimension=0,
        tiled=True,
    ).astype(jnp.float32)
    grad_w_mlp = (
        lax.all_to_all(
            summed.reshape(fsdp_count * shard_height, 3, 1, quarter).astype(jnp.bfloat16),
            "fsdp",
            split_axis=0,
            concat_axis=2,
            tiled=True,
        )
        .astype(jnp.float32)
        .reshape(shard_height, 3 * ff_width)
    )
    unused_out, pre_norm_back = jax.vjp(rms_norm, joined, gains[3])
    d_joined_part, d_gain_pre = pre_norm_back(d_ffn_in)
    d_joined = grad_after + d_joined_part
    d_half = d_joined / math.sqrt(2.0)
    unused_out, laurel_norm_back = jax.vjp(rms_norm, laurel_up, gains[1])
    d_laurel_up, d_gain_laurel = laurel_norm_back(d_half)
    unused_out, attn_norm_back = jax.vjp(rms_norm, attn_out, gains[2])
    d_attn_out, d_gain_attn = attn_norm_back(d_half)
    d_laurel_low = d_laurel_up.astype(jnp.bfloat16)
    d_attn_low = d_attn_out.astype(jnp.bfloat16)
    shard_rows = lax.all_gather(w_attn[:, in_cols:], ("fsdp", "ctx"), axis=0, tiled=True)
    d_latent = plain_dot(d_laurel_low, shard_rows[:, :RANK])
    d_mixed = plain_dot(d_attn_low, shard_rows[:, RANK:])
    d_grouped = d_mixed.astype(jnp.bfloat16).reshape(row_count, KVH, group_size, HEAD)
    again = jnp.einsum("qgrd,kgd->grqk", grouped, keys_all, preferred_element_type=jnp.float32)
    again = jnp.where(allowed[None, None], again, NEG_LARGE)
    probs = jnp.exp(again - log_total)
    d_probs = jnp.einsum(
        "qgrd,kgd->grqk", d_grouped, values_all, preferred_element_type=jnp.float32
    )
    inner_sum = jnp.sum(probs * d_probs, axis=-1, keepdims=True)
    d_scores = (probs * (d_probs - inner_sum)).astype(jnp.bfloat16)
    d_queries = jnp.einsum(
        "grqk,kgd->qgrd", d_scores, keys_all, preferred_element_type=jnp.float32
    ).reshape(row_count, QH, HEAD)
    d_keys_all = jnp.einsum("grqk,qgrd->kgd", d_scores, grouped, preferred_element_type=jnp.float32)
    d_values_all = jnp.einsum(
        "grqk,qgrd->kgd", probs.astype(jnp.bfloat16), d_grouped, preferred_element_type=jnp.float32
    )
    d_kv_all = jnp.concatenate(
        [d_keys_all.reshape(span_rows, kv_width), d_values_all.reshape(span_rows, kv_width)], axis=1
    )
    returned = d_kv_all[:row_count]
    for step_back in range(1, hop_count + 1):
        returned = (
            passed_along(returned.astype(jnp.bfloat16), "ctx", -1).astype(returned.dtype)
            + d_kv_all[step_back * row_count : (step_back + 1) * row_count]
        )
    d_keys_own = returned[:, :kv_width].reshape(row_count, KVH, HEAD)
    d_values_own = returned[:, kv_width:].reshape(row_count, KVH, HEAD)
    unused_out, query_back = jax.vjp(qk_prep, q_raw, head_gains[0])
    d_q_raw, d_head_query = query_back(d_queries)
    unused_out, key_back = jax.vjp(qk_prep, k_raw, head_gains[1])
    d_k_raw, d_head_key = key_back(d_keys_own)
    unused_out, value_back = jax.vjp(value_norm, v_raw)
    d_v_raw = value_back(d_values_own)[0]
    d_projected = jnp.concatenate(
        [
            d_q_raw.reshape(row_count, q_width),
            d_k_raw.reshape(row_count, kv_width),
            d_v_raw.reshape(row_count, kv_width),
            d_latent,
        ],
        axis=1,
    ).astype(jnp.bfloat16)
    d_normed_part = times_transposed(
        d_projected, lax.all_gather(w_attn[:, :in_cols], ("fsdp", "ctx"), axis=0, tiled=True)
    )
    unused_out, input_norm_back = jax.vjp(rms_norm, hidden, gains[0])
    d_hidden_part, d_gain_input = input_norm_back(d_half + d_normed_part)
    grad_hidden = d_half + d_hidden_part
    grad_w_attn = lax.psum_scatter(
        jnp.concatenate(
            [
                contract_rows(normed_low, d_projected),
                contract_rows(d_laurel_low, latent),
                contract_rows(d_attn_low, mixed),
            ],
            axis=1,
        ),
        ("fsdp", "ctx"),
        scatter_dimension=0,
        tiled=True,
    )
    gain_rows = jnp.stack(
        [d_gain_input, d_gain_laurel, d_gain_attn, d_gain_pre, d_gain_ffn, d_gain_vec]
    )
    head_rows = jnp.stack([d_head_query, d_head_key])
    grad_gains, grad_heads, grad_gate_all, grad_proj_all = lax.psum(
        (gain_rows, head_rows, grad_pl_gate, grad_pl_proj), ("fsdp", "ctx")
    )
    return (
        result_out.astype(jnp.bfloat16),
        grad_hidden,
        d_vector_in,
        grad_w_attn,
        grad_w_mlp,
        grad_gate_all,
        grad_proj_all,
        grad_gains,
        grad_heads,
    )

MESH = pl.DeviceIdType.MESH
VMEM_LIMIT = 63 * 1024 * 1024
ORDER = ((0, 0), (0, 1), (1, 0), (1, 1), (2, 0), (2, 1), (3, 0), (3, 1))


class Place:
    def __init__(self):
        self.f = lax.axis_index("fsdp")
        self.c = lax.axis_index("ctx")
        self.z = self.c // 2
        self.k = self.c % 2
        self.x_side = self.f + 1 - 2 * (self.f % 2)
        self.y_side = (self.f + 2) % 4
        self.diag = 3 - self.f
        self.sibling = (self.f, self.c + 1 - 2 * self.k)
        self.up = (self.f, self.c + 2)
        self.down = (self.f, self.c - 2)
        self.has_up = self.z < 3
        self.has_down = self.z > 0

    def partner(self, which):
        z = self.z
        return (z, z + 1 - 2 * (z % 2), (z + 2) % 4, 3 - z)[which]

    def peer(self, i):
        which, other = ORDER[i]
        return self.partner(which) * 2 + (self.k + other) % 2


def rows_at(start, count):
    return pl.ds(pl.multiple_of(start, 16), count)


def cols_at(start, count):
    if isinstance(start, int):
        return pl.ds(start, count)
    return pl.ds(pl.multiple_of(start, 128), count)


def remote(src, dst, send_sem, recv_sem, target):
    return pltpu.make_async_remote_copy(
        src_ref=src,
        dst_ref=dst,
        send_sem=send_sem,
        recv_sem=recv_sem,
        device_id=target,
        device_id_type=MESH,
    )


def greet(place, line, plane):
    barrier = pltpu.get_barrier_semaphore()
    count = 0

    def tell(target):
        pl.semaphore_signal(barrier, inc=1, device_id=target, device_id_type=MESH)

    if line == "all":
        for i in range(1, 8):
            tell((place.f, place.peer(i)))
        count += 7
    elif line == "chain":
        tell(place.sibling)
        for distance in (1, 3):
            tell((place.f, (place.z + distance) % 4 * 2 + place.k))
        count += 3
    if plane:
        tell((place.x_side, place.c))
        tell((place.y_side, place.c))
        count += 2
    pl.semaphore_wait(barrier, count)


class ChainGather:
    SEMS = [pltpu.SemaphoreType.DMA((2, 10)), pltpu.SemaphoreType.DMA((1,))]

    def __init__(self, place, own, out, sems, stride=None, offset=0):
        self.place, self.own, self.out = place, own, out
        self.sems, self.local_sem = sems
        self.rows = own.shape[0]
        self.stride, self.offset = stride or self.rows, offset

    def block(self, origin_z, core=None):
        core = self.place.k if core is None else core
        return self.out.at[
            rows_at((origin_z * 2 + core) * self.stride + self.offset, self.rows)
        ]

    def copy(self, src, dst, index, target):
        return remote(src, dst, self.sems.at[0, index], self.sems.at[1, index], target)

    def local(self):
        return pltpu.make_async_copy(self.own, self.block(self.place.z), self.local_sem.at[0])

    def upward(self, step):
        src = self.own if step == 0 else self.block(self.place.z - step)
        return self.copy(src, self.block(self.place.z - step), step, self.place.up)

    def downward(self, step):
        src = self.own if step == 0 else self.block(self.place.z + step)
        return self.copy(src, self.block(self.place.z + step), 3 + step, self.place.down)

    def across(self, origin_z, own=False):
        src = self.own if own else self.block(origin_z)
        return self.copy(src, self.block(origin_z), 6 + origin_z, self.place.sibling)

    def start(self):
        place = self.place

        @pl.when(place.has_up)
        def _():
            self.upward(0).start()

        @pl.when(place.has_down)
        def _():
            self.downward(0).start()

        self.across(place.z, True).start()
        self.local().start()

    def step(self, step):
        place = self.place

        @pl.when(place.z - step >= 0)
        def _():
            self.copy(self.own, self.block(place.z - step), step - 1, place.up).wait_recv()
            if step < 3:

                @pl.when(place.has_up)
                def _():
                    self.upward(step).start()

            self.across(place.z - step).start()

        @pl.when(place.z + step <= 3)
        def _():
            self.copy(self.own, self.block(place.z + step), 3 + step - 1, place.down).wait_recv()
            if step < 3:

                @pl.when(place.has_down)
                def _():
                    self.downward(step).start()

            self.across(place.z + step).start()

    def finish(self):
        self.arrive()
        self.settle()

    def from_sibling(self, origin):
        return self.copy(
            self.own, self.block(origin, 1 - self.place.k), 6 + origin, self.place.sibling
        )

    def near_first(self, n):
        upper = self.place.z // 2
        near = (1 - upper) * self.place.z + upper * (3 - self.place.z)
        late = n // 2
        chip = late * n + (1 - late) * ((near + n) % 2)
        return (1 - upper) * chip + upper * (3 - chip)

    def arrive(self):
        self.local().wait()
        for origin in range(4):
            self.from_sibling(origin).wait_recv()

    def settle(self):
        place = self.place
        for origin in range(4):
            self.from_sibling(origin).wait_send()
        for step in range(3):

            @pl.when((place.z - step >= 0) & place.has_up)
            def _(step=step):
                self.upward(step).wait_send()

            @pl.when((place.z + step <= 3) & place.has_down)
            def _(step=step):
                self.downward(step).wait_send()


class ChainScatter:
    PARTS = 2

    @staticmethod
    def scratch(rows, cols):
        return [
            pltpu.VMEM((4, rows, cols), jnp.bfloat16),
            pltpu.VMEM((6, rows, cols), jnp.bfloat16),
            pltpu.SemaphoreType.DMA((2, 4 + 6 * ChainScatter.PARTS)),
        ]

    def __init__(self, place, partial, scratch):
        self.place, self.partial = place, partial
        self.from_sibling, self.moving, self.sems = scratch
        self.rows = partial.shape[0] // 8

    def block(self, origin_z, core):
        return self.partial.at[rows_at((origin_z * 2 + core) * self.rows, self.rows)]

    def across(self, dest):
        return remote(
            self.block(dest, 1 - self.place.k),
            self.from_sibling.at[dest],
            self.sems.at[0, dest],
            self.sems.at[1, dest],
            self.place.sibling,
        )

    def moved(self, slot, part, target):
        count = self.rows // self.PARTS
        ref = self.moving.at[slot, pl.ds(part * count, count)]
        index = 4 + slot * self.PARTS + part
        return remote(ref, ref, self.sems.at[0, index], self.sems.at[1, index], target)

    def start(self):
        for dest in (3, 0, 2, 1):
            self.across(dest).start()

    def pair_sum(self, dest, part):
        count = self.rows // self.PARTS
        start = (dest * 2 + self.place.k) * self.rows + part * count
        return self.partial[rows_at(start, count)].astype(jnp.float32) + self.from_sibling[
            dest, part * count : (part + 1) * count
        ].astype(jnp.float32)

    def pass_on(self, dest, upward, inner=False, parts=(0, 1)):
        place = self.place
        slot = dest - 1 if upward else 3 + dest
        target = place.up if upward else place.down
        count = self.rows // self.PARTS
        if parts[0] == 0:
            self.across(dest).wait_recv()
        for part in parts:
            rows = slice(part * count, (part + 1) * count)
            total = self.pair_sum(dest, part)
            if inner:
                self.moved(slot, part, target).wait_recv()
                total = total + self.moving[slot, rows].astype(jnp.float32)
            self.moving[slot, rows] = total.astype(jnp.bfloat16)
            self.moved(slot, part, target).start()

    def ends_after(self, n):
        z = self.place.z

        @pl.when((n > 0) & (z == 0))
        def _():
            self.pass_on(4 - n, True)

        @pl.when((n > 0) & (z == 3))
        def _():
            self.pass_on(n - 1, False)

    def ends(self, parts=(0, 1)):
        z = self.place.z

        @pl.when(z == 0)
        def _():
            for dest in (3, 2, 1):
                self.pass_on(dest, True, False, parts)

        @pl.when(z == 3)
        def _():
            for dest in (0, 1, 2):
                self.pass_on(dest, False, False, parts)

    def inner(self, i, parts=(0, 1)):
        z = self.place.z

        @pl.when(z == 1)
        def _():
            if i == 0:
                self.pass_on(3, True, True, parts)
            else:
                self.pass_on(0, False, True, parts)
                self.pass_on(2, True, True, parts)

        @pl.when(z == 2)
        def _():
            if i == 0:
                self.pass_on(0, False, True, parts)
            else:
                self.pass_on(3, True, True, parts)
                self.pass_on(1, False, True, parts)

    def late_ends_after(self, n):
        z = self.place.z

        @pl.when((n > 1) & (z == 0))
        def _():
            self.pass_on(n - 1, True)

        @pl.when((n > 1) & (z == 3))
        def _():
            self.pass_on(4 - n, False)

    def late_inner(self, i):
        z = self.place.z

        @pl.when(z == 1)
        def _():
            dest = (2, 3, 0)[i]
            self.pass_on(dest, dest > 1, True)

        @pl.when(z == 2)
        def _():
            dest = (1, 0, 3)[i]
            self.pass_on(dest, dest > 1, True)

    def finish(self, out):
        self.total(out)
        self.settle()

    def total(self, out, parts=(0, 1)):
        place = self.place
        count = self.rows // self.PARTS
        for dest in range(4):

            @pl.when(place.z == dest)
            def _(dest=dest):
                if parts[0] == 0:
                    self.across(dest).wait_recv()
                for part in parts:
                    rows = slice(part * count, (part + 1) * count)
                    total = self.pair_sum(dest, part)
                    if dest > 0:
                        self.moved(dest - 1, part, place.up).wait_recv()
                        total = total + self.moving[dest - 1, rows].astype(jnp.float32)
                    if dest < 3:
                        self.moved(3 + dest, part, place.down).wait_recv()
                        total = total + self.moving[3 + dest, rows].astype(jnp.float32)
                    out[rows] = total

    def settle(self):
        place = self.place
        for dest in range(4):
            self.across(dest).wait_send()
        for i in range(3):
            top, bottom = 3 - i, i
            for part in range(self.PARTS):

                @pl.when(place.z < top)
                def _(top=top, part=part):
                    self.moved(top - 1, part, place.up).wait_send()

                @pl.when(place.z > bottom)
                def _(bottom=bottom, part=part):
                    self.moved(3 + bottom, part, place.down).wait_send()


class Spread:
    @staticmethod
    def sems(pieces, outs):
        return [
            pltpu.SemaphoreType.DMA((2, 8, pieces)),
            pltpu.SemaphoreType.DMA((2, 4, 8, outs)),
        ]

    def __init__(self, place, weight, outs, pieces, sems):
        self.place, self.weight, self.outs, self.pieces = place, weight, outs, pieces
        self.swap_sems, self.plane_sems = sems
        self.rows = weight.shape[0]

    def spot(self, f, c):
        return (f * 8 + c) * self.rows

    def swap(self, i, p, origin):
        column, width, out, out_column = self.pieces[p]
        peer = self.place.peer(i)
        src = self.weight.at[:, cols_at(column(peer), width)]
        dst = self.outs[out].at[
            rows_at(self.spot(self.place.f, origin), self.rows), pl.ds(out_column, width)
        ]
        if i == 0:
            return pltpu.make_async_copy(src, dst, self.swap_sems.at[0, 0, p])
        return remote(
            src,
            dst,
            self.swap_sems.at[0, i, p],
            self.swap_sems.at[1, i, p],
            (self.place.f, peer),
        )

    def whole(self, f, c, out):
        return self.outs[out].at[rows_at(self.spot(f, c), self.rows)]

    def part(self, f, c, out, half):
        count = self.rows // 2
        return self.outs[out].at[rows_at(self.spot(f, c) + half * count, count)]

    def plane(self, kind, i, out, ref, target):
        return remote(
            ref,
            ref,
            self.plane_sems.at[0, kind, i, out],
            self.plane_sems.at[1, kind, i, out],
            (target, self.place.c),
        )

    def start(self, first=0, last=8):
        for i in range(first, last):
            for p in range(len(self.pieces)):
                self.swap(i, p, self.place.c).start()

    def forward(self, i):
        place = self.place
        origin = place.peer(i)
        for p in range(len(self.pieces)):
            copy = self.swap(i, p, origin)
            if i == 0:
                copy.wait()
            else:
                copy.wait_recv()
        for out in range(len(self.outs)):
            ref = self.whole(place.f, origin, out)
            self.plane(0, i, out, ref, place.x_side).start()
            self.plane(1, i, out, ref, place.y_side).start()

    def relay(self, i):
        place = self.place
        origin = place.peer(i)
        for out in range(len(self.outs)):
            self.plane(0, i, out, self.whole(place.x_side, origin, out), place.x_side).wait_recv()
            self.plane(2, i, out, self.part(place.x_side, origin, out, 0), place.y_side).start()
            self.plane(1, i, out, self.whole(place.y_side, origin, out), place.y_side).wait_recv()
            self.plane(3, i, out, self.part(place.y_side, origin, out, 1), place.x_side).start()

    def finish(self, first=0, last=8):
        self.arrive(first, last)
        self.settle(first, last)

    def arrive(self, first=0, last=8):
        place = self.place
        for i in range(first, last):
            origin = place.peer(i)
            for out in range(len(self.outs)):
                self.plane(
                    2, i, out, self.part(place.diag, origin, out, 0), place.y_side
                ).wait_recv()
                self.plane(
                    3, i, out, self.part(place.diag, origin, out, 1), place.x_side
                ).wait_recv()

    def settle(self, first=0, last=8):
        place = self.place
        for i in range(first, last):
            origin = place.peer(i)
            if i:
                for p in range(len(self.pieces)):
                    self.swap(i, p, place.c).wait_send()
            for out in range(len(self.outs)):
                own = self.whole(place.f, origin, out)
                self.plane(0, i, out, own, place.x_side).wait_send()
                self.plane(1, i, out, own, place.y_side).wait_send()
                half = self.part(place.f, origin, out, 0)
                self.plane(2, i, out, half, place.y_side).wait_send()
                self.plane(3, i, out, half, place.x_side).wait_send()


class PlaneGather:
    SEMS = [pltpu.SemaphoreType.DMA((2, 4))]

    def __init__(self, place, out, sems):
        self.place, self.out = place, out
        self.sems = sems[0]
        self.rows = out.shape[0] // 4

    def copy(self, kind, f, target):
        count = self.rows // 2 if kind > 1 else self.rows
        start = f * self.rows + (count if kind == 3 else 0)
        ref = self.out.at[rows_at(start, count)]
        return remote(
            ref, ref, self.sems.at[0, kind], self.sems.at[1, kind], (target, self.place.c)
        )

    def start(self):
        place = self.place
        self.copy(0, place.f, place.x_side).start()
        self.copy(1, place.f, place.y_side).start()

    def relay(self):
        place = self.place
        self.copy(0, place.x_side, place.x_side).wait_recv()
        self.copy(2, place.x_side, place.y_side).start()
        self.copy(1, place.y_side, place.y_side).wait_recv()
        self.copy(3, place.y_side, place.x_side).start()

    def finish(self):
        place = self.place
        self.copy(2, place.diag, place.y_side).wait_recv()
        self.copy(3, place.diag, place.x_side).wait_recv()
        self.copy(0, place.f, place.x_side).wait_send()
        self.copy(1, place.f, place.y_side).wait_send()
        self.copy(2, place.x_side, place.y_side).wait_send()
        self.copy(3, place.y_side, place.x_side).wait_send()


DRAIN_ORDER = (0, 1, 4, 5, 2, 3, 6, 7)


class Drain:
    @staticmethod
    def scratch(rows, widths, peers=8):
        half = rows // 2
        lists = []
        for width in widths:
            lists += [
                pltpu.VMEM((2, peers, 2, half, width), jnp.bfloat16),
                pltpu.VMEM((2, peers, half, width), jnp.bfloat16),
            ]
        return lists

    @staticmethod
    def sems(pieces, outs, peers=8):
        return [
            pltpu.SemaphoreType.DMA((2, 2, peers, 2, outs)),
            pltpu.SemaphoreType.DMA((2, 2, peers, outs)),
            pltpu.SemaphoreType.DMA((2, peers, pieces, 2)),
        ]

    def __init__(self, place, grads, land, pieces, scratch, sems, base=0, peers=8, adds=None):
        self.place, self.grads, self.land, self.pieces = place, grads, land, pieces
        self.adds = adds or grads
        self.first = scratch[0::2]
        self.second = scratch[1::2]
        self.first_sems, self.second_sems, self.swap_sems = sems
        self.rows = land.shape[0]
        self.half = self.rows // 2
        self.units = grads[0].shape[0] < 32 * self.rows or peers < 8
        self.base, self.peers = base, peers

    def peer(self, i):
        return self.place.peer(DRAIN_ORDER[self.base + i])

    def part(self, g, f, i, half, adds=False):
        refs = self.adds if adds else self.grads
        peer = self.peer(i)
        if self.units:
            start = (i // 2 * 8 + f * 2 + peer % 2) * self.rows + half * self.half
            return refs[g].at[rows_at(start, self.half)]
        return refs[g].at[rows_at((f * 8 + peer) * self.rows + half * self.half, self.half)]

    def sides(self, axis):
        place = self.place
        return (place.x_side, place.y_side) if axis == 0 else (place.y_side, place.x_side)

    def first_copy(self, axis, i, which, g):
        near, _ = self.sides(axis)
        f = near if which == 0 else self.place.diag
        return remote(
            self.part(g, f, i, axis),
            self.first[g].at[axis, i, which],
            self.first_sems.at[0, axis, i, which, g],
            self.first_sems.at[1, axis, i, which, g],
            (near, self.place.c),
        )

    def second_copy(self, axis, i, g):
        _, far = self.sides(axis)
        return remote(
            self.first[g].at[axis, i, 1],
            self.second[g].at[axis, i],
            self.second_sems.at[0, axis, i, g],
            self.second_sems.at[1, axis, i, g],
            (far, self.place.c),
        )

    def swap(self, i, p, half, origin):
        column, width, g, g_column = self.pieces[p]
        src = self.first[g].at[half, i, 0, :, pl.ds(g_column, width)]
        dst = self.land.at[pl.ds(half * self.half, self.half), cols_at(column(origin), width)]
        if self.base + i == 0:
            return pltpu.make_async_copy(src, dst, self.swap_sems.at[0, i, p, half])
        return remote(
            src,
            dst,
            self.swap_sems.at[0, i, p, half],
            self.swap_sems.at[1, i, p, half],
            (self.place.f, self.peer(i)),
        )

    def start(self, i):
        for g in range(len(self.grads)):
            for which in (1, 0):
                for axis in range(2):
                    self.first_copy(axis, i, which, g).start()

    def middle(self, i):
        place = self.place
        for g in range(len(self.grads)):
            for axis in range(2):
                _, far = self.sides(axis)
                self.first_copy(axis, i, 1, g).wait_recv()
                mine = self.part(g, far, i, axis, True)
                self.first[g][axis, i, 1] = (
                    mine[...].astype(jnp.float32) + self.first[g][axis, i, 1].astype(jnp.float32)
                ).astype(jnp.bfloat16)
                self.second_copy(axis, i, g).start()

    def last(self, i):
        place = self.place
        for g in range(len(self.grads)):
            for axis in range(2):
                self.first_copy(axis, i, 0, g).wait_recv()
                self.second_copy(axis, i, g).wait_recv()
                mine = self.part(g, place.f, i, axis, True)
                self.first[g][axis, i, 0] = (
                    mine[...].astype(jnp.float32)
                    + self.first[g][axis, i, 0].astype(jnp.float32)
                    + self.second[g][axis, i].astype(jnp.float32)
                ).astype(jnp.bfloat16)
        for p in range(len(self.pieces)):
            for half in range(2):
                self.swap(i, p, half, place.c).start()

    def finish(self):
        place = self.place
        for i in range(self.peers):
            for p in range(len(self.pieces)):
                for half in range(2):
                    copy = self.swap(i, p, half, self.peer(i))
                    if self.base + i == 0:
                        copy.wait()
                    else:
                        copy.wait_recv()
                        copy.wait_send()
            for g in range(len(self.grads)):
                for axis in range(2):
                    for which in range(2):
                        self.first_copy(axis, i, which, g).wait_send()
                    self.second_copy(axis, i, g).wait_send()


ANY = pl.BlockSpec(memory_space=pl.ANY)
VMEM = pl.BlockSpec(memory_space=pltpu.VMEM)


def comm_call(kernel, ident, out_shape, in_specs, out_specs, scratch, aliases=None):
    return pl.pallas_call(
        kernel,
        input_output_aliases=aliases or {},
        out_shape=out_shape,
        in_specs=in_specs,
        out_specs=out_specs,
        scratch_shapes=scratch,
        compiler_params=pltpu.CompilerParams(
            collective_id=ident, has_side_effects=True, vmem_limit_bytes=VMEM_LIMIT
        ),
    )


class Local:
    def __init__(self, sems):
        self.sems, self.copies = sems, []

    def start(self, src, dst):
        self.copies.append(pltpu.make_async_copy(src, dst, self.sems.at[len(self.copies)]))
        self.copies[-1].start()
        return len(self.copies) - 1

    def wait(self, *indices):
        for index in indices:
            self.copies[index].wait()


def bf16(*shape):
    return jax.ShapeDtypeStruct(shape, jnp.bfloat16)


ATTN_PIECES = (
    (lambda c: 256 * c, 256, 0, 0),
    (lambda c: 2048 + 256 * (c // 4), 256, 0, 256),
    (lambda c: 2560 + 256 * (c // 4), 256, 0, 512),
    (lambda c: 3200 + 256 * c, 256, 1, 0),
    (lambda c: 3072, 128, 2, 0),
)
ATTN_LAND = (
    (lambda c: 1152 * c, 896, 0, 0),
    (lambda c: 1152 * c + 896, 256, 1, 0),
)
MLP_PIECES = (
    (lambda c: 1024 * c, 1024, 0, 0),
    (lambda c: 8192 + 1024 * c, 1024, 0, 1024),
    (lambda c: 16384 + 1024 * c, 1024, 1, 0),
)
EARLY_UNITS = 2
VEC_LAND = ((lambda c: 512 * c, 512, 0, 0),)


def turn(values, cosine, sine):
    half = HEAD // 2
    first, second = values[:, :half], values[:, half:]
    return jnp.concatenate(
        [first * cosine - second * sine, second * cosine + first * sine], axis=1
    )


def allowed_pairs(first_query, first_key, positions):
    shape = (positions.shape[0], 768)
    distance = (
        lax.broadcasted_iota(jnp.int32, shape, 0)
        - lax.broadcasted_iota(jnp.int32, shape, 1)
        + (first_query - first_key)
    )
    return (distance >= 0) & (distance <= jnp.minimum(positions, WINDOW - 1))


def positions_of(parts):
    return (parts[:, 0:1].astype(jnp.float32) * 256.0 + parts[:, 1:2].astype(jnp.float32)).astype(
        jnp.int32
    )


def attention_forward(own_pos, w_attn, w_mlp, hidden, gains, head_gains, tables, ident):
    height = 32 * w_attn.shape[0]
    rows, width = hidden.shape
    total = 8 * rows
    query_block, key_span = 2 * rows, 768
    scatter_scratch = ChainScatter.scratch(rows, width)

    def kernel(*refs):
        ins, outs, held = split_refs(refs, 7, 17, len(refs) - 24)
        pos_ref, attn_ref, mlp_ref, hidden_ref, gains_ref, head_ref, tables_ref = ins
        (row_hbm, qkv_hbm, out_hbm, laurel_ref, row_pos, gate_up_ref, down_ref, row_ffn,
         projected_hbm, q_low, k_low, v_low, mixed, latent_ref, laurel_up, attn_out, joined) = outs
        scratch, scat, attn_m, mlp_m, gather_m, local_m = split_refs(
            held, 8, len(scatter_scratch), 2, 2, 8, 1
        )
        (own_ffn, partial, own_ref, normed_ref, row_ref, qkv_ref, out_ref, projected) = scratch
        place = Place()
        local = Local(local_m[0])
        normed_ref[...] = rms_norm(hidden_ref[...].astype(jnp.float32), gains_ref[0:1])
        own_ref[...] = normed_ref[...].astype(jnp.bfloat16)
        greet(place, "all", True)
        attn = Spread(place, attn_ref, [qkv_ref, out_ref, laurel_ref], ATTN_PIECES, attn_m)
        mlp = Spread(place, mlp_ref, [gate_up_ref, down_ref], MLP_PIECES, mlp_m)
        gathers = [
            ChainGather(place, own_ref, row_ref, gather_m[0:2]),
            ChainGather(place, pos_ref, row_pos, gather_m[2:4]),
        ]
        last = [
            ChainGather(
                place, own_ffn.at[pl.ds(part * (rows // 2), rows // 2)], row_ffn,
                gather_m[4 + 2 * part : 6 + 2 * part], rows, part * (rows // 2),
            )
            for part in range(2)
        ]
        scatter = ChainScatter(place, partial, scat)

        def step(n):
            for gather in gathers:
                gather.step(n)

        for gather in gathers:
            gather.start()
        attn.start(0, 4)
        mlp.start(0, 2)
        attn.forward(0)
        attn.forward(1)
        mlp.forward(0)
        step(1)
        attn.start(4, 6)
        mlp.start(4, 5)
        attn.forward(2)
        attn.forward(3)
        attn.relay(0)
        attn.relay(1)
        step(2)
        attn.start(6, 8)
        mlp.start(5, 6)
        attn.forward(4)
        attn.forward(5)
        attn.relay(2)
        attn.relay(3)
        step(3)
        attn.forward(6)
        attn.forward(7)
        mlp.start(2, 4)
        attn.relay(4)
        attn.relay(5)
        mlp.relay(0)
        attn.relay(6)
        attn.relay(7)
        for gather in gathers:
            gather.arrive()
        attn.arrive()
        mlp.forward(1)
        mlp.start(6, 7)
        local.start(row_ref, row_hbm)
        local.start(qkv_ref, qkv_hbm)
        local.start(out_ref, out_hbm)

        @pl.loop(0, total // query_block)
        def _(n):
            here = rows_at(n * query_block, query_block)
            block = plain_dot(row_ref[here], qkv_ref[...])
            projected[here] = block
            cosine, sine = tables_ref[here, : HEAD // 2], tables_ref[here, HEAD // 2 :]
            q_low[here] = turn(
                rms_norm(block[:, :HEAD], head_ref[0:1]), cosine, sine
            ).astype(jnp.bfloat16)
            k_low[here] = turn(
                rms_norm(block[:, HEAD : 2 * HEAD], head_ref[1:2]), cosine, sine
            ).astype(jnp.bfloat16)
            v_low[here] = value_norm(block[:, 2 * HEAD :]).astype(jnp.bfloat16)

        mlp.start(7, 8)
        local.start(projected, projected_hbm)
        upper = place.z // 2

        @pl.loop(0, total // query_block)
        def _(n):
            d = n * upper + (3 - n) * (1 - upper)
            here = rows_at(d * query_block, query_block)
            first_key = (d // 2) * (d - 2) * query_block
            there = rows_at(first_key, key_span)
            scores = jnp.where(
                allowed_pairs(d * query_block, first_key, positions_of(row_pos[here])),
                times_transposed(q_low[here], k_low[there]),
                NEG_LARGE,
            )
            weights = jnp.exp(scores - jnp.max(scores, axis=-1, keepdims=True))
            probs = (weights / jnp.sum(weights, axis=-1, keepdims=True)).astype(jnp.bfloat16)
            block = plain_dot(probs, v_low[there]).astype(jnp.bfloat16)
            mixed[here] = block
            partial[here] = times_transposed(block, out_ref[...]).astype(jnp.bfloat16)
            scatter.across(d).start()

        scatter.ends((0,))
        scatter.ends((1,))
        mlp.relay(1)
        mlp.forward(2)
        mlp.forward(3)
        scatter.inner(0, (0,))
        mlp.forward(4)
        low = plain_dot(own_ref[...], laurel_ref[...])
        latent_ref[...] = low.astype(jnp.bfloat16)
        lanes = lax.broadcasted_iota(jnp.int32, low.shape, 1)
        shifted = jnp.where(lanes >= RANK, pltpu.roll(low, RANK, 1), 0.0).astype(jnp.bfloat16)
        laurel_up[...] = times_transposed(shifted, laurel_ref[...])
        scatter.inner(1, (0,))
        mlp.forward(5)

        def close(part):
            here = slice(part * (rows // 2), (part + 1) * (rows // 2))
            laurel_res = normed_ref[here] + rms_norm(laurel_up[here], gains_ref[1:2])
            after_attn = hidden_ref[here].astype(jnp.float32) + rms_norm(
                attn_out[here], gains_ref[2:3]
            )
            joined[here] = (after_attn + laurel_res) / math.sqrt(2.0)
            own_ffn[here] = rms_norm(joined[here], gains_ref[3:4]).astype(jnp.bfloat16)

        scatter.total(attn_out, (0,))
        close(0)
        last[0].start()
        scatter.inner(0, (1,))
        scatter.inner(1, (1,))
        mlp.relay(2)
        mlp.relay(3)
        last[0].step(1)
        scatter.total(attn_out, (1,))
        close(1)
        last[1].start()
        mlp.relay(4)
        mlp.forward(6)
        mlp.forward(7)
        last[0].step(2)
        last[1].step(1)
        mlp.relay(5)
        last[0].step(3)
        mlp.relay(6)
        last[1].step(2)
        mlp.relay(7)
        last[1].step(3)
        scatter.settle()
        mlp.arrive()
        for gather in last:
            gather.arrive()
        attn.settle()
        mlp.settle()
        for gather in gathers + last:
            gather.settle()
        local.wait(0, 1, 2, 3)

    def f32(*shape):
        return jax.ShapeDtypeStruct(shape, jnp.float32)

    token_f32 = f32(rows, width)
    head = bf16(total, HEAD)
    outs = [bf16(total, width), bf16(height, 768), bf16(height, 256), bf16(height, 128)]
    outs += [bf16(total, 128), bf16(height, 2048), bf16(height, 1024), bf16(total, width)]
    outs += [f32(total, 768), head, head, head, head, bf16(rows, 128)]
    outs += [token_f32, token_f32, token_f32]
    return comm_call(
        kernel,
        ident,
        outs,
        [VMEM, ANY, ANY] + [VMEM] * 4,
        [ANY] * 3 + [VMEM] * 2 + [ANY] * 4 + [VMEM] * 8,
        [
            pltpu.VMEM((rows, width), jnp.bfloat16),
            pltpu.VMEM((total, width), jnp.bfloat16),
            pltpu.VMEM((rows, width), jnp.bfloat16),
            pltpu.VMEM((rows, width), jnp.float32),
            pltpu.VMEM((total, width), jnp.bfloat16),
            pltpu.VMEM((height, 768), jnp.bfloat16),
            pltpu.VMEM((height, 256), jnp.bfloat16),
            pltpu.VMEM((total, 768), jnp.float32),
        ]
        + scatter_scratch
        + Spread.sems(len(ATTN_PIECES), 3)
        + Spread.sems(len(MLP_PIECES), 2)
        + ChainGather.SEMS * 4
        + [pltpu.SemaphoreType.DMA((4,))],
    )(own_pos, w_attn, w_mlp, hidden, gains, head_gains, tables)


def split_refs(refs, *counts):
    refs, parts = list(refs), []
    for count in counts:
        parts.append(refs[:count])
        refs = refs[count:]
    return parts


def turn_back(grads, cosine, sine):
    half = HEAD // 2
    first, second = grads[:, :half], grads[:, half:]
    return jnp.concatenate(
        [first * cosine + second * sine, second * cosine - first * sine], axis=1
    )


def norm_back(values, scale_vec, grads):
    inverse = lax.rsqrt(jnp.mean(values * values, axis=-1, keepdims=True) + EPSILON)
    unit = values * inverse
    scaled = grads * scale_vec
    back = (scaled - unit * jnp.mean(unit * scaled, axis=-1, keepdims=True)) * inverse
    return back, jnp.sum(grads * unit, axis=0, keepdims=True)


def unit_gradient(place, n, tokens_ref, grad_ref, out, turned_ref):
    zz = place.partner(ORDER[DRAIN_ORDER[2 * n]][0])
    unit_rows = turned_ref.shape[0]
    count = unit_rows // 4
    for f in range(4):
        columns = cols_at((f * 4 + zz) * count, count)
        turned_ref[f * count : (f + 1) * count] = tokens_ref[:, columns].T
    step = 512

    @pl.loop(0, grad_ref.shape[1] // step)
    def _(t):
        columns = cols_at(t * step, step)
        out[n * unit_rows : (n + 1) * unit_rows, columns] = plain_dot(
            turned_ref[...], grad_ref[:, columns]
        ).astype(jnp.bfloat16)


def gelu_pair(values):
    scale = math.sqrt(2.0 / math.pi)
    squares = values * values
    bend = jnp.tanh(scale * values * (1.0 + 0.044715 * squares))
    half = 0.5 * (1.0 + bend)
    slope = half + 0.5 * values * (1.0 - bend * bend) * scale * (1.0 + 3.0 * 0.044715 * squares)
    return values * half, slope


def ffn_layer(
    row_ffn, w_gate_up, w_down, joined, attn_out, laurel_up, gains, layer_vec, pl_gate, pl_proj,
    out_grad, shard_height, mlp_cols, ident
):
    rows, width = joined.shape
    total, hidden_units = 8 * rows, w_down.shape[1]
    block, chunk = 2 * rows, hidden_units // 2
    vec_width = 2 * pl_gate.shape[1]
    unit_rows = 8 * shard_height
    scatter_scratch = ChainScatter.scratch(rows, width)
    early, late = 2 * EARLY_UNITS, 4 - EARLY_UNITS
    mlp_scratch = Drain.scratch(shard_height, (2 * hidden_units, hidden_units), early)
    mlp_sems = Drain.sems(len(MLP_PIECES), 2, early)
    vec_scratch = Drain.scratch(shard_height, (vec_width,))
    vec_sems = Drain.sems(1, 1)

    def kernel(*refs):
        ins, outs, held = split_refs(refs, 11, 10, len(refs) - 21)
        ffn_hbm, gate_up_hbm, down_hbm = ins[:3]
        (joined_ref, attn_ref, laurel_ref, gains_ref, vector_ref, pl_gate_ref, pl_proj_ref,
         out_grad_ref) = ins[3:]
        (result_ref, d_vector_ref, d_half_ref, d_attn_ref, d_laurel_ref, gain_ref, mlp_land,
         vec_land, late_wide, late_narrow) = outs
        scratch, scat, mlp_s, mlp_m, vec_s, vec_m, gather_m, last = split_refs(
            held, 12, len(scatter_scratch), len(mlp_scratch), 3, len(vec_scratch), 3, 2, 1
        )
        (ffn_ref, gate_up_ref, down_ref, slopes, active, row_grad, partial, turned, vec_grad,
         own_grad, ffn_out, grad_after) = scratch
        place = Place()
        local = Local(last[0])
        local.start(ffn_hbm, ffn_ref)
        local.start(gate_up_hbm, gate_up_ref)
        down_copy = local.start(down_hbm, down_ref)
        greet(place, "all", True)
        scatter = ChainScatter(place, partial, scat)
        gather = ChainGather(place, own_grad, row_grad, gather_m)
        mlp = Drain(
            place, [gate_up_ref, down_ref], mlp_land, MLP_PIECES, mlp_s, mlp_m, 0, early
        )
        vec = Drain(place, [vec_grad], vec_land, VEC_LAND, vec_s, vec_m)
        upper = place.z // 2

        local.wait(0, 1, down_copy)

        @pl.loop(0, total // block)
        def _(n):
            d = n * upper + (3 - n) * (1 - upper)
            here = rows_at(d * block, block)
            for t in range(2):
                gates = pl.ds(t * chunk, chunk)
                ups = pl.ds(hidden_units + t * chunk, chunk)
                gate = plain_dot(ffn_ref[here], gate_up_ref[:, gates])
                up = plain_dot(ffn_ref[here], gate_up_ref[:, ups])
                value, slope = gelu_pair(gate)
                active[here, gates] = (value * up).astype(jnp.bfloat16)
                slopes[here, gates] = (slope * up).astype(jnp.bfloat16)
                slopes[here, ups] = value.astype(jnp.bfloat16)
            partial[here] = times_transposed(active[here], down_ref[...]).astype(jnp.bfloat16)
            scatter.across(d).start()
            scatter.ends_after(n)

        scatter.inner(0)
        scatter.inner(1)
        scatter.finish(ffn_out)

        after = joined_ref[...] + rms_norm(ffn_out[...], gains_ref[4:5])
        after_low = after.astype(jnp.bfloat16)
        vec_gate = plain_dot(after_low, pl_gate_ref[...])
        vector = vector_ref[...].astype(jnp.float32)
        value, slope = gelu_pair(vec_gate)
        vec_mixed = (value * vector).astype(jnp.bfloat16)
        vec_out = plain_dot(vec_mixed, pl_proj_ref[...])
        result_ref[...] = (after + rms_norm(vec_out, gains_ref[5:6])).astype(jnp.bfloat16)
        upstream = out_grad_ref[...].astype(jnp.float32)
        d_vec_out, d_scale = norm_back(vec_out, gains_ref[5:6], upstream)
        gain_ref[...] = jnp.zeros_like(gain_ref)
        gain_ref[5:6] = d_scale
        d_vec_out_low = d_vec_out.astype(jnp.bfloat16)
        d_vec_mixed = times_transposed(d_vec_out_low, pl_proj_ref[...])
        d_vector_ref[...] = d_vec_mixed * value
        d_vec_gate_low = (d_vec_mixed * vector * slope).astype(jnp.bfloat16)
        grad_after[...] = upstream + times_transposed(d_vec_gate_low, pl_gate_ref[...])
        d_ffn_out, d_scale = norm_back(ffn_out[...], gains_ref[4:5], grad_after[...])
        gain_ref[4:5] = d_scale
        own_grad[...] = d_ffn_out.astype(jnp.bfloat16)
        gather.start()
        half = vec_width // 2
        vec_grad[:, :half] = contract_rows(after_low, d_vec_gate_low).astype(jnp.bfloat16)
        vec_grad[:, half:] = contract_rows(d_vec_out_low, vec_mixed).astype(jnp.bfloat16)
        for i in range(8):
            vec.start(i)
        gather.local().wait()

        @pl.loop(0, total // block)
        def _(n):
            for step in (1, 2, 3):

                @pl.when(n == step)
                def _(step=step):
                    gather.step(step)
                    for i in ((), range(4), range(4, 8), ())[step]:
                        vec.middle(i)
                    for i in ((), (), range(4), range(4, 8))[step]:
                        vec.last(i)

            d = gather.near_first(n)
            gather.from_sibling(d).wait_recv()
            here = rows_at(d * block, block)
            for t in range(2):
                gates = pl.ds(t * chunk, chunk)
                ups = pl.ds(hidden_units + t * chunk, chunk)
                d_active = plain_dot(row_grad[here], down_ref[:, gates])
                slopes[here, gates] = (d_active * slopes[here, gates].astype(jnp.float32)).astype(
                    jnp.bfloat16
                )
                slopes[here, ups] = (d_active * slopes[here, ups].astype(jnp.float32)).astype(
                    jnp.bfloat16
                )
            partial[here] = times_transposed(slopes[here], gate_up_ref[...]).astype(jnp.bfloat16)
            scatter.across(d).start()
            scatter.late_ends_after(n)

        scatter.late_ends_after(4)

        def unit(n):
            unit_gradient(place, n, ffn_ref, slopes, gate_up_ref, turned)
            unit_gradient(place, n, row_grad, active, down_ref, turned)

        first = EARLY_UNITS - 1
        scatter.late_inner(0)
        unit(first)
        mlp.start(2 * first)
        mlp.start(2 * first + 1)
        scatter.late_inner(1)
        unit(1 - first)
        scatter.late_inner(2)
        for i in range(2 * first):
            mlp.start(i)
        mlp.middle(2 * first)
        mlp.middle(2 * first + 1)
        unit(2)
        mlp.last(2 * first)
        mlp.last(2 * first + 1)
        unit(3)
        kept = [
            local.start(ref.at[pl.ds(EARLY_UNITS * unit_rows, late * unit_rows)], out)
            for ref, out in ((gate_up_ref, late_wide), (down_ref, late_narrow))
        ]
        for i in range(2 * first):
            mlp.middle(i)
        scatter.finish(ffn_out)
        d_joined, d_scale = norm_back(joined_ref[...], gains_ref[3:4], ffn_out[...])
        gain_ref[3:4] = d_scale
        d_half = (grad_after[...] + d_joined) / math.sqrt(2.0)
        d_half_ref[...] = d_half
        d_attn, d_scale = norm_back(attn_ref[...], gains_ref[2:3], d_half)
        gain_ref[2:3] = d_scale
        d_attn_ref[...] = d_attn.astype(jnp.bfloat16)
        d_laurel, d_scale = norm_back(laurel_ref[...], gains_ref[1:2], d_half)
        gain_ref[1:2] = d_scale
        d_laurel_ref[...] = d_laurel.astype(jnp.bfloat16)
        for i in range(2 * first):
            mlp.last(i)
        gather.settle()
        vec.finish()
        local.wait(*kept)
        mlp.finish()

    def f32(*shape):
        return jax.ShapeDtypeStruct(shape, jnp.float32)

    def held_bf16(*shape):
        return pltpu.VMEM(shape, jnp.bfloat16)

    return comm_call(
        kernel,
        ident,
        [
            bf16(rows, width),
            f32(rows, vec_width // 2),
            f32(rows, width),
            bf16(rows, width),
            bf16(rows, width),
            f32(8, width),
            bf16(shard_height, mlp_cols),
            bf16(shard_height, 8 * vec_width),
            bf16(late * unit_rows, 2 * hidden_units),
            bf16(late * unit_rows, hidden_units),
        ],
        [ANY] * 3 + [VMEM] * 8,
        [VMEM] * 6 + [ANY] * 4,
        [
            held_bf16(total, width),
            held_bf16(*w_gate_up.shape),
            held_bf16(*w_down.shape),
            held_bf16(total, 2 * hidden_units),
            held_bf16(total, hidden_units),
            held_bf16(total, width),
            held_bf16(total, width),
            held_bf16(unit_rows, total),
            held_bf16(width, vec_width),
            held_bf16(rows, width),
            pltpu.VMEM((rows, width), jnp.float32),
            pltpu.VMEM((rows, width), jnp.float32),
        ]
        + scatter_scratch
        + mlp_scratch
        + mlp_sems
        + vec_scratch
        + vec_sems
        + ChainGather.SEMS
        + [pltpu.SemaphoreType.DMA((5,))],
    )(
        row_ffn, w_gate_up, w_down, joined, attn_out, laurel_up, gains, layer_vec, pl_gate,
        pl_proj, out_grad,
    )


def sum_everywhere(place, own, arrived, sems):
    k, f = place.k, place.f
    targets = [
        place.sibling,
        (place.x_side, place.c),
        (place.y_side, place.c),
        (f, place.partner(1) * 2 + k),
        (f, place.partner(3) * 2 + k),
    ]
    return [
        remote(own.at[n], arrived.at[n], sems.at[0, n], sems.at[1, n], target)
        for n, target in enumerate(targets)
    ]


def attention_backward(
    d_attn_low, d_laurel_low, d_half, weights, kept, tables, head_gains, hidden, gains,
    other_gains, mlp_grads, mlp_land, vec_land, ident
):
    w_qkv, w_out, w_laurel = weights
    queries, keys, values, mixed, latent, projected, row_normed, row_parts = kept
    rows, width = d_half.shape
    total = 8 * rows
    query_block, key_span = 2 * rows, 768
    shard_height, vec_width = vec_land.shape[0], vec_land.shape[1] // 8
    qkv_width, laurel_width = w_qkv.shape[1], w_laurel.shape[1]
    attn_widths = (qkv_width + laurel_width, w_out.shape[1])
    scatter_scratch = ChainScatter.scratch(rows, width)
    first_late, late = 2 * EARLY_UNITS, 8 - 2 * EARLY_UNITS
    mlp_scratch = Drain.scratch(shard_height, [grad.shape[1] for grad in mlp_grads], late)
    mlp_sems = Drain.sems(len(MLP_PIECES), 2, late)
    loads = [*mlp_grads, w_out, queries, keys, values, tables, projected, w_qkv, mixed, row_normed]
    attn_scratch = Drain.scratch(shard_height, attn_widths)
    attn_sems = Drain.sems(len(ATTN_LAND), 2)
    gain_rows = other_gains.shape[0]

    def kernel(*refs):
        ins, outs, held = split_refs(refs, 23, 5, len(refs) - 28)
        (own_ref, row_pos, head_ref, hidden_ref, gains_ref, base_ref, other_ref, laurel_ref,
         vec_ref, w_laurel_ref, latent_ref) = ins[:11]
        wide_hbm, narrow_hbm = ins[11:13]
        out_ref, gain_ref, land_ref, attn_land, vec_all = outs
        (scratch, loaded, local_sems, gain_s, scat, mlp_s, mlp_m, attn_s, attn_m, vec_m, gather_m) = (
            split_refs(
                held, 9, 11, 1, 3, len(scatter_scratch), len(mlp_scratch), 3, len(attn_scratch), 3,
                3, 2,
            )
        )
        (vec_own, row_grad, d_mixed, d_keys, d_values, d_projected, qkv_grad, out_grad,
         laurel_back) = scratch
        (wide_ref, narrow_ref, w_out_ref, q_low, k_low, v_low, tables_ref, projected_ref, qkv_ref,
         mixed_ref, row_ref) = loaded
        held_gains, arrived_gains, gain_sems = gain_s
        place = Place()
        local = Local(local_sems[0])
        for src, dst in zip(ins[11:22], loaded):
            local.start(src, dst)
        greet(place, "all", True)
        gather = ChainGather(place, own_ref, row_grad, gather_m)
        scatter = ChainScatter(place, row_grad, scat)
        mlp = Drain(
            place, [wide_hbm, narrow_hbm], land_ref, MLP_PIECES, mlp_s, mlp_m, first_late, late,
            [wide_ref, narrow_ref],
        )
        attn = Drain(place, [qkv_grad, out_grad], attn_land, ATTN_LAND, attn_s, attn_m)
        vec = ChainGather(
            place, vec_own, vec_all.at[rows_at(place.f * 8 * shard_height, 8 * shard_height)],
            vec_m[:2],
        )
        plane = PlaneGather(place, vec_all, vec_m[2:])
        rounds = sum_everywhere(place, held_gains, arrived_gains, gain_sems)

        def gain_round(n):
            rounds[n].wait_recv()
            held_gains[n + 1] = held_gains[n] + arrived_gains[n]
            if n < 4:
                rounds[n + 1].start()

        gather.start()
        mlp.start(0)
        mlp.start(1)
        vec_sum = vec_ref[:, 0:vec_width].astype(jnp.float32)
        for c in range(1, 8):
            vec_sum = vec_sum + vec_ref[:, c * vec_width : (c + 1) * vec_width].astype(jnp.float32)
        vec_own[...] = vec_sum.astype(jnp.bfloat16)
        vec.start()
        d_keys[...] = jnp.zeros_like(d_keys)
        d_values[...] = jnp.zeros_like(d_values)
        held_gains[0] = other_ref[...]
        low = plain_dot(laurel_ref[...], w_laurel_ref[...])
        lanes = lax.broadcasted_iota(jnp.int32, low.shape, 1)
        d_latent = jnp.where(lanes < RANK, pltpu.roll(low, RANK, 1), 0.0).astype(jnp.bfloat16)
        laurel_back[...] = base_ref[...] + times_transposed(d_latent, w_laurel_ref[...])
        normed_low = rms_norm(hidden_ref[...].astype(jnp.float32), gains_ref[0:1]).astype(
            jnp.bfloat16
        )
        shifted = pltpu.roll(latent_ref[...].astype(jnp.float32), RANK, 1)
        up_side = jnp.where(lanes >= RANK, shifted, 0.0).astype(jnp.bfloat16)
        qkv_grad[:, qkv_width:] = (
            contract_rows(normed_low, d_latent) + contract_rows(laurel_ref[...], up_side)
        ).astype(jnp.bfloat16)
        local.wait(0, 1)
        gather.step(1)
        vec.step(1)
        mlp.middle(0)
        mlp.middle(1)
        for i in range(2, late):
            mlp.start(i)
        gather.step(2)
        vec.step(2)
        mlp.last(0)
        mlp.last(1)
        gather.step(3)
        vec.step(3)
        gather.arrive()
        vec.arrive()
        plane.start()
        local.wait(2, 3, 4, 5, 6, 7)

        @pl.loop(0, total // query_block)
        def _(n):
            here = rows_at(n * query_block, query_block)
            d_mixed[here] = plain_dot(row_grad[here], w_out_ref[...]).astype(jnp.bfloat16)

        for i in range(2, late):
            mlp.middle(i)

        @pl.loop(0, total // query_block)
        def _(d):
            here = rows_at(d * query_block, query_block)
            first_key = (d // 2) * (d - 2) * query_block
            there = rows_at(first_key, key_span)
            query, key, value, d_mix = q_low[here], k_low[there], v_low[there], d_mixed[here]
            scores = jnp.where(
                allowed_pairs(d * query_block, first_key, positions_of(row_pos[here])),
                times_transposed(query, key),
                NEG_LARGE,
            )
            exps = jnp.exp(scores - jnp.max(scores, axis=-1, keepdims=True))
            probs = exps / jnp.sum(exps, axis=-1, keepdims=True)
            d_probs = times_transposed(d_mix, value)
            inner_sum = jnp.sum(probs * d_probs, axis=-1, keepdims=True)
            d_scores = (probs * (d_probs - inner_sum)).astype(jnp.bfloat16)
            d_keys[there] += contract_rows(d_scores, query)
            d_values[there] += contract_rows(probs.astype(jnp.bfloat16), d_mix)
            cosine, sine = tables_ref[here, : HEAD // 2], tables_ref[here, HEAD // 2 :]
            d_query, d_scale = norm_back(
                projected_ref[here, :HEAD],
                head_ref[0:1],
                turn_back(plain_dot(d_scores, key), cosine, sine),
            )
            d_projected[here, :HEAD] = d_query.astype(jnp.bfloat16)
            held_gains[0, 6:7, :HEAD] += d_scale

        for i in range(2, late):
            mlp.last(i)

        @pl.loop(0, total // query_block)
        def _(n):
            here = rows_at(n * query_block, query_block)
            cosine, sine = tables_ref[here, : HEAD // 2], tables_ref[here, HEAD // 2 :]
            d_key, d_scale = norm_back(
                projected_ref[here, HEAD : 2 * HEAD],
                head_ref[1:2],
                turn_back(d_keys[here], cosine, sine),
            )
            d_projected[here, HEAD : 2 * HEAD] = d_key.astype(jnp.bfloat16)
            held_gains[0, 6:7, HEAD : 2 * HEAD] += d_scale
            d_value, _ = norm_back(projected_ref[here, 2 * HEAD :], 1.0, d_values[here])
            d_projected[here, 2 * HEAD :] = d_value.astype(jnp.bfloat16)

        quarter = width // 4
        local.wait(8, 9, 10)

        @pl.loop(0, 4)
        def _(n):
            columns = cols_at(n * quarter, quarter)
            out_grad[rows_at(n * quarter, quarter)] = contract_rows(
                row_grad[:, columns], mixed_ref[...]
            ).astype(jnp.bfloat16)

        gather.settle()
        upper = place.z // 2

        @pl.loop(0, total // query_block)
        def _(n):
            d = n * upper + (3 - n) * (1 - upper)
            here = rows_at(d * query_block, query_block)
            row_grad[here] = times_transposed(d_projected[here], qkv_ref[...]).astype(jnp.bfloat16)
            scatter.across(d).start()

        scatter.ends()

        @pl.loop(0, 4)
        def _(n):
            columns = cols_at(n * quarter, quarter)
            qkv_grad[rows_at(n * quarter, quarter), :qkv_width] = contract_rows(
                row_ref[:, columns], d_projected[...]
            ).astype(jnp.bfloat16)

        attn.start(0)
        attn.start(1)
        attn.start(2)
        attn.start(3)
        scatter.inner(0)
        plane.relay()
        scatter.inner(1)
        attn.middle(0)
        attn.start(4)
        attn.middle(1)
        attn.start(5)
        attn.last(0)
        attn.middle(2)
        attn.start(6)
        attn.last(1)
        scatter.finish(out_ref)
        d_normed = laurel_back[...] + out_ref[...]
        d_hidden, d_scale = norm_back(
            hidden_ref[...].astype(jnp.float32), gains_ref[0:1], d_normed
        )
        out_ref[...] = d_hidden
        held_gains[0, 0:1] = d_scale
        rounds[0].start()
        attn.start(7)
        for i in range(3, 8):
            attn.middle(i)
            attn.last(i - 1)
            gain_round(i - 3)
        attn.last(7)
        gain_ref[...] = held_gains[5]
        for copy in rounds:
            copy.wait_send()
        vec.settle()
        plane.finish()
        mlp.finish()
        attn.finish()

    return comm_call(
        kernel,
        ident,
        [
            jax.ShapeDtypeStruct((rows, width), jnp.float32),
            jax.ShapeDtypeStruct((gain_rows, width), jnp.float32),
            bf16(*mlp_land.shape),
            bf16(shard_height, 8 * sum(attn_widths)),
            bf16(32 * shard_height, vec_width),
        ],
        [VMEM] * 11 + [ANY] * 12,
        [VMEM, VMEM, ANY, ANY, ANY],
        [
            pltpu.VMEM((shard_height, vec_width), jnp.bfloat16),
            pltpu.VMEM((total, width), jnp.bfloat16),
            pltpu.VMEM((total, HEAD), jnp.bfloat16),
            pltpu.VMEM((total, HEAD), jnp.float32),
            pltpu.VMEM((total, HEAD), jnp.float32),
            pltpu.VMEM((total, qkv_width), jnp.bfloat16),
            pltpu.VMEM((width, attn_widths[0]), jnp.bfloat16),
            pltpu.VMEM((width, attn_widths[1]), jnp.bfloat16),
            pltpu.VMEM((rows, width), jnp.float32),
        ]
        + [pltpu.VMEM(array.shape, array.dtype) for array in loads]
        + [
            pltpu.SemaphoreType.DMA((len(loads),)),
            pltpu.VMEM((6, gain_rows, width), jnp.float32),
            pltpu.VMEM((5, gain_rows, width), jnp.float32),
            pltpu.SemaphoreType.DMA((2, 5)),
        ]
        + scatter_scratch
        + mlp_scratch
        + mlp_sems
        + attn_scratch
        + attn_sems
        + ChainGather.SEMS
        + PlaneGather.SEMS
        + ChainGather.SEMS,
        {22: 2},
    )(
        d_attn_low, row_parts, head_gains, hidden, gains, d_half, other_gains, d_laurel_low,
        vec_land, w_laurel, latent, *loads, mlp_land,
    )


def finish_outputs(mlp_land, attn_land, vec_all, d_half, d_hidden_part, attn_cols):
    height, mlp_cols = mlp_land.shape
    rows, width = d_half.shape
    model, vec_width = vec_all.shape
    per_source = attn_land.shape[1] // 8
    half = vec_width // 2
    group = QH // KVH
    kv_first, laurel_first, out_first = QH * HEAD, (QH + 2 * KVH) * HEAD, 3200

    def kernel(mlp_ref, attn_ref, vec_ref, half_ref, part_ref, *outs):
        mlp_out, attn_out, gate_out, proj_out, hidden_out = outs
        c = pl.program_id(0)
        mlp_out[...] = mlp_ref[...].astype(jnp.float32)
        gate_out[...] = vec_ref[:, :half].astype(jnp.float32)
        proj_out[...] = vec_ref[:, half:].astype(jnp.float32).T
        hidden_out[...] = half_ref[...] + part_ref[...]
        landed = attn_ref[...].astype(jnp.float32)
        attn_out[:, cols_at(c * HEAD, HEAD)] = landed[:, :HEAD]
        attn_out[:, cols_at(out_first + c * HEAD, HEAD)] = landed[:, per_source - HEAD :]

        def add(first, count, start, fresh):
            columns = cols_at(first, count)
            value = landed[:, start : start + count]

            @pl.when(fresh)
            def _():
                attn_out[:, columns] = value

            @pl.when(jnp.logical_not(fresh))
            def _():
                attn_out[:, columns] += value

        add(kv_first + c // group * HEAD, HEAD, HEAD, c % group == 0)
        add(kv_first + (KVH + c // group) * HEAD, HEAD, 2 * HEAD, c % group == 0)
        add(laurel_first, 2 * RANK, 3 * HEAD, c == 0)

    def spec(block, by_column):
        return pl.BlockSpec(block, (lambda c: (0, c)) if by_column else (lambda c: (c, 0)))

    f32 = jnp.float32
    return pl.pallas_call(
        kernel,
        grid=(8,),
        out_shape=[
            jax.ShapeDtypeStruct((height, mlp_cols), f32),
            jax.ShapeDtypeStruct((height, attn_cols), f32),
            jax.ShapeDtypeStruct((model, half), f32),
            jax.ShapeDtypeStruct((half, model), f32),
            jax.ShapeDtypeStruct((rows, width), f32),
        ],
        in_specs=[
            spec((height, mlp_cols // 8), True),
            spec((height, per_source), True),
            spec((model // 8, vec_width), False),
            spec((rows // 8, width), False),
            spec((rows // 8, width), False),
        ],
        out_specs=[
            spec((height, mlp_cols // 8), True),
            pl.BlockSpec((height, attn_cols), lambda c: (0, 0)),
            spec((model // 8, half), False),
            spec((half, model // 8), True),
            spec((rows // 8, width), False),
        ],
    )(mlp_land, attn_land, vec_all, d_half, d_hidden_part)


def per_device_split(
    hidden_in, layer_vec, positions, w_attn, w_mlp, pl_gate, pl_proj, gains, head_gains, out_grad
):
    shard_height = w_attn.shape[0]
    row_total = QH * positions.shape[0]
    lanes = jnp.arange(128, dtype=jnp.int32)[None, :]
    own_pos = jnp.where(lanes == 0, positions[:, None] // 256, positions[:, None] % 256)

    frequency = np.exp(np.arange(HEAD // 2) * (-2.0 * math.log(THETA) / HEAD))
    angles = np.arange(row_total)[:, None] * frequency[None, :]
    tables = jnp.asarray(np.concatenate([np.cos(angles), np.sin(angles)], axis=1), jnp.float32)

    (
        row_normed, w_qkv, w_out, w_laurel, row_parts, w_gate_up, w_down, row_ffn, projected,
        queries, keys, values, mixed, latent, laurel_up, attn_out, joined,
    ) = attention_forward(
        own_pos.astype(jnp.bfloat16), w_attn, w_mlp, hidden_in, gains, head_gains, tables, 1
    )
    (
        result_out, d_vector_in, d_half, d_attn_low, d_laurel_low, other_gains, mlp_land,
        vec_land, late_wide, late_narrow,
    ) = ffn_layer(
        row_ffn, w_gate_up, w_down, joined, attn_out, laurel_up, gains, layer_vec, pl_gate,
        pl_proj, out_grad, shard_height, w_mlp.shape[1], 2,
    )
    d_hidden_part, all_gains, mlp_land, attn_land, vec_all = attention_backward(
        d_attn_low,
        d_laurel_low,
        d_half,
        (w_qkv, w_out, w_laurel),
        (queries, keys, values, mixed, latent, projected, row_normed, row_parts),
        tables,
        head_gains,
        hidden_in,
        gains,
        other_gains,
        (late_wide, late_narrow),
        mlp_land,
        vec_land,
        3,
    )
    grad_w_mlp, grad_w_attn, grad_gate_all, grad_proj_all, grad_hidden = finish_outputs(
        mlp_land, attn_land, vec_all, d_half, d_hidden_part, w_attn.shape[1]
    )
    grad_gains, grad_heads = all_gains[:6], all_gains[6, : 2 * HEAD].reshape(2, HEAD)
    return (
        result_out,
        grad_hidden,
        d_vector_in,
        grad_w_attn,
        grad_w_mlp,
        grad_gate_all,
        grad_proj_all,
        grad_gains,
        grad_heads,
    )


def solution(mesh):
    fits = mesh.shape["ctx"] == QH and mesh.shape["fsdp"] == 4
    body = per_device_split if fits else per_device
    return jax.shard_map(
        body,
        mesh=mesh,
        in_specs=(
            P(("fsdp", "ctx"), None),
            P(("fsdp", "ctx"), None),
            P(("fsdp", "ctx")),
            P(("fsdp", "ctx"), None),
            P(("fsdp", "ctx"), None),
            P(),
            P(),
            P(),
            P(),
            P(("fsdp", "ctx"), None),
        ),
        out_specs=(
            P(("fsdp", "ctx"), None),
            P(("fsdp", "ctx"), None),
            P(("fsdp", "ctx"), None),
            P(("fsdp", "ctx"), None),
            P(("fsdp", "ctx"), None),
            P(),
            P(),
            P(),
            P(),
        ),
        check_vma=False,
    )
```

```python
import math

import jax
import jax.numpy as jnp
import numpy as np
from jax import lax
from jax.experimental import pallas as pl
from jax.experimental.pallas import tpu as pltpu
from jax.sharding import PartitionSpec as P

QH = 8
KVH = 2
HEAD = 256
RANK = 64
WINDOW = 512


EPSILON = 1e-06
THETA = 10000.0
NEG_LARGE = -1e30


def passed_along(block, axis, distance):
    devices = range(lax.axis_size(axis))
    route = [(i - distance, i) for i in devices if i - distance in devices]
    return lax.ppermute(block, axis, route)


def rms_norm(values, scale_vec):
    return (
        values * lax.rsqrt(jnp.mean(values * values, axis=-1, keepdims=True) + EPSILON) * scale_vec
    )


def value_norm(values):
    return rms_norm(values, 1.0)


def rotary(values, positions):
    half_size = values.shape[-1] // 2
    frequency = jnp.exp(
        jnp.arange(half_size, dtype=jnp.float32) * (-2.0 * math.log(THETA) / values.shape[-1])
    )
    angles = positions.astype(jnp.float32)[:, None] * frequency[None, :]
    cosine = jnp.cos(angles)[:, None, :]
    sine_part = jnp.sin(angles)[:, None, :]
    first_half = values[..., :half_size]
    second_half = values[..., half_size:]
    return jnp.concatenate(
        [
            first_half * cosine - second_half * sine_part,
            second_half * cosine + first_half * sine_part,
        ],
        axis=-1,
    )


def plain_dot(left_side, right_side):
    return jnp.dot(left_side, right_side, preferred_element_type=jnp.float32)


def times_transposed(left_side, right_side):
    return lax.dot_general(
        left_side, right_side, (((1,), (1,)), ((), ())), preferred_element_type=jnp.float32
    )


def contract_rows(left_side, right_side):
    return lax.dot_general(
        left_side, right_side, (((0,), (0,)), ((), ())), preferred_element_type=jnp.float32
    )


def activate(gate_up_val):
    half_cols = gate_up_val.shape[1] // 2
    return jax.nn.gelu(gate_up_val[:, :half_cols], approximate=True) * gate_up_val[:, half_cols:]


def vec_mix(gate_val, vector_val):
    return jax.nn.gelu(gate_val, approximate=True) * vector_val


def per_device(
    hidden_in, layer_vec, positions, w_attn, w_mlp, pl_gate, pl_proj, gains, head_gains, out_grad
):
    row_count = hidden_in.shape[0]
    model_width = hidden_in.shape[1]
    q_width = QH * HEAD
    kv_width = KVH * HEAD
    in_cols = q_width + 2 * kv_width + RANK
    group_size = QH // KVH
    ff_width = w_mlp.shape[1] // 3
    shard_height = w_mlp.shape[0]
    fsdp_count = lax.axis_size("fsdp")
    ctx_count = lax.axis_size("ctx")
    quarter = ff_width // fsdp_count

    def permute_cols(matrix):
        return (
            matrix.reshape(-1, fsdp_count, ctx_count, shard_height)
            .transpose(0, 2, 1, 3)
            .reshape(-1, model_width)
        )

    def restore_cols(matrix):
        return (
            matrix.reshape(-1, ctx_count, fsdp_count, shard_height)
            .transpose(0, 2, 1, 3)
            .reshape(-1, model_width)
        )

    def qk_prep(raw_heads, scale_vec):
        return rotary(rms_norm(raw_heads, scale_vec), positions)

    hidden = hidden_in.astype(jnp.float32)
    normed_in = rms_norm(hidden, gains[0])
    normed_low = normed_in.astype(jnp.bfloat16)
    projected = plain_dot(
        normed_low, lax.all_gather(w_attn[:, :in_cols], ("fsdp", "ctx"), axis=0, tiled=True)
    )
    q_raw = projected[:, :q_width].reshape(row_count, QH, HEAD)
    k_raw = projected[:, q_width : q_width + kv_width].reshape(row_count, KVH, HEAD)
    v_raw = projected[:, q_width + kv_width : q_width + 2 * kv_width].reshape(row_count, KVH, HEAD)
    latent = projected[:, q_width + 2 * kv_width :].astype(jnp.bfloat16)
    queries = qk_prep(q_raw, head_gains[0]).astype(jnp.bfloat16)
    keys_own = qk_prep(k_raw, head_gains[1]).astype(jnp.bfloat16)
    values_own = value_norm(v_raw).astype(jnp.bfloat16)
    kv_own = jnp.concatenate(
        [keys_own.reshape(row_count, kv_width), values_own.reshape(row_count, kv_width)], axis=1
    )
    hop_count = (WINDOW - 1) // row_count + 1
    earlier = []
    moving = kv_own
    for step_back in range(hop_count):
        moving = passed_along(moving, "ctx", 1)
        earlier.append(moving)
    kv_all = jnp.concatenate(earlier[::-1] + [kv_own], axis=0)
    span_rows = kv_all.shape[0]
    keys_all = kv_all[:, :kv_width].reshape(span_rows, KVH, HEAD)
    values_all = kv_all[:, kv_width:].reshape(span_rows, KVH, HEAD)
    grouped = queries.reshape(row_count, KVH, group_size, HEAD)
    distance = (
        jnp.arange(row_count, dtype=jnp.int32)[:, None]
        + hop_count * row_count
        - jnp.arange(span_rows, dtype=jnp.int32)[None, :]
    )
    allowed = (distance >= 0) & (distance <= jnp.minimum(positions, WINDOW - 1)[:, None])
    scores = jnp.einsum("qgrd,kgd->grqk", grouped, keys_all, preferred_element_type=jnp.float32)
    scores = jnp.where(allowed[None, None], scores, NEG_LARGE)
    row_max = jnp.max(scores, axis=-1, keepdims=True)
    exp_scores = jnp.exp(scores - row_max)
    row_sum = jnp.sum(exp_scores, axis=-1, keepdims=True)
    log_total = row_max + jnp.log(row_sum)
    probs_low = (exp_scores / row_sum).astype(jnp.bfloat16)
    mixed = jnp.einsum("grqk,kgd->qgrd", probs_low, values_all, preferred_element_type=jnp.float32)
    mixed = mixed.reshape(row_count, q_width).astype(jnp.bfloat16)
    shard_rows = lax.all_gather(w_attn[:, in_cols:], ("fsdp", "ctx"), axis=0, tiled=True)
    laurel_part = times_transposed(latent, shard_rows[:, :RANK])
    attn_part = times_transposed(mixed, shard_rows[:, RANK:])
    out_pair = jnp.stack([laurel_part, attn_part], axis=1)
    laurel_up = out_pair[:, 0]
    attn_out = out_pair[:, 1]
    laurel_res = normed_in + rms_norm(laurel_up, gains[1])
    after_attn = hidden + rms_norm(attn_out, gains[2])
    joined = (after_attn + laurel_res) / math.sqrt(2.0)
    ffn_low = rms_norm(joined, gains[3]).astype(jnp.bfloat16)
    sent_rows = w_mlp.reshape(shard_height, 3, fsdp_count, quarter)
    sent_tokens = jnp.broadcast_to(
        ffn_low[:, None, None, :], (row_count, 1, fsdp_count, model_width)
    )
    got_rows, got_tokens = (
        lax.all_to_all(sent_rows, "fsdp", split_axis=2, concat_axis=0, tiled=True),
        lax.all_to_all(sent_tokens, "fsdp", split_axis=2, concat_axis=0, tiled=True),
    )
    quarter_rows = lax.all_gather(got_rows, "ctx", axis=0, tiled=True).reshape(
        model_width, 3, quarter
    )
    w_gate_up = quarter_rows[:, :2].reshape(model_width, 2 * quarter)
    w_down = quarter_rows[:, 2]
    ffn_perm = permute_cols(got_tokens.reshape(fsdp_count * row_count, model_width))
    gate_up = plain_dot(ffn_perm, w_gate_up)
    activated = activate(gate_up).astype(jnp.bfloat16)
    ffn_out = lax.psum_scatter(
        restore_cols(times_transposed(activated, w_down)), "fsdp", scatter_dimension=0, tiled=True
    )
    after_ffn = joined + rms_norm(ffn_out, gains[4])
    after_low = after_ffn.astype(jnp.bfloat16)
    vec_gate = plain_dot(after_low, pl_gate)
    vector_in = layer_vec.astype(jnp.float32)
    vec_mixed = vec_mix(vec_gate, vector_in).astype(jnp.bfloat16)
    vec_out = plain_dot(vec_mixed, pl_proj)
    result_out = after_ffn + rms_norm(vec_out, gains[5])
    upstream = out_grad.astype(jnp.float32)
    unused_out, vec_norm_back = jax.vjp(rms_norm, vec_out, gains[5])
    d_vec_out, d_gain_vec = vec_norm_back(upstream)
    d_vec_out_low = d_vec_out.astype(jnp.bfloat16)
    d_vec_mixed = times_transposed(d_vec_out_low, pl_proj)
    grad_pl_proj = contract_rows(vec_mixed, d_vec_out_low)
    unused_out, mix_back = jax.vjp(vec_mix, vec_gate, vector_in)
    d_vec_gate, d_vector_in = mix_back(d_vec_mixed)
    d_vec_gate_low = d_vec_gate.astype(jnp.bfloat16)
    grad_after = upstream + times_transposed(d_vec_gate_low, pl_gate)
    grad_pl_gate = contract_rows(after_low, d_vec_gate_low)
    unused_out, ffn_norm_back = jax.vjp(rms_norm, ffn_out, gains[4])
    d_ffn_out, d_gain_ffn = ffn_norm_back(grad_after)
    d_ffn_low = d_ffn_out.astype(jnp.bfloat16)
    unused_out, act_back = jax.vjp(activate, gate_up)
    d_ffn_all = lax.all_gather(d_ffn_low, "fsdp", axis=0, tiled=True)
    d_ffn_perm = permute_cols(d_ffn_all)
    d_activated = plain_dot(d_ffn_perm, w_down)
    d_gate_up = act_back(d_activated)[0].astype(jnp.bfloat16)
    d_ffn_in = lax.psum_scatter(
        restore_cols(times_transposed(d_gate_up, w_gate_up)).astype(jnp.bfloat16),
        "fsdp",
        scatter_dimension=0,
        tiled=True,
    ).astype(jnp.float32)
    summed = lax.psum_scatter(
        jnp.concatenate(
            [contract_rows(ffn_perm, d_gate_up), contract_rows(d_ffn_perm, activated)], axis=1
        ).astype(jnp.bfloat16),
        "ctx",
        scatter_dimension=0,
        tiled=True,
    ).astype(jnp.float32)
    grad_w_mlp = (
        lax.all_to_all(
            summed.reshape(fsdp_count * shard_height, 3, 1, quarter).astype(jnp.bfloat16),
            "fsdp",
            split_axis=0,
            concat_axis=2,
            tiled=True,
        )
        .astype(jnp.float32)
        .reshape(shard_height, 3 * ff_width)
    )
    unused_out, pre_norm_back = jax.vjp(rms_norm, joined, gains[3])
    d_joined_part, d_gain_pre = pre_norm_back(d_ffn_in)
    d_joined = grad_after + d_joined_part
    d_half = d_joined / math.sqrt(2.0)
    unused_out, laurel_norm_back = jax.vjp(rms_norm, laurel_up, gains[1])
    d_laurel_up, d_gain_laurel = laurel_norm_back(d_half)
    unused_out, attn_norm_back = jax.vjp(rms_norm, attn_out, gains[2])
    d_attn_out, d_gain_attn = attn_norm_back(d_half)
    d_laurel_low = d_laurel_up.astype(jnp.bfloat16)
    d_attn_low = d_attn_out.astype(jnp.bfloat16)
    shard_rows = lax.all_gather(w_attn[:, in_cols:], ("fsdp", "ctx"), axis=0, tiled=True)
    d_latent = plain_dot(d_laurel_low, shard_rows[:, :RANK])
    d_mixed = plain_dot(d_attn_low, shard_rows[:, RANK:])
    d_grouped = d_mixed.astype(jnp.bfloat16).reshape(row_count, KVH, group_size, HEAD)
    again = jnp.einsum("qgrd,kgd->grqk", grouped, keys_all, preferred_element_type=jnp.float32)
    again = jnp.where(allowed[None, None], again, NEG_LARGE)
    probs = jnp.exp(again - log_total)
    d_probs = jnp.einsum(
        "qgrd,kgd->grqk", d_grouped, values_all, preferred_element_type=jnp.float32
    )
    inner_sum = jnp.sum(probs * d_probs, axis=-1, keepdims=True)
    d_scores = (probs * (d_probs - inner_sum)).astype(jnp.bfloat16)
    d_queries = jnp.einsum(
        "grqk,kgd->qgrd", d_scores, keys_all, preferred_element_type=jnp.float32
    ).reshape(row_count, QH, HEAD)
    d_keys_all = jnp.einsum("grqk,qgrd->kgd", d_scores, grouped, preferred_element_type=jnp.float32)
    d_values_all = jnp.einsum(
        "grqk,qgrd->kgd", probs.astype(jnp.bfloat16), d_grouped, preferred_element_type=jnp.float32
    )
    d_kv_all = jnp.concatenate(
        [d_keys_all.reshape(span_rows, kv_width), d_values_all.reshape(span_rows, kv_width)], axis=1
    )
    returned = d_kv_all[:row_count]
    for step_back in range(1, hop_count + 1):
        returned = (
            passed_along(returned.astype(jnp.bfloat16), "ctx", -1).astype(returned.dtype)
            + d_kv_all[step_back * row_count : (step_back + 1) * row_count]
        )
    d_keys_own = returned[:, :kv_width].reshape(row_count, KVH, HEAD)
    d_values_own = returned[:, kv_width:].reshape(row_count, KVH, HEAD)
    unused_out, query_back = jax.vjp(qk_prep, q_raw, head_gains[0])
    d_q_raw, d_head_query = query_back(d_queries)
    unused_out, key_back = jax.vjp(qk_prep, k_raw, head_gains[1])
    d_k_raw, d_head_key = key_back(d_keys_own)
    unused_out, value_back = jax.vjp(value_norm, v_raw)
    d_v_raw = value_back(d_values_own)[0]
    d_projected = jnp.concatenate(
        [
            d_q_raw.reshape(row_count, q_width),
            d_k_raw.reshape(row_count, kv_width),
            d_v_raw.reshape(row_count, kv_width),
            d_latent,
        ],
        axis=1,
    ).astype(jnp.bfloat16)
    d_normed_part = times_transposed(
        d_projected, lax.all_gather(w_attn[:, :in_cols], ("fsdp", "ctx"), axis=0, tiled=True)
    )
    unused_out, input_norm_back = jax.vjp(rms_norm, hidden, gains[0])
    d_hidden_part, d_gain_input = input_norm_back(d_half + d_normed_part)
    grad_hidden = d_half + d_hidden_part
    grad_w_attn = lax.psum_scatter(
        jnp.concatenate(
            [
                contract_rows(normed_low, d_projected),
                contract_rows(d_laurel_low, latent),
                contract_rows(d_attn_low, mixed),
            ],
            axis=1,
        ),
        ("fsdp", "ctx"),
        scatter_dimension=0,
        tiled=True,
    )
    gain_rows = jnp.stack(
        [d_gain_input, d_gain_laurel, d_gain_attn, d_gain_pre, d_gain_ffn, d_gain_vec]
    )
    head_rows = jnp.stack([d_head_query, d_head_key])
    grad_gains, grad_heads, grad_gate_all, grad_proj_all = lax.psum(
        (gain_rows, head_rows, grad_pl_gate, grad_pl_proj), ("fsdp", "ctx")
    )
    return (
        result_out.astype(jnp.bfloat16),
        grad_hidden,
        d_vector_in,
        grad_w_attn,
        grad_w_mlp,
        grad_gate_all,
        grad_proj_all,
        grad_gains,
        grad_heads,
    )

MESH = pl.DeviceIdType.MESH
VMEM_LIMIT = 63 * 1024 * 1024
ORDER = ((0, 0), (0, 1), (1, 0), (1, 1), (2, 0), (2, 1), (3, 0), (3, 1))


class Place:
    def __init__(self):
        self.f = lax.axis_index("fsdp")
        self.c = lax.axis_index("ctx")
        self.z = self.c // 2
        self.k = self.c % 2
        self.x_side = self.f + 1 - 2 * (self.f % 2)
        self.y_side = (self.f + 2) % 4
        self.diag = 3 - self.f
        self.sibling = (self.f, self.c + 1 - 2 * self.k)
        self.up = (self.f, self.c + 2)
        self.down = (self.f, self.c - 2)
        self.has_up = self.z < 3
        self.has_down = self.z > 0

    def partner(self, which):
        z = self.z
        return (z, z + 1 - 2 * (z % 2), (z + 2) % 4, 3 - z)[which]

    def peer(self, i):
        which, other = ORDER[i]
        return self.partner(which) * 2 + (self.k + other) % 2


def rows_at(start, count):
    return pl.ds(pl.multiple_of(start, 16), count)


def cols_at(start, count):
    if isinstance(start, int):
        return pl.ds(start, count)
    return pl.ds(pl.multiple_of(start, 128), count)


def remote(src, dst, send_sem, recv_sem, target):
    return pltpu.make_async_remote_copy(
        src_ref=src,
        dst_ref=dst,
        send_sem=send_sem,
        recv_sem=recv_sem,
        device_id=target,
        device_id_type=MESH,
    )


def greet(place, line, plane):
    barrier = pltpu.get_barrier_semaphore()
    count = 0

    def tell(target):
        pl.semaphore_signal(barrier, inc=1, device_id=target, device_id_type=MESH)

    if line == "all":
        for i in range(1, 8):
            tell((place.f, place.peer(i)))
        count += 7
    elif line == "chain":
        tell(place.sibling)
        for distance in (1, 3):
            tell((place.f, (place.z + distance) % 4 * 2 + place.k))
        count += 3
    if plane:
        tell((place.x_side, place.c))
        tell((place.y_side, place.c))
        count += 2
    pl.semaphore_wait(barrier, count)


class ChainGather:
    SEMS = [pltpu.SemaphoreType.DMA((2, 10)), pltpu.SemaphoreType.DMA((1,))]

    def __init__(self, place, own, out, sems, stride=None, offset=0):
        self.place, self.own, self.out = place, own, out
        self.sems, self.local_sem = sems
        self.rows = own.shape[0]
        self.stride, self.offset = stride or self.rows, offset

    def block(self, origin_z, core=None):
        core = self.place.k if core is None else core
        return self.out.at[
            rows_at((origin_z * 2 + core) * self.stride + self.offset, self.rows)
        ]

    def copy(self, src, dst, index, target):
        return remote(src, dst, self.sems.at[0, index], self.sems.at[1, index], target)

    def local(self):
        return pltpu.make_async_copy(self.own, self.block(self.place.z), self.local_sem.at[0])

    def upward(self, step):
        src = self.own if step == 0 else self.block(self.place.z - step)
        return self.copy(src, self.block(self.place.z - step), step, self.place.up)

    def downward(self, step):
        src = self.own if step == 0 else self.block(self.place.z + step)
        return self.copy(src, self.block(self.place.z + step), 3 + step, self.place.down)

    def across(self, origin_z, own=False):
        src = self.own if own else self.block(origin_z)
        return self.copy(src, self.block(origin_z), 6 + origin_z, self.place.sibling)

    def start(self):
        place = self.place

        @pl.when(place.has_up)
        def _():
            self.upward(0).start()

        @pl.when(place.has_down)
        def _():
            self.downward(0).start()

        self.across(place.z, True).start()
        self.local().start()

    def step(self, step):
        place = self.place

        @pl.when(place.z - step >= 0)
        def _():
            self.copy(self.own, self.block(place.z - step), step - 1, place.up).wait_recv()
            if step < 3:

                @pl.when(place.has_up)
                def _():
                    self.upward(step).start()

            self.across(place.z - step).start()

        @pl.when(place.z + step <= 3)
        def _():
            self.copy(self.own, self.block(place.z + step), 3 + step - 1, place.down).wait_recv()
            if step < 3:

                @pl.when(place.has_down)
                def _():
                    self.downward(step).start()

            self.across(place.z + step).start()

    def finish(self):
        self.arrive()
        self.settle()

    def from_sibling(self, origin):
        return self.copy(
            self.own, self.block(origin, 1 - self.place.k), 6 + origin, self.place.sibling
        )

    def near_first(self, n):
        upper = self.place.z // 2
        near = (1 - upper) * self.place.z + upper * (3 - self.place.z)
        late = n // 2
        chip = late * n + (1 - late) * ((near + n) % 2)
        return (1 - upper) * chip + upper * (3 - chip)

    def arrive(self):
        self.local().wait()
        for origin in range(4):
            self.from_sibling(origin).wait_recv()

    def settle(self):
        place = self.place
        for origin in range(4):
            self.from_sibling(origin).wait_send()
        for step in range(3):

            @pl.when((place.z - step >= 0) & place.has_up)
            def _(step=step):
                self.upward(step).wait_send()

            @pl.when((place.z + step <= 3) & place.has_down)
            def _(step=step):
                self.downward(step).wait_send()


class ChainScatter:
    PARTS = 2

    @staticmethod
    def scratch(rows, cols):
        return [
            pltpu.VMEM((4, rows, cols), jnp.bfloat16),
            pltpu.VMEM((6, rows, cols), jnp.bfloat16),
            pltpu.SemaphoreType.DMA((2, 4 + 6 * ChainScatter.PARTS)),
        ]

    def __init__(self, place, partial, scratch):
        self.place, self.partial = place, partial
        self.from_sibling, self.moving, self.sems = scratch
        self.rows = partial.shape[0] // 8

    def block(self, origin_z, core):
        return self.partial.at[rows_at((origin_z * 2 + core) * self.rows, self.rows)]

    def across(self, dest):
        return remote(
            self.block(dest, 1 - self.place.k),
            self.from_sibling.at[dest],
            self.sems.at[0, dest],
            self.sems.at[1, dest],
            self.place.sibling,
        )

    def moved(self, slot, part, target):
        count = self.rows // self.PARTS
        ref = self.moving.at[slot, pl.ds(part * count, count)]
        index = 4 + slot * self.PARTS + part
        return remote(ref, ref, self.sems.at[0, index], self.sems.at[1, index], target)

    def start(self):
        for dest in (3, 0, 2, 1):
            self.across(dest).start()

    def pair_sum(self, dest, part):
        count = self.rows // self.PARTS
        start = (dest * 2 + self.place.k) * self.rows + part * count
        return self.partial[rows_at(start, count)].astype(jnp.float32) + self.from_sibling[
            dest, part * count : (part + 1) * count
        ].astype(jnp.float32)

    def pass_on(self, dest, upward, inner=False, parts=(0, 1)):
        place = self.place
        slot = dest - 1 if upward else 3 + dest
        target = place.up if upward else place.down
        count = self.rows // self.PARTS
        if parts[0] == 0:
            self.across(dest).wait_recv()
        for part in parts:
            rows = slice(part * count, (part + 1) * count)
            total = self.pair_sum(dest, part)
            if inner:
                self.moved(slot, part, target).wait_recv()
                total = total + self.moving[slot, rows].astype(jnp.float32)
            self.moving[slot, rows] = total.astype(jnp.bfloat16)
            self.moved(slot, part, target).start()

    def ends_after(self, n):
        z = self.place.z

        @pl.when((n > 0) & (z == 0))
        def _():
            self.pass_on(4 - n, True)

        @pl.when((n > 0) & (z == 3))
        def _():
            self.pass_on(n - 1, False)

    def ends(self, parts=(0, 1)):
        z = self.place.z

        @pl.when(z == 0)
        def _():
            for dest in (3, 2, 1):
                self.pass_on(dest, True, False, parts)

        @pl.when(z == 3)
        def _():
            for dest in (0, 1, 2):
                self.pass_on(dest, False, False, parts)

    def inner(self, i, parts=(0, 1)):
        z = self.place.z

        @pl.when(z == 1)
        def _():
            if i == 0:
                self.pass_on(3, True, True, parts)
            else:
                self.pass_on(0, False, True, parts)
                self.pass_on(2, True, True, parts)

        @pl.when(z == 2)
        def _():
            if i == 0:
                self.pass_on(0, False, True, parts)
            else:
                self.pass_on(3, True, True, parts)
                self.pass_on(1, False, True, parts)

    def late_ends_after(self, n):
        z = self.place.z

        @pl.when((n > 1) & (z == 0))
        def _():
            self.pass_on(n - 1, True)

        @pl.when((n > 1) & (z == 3))
        def _():
            self.pass_on(4 - n, False)

    def late_inner(self, i):
        z = self.place.z

        @pl.when(z == 1)
        def _():
            dest = (2, 3, 0)[i]
            self.pass_on(dest, dest > 1, True)

        @pl.when(z == 2)
        def _():
            dest = (1, 0, 3)[i]
            self.pass_on(dest, dest > 1, True)

    def finish(self, out):
        self.total(out)
        self.settle()

    def total(self, out, parts=(0, 1)):
        place = self.place
        count = self.rows // self.PARTS
        for dest in range(4):

            @pl.when(place.z == dest)
            def _(dest=dest):
                if parts[0] == 0:
                    self.across(dest).wait_recv()
                for part in parts:
                    rows = slice(part * count, (part + 1) * count)
                    total = self.pair_sum(dest, part)
                    if dest > 0:
                        self.moved(dest - 1, part, place.up).wait_recv()
                        total = total + self.moving[dest - 1, rows].astype(jnp.float32)
                    if dest < 3:
                        self.moved(3 + dest, part, place.down).wait_recv()
                        total = total + self.moving[3 + dest, rows].astype(jnp.float32)
                    out[rows] = total

    def settle(self):
        place = self.place
        for dest in range(4):
            self.across(dest).wait_send()
        for i in range(3):
            top, bottom = 3 - i, i
            for part in range(self.PARTS):

                @pl.when(place.z < top)
                def _(top=top, part=part):
                    self.moved(top - 1, part, place.up).wait_send()

                @pl.when(place.z > bottom)
                def _(bottom=bottom, part=part):
                    self.moved(3 + bottom, part, place.down).wait_send()


class Spread:
    @staticmethod
    def sems(pieces, outs):
        return [
            pltpu.SemaphoreType.DMA((2, 8, pieces)),
            pltpu.SemaphoreType.DMA((2, 4, 8, outs)),
        ]

    def __init__(self, place, weight, outs, pieces, sems):
        self.place, self.weight, self.outs, self.pieces = place, weight, outs, pieces
        self.swap_sems, self.plane_sems = sems
        self.rows = weight.shape[0]

    def spot(self, f, c):
        return (f * 8 + c) * self.rows

    def swap(self, i, p, origin):
        column, width, out, out_column = self.pieces[p]
        peer = self.place.peer(i)
        src = self.weight.at[:, cols_at(column(peer), width)]
        dst = self.outs[out].at[
            rows_at(self.spot(self.place.f, origin), self.rows), pl.ds(out_column, width)
        ]
        if i == 0:
            return pltpu.make_async_copy(src, dst, self.swap_sems.at[0, 0, p])
        return remote(
            src,
            dst,
            self.swap_sems.at[0, i, p],
            self.swap_sems.at[1, i, p],
            (self.place.f, peer),
        )

    def whole(self, f, c, out):
        return self.outs[out].at[rows_at(self.spot(f, c), self.rows)]

    def part(self, f, c, out, half):
        count = self.rows // 2
        return self.outs[out].at[rows_at(self.spot(f, c) + half * count, count)]

    def plane(self, kind, i, out, ref, target):
        return remote(
            ref,
            ref,
            self.plane_sems.at[0, kind, i, out],
            self.plane_sems.at[1, kind, i, out],
            (target, self.place.c),
        )

    def start(self, first=0, last=8):
        for i in range(first, last):
            for p in range(len(self.pieces)):
                self.swap(i, p, self.place.c).start()

    def forward(self, i):
        place = self.place
        origin = place.peer(i)
        for p in range(len(self.pieces)):
            copy = self.swap(i, p, origin)
            if i == 0:
                copy.wait()
            else:
                copy.wait_recv()
        for out in range(len(self.outs)):
            ref = self.whole(place.f, origin, out)
            self.plane(0, i, out, ref, place.x_side).start()
            self.plane(1, i, out, ref, place.y_side).start()

    def relay(self, i):
        place = self.place
        origin = place.peer(i)
        for out in range(len(self.outs)):
            self.plane(0, i, out, self.whole(place.x_side, origin, out), place.x_side).wait_recv()
            self.plane(2, i, out, self.part(place.x_side, origin, out, 0), place.y_side).start()
            self.plane(1, i, out, self.whole(place.y_side, origin, out), place.y_side).wait_recv()
            self.plane(3, i, out, self.part(place.y_side, origin, out, 1), place.x_side).start()

    def finish(self, first=0, last=8):
        self.arrive(first, last)
        self.settle(first, last)

    def arrive(self, first=0, last=8):
        place = self.place
        for i in range(first, last):
            origin = place.peer(i)
            for out in range(len(self.outs)):
                self.plane(
                    2, i, out, self.part(place.diag, origin, out, 0), place.y_side
                ).wait_recv()
                self.plane(
                    3, i, out, self.part(place.diag, origin, out, 1), place.x_side
                ).wait_recv()

    def settle(self, first=0, last=8):
        place = self.place
        for i in range(first, last):
            origin = place.peer(i)
            if i:
                for p in range(len(self.pieces)):
                    self.swap(i, p, place.c).wait_send()
            for out in range(len(self.outs)):
                own = self.whole(place.f, origin, out)
                self.plane(0, i, out, own, place.x_side).wait_send()
                self.plane(1, i, out, own, place.y_side).wait_send()
                half = self.part(place.f, origin, out, 0)
                self.plane(2, i, out, half, place.y_side).wait_send()
                self.plane(3, i, out, half, place.x_side).wait_send()


class PlaneGather:
    SEMS = [pltpu.SemaphoreType.DMA((2, 4))]

    def __init__(self, place, out, sems):
        self.place, self.out = place, out
        self.sems = sems[0]
        self.rows = out.shape[0] // 4

    def copy(self, kind, f, target):
        count = self.rows // 2 if kind > 1 else self.rows
        start = f * self.rows + (count if kind == 3 else 0)
        ref = self.out.at[rows_at(start, count)]
        return remote(
            ref, ref, self.sems.at[0, kind], self.sems.at[1, kind], (target, self.place.c)
        )

    def start(self):
        place = self.place
        self.copy(0, place.f, place.x_side).start()
        self.copy(1, place.f, place.y_side).start()

    def relay(self):
        place = self.place
        self.copy(0, place.x_side, place.x_side).wait_recv()
        self.copy(2, place.x_side, place.y_side).start()
        self.copy(1, place.y_side, place.y_side).wait_recv()
        self.copy(3, place.y_side, place.x_side).start()

    def finish(self):
        place = self.place
        self.copy(2, place.diag, place.y_side).wait_recv()
        self.copy(3, place.diag, place.x_side).wait_recv()
        self.copy(0, place.f, place.x_side).wait_send()
        self.copy(1, place.f, place.y_side).wait_send()
        self.copy(2, place.x_side, place.y_side).wait_send()
        self.copy(3, place.y_side, place.x_side).wait_send()


DRAIN_ORDER = (0, 1, 4, 5, 2, 3, 6, 7)


class Drain:
    @staticmethod
    def scratch(rows, widths, peers=8):
        half = rows // 2
        lists = []
        for width in widths:
            lists += [
                pltpu.VMEM((2, peers, 2, half, width), jnp.bfloat16),
                pltpu.VMEM((2, peers, half, width), jnp.bfloat16),
            ]
        return lists

    @staticmethod
    def sems(pieces, outs, peers=8):
        return [
            pltpu.SemaphoreType.DMA((2, 2, peers, 2, outs)),
            pltpu.SemaphoreType.DMA((2, 2, peers, outs)),
            pltpu.SemaphoreType.DMA((2, peers, pieces, 2)),
        ]

    def __init__(self, place, grads, land, pieces, scratch, sems, base=0, peers=8, adds=None):
        self.place, self.grads, self.land, self.pieces = place, grads, land, pieces
        self.adds = adds or grads
        self.first = scratch[0::2]
        self.second = scratch[1::2]
        self.first_sems, self.second_sems, self.swap_sems = sems
        self.rows = land.shape[0]
        self.half = self.rows // 2
        self.units = grads[0].shape[0] < 32 * self.rows or peers < 8
        self.base, self.peers = base, peers

    def peer(self, i):
        return self.place.peer(DRAIN_ORDER[self.base + i])

    def part(self, g, f, i, half, adds=False):
        refs = self.adds if adds else self.grads
        peer = self.peer(i)
        if self.units:
            start = (i // 2 * 8 + f * 2 + peer % 2) * self.rows + half * self.half
            return refs[g].at[rows_at(start, self.half)]
        return refs[g].at[rows_at((f * 8 + peer) * self.rows + half * self.half, self.half)]

    def sides(self, axis):
        place = self.place
        return (place.x_side, place.y_side) if axis == 0 else (place.y_side, place.x_side)

    def first_copy(self, axis, i, which, g):
        near, _ = self.sides(axis)
        f = near if which == 0 else self.place.diag
        return remote(
            self.part(g, f, i, axis),
            self.first[g].at[axis, i, which],
            self.first_sems.at[0, axis, i, which, g],
            self.first_sems.at[1, axis, i, which, g],
            (near, self.place.c),
        )

    def second_copy(self, axis, i, g):
        _, far = self.sides(axis)
        return remote(
            self.first[g].at[axis, i, 1],
            self.second[g].at[axis, i],
            self.second_sems.at[0, axis, i, g],
            self.second_sems.at[1, axis, i, g],
            (far, self.place.c),
        )

    def swap(self, i, p, half, origin):
        column, width, g, g_column = self.pieces[p]
        src = self.first[g].at[half, i, 0, :, pl.ds(g_column, width)]
        dst = self.land.at[pl.ds(half * self.half, self.half), cols_at(column(origin), width)]
        if self.base + i == 0:
            return pltpu.make_async_copy(src, dst, self.swap_sems.at[0, i, p, half])
        return remote(
            src,
            dst,
            self.swap_sems.at[0, i, p, half],
            self.swap_sems.at[1, i, p, half],
            (self.place.f, self.peer(i)),
        )

    def start(self, i):
        for g in range(len(self.grads)):
            for which in (1, 0):
                for axis in range(2):
                    self.first_copy(axis, i, which, g).start()

    def middle(self, i):
        place = self.place
        for g in range(len(self.grads)):
            for axis in range(2):
                _, far = self.sides(axis)
                self.first_copy(axis, i, 1, g).wait_recv()
                mine = self.part(g, far, i, axis, True)
                self.first[g][axis, i, 1] = (
                    mine[...].astype(jnp.float32) + self.first[g][axis, i, 1].astype(jnp.float32)
                ).astype(jnp.bfloat16)
                self.second_copy(axis, i, g).start()

    def last(self, i):
        place = self.place
        for g in range(len(self.grads)):
            for axis in range(2):
                self.first_copy(axis, i, 0, g).wait_recv()
                self.second_copy(axis, i, g).wait_recv()
                mine = self.part(g, place.f, i, axis, True)
                self.first[g][axis, i, 0] = (
                    mine[...].astype(jnp.float32)
                    + self.first[g][axis, i, 0].astype(jnp.float32)
                    + self.second[g][axis, i].astype(jnp.float32)
                ).astype(jnp.bfloat16)
        for p in range(len(self.pieces)):
            for half in range(2):
                self.swap(i, p, half, place.c).start()

    def finish(self):
        place = self.place
        for i in range(self.peers):
            for p in range(len(self.pieces)):
                for half in range(2):
                    copy = self.swap(i, p, half, self.peer(i))
                    if self.base + i == 0:
                        copy.wait()
                    else:
                        copy.wait_recv()
                        copy.wait_send()
            for g in range(len(self.grads)):
                for axis in range(2):
                    for which in range(2):
                        self.first_copy(axis, i, which, g).wait_send()
                    self.second_copy(axis, i, g).wait_send()


ANY = pl.BlockSpec(memory_space=pl.ANY)
VMEM = pl.BlockSpec(memory_space=pltpu.VMEM)


def comm_call(kernel, ident, out_shape, in_specs, out_specs, scratch, aliases=None):
    return pl.pallas_call(
        kernel,
        input_output_aliases=aliases or {},
        out_shape=out_shape,
        in_specs=in_specs,
        out_specs=out_specs,
        scratch_shapes=scratch,
        compiler_params=pltpu.CompilerParams(
            collective_id=ident, has_side_effects=True, vmem_limit_bytes=VMEM_LIMIT
        ),
    )


class Local:
    def __init__(self, sems):
        self.sems, self.copies = sems, []

    def start(self, src, dst):
        self.copies.append(pltpu.make_async_copy(src, dst, self.sems.at[len(self.copies)]))
        self.copies[-1].start()
        return len(self.copies) - 1

    def wait(self, *indices):
        for index in indices:
            self.copies[index].wait()


def bf16(*shape):
    return jax.ShapeDtypeStruct(shape, jnp.bfloat16)


ATTN_PIECES = (
    (lambda c: 256 * c, 256, 0, 0),
    (lambda c: 2048 + 256 * (c // 4), 256, 0, 256),
    (lambda c: 2560 + 256 * (c // 4), 256, 0, 512),
    (lambda c: 3200 + 256 * c, 256, 1, 0),
    (lambda c: 3072, 128, 2, 0),
)
ATTN_LAND = (
    (lambda c: 1152 * c, 896, 0, 0),
    (lambda c: 1152 * c + 896, 256, 1, 0),
)
MLP_PIECES = (
    (lambda c: 1024 * c, 1024, 0, 0),
    (lambda c: 8192 + 1024 * c, 1024, 0, 1024),
    (lambda c: 16384 + 1024 * c, 1024, 1, 0),
)
EARLY_UNITS = 2
VEC_LAND = ((lambda c: 512 * c, 512, 0, 0),)


def turn(values, cosine, sine):
    half = HEAD // 2
    first, second = values[:, :half], values[:, half:]
    return jnp.concatenate(
        [first * cosine - second * sine, second * cosine + first * sine], axis=1
    )


def allowed_pairs(first_query, first_key, positions):
    shape = (positions.shape[0], 768)
    distance = (
        lax.broadcasted_iota(jnp.int32, shape, 0)
        - lax.broadcasted_iota(jnp.int32, shape, 1)
        + (first_query - first_key)
    )
    return (distance >= 0) & (distance <= jnp.minimum(positions, WINDOW - 1))


def positions_of(parts):
    return (parts[:, 0:1].astype(jnp.float32) * 256.0 + parts[:, 1:2].astype(jnp.float32)).astype(
        jnp.int32
    )


def attention_forward(own_pos, w_attn, w_mlp, hidden, gains, head_gains, tables, ident):
    height = 32 * w_attn.shape[0]
    rows, width = hidden.shape
    total = 8 * rows
    query_block, key_span = 2 * rows, 768
    scatter_scratch = ChainScatter.scratch(rows, width)

    def kernel(*refs):
        ins, outs, held = split_refs(refs, 7, 17, len(refs) - 24)
        pos_ref, attn_ref, mlp_ref, hidden_ref, gains_ref, head_ref, tables_ref = ins
        (row_hbm, qkv_hbm, out_hbm, laurel_ref, row_pos, gate_up_ref, down_ref, row_ffn,
         projected_hbm, q_low, k_low, v_low, mixed, latent_ref, laurel_up, attn_out, joined) = outs
        scratch, scat, attn_m, mlp_m, gather_m, local_m = split_refs(
            held, 8, len(scatter_scratch), 2, 2, 8, 1
        )
        (own_ffn, partial, own_ref, normed_ref, row_ref, qkv_ref, out_ref, projected) = scratch
        place = Place()
        local = Local(local_m[0])
        normed_ref[...] = rms_norm(hidden_ref[...].astype(jnp.float32), gains_ref[0:1])
        own_ref[...] = normed_ref[...].astype(jnp.bfloat16)
        greet(place, "all", True)
        attn = Spread(place, attn_ref, [qkv_ref, out_ref, laurel_ref], ATTN_PIECES, attn_m)
        mlp = Spread(place, mlp_ref, [gate_up_ref, down_ref], MLP_PIECES, mlp_m)
        gathers = [
            ChainGather(place, own_ref, row_ref, gather_m[0:2]),
            ChainGather(place, pos_ref, row_pos, gather_m[2:4]),
        ]
        last = [
            ChainGather(
                place, own_ffn.at[pl.ds(part * (rows // 2), rows // 2)], row_ffn,
                gather_m[4 + 2 * part : 6 + 2 * part], rows, part * (rows // 2),
            )
            for part in range(2)
        ]
        scatter = ChainScatter(place, partial, scat)

        def step(n):
            for gather in gathers:
                gather.step(n)

        for gather in gathers:
            gather.start()
        attn.start(0, 4)
        mlp.start(0, 2)
        attn.forward(0)
        attn.forward(1)
        mlp.forward(0)
        step(1)
        attn.start(4, 6)
        mlp.start(4, 5)
        attn.forward(2)
        attn.forward(3)
        attn.relay(0)
        attn.relay(1)
        step(2)
        attn.start(6, 8)
        mlp.start(5, 6)
        attn.forward(4)
        attn.forward(5)
        attn.relay(2)
        attn.relay(3)
        step(3)
        attn.forward(6)
        attn.forward(7)
        mlp.start(2, 4)
        attn.relay(4)
        attn.relay(5)
        mlp.relay(0)
        attn.relay(6)
        attn.relay(7)
        for gather in gathers:
            gather.arrive()
        attn.arrive()
        mlp.forward(1)
        mlp.start(6, 7)
        local.start(row_ref, row_hbm)
        local.start(qkv_ref, qkv_hbm)
        local.start(out_ref, out_hbm)

        @pl.loop(0, total // query_block)
        def _(n):
            here = rows_at(n * query_block, query_block)
            block = plain_dot(row_ref[here], qkv_ref[...])
            projected[here] = block
            cosine, sine = tables_ref[here, : HEAD // 2], tables_ref[here, HEAD // 2 :]
            q_low[here] = turn(
                rms_norm(block[:, :HEAD], head_ref[0:1]), cosine, sine
            ).astype(jnp.bfloat16)
            k_low[here] = turn(
                rms_norm(block[:, HEAD : 2 * HEAD], head_ref[1:2]), cosine, sine
            ).astype(jnp.bfloat16)
            v_low[here] = value_norm(block[:, 2 * HEAD :]).astype(jnp.bfloat16)

        mlp.start(7, 8)
        local.start(projected, projected_hbm)
        upper = place.z // 2

        @pl.loop(0, total // query_block)
        def _(n):
            d = n * upper + (3 - n) * (1 - upper)
            here = rows_at(d * query_block, query_block)
            first_key = (d // 2) * (d - 2) * query_block
            there = rows_at(first_key, key_span)
            scores = jnp.where(
                allowed_pairs(d * query_block, first_key, positions_of(row_pos[here])),
                times_transposed(q_low[here], k_low[there]),
                NEG_LARGE,
            )
            weights = jnp.exp(scores - jnp.max(scores, axis=-1, keepdims=True))
            probs = (weights / jnp.sum(weights, axis=-1, keepdims=True)).astype(jnp.bfloat16)
            block = plain_dot(probs, v_low[there]).astype(jnp.bfloat16)
            mixed[here] = block
            partial[here] = times_transposed(block, out_ref[...]).astype(jnp.bfloat16)
            scatter.across(d).start()

        scatter.ends((0,))
        scatter.ends((1,))
        mlp.relay(1)
        mlp.forward(2)
        mlp.forward(3)
        scatter.inner(0, (0,))
        mlp.forward(4)
        low = plain_dot(own_ref[...], laurel_ref[...])
        latent_ref[...] = low.astype(jnp.bfloat16)
        lanes = lax.broadcasted_iota(jnp.int32, low.shape, 1)
        shifted = jnp.where(lanes >= RANK, pltpu.roll(low, RANK, 1), 0.0).astype(jnp.bfloat16)
        laurel_up[...] = times_transposed(shifted, laurel_ref[...])
        scatter.inner(1, (0,))
        mlp.forward(5)

        def close(part):
            here = slice(part * (rows // 2), (part + 1) * (rows // 2))
            laurel_res = normed_ref[here] + rms_norm(laurel_up[here], gains_ref[1:2])
            after_attn = hidden_ref[here].astype(jnp.float32) + rms_norm(
                attn_out[here], gains_ref[2:3]
            )
            joined[here] = (after_attn + laurel_res) / math.sqrt(2.0)
            own_ffn[here] = rms_norm(joined[here], gains_ref[3:4]).astype(jnp.bfloat16)

        scatter.total(attn_out, (0,))
        close(0)
        last[0].start()
        scatter.inner(0, (1,))
        scatter.inner(1, (1,))
        mlp.relay(2)
        mlp.relay(3)
        last[0].step(1)
        scatter.total(attn_out, (1,))
        close(1)
        last[1].start()
        mlp.relay(4)
        mlp.forward(6)
        mlp.forward(7)
        last[0].step(2)
        last[1].step(1)
        mlp.relay(5)
        last[0].step(3)
        mlp.relay(6)
        last[1].step(2)
        mlp.relay(7)
        last[1].step(3)
        scatter.settle()
        mlp.arrive()
        for gather in last:
            gather.arrive()
        attn.settle()
        mlp.settle()
        for gather in gathers + last:
            gather.settle()
        local.wait(0, 1, 2, 3)

    def f32(*shape):
        return jax.ShapeDtypeStruct(shape, jnp.float32)

    token_f32 = f32(rows, width)
    head = bf16(total, HEAD)
    outs = [bf16(total, width), bf16(height, 768), bf16(height, 256), bf16(height, 128)]
    outs += [bf16(total, 128), bf16(height, 2048), bf16(height, 1024), bf16(total, width)]
    outs += [f32(total, 768), head, head, head, head, bf16(rows, 128)]
    outs += [token_f32, token_f32, token_f32]
    return comm_call(
        kernel,
        ident,
        outs,
        [VMEM, ANY, ANY] + [VMEM] * 4,
        [ANY] * 3 + [VMEM] * 2 + [ANY] * 4 + [VMEM] * 8,
        [
            pltpu.VMEM((rows, width), jnp.bfloat16),
            pltpu.VMEM((total, width), jnp.bfloat16),
            pltpu.VMEM((rows, width), jnp.bfloat16),
            pltpu.VMEM((rows, width), jnp.float32),
            pltpu.VMEM((total, width), jnp.bfloat16),
            pltpu.VMEM((height, 768), jnp.bfloat16),
            pltpu.VMEM((height, 256), jnp.bfloat16),
            pltpu.VMEM((total, 768), jnp.float32),
        ]
        + scatter_scratch
        + Spread.sems(len(ATTN_PIECES), 3)
        + Spread.sems(len(MLP_PIECES), 2)
        + ChainGather.SEMS * 4
        + [pltpu.SemaphoreType.DMA((4,))],
    )(own_pos, w_attn, w_mlp, hidden, gains, head_gains, tables)


def split_refs(refs, *counts):
    refs, parts = list(refs), []
    for count in counts:
        parts.append(refs[:count])
        refs = refs[count:]
    return parts


def turn_back(grads, cosine, sine):
    half = HEAD // 2
    first, second = grads[:, :half], grads[:, half:]
    return jnp.concatenate(
        [first * cosine + second * sine, second * cosine - first * sine], axis=1
    )


def norm_back(values, scale_vec, grads):
    inverse = lax.rsqrt(jnp.mean(values * values, axis=-1, keepdims=True) + EPSILON)
    unit = values * inverse
    scaled = grads * scale_vec
    back = (scaled - unit * jnp.mean(unit * scaled, axis=-1, keepdims=True)) * inverse
    return back, jnp.sum(grads * unit, axis=0, keepdims=True)


def unit_gradient(place, n, tokens_ref, grad_ref, out, turned_ref):
    zz = place.partner(ORDER[DRAIN_ORDER[2 * n]][0])
    unit_rows = turned_ref.shape[0]
    count = unit_rows // 4
    for f in range(4):
        columns = cols_at((f * 4 + zz) * count, count)
        turned_ref[f * count : (f + 1) * count] = tokens_ref[:, columns].T
    step = 512

    @pl.loop(0, grad_ref.shape[1] // step)
    def _(t):
        columns = cols_at(t * step, step)
        out[n * unit_rows : (n + 1) * unit_rows, columns] = plain_dot(
            turned_ref[...], grad_ref[:, columns]
        ).astype(jnp.bfloat16)


def gelu_pair(values):
    scale = math.sqrt(2.0 / math.pi)
    squares = values * values
    bend = jnp.tanh(scale * values * (1.0 + 0.044715 * squares))
    half = 0.5 * (1.0 + bend)
    slope = half + 0.5 * values * (1.0 - bend * bend) * scale * (1.0 + 3.0 * 0.044715 * squares)
    return values * half, slope


def ffn_layer(
    row_ffn, w_gate_up, w_down, joined, attn_out, laurel_up, gains, layer_vec, pl_gate, pl_proj,
    out_grad, shard_height, mlp_cols, ident
):
    rows, width = joined.shape
    total, hidden_units = 8 * rows, w_down.shape[1]
    block, chunk = 2 * rows, hidden_units // 2
    vec_width = 2 * pl_gate.shape[1]
    unit_rows = 8 * shard_height
    scatter_scratch = ChainScatter.scratch(rows, width)
    early, late = 2 * EARLY_UNITS, 4 - EARLY_UNITS
    mlp_scratch = Drain.scratch(shard_height, (2 * hidden_units, hidden_units), early)
    mlp_sems = Drain.sems(len(MLP_PIECES), 2, early)
    vec_scratch = Drain.scratch(shard_height, (vec_width,))
    vec_sems = Drain.sems(1, 1)

    def kernel(*refs):
        ins, outs, held = split_refs(refs, 11, 10, len(refs) - 21)
        ffn_hbm, gate_up_hbm, down_hbm = ins[:3]
        (joined_ref, attn_ref, laurel_ref, gains_ref, vector_ref, pl_gate_ref, pl_proj_ref,
         out_grad_ref) = ins[3:]
        (result_ref, d_vector_ref, d_half_ref, d_attn_ref, d_laurel_ref, gain_ref, mlp_land,
         vec_land, late_wide, late_narrow) = outs
        scratch, scat, mlp_s, mlp_m, vec_s, vec_m, gather_m, last = split_refs(
            held, 12, len(scatter_scratch), len(mlp_scratch), 3, len(vec_scratch), 3, 2, 1
        )
        (ffn_ref, gate_up_ref, down_ref, slopes, active, row_grad, partial, turned, vec_grad,
         own_grad, ffn_out, grad_after) = scratch
        place = Place()
        local = Local(last[0])
        local.start(ffn_hbm, ffn_ref)
        local.start(gate_up_hbm, gate_up_ref)
        down_copy = local.start(down_hbm, down_ref)
        greet(place, "all", True)
        scatter = ChainScatter(place, partial, scat)
        gather = ChainGather(place, own_grad, row_grad, gather_m)
        mlp = Drain(
            place, [gate_up_ref, down_ref], mlp_land, MLP_PIECES, mlp_s, mlp_m, 0, early
        )
        vec = Drain(place, [vec_grad], vec_land, VEC_LAND, vec_s, vec_m)
        upper = place.z // 2

        local.wait(0, 1, down_copy)

        @pl.loop(0, total // block)
        def _(n):
            d = n * upper + (3 - n) * (1 - upper)
            here = rows_at(d * block, block)
            for t in range(2):
                gates = pl.ds(t * chunk, chunk)
                ups = pl.ds(hidden_units + t * chunk, chunk)
                gate = plain_dot(ffn_ref[here], gate_up_ref[:, gates])
                up = plain_dot(ffn_ref[here], gate_up_ref[:, ups])
                value, slope = gelu_pair(gate)
                active[here, gates] = (value * up).astype(jnp.bfloat16)
                slopes[here, gates] = (slope * up).astype(jnp.bfloat16)
                slopes[here, ups] = value.astype(jnp.bfloat16)
            partial[here] = times_transposed(active[here], down_ref[...]).astype(jnp.bfloat16)
            scatter.across(d).start()
            scatter.ends_after(n)

        scatter.inner(0)
        scatter.inner(1)
        scatter.finish(ffn_out)

        after = joined_ref[...] + rms_norm(ffn_out[...], gains_ref[4:5])
        after_low = after.astype(jnp.bfloat16)
        vec_gate = plain_dot(after_low, pl_gate_ref[...])
        vector = vector_ref[...].astype(jnp.float32)
        value, slope = gelu_pair(vec_gate)
        vec_mixed = (value * vector).astype(jnp.bfloat16)
        vec_out = plain_dot(vec_mixed, pl_proj_ref[...])
        result_ref[...] = (after + rms_norm(vec_out, gains_ref[5:6])).astype(jnp.bfloat16)
        upstream = out_grad_ref[...].astype(jnp.float32)
        d_vec_out, d_scale = norm_back(vec_out, gains_ref[5:6], upstream)
        gain_ref[...] = jnp.zeros_like(gain_ref)
        gain_ref[5:6] = d_scale
        d_vec_out_low = d_vec_out.astype(jnp.bfloat16)
        d_vec_mixed = times_transposed(d_vec_out_low, pl_proj_ref[...])
        d_vector_ref[...] = d_vec_mixed * value
        d_vec_gate_low = (d_vec_mixed * vector * slope).astype(jnp.bfloat16)
        grad_after[...] = upstream + times_transposed(d_vec_gate_low, pl_gate_ref[...])
        d_ffn_out, d_scale = norm_back(ffn_out[...], gains_ref[4:5], grad_after[...])
        gain_ref[4:5] = d_scale
        own_grad[...] = d_ffn_out.astype(jnp.bfloat16)
        gather.start()
        half = vec_width // 2
        vec_grad[:, :half] = contract_rows(after_low, d_vec_gate_low).astype(jnp.bfloat16)
        vec_grad[:, half:] = contract_rows(d_vec_out_low, vec_mixed).astype(jnp.bfloat16)
        for i in range(8):
            vec.start(i)
        gather.local().wait()

        @pl.loop(0, total // block)
        def _(n):
            for step in (1, 2, 3):

                @pl.when(n == step)
                def _(step=step):
                    gather.step(step)
                    for i in ((), range(4), range(4, 8), ())[step]:
                        vec.middle(i)
                    for i in ((), (), range(4), range(4, 8))[step]:
                        vec.last(i)

            d = gather.near_first(n)
            gather.from_sibling(d).wait_recv()
            here = rows_at(d * block, block)
            for t in range(2):
                gates = pl.ds(t * chunk, chunk)
                ups = pl.ds(hidden_units + t * chunk, chunk)
                d_active = plain_dot(row_grad[here], down_ref[:, gates])
                slopes[here, gates] = (d_active * slopes[here, gates].astype(jnp.float32)).astype(
                    jnp.bfloat16
                )
                slopes[here, ups] = (d_active * slopes[here, ups].astype(jnp.float32)).astype(
                    jnp.bfloat16
                )
            partial[here] = times_transposed(slopes[here], gate_up_ref[...]).astype(jnp.bfloat16)
            scatter.across(d).start()
            scatter.late_ends_after(n)

        scatter.late_ends_after(4)

        def unit(n):
            unit_gradient(place, n, ffn_ref, slopes, gate_up_ref, turned)
            unit_gradient(place, n, row_grad, active, down_ref, turned)

        first = EARLY_UNITS - 1
        scatter.late_inner(0)
        unit(first)
        mlp.start(2 * first)
        mlp.start(2 * first + 1)
        scatter.late_inner(1)
        unit(1 - first)
        scatter.late_inner(2)
        for i in range(2 * first):
            mlp.start(i)
        mlp.middle(2 * first)
        mlp.middle(2 * first + 1)
        unit(2)
        mlp.last(2 * first)
        mlp.last(2 * first + 1)
        for i in range(2 * first):
            mlp.middle(i)
        unit(3)
        kept = [
            local.start(ref.at[pl.ds(EARLY_UNITS * unit_rows, late * unit_rows)], out)
            for ref, out in ((gate_up_ref, late_wide), (down_ref, late_narrow))
        ]
        scatter.finish(ffn_out)
        d_joined, d_scale = norm_back(joined_ref[...], gains_ref[3:4], ffn_out[...])
        gain_ref[3:4] = d_scale
        d_half = (grad_after[...] + d_joined) / math.sqrt(2.0)
        d_half_ref[...] = d_half
        d_attn, d_scale = norm_back(attn_ref[...], gains_ref[2:3], d_half)
        gain_ref[2:3] = d_scale
        d_attn_ref[...] = d_attn.astype(jnp.bfloat16)
        d_laurel, d_scale = norm_back(laurel_ref[...], gains_ref[1:2], d_half)
        gain_ref[1:2] = d_scale
        d_laurel_ref[...] = d_laurel.astype(jnp.bfloat16)
        for i in range(2 * first):
            mlp.last(i)
        gather.settle()
        vec.finish()
        local.wait(*kept)
        mlp.finish()

    def f32(*shape):
        return jax.ShapeDtypeStruct(shape, jnp.float32)

    def held_bf16(*shape):
        return pltpu.VMEM(shape, jnp.bfloat16)

    return comm_call(
        kernel,
        ident,
        [
            bf16(rows, width),
            f32(rows, vec_width // 2),
            f32(rows, width),
            bf16(rows, width),
            bf16(rows, width),
            f32(8, width),
            bf16(shard_height, mlp_cols),
            bf16(shard_height, 8 * vec_width),
            bf16(late * unit_rows, 2 * hidden_units),
            bf16(late * unit_rows, hidden_units),
        ],
        [ANY] * 3 + [VMEM] * 8,
        [VMEM] * 6 + [ANY] * 4,
        [
            held_bf16(total, width),
            held_bf16(*w_gate_up.shape),
            held_bf16(*w_down.shape),
            held_bf16(total, 2 * hidden_units),
            held_bf16(total, hidden_units),
            held_bf16(total, width),
            held_bf16(total, width),
            held_bf16(unit_rows, total),
            held_bf16(width, vec_width),
            held_bf16(rows, width),
            pltpu.VMEM((rows, width), jnp.float32),
            pltpu.VMEM((rows, width), jnp.float32),
        ]
        + scatter_scratch
        + mlp_scratch
        + mlp_sems
        + vec_scratch
        + vec_sems
        + ChainGather.SEMS
        + [pltpu.SemaphoreType.DMA((5,))],
    )(
        row_ffn, w_gate_up, w_down, joined, attn_out, laurel_up, gains, layer_vec, pl_gate,
        pl_proj, out_grad,
    )


def sum_everywhere(place, own, arrived, sems):
    k, f = place.k, place.f
    targets = [
        place.sibling,
        (place.x_side, place.c),
        (place.y_side, place.c),
        (f, place.partner(1) * 2 + k),
        (f, place.partner(3) * 2 + k),
    ]
    return [
        remote(own.at[n], arrived.at[n], sems.at[0, n], sems.at[1, n], target)
        for n, target in enumerate(targets)
    ]


def attention_backward(
    d_attn_low, d_laurel_low, d_half, weights, kept, tables, head_gains, hidden, gains,
    other_gains, mlp_grads, mlp_land, vec_land, ident
):
    w_qkv, w_out, w_laurel = weights
    queries, keys, values, mixed, latent, projected, row_normed, row_parts = kept
    rows, width = d_half.shape
    total = 8 * rows
    query_block, key_span = 2 * rows, 768
    shard_height, vec_width = vec_land.shape[0], vec_land.shape[1] // 8
    qkv_width, laurel_width = w_qkv.shape[1], w_laurel.shape[1]
    attn_widths = (qkv_width + laurel_width, w_out.shape[1])
    scatter_scratch = ChainScatter.scratch(rows, width)
    first_late, late = 2 * EARLY_UNITS, 8 - 2 * EARLY_UNITS
    mlp_scratch = Drain.scratch(shard_height, [grad.shape[1] for grad in mlp_grads], late)
    mlp_sems = Drain.sems(len(MLP_PIECES), 2, late)
    loads = [*mlp_grads, w_out, queries, keys, values, tables, projected, w_qkv, mixed, row_normed]
    attn_scratch = Drain.scratch(shard_height, attn_widths)
    attn_sems = Drain.sems(len(ATTN_LAND), 2)
    gain_rows = other_gains.shape[0]

    def kernel(*refs):
        ins, outs, held = split_refs(refs, 23, 5, len(refs) - 28)
        (own_ref, row_pos, head_ref, hidden_ref, gains_ref, base_ref, other_ref, laurel_ref,
         vec_ref, w_laurel_ref, latent_ref) = ins[:11]
        wide_hbm, narrow_hbm = ins[11:13]
        out_ref, gain_ref, land_ref, attn_land, vec_all = outs
        (scratch, loaded, local_sems, gain_s, scat, mlp_s, mlp_m, attn_s, attn_m, vec_m, gather_m) = (
            split_refs(
                held, 9, 11, 1, 3, len(scatter_scratch), len(mlp_scratch), 3, len(attn_scratch), 3,
                3, 2,
            )
        )
        (vec_own, row_grad, d_mixed, d_keys, d_values, d_projected, qkv_grad, out_grad,
         laurel_back) = scratch
        (wide_ref, narrow_ref, w_out_ref, q_low, k_low, v_low, tables_ref, projected_ref, qkv_ref,
         mixed_ref, row_ref) = loaded
        held_gains, arrived_gains, gain_sems = gain_s
        place = Place()
        local = Local(local_sems[0])
        for src, dst in zip(ins[11:22], loaded):
            local.start(src, dst)
        greet(place, "all", True)
        gather = ChainGather(place, own_ref, row_grad, gather_m)
        scatter = ChainScatter(place, row_grad, scat)
        mlp = Drain(
            place, [wide_hbm, narrow_hbm], land_ref, MLP_PIECES, mlp_s, mlp_m, first_late, late,
            [wide_ref, narrow_ref],
        )
        attn = Drain(place, [qkv_grad, out_grad], attn_land, ATTN_LAND, attn_s, attn_m)
        vec = ChainGather(
            place, vec_own, vec_all.at[rows_at(place.f * 8 * shard_height, 8 * shard_height)],
            vec_m[:2],
        )
        plane = PlaneGather(place, vec_all, vec_m[2:])
        rounds = sum_everywhere(place, held_gains, arrived_gains, gain_sems)

        def gain_round(n):
            rounds[n].wait_recv()
            held_gains[n + 1] = held_gains[n] + arrived_gains[n]
            if n < 4:
                rounds[n + 1].start()

        gather.start()
        mlp.start(0)
        mlp.start(1)
        vec_sum = vec_ref[:, 0:vec_width].astype(jnp.float32)
        for c in range(1, 8):
            vec_sum = vec_sum + vec_ref[:, c * vec_width : (c + 1) * vec_width].astype(jnp.float32)
        vec_own[...] = vec_sum.astype(jnp.bfloat16)
        vec.start()
        d_keys[...] = jnp.zeros_like(d_keys)
        d_values[...] = jnp.zeros_like(d_values)
        held_gains[0] = other_ref[...]
        low = plain_dot(laurel_ref[...], w_laurel_ref[...])
        lanes = lax.broadcasted_iota(jnp.int32, low.shape, 1)
        d_latent = jnp.where(lanes < RANK, pltpu.roll(low, RANK, 1), 0.0).astype(jnp.bfloat16)
        laurel_back[...] = base_ref[...] + times_transposed(d_latent, w_laurel_ref[...])
        normed_low = rms_norm(hidden_ref[...].astype(jnp.float32), gains_ref[0:1]).astype(
            jnp.bfloat16
        )
        shifted = pltpu.roll(latent_ref[...].astype(jnp.float32), RANK, 1)
        up_side = jnp.where(lanes >= RANK, shifted, 0.0).astype(jnp.bfloat16)
        qkv_grad[:, qkv_width:] = (
            contract_rows(normed_low, d_latent) + contract_rows(laurel_ref[...], up_side)
        ).astype(jnp.bfloat16)
        local.wait(0, 1)
        gather.step(1)
        vec.step(1)
        mlp.middle(0)
        mlp.middle(1)
        for i in range(2, late):
            mlp.start(i)
        gather.step(2)
        vec.step(2)
        mlp.last(0)
        mlp.last(1)
        gather.step(3)
        vec.step(3)
        gather.arrive()
        vec.arrive()
        plane.start()
        local.wait(2, 3, 4, 5, 6, 7)

        @pl.loop(0, total // query_block)
        def _(n):
            here = rows_at(n * query_block, query_block)
            d_mixed[here] = plain_dot(row_grad[here], w_out_ref[...]).astype(jnp.bfloat16)

        for i in range(2, late):
            mlp.middle(i)

        @pl.loop(0, total // query_block)
        def _(d):
            here = rows_at(d * query_block, query_block)
            first_key = (d // 2) * (d - 2) * query_block
            there = rows_at(first_key, key_span)
            query, key, value, d_mix = q_low[here], k_low[there], v_low[there], d_mixed[here]
            scores = jnp.where(
                allowed_pairs(d * query_block, first_key, positions_of(row_pos[here])),
                times_transposed(query, key),
                NEG_LARGE,
            )
            exps = jnp.exp(scores - jnp.max(scores, axis=-1, keepdims=True))
            probs = exps / jnp.sum(exps, axis=-1, keepdims=True)
            d_probs = times_transposed(d_mix, value)
            inner_sum = jnp.sum(probs * d_probs, axis=-1, keepdims=True)
            d_scores = (probs * (d_probs - inner_sum)).astype(jnp.bfloat16)
            d_keys[there] += contract_rows(d_scores, query)
            d_values[there] += contract_rows(probs.astype(jnp.bfloat16), d_mix)
            cosine, sine = tables_ref[here, : HEAD // 2], tables_ref[here, HEAD // 2 :]
            d_query, d_scale = norm_back(
                projected_ref[here, :HEAD],
                head_ref[0:1],
                turn_back(plain_dot(d_scores, key), cosine, sine),
            )
            d_projected[here, :HEAD] = d_query.astype(jnp.bfloat16)
            held_gains[0, 6:7, :HEAD] += d_scale

        for i in range(2, late):
            mlp.last(i)

        @pl.loop(0, total // query_block)
        def _(n):
            here = rows_at(n * query_block, query_block)
            cosine, sine = tables_ref[here, : HEAD // 2], tables_ref[here, HEAD // 2 :]
            d_key, d_scale = norm_back(
                projected_ref[here, HEAD : 2 * HEAD],
                head_ref[1:2],
                turn_back(d_keys[here], cosine, sine),
            )
            d_projected[here, HEAD : 2 * HEAD] = d_key.astype(jnp.bfloat16)
            held_gains[0, 6:7, HEAD : 2 * HEAD] += d_scale
            d_value, _ = norm_back(projected_ref[here, 2 * HEAD :], 1.0, d_values[here])
            d_projected[here, 2 * HEAD :] = d_value.astype(jnp.bfloat16)

        quarter = width // 4
        local.wait(8, 9, 10)

        @pl.loop(0, 4)
        def _(n):
            columns = cols_at(n * quarter, quarter)
            out_grad[rows_at(n * quarter, quarter)] = contract_rows(
                row_grad[:, columns], mixed_ref[...]
            ).astype(jnp.bfloat16)

        gather.settle()
        upper = place.z // 2

        @pl.loop(0, total // query_block)
        def _(n):
            d = n * upper + (3 - n) * (1 - upper)
            here = rows_at(d * query_block, query_block)
            row_grad[here] = times_transposed(d_projected[here], qkv_ref[...]).astype(jnp.bfloat16)
            scatter.across(d).start()

        scatter.ends()

        @pl.loop(0, 4)
        def _(n):
            columns = cols_at(n * quarter, quarter)
            qkv_grad[rows_at(n * quarter, quarter), :qkv_width] = contract_rows(
                row_ref[:, columns], d_projected[...]
            ).astype(jnp.bfloat16)

        attn.start(0)
        attn.start(1)
        attn.start(2)
        attn.start(3)
        scatter.inner(0)
        plane.relay()
        scatter.inner(1)
        attn.middle(0)
        attn.start(4)
        attn.middle(1)
        attn.start(5)
        attn.last(0)
        attn.middle(2)
        attn.start(6)
        attn.last(1)
        scatter.finish(out_ref)
        d_normed = laurel_back[...] + out_ref[...]
        d_hidden, d_scale = norm_back(
            hidden_ref[...].astype(jnp.float32), gains_ref[0:1], d_normed
        )
        out_ref[...] = d_hidden
        held_gains[0, 0:1] = d_scale
        rounds[0].start()
        attn.start(7)
        for i in range(3, 8):
            attn.middle(i)
            attn.last(i - 1)
            gain_round(i - 3)
        attn.last(7)
        gain_ref[...] = held_gains[5]
        for copy in rounds:
            copy.wait_send()
        vec.settle()
        plane.finish()
        mlp.finish()
        attn.finish()

    return comm_call(
        kernel,
        ident,
        [
            jax.ShapeDtypeStruct((rows, width), jnp.float32),
            jax.ShapeDtypeStruct((gain_rows, width), jnp.float32),
            bf16(*mlp_land.shape),
            bf16(shard_height, 8 * sum(attn_widths)),
            bf16(32 * shard_height, vec_width),
        ],
        [VMEM] * 11 + [ANY] * 12,
        [VMEM, VMEM, ANY, ANY, ANY],
        [
            pltpu.VMEM((shard_height, vec_width), jnp.bfloat16),
            pltpu.VMEM((total, width), jnp.bfloat16),
            pltpu.VMEM((total, HEAD), jnp.bfloat16),
            pltpu.VMEM((total, HEAD), jnp.float32),
            pltpu.VMEM((total, HEAD), jnp.float32),
            pltpu.VMEM((total, qkv_width), jnp.bfloat16),
            pltpu.VMEM((width, attn_widths[0]), jnp.bfloat16),
            pltpu.VMEM((width, attn_widths[1]), jnp.bfloat16),
            pltpu.VMEM((rows, width), jnp.float32),
        ]
        + [pltpu.VMEM(array.shape, array.dtype) for array in loads]
        + [
            pltpu.SemaphoreType.DMA((len(loads),)),
            pltpu.VMEM((6, gain_rows, width), jnp.float32),
            pltpu.VMEM((5, gain_rows, width), jnp.float32),
            pltpu.SemaphoreType.DMA((2, 5)),
        ]
        + scatter_scratch
        + mlp_scratch
        + mlp_sems
        + attn_scratch
        + attn_sems
        + ChainGather.SEMS
        + PlaneGather.SEMS
        + ChainGather.SEMS,
        {22: 2},
    )(
        d_attn_low, row_parts, head_gains, hidden, gains, d_half, other_gains, d_laurel_low,
        vec_land, w_laurel, latent, *loads, mlp_land,
    )


def finish_outputs(mlp_land, attn_land, vec_all, d_half, d_hidden_part, attn_cols):
    height, mlp_cols = mlp_land.shape
    rows, width = d_half.shape
    model, vec_width = vec_all.shape
    per_source = attn_land.shape[1] // 8
    half = vec_width // 2
    group = QH // KVH
    kv_first, laurel_first, out_first = QH * HEAD, (QH + 2 * KVH) * HEAD, 3200

    def kernel(mlp_ref, attn_ref, vec_ref, half_ref, part_ref, *outs):
        mlp_out, attn_out, gate_out, proj_out, hidden_out = outs
        c = pl.program_id(0)
        mlp_out[...] = mlp_ref[...].astype(jnp.float32)
        gate_out[...] = vec_ref[:, :half].astype(jnp.float32)
        proj_out[...] = vec_ref[:, half:].astype(jnp.float32).T
        hidden_out[...] = half_ref[...] + part_ref[...]
        landed = attn_ref[...].astype(jnp.float32)
        attn_out[:, cols_at(c * HEAD, HEAD)] = landed[:, :HEAD]
        attn_out[:, cols_at(out_first + c * HEAD, HEAD)] = landed[:, per_source - HEAD :]

        def add(first, count, start, fresh):
            columns = cols_at(first, count)
            value = landed[:, start : start + count]

            @pl.when(fresh)
            def _():
                attn_out[:, columns] = value

            @pl.when(jnp.logical_not(fresh))
            def _():
                attn_out[:, columns] += value

        add(kv_first + c // group * HEAD, HEAD, HEAD, c % group == 0)
        add(kv_first + (KVH + c // group) * HEAD, HEAD, 2 * HEAD, c % group == 0)
        add(laurel_first, 2 * RANK, 3 * HEAD, c == 0)

    def spec(block, by_column):
        return pl.BlockSpec(block, (lambda c: (0, c)) if by_column else (lambda c: (c, 0)))

    f32 = jnp.float32
    return pl.pallas_call(
        kernel,
        grid=(8,),
        out_shape=[
            jax.ShapeDtypeStruct((height, mlp_cols), f32),
            jax.ShapeDtypeStruct((height, attn_cols), f32),
            jax.ShapeDtypeStruct((model, half), f32),
            jax.ShapeDtypeStruct((half, model), f32),
            jax.ShapeDtypeStruct((rows, width), f32),
        ],
        in_specs=[
            spec((height, mlp_cols // 8), True),
            spec((height, per_source), True),
            spec((model // 8, vec_width), False),
            spec((rows // 8, width), False),
            spec((rows // 8, width), False),
        ],
        out_specs=[
            spec((height, mlp_cols // 8), True),
            pl.BlockSpec((height, attn_cols), lambda c: (0, 0)),
            spec((model // 8, half), False),
            spec((half, model // 8), True),
            spec((rows // 8, width), False),
        ],
    )(mlp_land, attn_land, vec_all, d_half, d_hidden_part)


def per_device_split(
    hidden_in, layer_vec, positions, w_attn, w_mlp, pl_gate, pl_proj, gains, head_gains, out_grad
):
    shard_height = w_attn.shape[0]
    row_total = QH * positions.shape[0]
    lanes = jnp.arange(128, dtype=jnp.int32)[None, :]
    own_pos = jnp.where(lanes == 0, positions[:, None] // 256, positions[:, None] % 256)

    frequency = np.exp(np.arange(HEAD // 2) * (-2.0 * math.log(THETA) / HEAD))
    angles = np.arange(row_total)[:, None] * frequency[None, :]
    tables = jnp.asarray(np.concatenate([np.cos(angles), np.sin(angles)], axis=1), jnp.float32)

    (
        row_normed, w_qkv, w_out, w_laurel, row_parts, w_gate_up, w_down, row_ffn, projected,
        queries, keys, values, mixed, latent, laurel_up, attn_out, joined,
    ) = attention_forward(
        own_pos.astype(jnp.bfloat16), w_attn, w_mlp, hidden_in, gains, head_gains, tables, 1
    )
    (
        result_out, d_vector_in, d_half, d_attn_low, d_laurel_low, other_gains, mlp_land,
        vec_land, late_wide, late_narrow,
    ) = ffn_layer(
        row_ffn, w_gate_up, w_down, joined, attn_out, laurel_up, gains, layer_vec, pl_gate,
        pl_proj, out_grad, shard_height, w_mlp.shape[1], 2,
    )
    d_hidden_part, all_gains, mlp_land, attn_land, vec_all = attention_backward(
        d_attn_low,
        d_laurel_low,
        d_half,
        (w_qkv, w_out, w_laurel),
        (queries, keys, values, mixed, latent, projected, row_normed, row_parts),
        tables,
        head_gains,
        hidden_in,
        gains,
        other_gains,
        (late_wide, late_narrow),
        mlp_land,
        vec_land,
        3,
    )
    grad_w_mlp, grad_w_attn, grad_gate_all, grad_proj_all, grad_hidden = finish_outputs(
        mlp_land, attn_land, vec_all, d_half, d_hidden_part, w_attn.shape[1]
    )
    grad_gains, grad_heads = all_gains[:6], all_gains[6, : 2 * HEAD].reshape(2, HEAD)
    return (
        result_out,
        grad_hidden,
        d_vector_in,
        grad_w_attn,
        grad_w_mlp,
        grad_gate_all,
        grad_proj_all,
        grad_gains,
        grad_heads,
    )


def solution(mesh):
    fits = mesh.shape["ctx"] == QH and mesh.shape["fsdp"] == 4
    body = per_device_split if fits else per_device
    return jax.shard_map(
        body,
        mesh=mesh,
        in_specs=(
            P(("fsdp", "ctx"), None),
            P(("fsdp", "ctx"), None),
            P(("fsdp", "ctx")),
            P(("fsdp", "ctx"), None),
            P(("fsdp", "ctx"), None),
            P(),
            P(),
            P(),
            P(),
            P(("fsdp", "ctx"), None),
        ),
        out_specs=(
            P(("fsdp", "ctx"), None),
            P(("fsdp", "ctx"), None),
            P(("fsdp", "ctx"), None),
            P(("fsdp", "ctx"), None),
            P(("fsdp", "ctx"), None),
            P(),
            P(),
            P(),
            P(),
        ),
        check_vma=False,
    )
```
